32 devices in a mesh: ctx: 8 (over y, x, core), head: 4 (over z).
Axes of the slice: x: 2, y: 2, z: 4, core: 2. Of those that a mesh axis runs over, the one named last changes fastest.
Arguments:
- queries: bfloat16 [8192, 2048], P('ctx', 'head'), may hold values from -4.5 to 4.5
- keys: bfloat16 [8192, 2048], P('ctx', 'head'), may hold values from -4.5 to 4.5
- values: bfloat16 [8192, 2048], P('ctx', 'head'), may hold values from -6 to 6
- out_weight: bfloat16 [2048, 2048], P('head'), may hold values from -0.5 to 0.5
Outputs:
- mixed: bfloat16 [8192, 2048], P(('ctx', 'head'))
The draws below stay inside these ranges and needn't reach their ends.
All inputs are finite; a program needn't handle non-finite values.
Results may differ from the reference program's by a relative error of at most 0.019.
Values may be sent and summed in bfloat16 or wider, within the bound.
No kernel may reach another device: no remote copies, remote signals or barrier semaphores. Data moves between devices by JAX's collectives and lax.ppermute only.
A program may use at most 64 MiB of HBM per device.

```python
import jax
import jax.numpy as jnp
from jax import lax

D = 2048
HEADS = 16
HEAD_SIZE = 128
WINDOW = 512
STRIDE = 16
BLOCK = 128
SUMCOLS = 8
SEQUENCE_TOKENS = 8192
N_HEAD = 4


def drawn_pair(key):
    width = HEADS * HEAD_SIZE
    query_seed = jax.random.fold_in(key, 101)
    keys_seed = jax.random.fold_in(key, 202)
    query_draw = jnp.clip(jax.random.normal(query_seed, (SEQUENCE_TOKENS, width), jnp.float32), -4.5, 4.5)
    keys_draw = jnp.clip(jax.random.normal(keys_seed, (SEQUENCE_TOKENS, width), jnp.float32), -4.5, 4.5)
    return (query_draw, keys_draw)


def draw_queries(key, part):
    return drawn_pair(key)[0].astype(jnp.bfloat16)


def draw_keys(key, part):
    return drawn_pair(key)[1].astype(jnp.bfloat16)


def block_levels(rng, dims, shards, low, largest):
    def one(dim, shards_of):
        draws = jax.random.uniform(jax.random.fold_in(jax.random.fold_in(rng, 6), dim), (shards_of,), jnp.float32, low / len(shards), largest / len(shards))
        return jnp.repeat(jnp.exp(draws), dims[dim] // shards_of).reshape((-1,) + (1,) * (len(dims) - dim - 1))

    loudness = one(*shards[0])
    for cut in shards[1:]:
        loudness = loudness * one(*cut)
    return loudness


def bell_draw(stream_key, shape, scale, most, shards=(), held_as=jnp.bfloat16):
    values = jax.random.normal(stream_key, shape, jnp.float32) * scale
    if len(shards) > 0:
        values = block_levels(stream_key, shape, shards, -0.22, 0.18) * values
    return jnp.clip(values, min=-most, max=most).astype(held_as)


def setup_inputs(seed: int = 0) -> dict:
    streams_of = jax.random.split(jax.random.key(seed), 5)
    return {
        "queries": draw_queries(jax.random.fold_in(streams_of[4], 71), 0),
        "keys": draw_keys(jax.random.fold_in(streams_of[4], 71), 0),
        "values": bell_draw(streams_of[2], (SEQUENCE_TOKENS, HEADS * HEAD_SIZE), 1.0, 6.0, ((0, 8), (1, 4))),
        "out_weight": bell_draw(streams_of[3], (HEADS * HEAD_SIZE, D), HEAD_SIZE ** -0.5, 0.5, ((0, 4),)),
    }


BIG_NEG = -1e30


def to_float(array):
    return array.astype(jnp.float32)


def round_trip(array):
    return lax.optimization_barrier(array.astype(jnp.bfloat16)).astype(jnp.float32)


def softmax_weighted(logit_scores, permitted_mask, value_rows, form):
    masked = jnp.where(permitted_mask, logit_scores, BIG_NEG)
    row_top = jnp.max(masked, axis=-1, keepdims=True)
    exponent = jnp.where(permitted_mask, jnp.exp(masked - row_top), 0.0)
    total = jnp.sum(exponent, axis=-1, keepdims=True)
    return jnp.einsum(form, round_trip(exponent), value_rows) / total


def local_head(query, key_rows, value_rows):
    score_scale = HEAD_SIZE ** -0.5
    blocks = SEQUENCE_TOKENS // WINDOW
    query_block_rows = to_float(query).reshape(blocks, WINDOW, HEAD_SIZE)
    padding = jnp.zeros((WINDOW, HEAD_SIZE), jnp.float32)
    key_ext = jnp.concatenate([padding, to_float(key_rows)]).reshape(blocks + 1, WINDOW, HEAD_SIZE)
    value_ext = jnp.concatenate([padding, to_float(value_rows)]).reshape(blocks + 1, WINDOW, HEAD_SIZE)
    paired_keys = jnp.concatenate([key_ext[:-1], key_ext[1:]], axis=1)
    paired_values = jnp.concatenate([value_ext[:-1], value_ext[1:]], axis=1)
    logit_scores = jnp.einsum("vix,vox->vio", query_block_rows, paired_keys) * score_scale
    block_ids = jnp.arange(blocks)[:, None, None]
    row_ids = jnp.arange(WINDOW)[None, :, None]
    col_ids = jnp.arange(2 * WINDOW)[None, None, :]
    query_pos = block_ids * WINDOW + row_ids
    key_pos = (block_ids - 1) * WINDOW + col_ids
    permitted_mask = (key_pos <= query_pos) & (key_pos > query_pos - WINDOW) & (key_pos >= 0)
    return softmax_weighted(logit_scores, permitted_mask, paired_values, "vzw,vwf->vzf").reshape(SEQUENCE_TOKENS, HEAD_SIZE)


def stride_head(query, key_rows, value_rows):
    score_scale = HEAD_SIZE ** -0.5
    row_count = SEQUENCE_TOKENS // STRIDE
    query_phase = to_float(query).reshape(row_count, STRIDE, HEAD_SIZE).transpose(1, 0, 2)
    key_phase = to_float(key_rows).reshape(row_count, STRIDE, HEAD_SIZE).transpose(1, 0, 2)
    value_phase = to_float(value_rows).reshape(row_count, STRIDE, HEAD_SIZE).transpose(1, 0, 2)
    order = jnp.arange(row_count)
    permitted_mask = order[None, :] <= order[:, None]

    def one_phase(operands):
        phase_query, phase_keys, phase_values = operands
        logit_scores = jnp.einsum("qd,kd->qk", phase_query, phase_keys) * score_scale
        return softmax_weighted(logit_scores, permitted_mask, phase_values, "qk,kd->qd")

    result = lax.map(one_phase, (query_phase, key_phase, value_phase))
    return result.transpose(1, 0, 2).reshape(SEQUENCE_TOKENS, HEAD_SIZE)


def summary_head(query, key_rows, value_rows):
    score_scale = HEAD_SIZE ** -0.5
    total_keys = SEQUENCE_TOKENS // BLOCK * SUMCOLS
    key_sum = to_float(key_rows).reshape(SEQUENCE_TOKENS // BLOCK, BLOCK, HEAD_SIZE)[:, BLOCK - SUMCOLS:].reshape(total_keys, HEAD_SIZE)
    value_sum = to_float(value_rows).reshape(SEQUENCE_TOKENS // BLOCK, BLOCK, HEAD_SIZE)[:, BLOCK - SUMCOLS:].reshape(total_keys, HEAD_SIZE)
    index = jnp.arange(total_keys)
    key_pos = index // SUMCOLS * BLOCK + BLOCK - SUMCOLS + index % SUMCOLS
    step_rows = min(SEQUENCE_TOKENS, 512)
    count_blocks = SEQUENCE_TOKENS // step_rows
    query_block_rows = to_float(query).reshape(count_blocks, step_rows, HEAD_SIZE)
    key_blocks = to_float(key_rows).reshape(count_blocks, step_rows, HEAD_SIZE)
    value_blocks = to_float(value_rows).reshape(count_blocks, step_rows, HEAD_SIZE)

    def one_block(operands):
        number, block_query, block_keys, block_values = operands
        query_pos = number * step_rows + jnp.arange(step_rows)
        logit_scores = jnp.einsum("qd,kd->qk", block_query, key_sum) * score_scale
        permitted_mask = key_pos[None, :] <= query_pos[:, None]
        own_score = jnp.sum(block_query * block_keys, axis=-1) * score_scale
        own_allowed = query_pos % BLOCK < BLOCK - SUMCOLS
        masked = jnp.where(permitted_mask, logit_scores, BIG_NEG)
        own_masked = jnp.where(own_allowed, own_score, BIG_NEG)
        row_top = jnp.maximum(jnp.max(masked, axis=-1), own_masked)
        exponent = jnp.where(permitted_mask, jnp.exp(masked - row_top[:, None]), 0.0)
        own_exponent = jnp.where(own_allowed, jnp.exp(own_masked - row_top), 0.0)
        total = jnp.sum(exponent, axis=-1) + own_exponent
        result = jnp.einsum("qk,kd->qd", round_trip(exponent), value_sum)
        result = result + round_trip(own_exponent)[:, None] * block_values
        return result / total[:, None]

    result = lax.map(one_block, (jnp.arange(count_blocks), query_block_rows, key_blocks, value_blocks))
    return result.reshape(SEQUENCE_TOKENS, HEAD_SIZE)


def reference(queries, keys, values, out_weight):
    def split_heads(array):
        return array.reshape(SEQUENCE_TOKENS, HEADS, HEAD_SIZE).transpose(1, 0, 2)

    def per_head(operands):
        query, key_rows, value_rows = operands
        return local_head(query, key_rows, value_rows) + stride_head(query, key_rows, value_rows) + summary_head(query, key_rows, value_rows)

    sections = lax.map(per_head, (split_heads(queries), split_heads(keys), split_heads(values)))
    attended = sections.transpose(1, 0, 2).reshape(SEQUENCE_TOKENS, HEADS * HEAD_SIZE).astype(jnp.bfloat16)
    group_width = HEADS // N_HEAD * HEAD_SIZE
    attended_groups = attended.reshape(SEQUENCE_TOKENS, N_HEAD, group_width).transpose(1, 0, 2)
    weight_groups = out_weight.reshape(N_HEAD, group_width, D)

    def add_group(carry, operands):
        group_rows, group_weight = operands
        partial_value = jnp.dot(group_rows, group_weight, preferred_element_type=jnp.float32)
        return carry + round_trip(partial_value), None

    summed, unused = lax.scan(add_group, jnp.zeros((SEQUENCE_TOKENS, D), jnp.float32), (attended_groups, weight_groups))
    return summed.astype(jnp.bfloat16)
```

```python
import functools
import math

import jax
import jax.numpy as jnp
from jax import lax
from jax.experimental import pallas as pl
from jax.experimental.pallas import tpu as pltpu
from jax.sharding import PartitionSpec as P

HEAD_SIZE = 128
WINDOW = 512
STRIDE = 16
BLOCK = 128
SUMCOLS = 8

BIG_NEG = -1e30
TILE = 256
LOG_SCALE = HEAD_SIZE ** (-0.5) * math.log2(math.e)
F32 = jnp.float32
BF16 = jnp.bfloat16


def params(mib):
    return pltpu.CompilerParams(vmem_limit_bytes=mib * 1024 * 1024)


def cost(flops, bytes_accessed, exps=0):
    return pl.CostEstimate(
        flops=int(flops), bytes_accessed=int(bytes_accessed), transcendentals=int(exps)
    )


def iota2(shape, dim):
    return lax.broadcasted_iota(jnp.int32, shape, dim)


def scores(query, key_rows):
    return lax.dot_general(query, key_rows, (((1,), (1,)), ((), ())), preferred_element_type=F32)


def dot(left, right):
    return jnp.dot(left, right, preferred_element_type=F32)


def regroup_matrix():
    rows = iota2((TILE, TILE), 0)
    cols = iota2((TILE, TILE), 1)
    return (cols == (rows & 15) * 16 + (rows >> 4)).astype(BF16)


def with_ones(value_rows):
    return jnp.concatenate([value_rows, jnp.ones_like(value_rows)], axis=1)


def weighted(score_blocks, value_blocks, extra=None):
    top = functools.reduce(jnp.maximum, score_blocks)
    top = jnp.max(top, axis=-1, keepdims=True)
    if extra is not None:
        top = jnp.maximum(top, extra[0])
    total = None
    for block, value_block in zip(score_blocks, value_blocks):
        weights = jnp.exp2((block - top) * LOG_SCALE).astype(BF16)
        part = dot(weights, value_block)
        total = part if total is None else total + part
    if extra is not None:
        own = jnp.exp2((extra[0] - top) * LOG_SCALE).astype(BF16).astype(F32)
        total = total + own * extra[1].astype(F32)
    return total[:, :HEAD_SIZE] / total[:, HEAD_SIZE:]


def prep_kernel(q_ref, k_ref, v_ref, *refs, rim_start, chunks):
    send_refs, rim_ref, sum_ref = refs[:chunks], refs[chunks], refs[chunks + 1]
    step = pl.program_id(0)
    matrix = regroup_matrix()
    ctx, _, per, rows, width = send_refs[0].shape
    for number, ref in enumerate((q_ref, k_ref, v_ref)):
        grouped = dot(matrix, ref[...]).astype(BF16)
        for chunk in range(chunks):
            send_refs[chunk][:, number] = grouped[:, chunk * width : (chunk + 1) * width].reshape(
                ctx, per, rows, width
            )
    picks = TILE // BLOCK * SUMCOLS
    row = iota2((picks, TILE), 0)
    col = iota2((picks, TILE), 1)
    pick = (col == (row // SUMCOLS) * BLOCK + BLOCK - SUMCOLS + row % SUMCOLS).astype(BF16)
    sum_ref[0] = dot(pick, k_ref[...]).astype(BF16)
    sum_ref[1] = dot(pick, v_ref[...]).astype(BF16)

    @pl.when(step >= rim_start)
    def _():
        rim_ref[0] = k_ref[...]
        rim_ref[1] = v_ref[...]


def prepare(queries, keys, values, ctx, chunks):
    tokens_dev, width = queries.shape
    tiles = tokens_dev // TILE
    per = STRIDE // ctx
    rows = tokens_dev // STRIDE
    part = width // chunks
    rim_start = tiles - WINDOW // TILE
    picks = TILE // BLOCK * SUMCOLS
    source = pl.BlockSpec((TILE, width), lambda b: (b, 0))
    return pl.pallas_call(
        functools.partial(prep_kernel, rim_start=rim_start, chunks=chunks),
        grid=(tiles,),
        in_specs=[source] * 3,
        out_specs=[
            pl.BlockSpec((ctx, 3, per, TILE // STRIDE, part), lambda b: (0, 0, 0, b, 0))
        ]
        * chunks
        + [
            pl.BlockSpec((2, TILE, width), lambda b: (0, jnp.maximum(b - rim_start, 0), 0)),
            pl.BlockSpec((2, picks, width), lambda b: (0, b, 0)),
        ],
        out_shape=[jax.ShapeDtypeStruct((ctx, 3, per, rows, part), BF16)] * chunks
        + [
            jax.ShapeDtypeStruct((2, WINDOW, width), BF16),
            jax.ShapeDtypeStruct((2, tiles * picks, width), BF16),
        ],
        compiler_params=params(24),
        cost_estimate=cost(6 * tokens_dev * TILE * width, 16 * tokens_dev * width),
        name="prepare",
    )(queries, keys, values)


def home_kernel(place_ref, q_ref, k_ref, v_ref, rim_ref, sum_ref, o_ref):
    place = place_ref[0]
    tokens_dev = q_ref.shape[0]
    back = WINDOW // TILE
    key_blocks = [rim_ref[0, e * TILE : (e + 1) * TILE] for e in range(back)]
    value_blocks = [with_ones(rim_ref[1, e * TILE : (e + 1) * TILE]) for e in range(back)]
    for e in range(tokens_dev // TILE):
        key_blocks.append(k_ref[e * TILE : (e + 1) * TILE])
        value_blocks.append(with_ones(v_ref[e * TILE : (e + 1) * TILE]))
    order = gathered_order(sum_ref.shape[1])
    sum_keys = jnp.concatenate([sum_ref[0, i] for i in order])
    sum_values = with_ones(jnp.concatenate([sum_ref[1, i] for i in order]))
    row = iota2((TILE, TILE), 0)
    col = iota2((TILE, TILE), 1)
    sum_col = iota2((TILE, sum_keys.shape[0]), 1)
    for b in range(tokens_dev // TILE):
        query = q_ref[b * TILE : (b + 1) * TILE]
        blocks = []
        for e in range(back + 1):
            block = scores(query, key_blocks[b + e])
            allowed = None
            if e == 0:
                allowed = col > row
            if e == back:
                allowed = col <= row
            if b + e < back:
                held = place > 0
                allowed = held if allowed is None else allowed & held
            if allowed is not None:
                block = jnp.where(allowed, block, BIG_NEG)
            blocks.append(block)
        local = weighted(blocks, value_blocks[b : b + back + 1])
        pos = place * tokens_dev + b * TILE + iota2((TILE, 1), 0)
        within = pos % BLOCK
        held = pos // BLOCK * SUMCOLS + jnp.maximum(within - (BLOCK - SUMCOLS - 1), 0)
        block = jnp.where(sum_col < held, scores(query, sum_keys), BIG_NEG)
        own_key = key_blocks[b + back].astype(F32)
        own = jnp.sum(query.astype(F32) * own_key, axis=-1, keepdims=True)
        own = jnp.where(within < BLOCK - SUMCOLS, own, BIG_NEG)
        summary = weighted([block], [sum_values], (own, value_blocks[b + back]))
        o_ref[b * TILE : (b + 1) * TILE] = local + summary


def home_sections(place, queries, keys, values, rim, summary):
    tokens_dev, width = queries.shape
    heads = width // HEAD_SIZE
    pieces, picks = summary.shape[1:3]
    total = pieces * picks
    own = pl.BlockSpec((tokens_dev, HEAD_SIZE), lambda h: (0, h))
    pairs = tokens_dev * (WINDOW + TILE + total) * heads
    return pl.pallas_call(
        home_kernel,
        grid=(heads,),
        in_specs=[
            pl.BlockSpec(memory_space=pltpu.SMEM),
            own,
            own,
            own,
            pl.BlockSpec((2, WINDOW, HEAD_SIZE), lambda h: (0, 0, h)),
            pl.BlockSpec((2, pieces, picks, HEAD_SIZE), lambda h: (0, 0, 0, h)),
        ],
        out_specs=own,
        out_shape=jax.ShapeDtypeStruct((tokens_dev, width), F32),
        compiler_params=params(32),
        cost_estimate=cost(8 * pairs * HEAD_SIZE, 14 * tokens_dev * width, pairs),
        name="home",
    )(place, queries, keys, values, rim, summary)


def stride_kernel(x_ref, o_ref):
    ctx, _, _, rows, _ = x_ref.shape
    count = ctx * rows
    query = x_ref[:, 0, 0].reshape(count, HEAD_SIZE)
    key_rows = x_ref[:, 1, 0].reshape(count, HEAD_SIZE)
    value_rows = with_ones(x_ref[:, 2, 0].reshape(count, HEAD_SIZE))
    row = iota2((TILE, TILE), 0)
    col = iota2((TILE, TILE), 1)
    for b in range(count // TILE):
        part = query[b * TILE : (b + 1) * TILE]
        blocks = [scores(part, key_rows[e * TILE : (e + 1) * TILE]) for e in range(b + 1)]
        blocks[b] = jnp.where(col <= row, blocks[b], BIG_NEG)
        result = weighted(
            blocks, [value_rows[e * TILE : (e + 1) * TILE] for e in range(b + 1)]
        ).astype(BF16)
        sources = TILE // rows
        o_ref[b * sources : (b + 1) * sources, 0] = result.reshape(sources, rows, HEAD_SIZE)


def stride_attend(moved):
    ctx, _, per, rows, width = moved.shape
    count = ctx * rows
    heads = width // HEAD_SIZE
    pairs = per * heads * count * (count + TILE) // 2
    return pl.pallas_call(
        stride_kernel,
        grid=(heads, per),
        in_specs=[pl.BlockSpec((ctx, 3, 1, rows, HEAD_SIZE), lambda h, r: (0, 0, r, 0, h))],
        out_specs=pl.BlockSpec((ctx, 1, rows, HEAD_SIZE), lambda h, r: (0, r, 0, h)),
        out_shape=jax.ShapeDtypeStruct((ctx, per, rows, width), BF16),
        compiler_params=params(32),
        cost_estimate=cost(8 * pairs * HEAD_SIZE, 8 * per * count * width, pairs),
        name="stride",
    )(moved)


def combine_kernel(home_ref, back_ref, o_ref):
    width = home_ref.shape[1]
    back = dot(regroup_matrix(), back_ref[...].reshape(TILE, width))
    o_ref[...] = (home_ref[...] + back).astype(BF16)


def combine(home, back, chunk):
    tokens_dev = home.shape[0]
    ctx, per, _, width = back.shape
    return pl.pallas_call(
        combine_kernel,
        grid=(tokens_dev // TILE,),
        in_specs=[
            pl.BlockSpec((TILE, width), lambda b: (b, chunk)),
            pl.BlockSpec((ctx, per, TILE // STRIDE, width), lambda b: (0, 0, b, 0)),
        ],
        out_specs=pl.BlockSpec((TILE, width), lambda b: (b, 0)),
        out_shape=jax.ShapeDtypeStruct((tokens_dev, width), BF16),
        compiler_params=params(24),
        cost_estimate=cost(2 * tokens_dev * TILE * width, 8 * tokens_dev * width),
        name="combine",
    )(home, back)


def project_kernel(side_ref, *refs, chunks):
    moved_refs = refs[:chunks]
    mine_ref, other_ref, o_ref = refs[chunks:]

    def add_up(weight_ref):
        total = None
        for group in range(weight_ref.shape[0]):
            partial_value = None
            for chunk, ref in enumerate(moved_refs):
                width = ref.shape[2]
                part = dot(ref[group], weight_ref[group, chunk * width : (chunk + 1) * width])
                partial_value = part if partial_value is None else partial_value + part
            rounded = partial_value.astype(BF16).astype(F32)
            total = rounded if total is None else total + rounded
        o_ref[...] = total.astype(BF16)

    @pl.when(pl.program_id(0) == 0)
    def _():
        add_up(mine_ref)

    @pl.when(pl.program_id(0) == 1)
    def _():
        add_up(other_ref)


def project(side, moved, mine, other):
    groups, tokens, part = moved[0].shape
    width, half = mine.shape[1:]
    tile = min(half, 512)
    tiles = half // tile
    return pl.pallas_call(
        functools.partial(project_kernel, chunks=len(moved)),
        grid_spec=pltpu.PrefetchScalarGridSpec(
            num_scalar_prefetch=1,
            grid=(2, tiles),
            in_specs=[pl.BlockSpec((groups, tokens, part), lambda s, j, side: (0, 0, 0))]
            * len(moved)
            + [
                pl.BlockSpec(
                    (groups, width, tile),
                    lambda s, j, side: (0, 0, jnp.where(s == 0, j, tiles - 1)),
                ),
                pl.BlockSpec(
                    (groups, width, tile), lambda s, j, side: (0, 0, jnp.where(s == 0, 0, j))
                ),
            ],
            out_specs=pl.BlockSpec(
                (tokens, tile), lambda s, j, side: (0, (s ^ side[0]) * tiles + j)
            ),
        ),
        out_shape=jax.ShapeDtypeStruct((tokens, 2 * half), BF16),
        compiler_params=params(40),
        cost_estimate=cost(
            4 * groups * tokens * width * half,
            4 * groups * width * half + 2 * groups * tokens * width + 4 * tokens * half,
        ),
        name="project",
    )(side, *moved, mine, other)


def gathered_order(count):
    if count & (count - 1):
        return list(range(count))
    bits = count.bit_length() - 1
    return [sum(((i >> b) & 1) << (bits - 1 - b) for b in range(bits)) for i in range(count)]


def gather_ctx(rows):
    count = lax.axis_size("ctx")
    if count & (count - 1):
        return lax.all_gather(rows, "ctx", axis=1)
    place = lax.axis_index("ctx")
    held = rows[:, None]
    distance = count // 2
    while distance:
        received = lax.ppermute(held, "ctx", [(i, i ^ distance) for i in range(count)])
        low = (place & distance) == 0
        held = jnp.concatenate(
            [jnp.where(low, held, received), jnp.where(low, received, held)], axis=1
        )
        distance //= 2
    return held


def stride_general(queries, keys, values):
    tokens_dev, width = queries.shape
    heads = width // HEAD_SIZE
    ctx = lax.axis_size("ctx")
    copies = max(ctx // STRIDE, 1)
    rows = tokens_dev // STRIDE
    held_rows = ctx * rows // copies
    own_copy = lax.axis_index("ctx") // STRIDE
    query_pos = (jnp.arange(held_rows) // (rows // copies)) * rows
    query_pos = query_pos + (jnp.arange(held_rows) % (rows // copies)) * copies + own_copy
    shaped = queries.reshape(1, rows // copies, ctx, width)
    query = lax.all_to_all(shaped, "ctx", split_axis=2, concat_axis=1, tiled=True)
    query = query.reshape(held_rows, heads, HEAD_SIZE)
    both = jnp.stack([keys, values]).reshape(2, rows, 1, STRIDE, width)
    both = jnp.broadcast_to(both, (2, rows, copies, STRIDE, width)).reshape(2, rows, ctx, width)
    both = lax.all_to_all(both, "ctx", split_axis=2, concat_axis=1, tiled=True)
    both = both.reshape(2, ctx * rows, heads, HEAD_SIZE)
    allowed = jnp.arange(ctx * rows)[None, :] <= query_pos[:, None]

    def one_head(operands):
        head_query, head_keys, head_values = operands
        masked = jnp.where(allowed, scores(head_query, head_keys), BIG_NEG)
        return weighted([masked], [with_ones(head_values)])

    result = lax.map(
        one_head,
        (query.transpose(1, 0, 2), both[0].transpose(1, 0, 2), both[1].transpose(1, 0, 2)),
    )
    result = result.transpose(1, 0, 2).reshape(ctx, rows // copies, 1, width).astype(BF16)
    back = lax.all_to_all(result, "ctx", split_axis=0, concat_axis=2, tiled=True)
    return back.reshape(tokens_dev, width)


def body(queries, keys, values, out_weight, chunks):
    tokens_dev, width = queries.shape
    ctx = lax.axis_size("ctx")
    groups = lax.axis_size("head")
    place = lax.axis_index("ctx")
    place_word = place.astype(jnp.int32).reshape(1)
    side = place % 2
    sibling = [(i, i ^ 1) for i in range(ctx)]

    half = out_weight.shape[1] // 2
    weight_half = lax.dynamic_slice_in_dim(out_weight, side * half, half, axis=1)
    mine = lax.all_gather(weight_half, "head", axis=0)
    other = lax.ppermute(mine, "ctx", sibling)

    if ctx > STRIDE:
        stride_out = stride_general(queries, keys, values)
        rim = jnp.stack([keys[tokens_dev - WINDOW :], values[tokens_dev - WINDOW :]])
        picked = jnp.stack([keys, values]).reshape(2, tokens_dev // BLOCK, BLOCK, width)
        picked = picked[:, :, BLOCK - SUMCOLS :].reshape(2, -1, width)
        send = None
    else:
        *send, rim, picked = prepare(queries, keys, values, ctx, chunks)
        send = [
            lax.all_to_all(part, "ctx", split_axis=0, concat_axis=0, tiled=True) for part in send
        ]
    before = lax.ppermute(rim, "ctx", [(i, i + 1) for i in range(ctx - 1)])
    summary = gather_ctx(picked)
    home = home_sections(place_word, queries, keys, values, before, summary)

    moved = []
    for chunk in range(chunks):
        if send is None:
            attended = (home + stride_out.astype(F32)).astype(BF16)
        else:
            result = stride_attend(send[chunk])
            back = lax.all_to_all(result, "ctx", split_axis=0, concat_axis=0, tiled=True)
            attended = combine(home, back, chunk)
        attended = attended.reshape(groups, tokens_dev // groups, width // chunks)
        moved.append(lax.all_to_all(attended, "head", split_axis=0, concat_axis=0, tiled=True))
    return project(side.astype(jnp.int32).reshape(1), moved, mine, other)


def solution(mesh):
    chunks = 1
    placed = (P("ctx", "head"), P("ctx", "head"), P("ctx", "head"), P("head", None))
    return jax.shard_map(
        functools.partial(body, chunks=chunks),
        mesh=mesh,
        in_specs=placed,
        out_specs=P(("ctx", "head"), None),
        check_vma=False,
    )
```

```python
import functools
import math

import jax
import jax.numpy as jnp
from jax import lax
from jax.experimental import pallas as pl
from jax.experimental.pallas import tpu as pltpu
from jax.sharding import PartitionSpec as P

HEADS = 16
HEAD_SIZE = 128
WINDOW = 512
STRIDE = 16
BLOCK = 128
SUMCOLS = 8

BIG_NEG = -1e30
TILE = 256
LOG_SCALE = HEAD_SIZE ** (-0.5) * math.log2(math.e)
F32 = jnp.float32
BF16 = jnp.bfloat16


def params(mib):
    return pltpu.CompilerParams(vmem_limit_bytes=mib * 1024 * 1024)


MARK = jax.ShapeDtypeStruct((8, 128), F32)


def mark_spec():
    return pl.BlockSpec(MARK.shape, lambda *place: (0, 0))


def moments(arrays):
    return [pl.BlockSpec(memory_space=pl.ANY)] * len(arrays)


def after(array, others):
    anywhere = pl.BlockSpec(memory_space=pl.ANY)
    return pl.pallas_call(
        lambda *refs: None,
        in_specs=[anywhere] * (1 + len(others)),
        out_specs=anywhere,
        out_shape=jax.ShapeDtypeStruct(array.shape, array.dtype),
        input_output_aliases={0: 0},
        compiler_params=params(2),
        cost_estimate=cost(0, 0),
        name="after",
    )(array, *others)


def cost(flops, bytes_accessed, exps=0):
    return pl.CostEstimate(
        flops=int(flops), bytes_accessed=int(bytes_accessed), transcendentals=int(exps)
    )


def partner(place, slot, count):
    assert count & (count - 1) == 0
    return place ^ slot


def iota2(shape, dim):
    return lax.broadcasted_iota(jnp.int32, shape, dim)


def scores(query, key_rows):
    return lax.dot_general(query, key_rows, (((1,), (1,)), ((), ())), preferred_element_type=F32)


def dot(left, right):
    return jnp.dot(left, right, preferred_element_type=F32)


def regroup_matrix():
    rows = iota2((TILE, TILE), 0)
    cols = iota2((TILE, TILE), 1)
    return (cols == (rows & 15) * 16 + (rows >> 4)).astype(BF16)


def with_ones(value_rows):
    return jnp.concatenate([value_rows, jnp.ones_like(value_rows)], axis=1)


def weighted(score_blocks, value_blocks, extra=None):
    top = functools.reduce(jnp.maximum, score_blocks)
    top = jnp.max(top, axis=-1, keepdims=True)
    if extra is not None:
        top = jnp.maximum(top, extra[0])
    total = None
    for block, value_block in zip(score_blocks, value_blocks):
        weights = jnp.exp2((block - top) * LOG_SCALE).astype(BF16)
        part = dot(weights, value_block)
        total = part if total is None else total + part
    if extra is not None:
        own = jnp.exp2((extra[0] - top) * LOG_SCALE).astype(BF16).astype(F32)
        total = total + own * extra[1].astype(F32)
    return total[:, :HEAD_SIZE] / total[:, HEAD_SIZE:]


def prep_kernel(q_ref, k_ref, v_ref, *refs, rim_start, chunks):
    send_refs, rim_ref, sum_ref = refs[:chunks], refs[chunks], refs[chunks + 1]
    step = pl.program_id(0)
    matrix = regroup_matrix()
    ctx, _, per, rows, width = send_refs[0].shape
    for number, ref in enumerate((q_ref, k_ref, v_ref)):
        grouped = dot(matrix, ref[...]).astype(BF16)
        for chunk in range(chunks):
            send_refs[chunk][:, number] = grouped[:, chunk * width : (chunk + 1) * width].reshape(
                ctx, per, rows, width
            )
    picks = TILE // BLOCK * SUMCOLS
    row = iota2((picks, TILE), 0)
    col = iota2((picks, TILE), 1)
    pick = (col == (row // SUMCOLS) * BLOCK + BLOCK - SUMCOLS + row % SUMCOLS).astype(BF16)
    sum_ref[0] = dot(pick, k_ref[...]).astype(BF16)
    sum_ref[1] = dot(pick, v_ref[...]).astype(BF16)

    @pl.when(step >= rim_start)
    def _():
        rim_ref[0] = k_ref[...]
        rim_ref[1] = v_ref[...]


def prepare(queries, keys, values, ctx, chunks):
    tokens_dev, width = queries.shape
    tiles = tokens_dev // TILE
    per = STRIDE // ctx
    rows = tokens_dev // STRIDE
    part = width // chunks
    rim_start = tiles - WINDOW // TILE
    picks = TILE // BLOCK * SUMCOLS
    source = pl.BlockSpec((TILE, width), lambda b: (b, 0))
    return pl.pallas_call(
        functools.partial(prep_kernel, rim_start=rim_start, chunks=chunks),
        grid=(tiles,),
        in_specs=[source] * 3,
        out_specs=[
            pl.BlockSpec((ctx, 3, per, TILE // STRIDE, part), lambda b: (0, 0, 0, b, 0))
        ]
        * chunks
        + [
            pl.BlockSpec((2, TILE, width), lambda b: (0, jnp.maximum(b - rim_start, 0), 0)),
            pl.BlockSpec((2, picks, width), lambda b: (0, b, 0)),
        ],
        out_shape=[jax.ShapeDtypeStruct((ctx, 3, per, rows, part), BF16)] * chunks
        + [
            jax.ShapeDtypeStruct((2, WINDOW, width), BF16),
            jax.ShapeDtypeStruct((2, tiles * picks, width), BF16),
        ],
        compiler_params=params(60),
        cost_estimate=cost(6 * tokens_dev * TILE * width, 16 * tokens_dev * width),
        name="prepare",
    )(queries, keys, values)


def home_kernel(place_ref, q_ref, k_ref, v_ref, rim_ref, sum_ref, *refs, order):
    o_ref, mark_ref = refs[-2:]
    mark_ref[...] = jnp.zeros_like(mark_ref)
    place = place_ref[0]
    tokens_dev = q_ref.shape[0]
    back = WINDOW // TILE
    key_blocks = [rim_ref[0, e * TILE : (e + 1) * TILE] for e in range(back)]
    value_blocks = [with_ones(rim_ref[1, e * TILE : (e + 1) * TILE]) for e in range(back)]
    for e in range(tokens_dev // TILE):
        key_blocks.append(k_ref[e * TILE : (e + 1) * TILE])
        value_blocks.append(with_ones(v_ref[e * TILE : (e + 1) * TILE]))
    pieces, picks = sum_ref.shape[1:3]
    sum_keys = sum_ref[0].reshape(pieces * picks, HEAD_SIZE)
    sum_values = with_ones(sum_ref[1].reshape(pieces * picks, HEAD_SIZE))
    sum_col = jnp.concatenate(
        [iota2((TILE, picks), 1) + (place ^ i) * picks for i in order], axis=1
    )
    row = iota2((TILE, TILE), 0)
    col = iota2((TILE, TILE), 1)
    for b in range(tokens_dev // TILE):
        query = q_ref[b * TILE : (b + 1) * TILE]
        blocks = []
        for e in range(back + 1):
            block = scores(query, key_blocks[b + e])
            allowed = None
            if e == 0:
                allowed = col > row
            if e == back:
                allowed = col <= row
            if b + e < back:
                held = place > 0
                allowed = held if allowed is None else allowed & held
            if allowed is not None:
                block = jnp.where(allowed, block, BIG_NEG)
            blocks.append(block)
        local = weighted(blocks, value_blocks[b : b + back + 1])
        pos = place * tokens_dev + b * TILE + iota2((TILE, 1), 0)
        within = pos % BLOCK
        held = pos // BLOCK * SUMCOLS + jnp.maximum(within - (BLOCK - SUMCOLS - 1), 0)
        block = jnp.where(sum_col < held, scores(query, sum_keys), BIG_NEG)
        own_key = key_blocks[b + back].astype(F32)
        own = jnp.sum(query.astype(F32) * own_key, axis=-1, keepdims=True)
        own = jnp.where(within < BLOCK - SUMCOLS, own, BIG_NEG)
        summary = weighted([block], [sum_values], (own, value_blocks[b + back]))
        o_ref[b * TILE : (b + 1) * TILE] = local + summary


def home_sections(place, queries, keys, values, rim, summary, order, chunk, chunks, waits):
    tokens_dev, width = queries.shape
    heads = width // chunks // HEAD_SIZE
    first = chunk * heads
    pieces, picks = summary.shape[1:3]
    total = pieces * picks
    own = pl.BlockSpec((tokens_dev, HEAD_SIZE), lambda h: (0, first + h))
    pairs = tokens_dev * (WINDOW + TILE + total) * heads
    return pl.pallas_call(
        functools.partial(home_kernel, order=order),
        grid=(heads,),
        in_specs=[
            pl.BlockSpec(memory_space=pltpu.SMEM),
            own,
            own,
            own,
            pl.BlockSpec((2, WINDOW, HEAD_SIZE), lambda h: (0, 0, first + h)),
            pl.BlockSpec((2, pieces, picks, HEAD_SIZE), lambda h: (0, 0, 0, first + h)),
        ]
        + moments(waits),
        out_specs=[pl.BlockSpec((tokens_dev, HEAD_SIZE), lambda h: (0, h)), mark_spec()],
        out_shape=[jax.ShapeDtypeStruct((tokens_dev, heads * HEAD_SIZE), F32), MARK],
        compiler_params=params(60),
        cost_estimate=cost(8 * pairs * HEAD_SIZE, 14 * tokens_dev * width, pairs),
        name="home",
    )(place, queries, keys, values, rim, summary, *waits)


def stride_kernel(place_ref, x_ref, *refs):
    ctx, _, _, rows, width = x_ref.shape
    o_refs, mark_ref, held_ref = refs[-ctx - 2 : -2], refs[-2], refs[-1]
    mark_ref[...] = jnp.zeros_like(mark_ref)
    count = ctx * rows
    row = iota2((TILE, TILE), 0)
    col = iota2((TILE, TILE), 1)
    sources = TILE // rows
    units = []
    for head in range(width // HEAD_SIZE):
        lanes = slice(head * HEAD_SIZE, (head + 1) * HEAD_SIZE)
        query = x_ref[:, 0, 0, :, lanes].reshape(count, HEAD_SIZE)
        key_rows = x_ref[:, 1, 0, :, lanes].reshape(count, HEAD_SIZE)
        value_rows = with_ones(x_ref[:, 2, 0, :, lanes].reshape(count, HEAD_SIZE))
        for b in range(count // TILE):
            part = query[b * TILE : (b + 1) * TILE]
            blocks = [scores(part, key_rows[e * TILE : (e + 1) * TILE]) for e in range(b + 1)]
            blocks[b] = jnp.where(col <= row, blocks[b], BIG_NEG)
            units.append((lanes, b, blocks, value_rows))
    for lanes, b, blocks, value_rows in units:
        result = weighted(
            blocks, [value_rows[e * TILE : (e + 1) * TILE] for e in range(b + 1)]
        ).astype(BF16)
        held_ref[b * sources : (b + 1) * sources, :, lanes] = result.reshape(
            sources, rows, HEAD_SIZE
        )
    for slot in range(ctx):
        o_refs[slot][0] = held_ref[partner(place_ref[0], slot, ctx)]


def stride_attend(place, moved, waits):
    ctx, _, per, rows, width = moved.shape
    count = ctx * rows
    pairs = per * (width // HEAD_SIZE) * count * (count + TILE) // 2
    return pl.pallas_call(
        stride_kernel,
        grid=(per,),
        in_specs=[
            pl.BlockSpec(memory_space=pltpu.SMEM),
            pl.BlockSpec((ctx, 3, 1, rows, width), lambda r: (0, 0, r, 0, 0)),
        ]
        + moments(waits),
        out_specs=[pl.BlockSpec((1, rows, width), lambda r: (r, 0, 0))] * ctx + [mark_spec()],
        out_shape=[jax.ShapeDtypeStruct((per, rows, width), BF16)] * ctx + [MARK],
        scratch_shapes=[pltpu.VMEM((ctx, rows, width), BF16)],
        compiler_params=params(24),
        cost_estimate=cost(8 * pairs * HEAD_SIZE, 8 * per * count * width, pairs),
        name="stride",
    )(place, moved, *waits)


def combine_kernel(seat_ref, home_ref, *refs, slots, ctx):
    back_refs, o_refs, mark_ref = refs[:ctx], refs[-slots - 1 : -1], refs[-1]
    mark_ref[...] = jnp.zeros_like(mark_ref)
    tokens_dev, width = home_ref.shape
    size = tokens_dev // slots
    per = STRIDE // ctx
    token = iota2((TILE, TILE), 0)
    col = iota2((TILE, TILE), 1)
    group = col >> 4
    residue = partner(seat_ref[1], group // per, ctx) * per + group % per
    matrix = (token == (col & 15) * 16 + residue).astype(BF16)
    for slot in range(slots):
        owner = partner(seat_ref[0], slot, slots)
        for b in range(size // TILE):
            first = owner * (size // TILE) + b
            here = pl.ds(pl.multiple_of(first * STRIDE, STRIDE), STRIDE)
            rows = [ref[r, here] for ref in back_refs for r in range(per)]
            back = dot(matrix, jnp.concatenate(rows))
            home = home_ref[pl.ds(pl.multiple_of(first * TILE, TILE), TILE)]
            o_refs[slot][b * TILE : (b + 1) * TILE] = (home + back).astype(BF16)


def combine(seat, home, backs, slots, waits):
    tokens_dev, width = home.shape
    size = tokens_dev // slots
    return pl.pallas_call(
        functools.partial(combine_kernel, slots=slots, ctx=len(backs)),
        in_specs=[pl.BlockSpec(memory_space=pltpu.SMEM)]
        + [pl.BlockSpec(memory_space=pltpu.VMEM)] * (1 + len(backs))
        + moments(waits),
        out_specs=[pl.BlockSpec(memory_space=pltpu.VMEM)] * (slots + 1),
        out_shape=[jax.ShapeDtypeStruct((size, width), BF16)] * slots + [MARK],
        compiler_params=params(24),
        cost_estimate=cost(2 * tokens_dev * TILE * width, 8 * tokens_dev * width),
        name="combine",
    )(seat, home, *backs, *waits)


def project_kernel(side_ref, *refs, slots, chunks):
    moved_refs, refs = refs[: slots * chunks], refs[slots * chunks :]
    mine_refs, other_refs, o_ref = refs[:chunks], refs[chunks : 2 * chunks], refs[-1]

    def add_up(weight_refs):
        total = None
        for slot in range(slots):
            group = partner(side_ref[1], slot, slots)
            for chunk in range(chunks):
                part = dot(moved_refs[chunk * slots + slot][...], weight_refs[chunk][group])
                total = part if total is None else total + part
        o_ref[...] = total.astype(o_ref.dtype)

    @pl.when(pl.program_id(0) == 0)
    def _():
        add_up(mine_refs)

    @pl.when(pl.program_id(0) == 1)
    def _():
        add_up(other_refs)


def project(side, moved, mine, other):
    chunks, slots = len(moved), len(moved[0])
    tokens, part = moved[0][0].shape
    half = mine[0].shape[2]
    tile = min(half, 512)
    tiles = half // tile
    block = (slots, part, tile)
    return pl.pallas_call(
        functools.partial(project_kernel, slots=slots, chunks=chunks),
        grid_spec=pltpu.PrefetchScalarGridSpec(
            num_scalar_prefetch=1,
            grid=(2, tiles),
            in_specs=[pl.BlockSpec((tokens, part), lambda s, j, side: (0, 0))] * (slots * chunks)
            + [pl.BlockSpec(block, lambda s, j, side: (0, 0, jnp.where(s == 0, j, tiles - 1)))]
            * chunks
            + [pl.BlockSpec(block, lambda s, j, side: (0, 0, jnp.where(s == 0, 0, j)))] * chunks,
            out_specs=pl.BlockSpec(
                (tokens, tile), lambda s, j, side: (0, (s ^ side[0]) * tiles + j)
            ),
        ),
        out_shape=jax.ShapeDtypeStruct((tokens, 2 * half), BF16),
        compiler_params=params(40),
        cost_estimate=cost(
            4 * chunks * slots * tokens * part * half,
            chunks * slots * part * (4 * half + 2 * tokens) + 4 * tokens * half,
        ),
        name="project",
    )(side, *[slab for slabs in moved for slab in slabs], *mine, *other)


def gather_ctx(rows):
    count = lax.axis_size("ctx")
    held = rows[:, None]
    steps = []
    distance = count // 2
    while distance:
        steps.append(distance)
        distance //= 2
    order = [0]
    for distance in steps:
        received = lax.ppermute(held, "ctx", [(i, i ^ distance) for i in range(count)])
        held = jnp.concatenate([held, received], axis=1)
        order = order + [i ^ distance for i in order]
    return held, order


def stride_general(queries, keys, values):
    tokens_dev, width = queries.shape
    heads = width // HEAD_SIZE
    ctx = lax.axis_size("ctx")
    copies = max(ctx // STRIDE, 1)
    rows = tokens_dev // STRIDE
    held_rows = ctx * rows // copies
    own_copy = lax.axis_index("ctx") // STRIDE
    query_pos = (jnp.arange(held_rows) // (rows // copies)) * rows
    query_pos = query_pos + (jnp.arange(held_rows) % (rows // copies)) * copies + own_copy
    shaped = queries.reshape(1, rows // copies, ctx, width)
    query = lax.all_to_all(shaped, "ctx", split_axis=2, concat_axis=1, tiled=True)
    query = query.reshape(held_rows, heads, HEAD_SIZE)
    both = jnp.stack([keys, values]).reshape(2, rows, 1, STRIDE, width)
    both = jnp.broadcast_to(both, (2, rows, copies, STRIDE, width)).reshape(2, rows, ctx, width)
    both = lax.all_to_all(both, "ctx", split_axis=2, concat_axis=1, tiled=True)
    both = both.reshape(2, ctx * rows, heads, HEAD_SIZE)
    allowed = jnp.arange(ctx * rows)[None, :] <= query_pos[:, None]

    def one_head(operands):
        head_query, head_keys, head_values = operands
        masked = jnp.where(allowed, scores(head_query, head_keys), BIG_NEG)
        return weighted([masked], [with_ones(head_values)])

    result = lax.map(
        one_head,
        (query.transpose(1, 0, 2), both[0].transpose(1, 0, 2), both[1].transpose(1, 0, 2)),
    )
    result = result.transpose(1, 0, 2).reshape(ctx, rows // copies, 1, width).astype(BF16)
    back = lax.all_to_all(result, "ctx", split_axis=0, concat_axis=2, tiled=True)
    return back.reshape(tokens_dev, width)


def body(queries, keys, values, out_weight, chunks):
    tokens_dev, width = queries.shape
    ctx = lax.axis_size("ctx")
    groups = lax.axis_size("head")
    place = lax.axis_index("ctx")
    place_word = place.astype(jnp.int32).reshape(1)
    side = place % 2
    sibling = [(i, i ^ 1) for i in range(ctx)]

    half = out_weight.shape[1] // 2
    part = width // chunks
    mine = []
    for chunk in range(chunks):
        piece = lax.dynamic_slice(out_weight, (chunk * part, side * half), (part, half))
        mine.append(lax.all_gather(piece, "head", axis=0))

    if ctx > STRIDE:
        stride_out = stride_general(queries, keys, values)
        rim = jnp.stack([keys[tokens_dev - WINDOW :], values[tokens_dev - WINDOW :]])
        picked = jnp.stack([keys, values]).reshape(2, tokens_dev // BLOCK, BLOCK, width)
        picked = picked[:, :, BLOCK - SUMCOLS :].reshape(2, -1, width)
    else:
        *send, rim, picked = prepare(queries, keys, values, ctx, chunks)
        received = [
            lax.all_to_all(part, "ctx", split_axis=0, concat_axis=0, tiled=True) for part in send
        ]
    summary, order = gather_ctx(picked)
    before = lax.ppermute(rim, "ctx", [(i, i + 1) for i in range(ctx - 1)])

    def home(chunk, waits):
        return home_sections(
            place_word, queries, keys, values, before, summary, order, chunk, chunks, waits
        )

    seat = lax.axis_index("head").astype(jnp.int32)

    def exchange(slabs, axis):
        count = len(slabs)
        moved = [slabs[0]]
        for slot in range(1, count):
            pairs = [(i, partner(i, slot, count)) for i in range(count)]
            moved.append(lax.ppermute(slabs[slot], axis, pairs))
        return moved

    moved, waits = [], ()
    if ctx > STRIDE:
        for chunk in range(chunks):
            lanes = slice(chunk * part, (chunk + 1) * part)
            homes, mark = home(chunk, waits)
            attended = (homes + stride_out[:, lanes].astype(F32)).astype(BF16)
            attended = attended.reshape(groups, tokens_dev // groups, part)
            owners = [partner(seat, slot, groups) for slot in range(groups)]
            moved.append(exchange([attended[owner] for owner in owners], "head"))
            waits = (mark,)
    else:
        seats = jnp.stack([seat, place.astype(jnp.int32)])
        sections, mark = home(0, ())
        for chunk in range(chunks):
            *slabs, mark = stride_attend(place_word, received[chunk], (mark,))
            backs = exchange(slabs, "ctx")
            here = sections
            if chunk < chunks - 1:
                sections, mark = home(chunk + 1, (mark,))
            arrived = moved[-1][1:] if moved else []
            *slabs, mark = combine(seats, here, backs, groups, (mark, *arrived))
            moved.append(exchange(slabs, "head"))
    sides = jnp.stack([side.astype(jnp.int32), seat])
    held = [after(piece, slabs[1:]) for piece, slabs in zip(mine, moved)]
    other = [lax.ppermute(piece, "ctx", sibling) for piece in held]
    return project(sides, moved, held, other)


def solution(mesh):
    chunks = 2 if HEADS // mesh.shape["head"] > 1 else 1
    placed = (P("ctx", "head"), P("ctx", "head"), P("ctx", "head"), P("head", None))
    return jax.shard_map(
        functools.partial(body, chunks=chunks),
        mesh=mesh,
        in_specs=placed,
        out_specs=P(("ctx", "head"), None),
        check_vma=False,
    )
```

```python
import functools
import math

import jax
import jax.numpy as jnp
from jax import lax
from jax.experimental import pallas as pl
from jax.experimental.pallas import tpu as pltpu
from jax.sharding import PartitionSpec as P

HEADS = 16
HEAD_SIZE = 128
WINDOW = 512
STRIDE = 16
BLOCK = 128
SUMCOLS = 8

BIG_NEG = -1e30
TILE = 256
LOG_SCALE = HEAD_SIZE ** (-0.5) * math.log2(math.e)
F32 = jnp.float32
BF16 = jnp.bfloat16


def params(mib):
    return pltpu.CompilerParams(vmem_limit_bytes=mib * 1024 * 1024)


MARK = jax.ShapeDtypeStruct((8, 128), F32)


def mark_spec():
    return pl.BlockSpec(MARK.shape, lambda *place: (0, 0))


def moments(arrays):
    return [pl.BlockSpec(memory_space=pl.ANY)] * len(arrays)


def after(array, others):
    anywhere = pl.BlockSpec(memory_space=pl.ANY)
    return pl.pallas_call(
        lambda *refs: None,
        in_specs=[anywhere] * (1 + len(others)),
        out_specs=anywhere,
        out_shape=jax.ShapeDtypeStruct(array.shape, array.dtype),
        input_output_aliases={0: 0},
        compiler_params=params(24),
        cost_estimate=cost(0, 0),
        name="after",
    )(array, *others)


def cost(flops, bytes_accessed, exps=0):
    return pl.CostEstimate(
        flops=int(flops), bytes_accessed=int(bytes_accessed), transcendentals=int(exps)
    )


def partner(place, slot, count):
    assert count & (count - 1) == 0
    return place ^ slot


def iota2(shape, dim):
    return lax.broadcasted_iota(jnp.int32, shape, dim)


def scores(query, key_rows):
    return lax.dot_general(query, key_rows, (((1,), (1,)), ((), ())), preferred_element_type=F32)


def dot(left, right):
    return jnp.dot(left, right, preferred_element_type=F32)


def regroup_matrix():
    rows = iota2((TILE, TILE), 0)
    cols = iota2((TILE, TILE), 1)
    return (cols == (rows & 15) * 16 + (rows >> 4)).astype(BF16)


def with_ones(value_rows):
    return jnp.concatenate([value_rows, jnp.ones_like(value_rows)], axis=1)


def weighted(score_blocks, value_blocks, extra=None):
    top = functools.reduce(jnp.maximum, score_blocks)
    top = jnp.max(top, axis=-1, keepdims=True)
    if extra is not None:
        top = jnp.maximum(top, extra[0])
    total = None
    for block, value_block in zip(score_blocks, value_blocks):
        weights = jnp.exp2((block - top) * LOG_SCALE).astype(BF16)
        part = dot(weights, value_block)
        total = part if total is None else total + part
    if extra is not None:
        own = jnp.exp2((extra[0] - top) * LOG_SCALE).astype(BF16).astype(F32)
        total = total + own * extra[1].astype(F32)
    return total[:, :HEAD_SIZE] / total[:, HEAD_SIZE:]


def prep_kernel(q_ref, k_ref, v_ref, *refs, rim_start, whole):
    send_ref = refs[2] if whole else refs[-1]
    matrix = regroup_matrix()
    ctx, _, per, rows, width = send_ref.shape
    for number, ref in enumerate((q_ref, k_ref, v_ref)):
        grouped = dot(matrix, ref[...]).astype(BF16)
        send_ref[:, number] = grouped.reshape(ctx, per, rows, width)
    if not whole:
        return
    all_keys, all_values, _, rim_ref, sum_ref = refs
    picks = TILE // BLOCK * SUMCOLS
    row = iota2((picks, TILE), 0)
    col = iota2((picks, TILE), 1)
    pick = (col == (row // SUMCOLS) * BLOCK + BLOCK - SUMCOLS + row % SUMCOLS).astype(BF16)
    sum_ref[0] = dot(pick, all_keys[...]).astype(BF16)
    sum_ref[1] = dot(pick, all_values[...]).astype(BF16)

    @pl.when(pl.program_id(0) >= rim_start)
    def _():
        rim_ref[0] = all_keys[...]
        rim_ref[1] = all_values[...]


def prepare(queries, keys, values, ctx, chunk, chunks, waits):
    tokens_dev, width = queries.shape
    whole = chunk == chunks - 1
    tiles = tokens_dev // TILE
    per = STRIDE // ctx
    rows = tokens_dev // STRIDE
    part = width // chunks
    rim_start = tiles - WINDOW // TILE
    picks = TILE // BLOCK * SUMCOLS
    source = pl.BlockSpec((TILE, part), lambda b: (b, chunk))
    full = pl.BlockSpec((TILE, width), lambda b: (b, 0))
    out_specs = [pl.BlockSpec((ctx, 3, per, TILE // STRIDE, part), lambda b: (0, 0, 0, b, 0))]
    out_shape = [jax.ShapeDtypeStruct((ctx, 3, per, rows, part), BF16)]
    if whole:
        out_specs += [
            pl.BlockSpec((2, TILE, width), lambda b: (0, jnp.maximum(b - rim_start, 0), 0)),
            pl.BlockSpec((2, picks, width), lambda b: (0, b, 0)),
        ]
        out_shape += [
            jax.ShapeDtypeStruct((2, WINDOW, width), BF16),
            jax.ShapeDtypeStruct((2, tiles * picks, width), BF16),
        ]
    return pl.pallas_call(
        functools.partial(prep_kernel, rim_start=rim_start, whole=whole),
        grid=(tiles,),
        in_specs=[source] * 3 + [full] * 2 * whole,
        out_specs=out_specs,
        out_shape=out_shape,
        compiler_params=params(60),
        cost_estimate=cost(6 * tokens_dev * TILE * part, 16 * tokens_dev * part),
        name="prepare",
    )(queries, keys, values, *([keys, values] * whole))


def home_kernel(place_ref, q_ref, k_ref, v_ref, rim_ref, *refs, order):
    sum_refs, (o_ref, mark_ref) = refs[: len(order)], refs[-2:]
    mark_ref[...] = jnp.zeros_like(mark_ref)
    place = place_ref[0]
    tokens_dev = q_ref.shape[0]
    back = WINDOW // TILE
    key_blocks = [rim_ref[0, e * TILE : (e + 1) * TILE] for e in range(back)]
    value_blocks = [with_ones(rim_ref[1, e * TILE : (e + 1) * TILE]) for e in range(back)]
    for e in range(tokens_dev // TILE):
        key_blocks.append(k_ref[e * TILE : (e + 1) * TILE])
        value_blocks.append(with_ones(v_ref[e * TILE : (e + 1) * TILE]))
    picks = sum_refs[0].shape[1]
    sum_keys = jnp.concatenate([ref[0] for ref in sum_refs])
    sum_values = with_ones(jnp.concatenate([ref[1] for ref in sum_refs]))
    sum_col = jnp.concatenate(
        [iota2((TILE, picks), 1) + (place ^ i) * picks for i in order], axis=1
    )
    row = iota2((TILE, TILE), 0)
    col = iota2((TILE, TILE), 1)
    for b in range(tokens_dev // TILE):
        query = q_ref[b * TILE : (b + 1) * TILE]
        blocks = []
        for e in range(back + 1):
            block = scores(query, key_blocks[b + e])
            allowed = None
            if e == 0:
                allowed = col > row
            if e == back:
                allowed = col <= row
            if b + e < back:
                held = place > 0
                allowed = held if allowed is None else allowed & held
            if allowed is not None:
                block = jnp.where(allowed, block, BIG_NEG)
            blocks.append(block)
        local = weighted(blocks, value_blocks[b : b + back + 1])
        pos = place * tokens_dev + b * TILE + iota2((TILE, 1), 0)
        within = pos % BLOCK
        held = pos // BLOCK * SUMCOLS + jnp.maximum(within - (BLOCK - SUMCOLS - 1), 0)
        block = jnp.where(sum_col < held, scores(query, sum_keys), BIG_NEG)
        own_key = key_blocks[b + back].astype(F32)
        own = jnp.sum(query.astype(F32) * own_key, axis=-1, keepdims=True)
        own = jnp.where(within < BLOCK - SUMCOLS, own, BIG_NEG)
        summary = weighted([block], [sum_values], (own, value_blocks[b + back]))
        o_ref[b * TILE : (b + 1) * TILE] = local + summary


def home_sections(place, queries, keys, values, rim, summary, order, chunk, chunks, waits):
    tokens_dev, width = queries.shape
    heads = width // chunks // HEAD_SIZE
    first = chunk * heads
    picks = summary[0].shape[1]
    total = len(summary) * picks
    own = pl.BlockSpec((tokens_dev, HEAD_SIZE), lambda h: (0, first + h))
    pairs = tokens_dev * (WINDOW + TILE + total) * heads
    return pl.pallas_call(
        functools.partial(home_kernel, order=order),
        grid=(heads,),
        in_specs=[
            pl.BlockSpec(memory_space=pltpu.SMEM),
            own,
            own,
            own,
            pl.BlockSpec((2, WINDOW, HEAD_SIZE), lambda h: (0, 0, first + h)),
        ]
        + [pl.BlockSpec((2, picks, HEAD_SIZE), lambda h: (0, 0, first + h))] * len(summary)
        + moments(waits),
        out_specs=[pl.BlockSpec((tokens_dev, HEAD_SIZE), lambda h: (0, h)), mark_spec()],
        out_shape=[jax.ShapeDtypeStruct((tokens_dev, heads * HEAD_SIZE), F32), MARK],
        compiler_params=params(24),
        cost_estimate=cost(8 * pairs * HEAD_SIZE, 14 * tokens_dev * width, pairs),
        name="home",
    )(place, queries, keys, values, rim, *summary, *waits)


def stride_kernel(place_ref, x_ref, *refs):
    ctx, _, _, rows, width = x_ref.shape
    o_refs, mark_ref, held_ref = refs[-ctx - 2 : -2], refs[-2], refs[-1]
    mark_ref[...] = jnp.zeros_like(mark_ref)
    count = ctx * rows
    row = iota2((TILE, TILE), 0)
    col = iota2((TILE, TILE), 1)
    sources = TILE // rows
    units = []
    for head in range(width // HEAD_SIZE):
        lanes = slice(head * HEAD_SIZE, (head + 1) * HEAD_SIZE)
        query = x_ref[:, 0, 0, :, lanes].reshape(count, HEAD_SIZE)
        key_rows = x_ref[:, 1, 0, :, lanes].reshape(count, HEAD_SIZE)
        value_rows = with_ones(x_ref[:, 2, 0, :, lanes].reshape(count, HEAD_SIZE))
        for b in range(count // TILE):
            part = query[b * TILE : (b + 1) * TILE]
            blocks = [scores(part, key_rows[e * TILE : (e + 1) * TILE]) for e in range(b + 1)]
            blocks[b] = jnp.where(col <= row, blocks[b], BIG_NEG)
            units.append((lanes, b, blocks, value_rows))
    for lanes, b, blocks, value_rows in units:
        result = weighted(
            blocks, [value_rows[e * TILE : (e + 1) * TILE] for e in range(b + 1)]
        ).astype(BF16)
        held_ref[b * sources : (b + 1) * sources, :, lanes] = result.reshape(
            sources, rows, HEAD_SIZE
        )
    for slot in range(ctx):
        o_refs[slot][0] = held_ref[partner(place_ref[0], slot, ctx)]


def stride_attend(place, moved, waits):
    ctx, _, per, rows, width = moved.shape
    count = ctx * rows
    pairs = per * (width // HEAD_SIZE) * count * (count + TILE) // 2
    return pl.pallas_call(
        stride_kernel,
        grid=(per,),
        in_specs=[
            pl.BlockSpec(memory_space=pltpu.SMEM),
            pl.BlockSpec((ctx, 3, 1, rows, width), lambda r: (0, 0, r, 0, 0)),
        ]
        + moments(waits),
        out_specs=[pl.BlockSpec((1, rows, width), lambda r: (r, 0, 0))] * ctx + [mark_spec()],
        out_shape=[jax.ShapeDtypeStruct((per, rows, width), BF16)] * ctx + [MARK],
        scratch_shapes=[pltpu.VMEM((ctx, rows, width), BF16)],
        compiler_params=params(24),
        cost_estimate=cost(8 * pairs * HEAD_SIZE, 8 * per * count * width, pairs),
        name="stride",
    )(place, moved, *waits)


def combine_kernel(seat_ref, home_ref, *refs, slots, ctx):
    back_refs, o_refs, mark_ref = refs[:ctx], refs[-slots - 1 : -1], refs[-1]
    mark_ref[...] = jnp.zeros_like(mark_ref)
    tokens_dev, width = home_ref.shape
    size = tokens_dev // slots
    per = STRIDE // ctx
    token = iota2((TILE, TILE), 0)
    col = iota2((TILE, TILE), 1)
    group = col >> 4
    residue = partner(seat_ref[1], group // per, ctx) * per + group % per
    matrix = (token == (col & 15) * 16 + residue).astype(BF16)
    for slot in range(slots):
        owner = partner(seat_ref[0], slot, slots)
        for b in range(size // TILE):
            first = owner * (size // TILE) + b
            here = pl.ds(pl.multiple_of(first * STRIDE, STRIDE), STRIDE)
            rows = [ref[r, here] for ref in back_refs for r in range(per)]
            back = dot(matrix, jnp.concatenate(rows))
            home = home_ref[pl.ds(pl.multiple_of(first * TILE, TILE), TILE)]
            o_refs[slot][b * TILE : (b + 1) * TILE] = (home + back).astype(BF16)


def combine(seat, home, backs, slots, waits):
    tokens_dev, width = home.shape
    size = tokens_dev // slots
    return pl.pallas_call(
        functools.partial(combine_kernel, slots=slots, ctx=len(backs)),
        in_specs=[pl.BlockSpec(memory_space=pltpu.SMEM)]
        + [pl.BlockSpec(memory_space=pltpu.VMEM)] * (1 + len(backs))
        + moments(waits),
        out_specs=[pl.BlockSpec(memory_space=pltpu.VMEM)] * (slots + 1),
        out_shape=[jax.ShapeDtypeStruct((size, width), BF16)] * slots + [MARK],
        compiler_params=params(24),
        cost_estimate=cost(2 * tokens_dev * TILE * width, 8 * tokens_dev * width),
        name="combine",
    )(seat, home, *backs, *waits)


def project_kernel(side_ref, *refs, slots, chunks):
    moved_refs, weight_refs = refs[: slots * chunks], refs[slots * chunks : (slots + 1) * chunks]
    total = None
    for slot in range(slots):
        group = partner(side_ref[1], slot, slots)
        for chunk in range(chunks):
            part = dot(moved_refs[chunk * slots + slot][...], weight_refs[chunk][group])
            total = part if total is None else total + part
    refs[-1][...] = total.astype(BF16)


def project(side, moved, weights, result):
    chunks, slots = len(moved), len(moved[0])
    tokens, part = moved[0][0].shape
    half = weights[0].shape[2]
    tile = min(half, 256)
    tiles = half // tile
    later = 0 if result is None else 1
    return pl.pallas_call(
        functools.partial(project_kernel, slots=slots, chunks=chunks),
        grid_spec=pltpu.PrefetchScalarGridSpec(
            num_scalar_prefetch=1,
            grid=(tiles,),
            in_specs=[pl.BlockSpec((tokens, part), lambda j, side: (0, 0))] * (slots * chunks)
            + [pl.BlockSpec((slots, part, tile), lambda j, side: (0, 0, j))] * chunks
            + [pl.BlockSpec(memory_space=pl.ANY)] * later,
            out_specs=pl.BlockSpec(
                (tokens, tile), lambda j, side: (0, (side[0] ^ later) * tiles + j)
            ),
        ),
        out_shape=jax.ShapeDtypeStruct((tokens, 2 * half), BF16),
        input_output_aliases={1 + (slots + 1) * chunks: 0} if later else {},
        compiler_params=params(24),
        cost_estimate=cost(
            2 * chunks * slots * tokens * part * half,
            chunks * slots * part * 2 * (half + tokens) + 2 * tokens * half,
        ),
        name="project",
    )(side, *[slab for slabs in moved for slab in slabs], *weights, *([result] * later))


def gather_ctx(rows):
    count = lax.axis_size("ctx")

    def swapped(piece, distance):
        return lax.ppermute(piece, "ctx", [(i, i ^ distance) for i in range(count)])

    order = list(range(0, count, 2))
    pieces = [rows] + [swapped(rows, distance) for distance in order[1:]]
    return pieces + [swapped(piece, 1) for piece in pieces], order + [i ^ 1 for i in order]


def stride_general(queries, keys, values):
    tokens_dev, width = queries.shape
    heads = width // HEAD_SIZE
    ctx = lax.axis_size("ctx")
    copies = max(ctx // STRIDE, 1)
    rows = tokens_dev // STRIDE
    held_rows = ctx * rows // copies
    own_copy = lax.axis_index("ctx") // STRIDE
    query_pos = (jnp.arange(held_rows) // (rows // copies)) * rows
    query_pos = query_pos + (jnp.arange(held_rows) % (rows // copies)) * copies + own_copy
    shaped = queries.reshape(1, rows // copies, ctx, width)
    query = lax.all_to_all(shaped, "ctx", split_axis=2, concat_axis=1, tiled=True)
    query = query.reshape(held_rows, heads, HEAD_SIZE)
    both = jnp.stack([keys, values]).reshape(2, rows, 1, STRIDE, width)
    both = jnp.broadcast_to(both, (2, rows, copies, STRIDE, width)).reshape(2, rows, ctx, width)
    both = lax.all_to_all(both, "ctx", split_axis=2, concat_axis=1, tiled=True)
    both = both.reshape(2, ctx * rows, heads, HEAD_SIZE)
    allowed = jnp.arange(ctx * rows)[None, :] <= query_pos[:, None]

    def one_head(operands):
        head_query, head_keys, head_values = operands
        masked = jnp.where(allowed, scores(head_query, head_keys), BIG_NEG)
        return weighted([masked], [with_ones(head_values)])

    result = lax.map(
        one_head,
        (query.transpose(1, 0, 2), both[0].transpose(1, 0, 2), both[1].transpose(1, 0, 2)),
    )
    result = result.transpose(1, 0, 2).reshape(ctx, rows // copies, 1, width).astype(BF16)
    back = lax.all_to_all(result, "ctx", split_axis=0, concat_axis=2, tiled=True)
    return back.reshape(tokens_dev, width)


def body(queries, keys, values, out_weight, chunks):
    tokens_dev, width = queries.shape
    ctx = lax.axis_size("ctx")
    groups = lax.axis_size("head")
    place = lax.axis_index("ctx")
    place_word = place.astype(jnp.int32).reshape(1)
    side = place % 2
    sibling = [(i, i ^ 1) for i in range(ctx)]

    half = out_weight.shape[1] // 2
    part = width // chunks
    mine = []
    for chunk in range(chunks):
        piece = lax.dynamic_slice(out_weight, (chunk * part, side * half), (part, half))
        mine.append(lax.all_gather(piece, "head", axis=0))

    if ctx > STRIDE:
        stride_out = stride_general(queries, keys, values)
        rim = jnp.stack([keys[tokens_dev - WINDOW :], values[tokens_dev - WINDOW :]])
        picked = jnp.stack([keys, values]).reshape(2, tokens_dev // BLOCK, BLOCK, width)
        picked = picked[:, :, BLOCK - SUMCOLS :].reshape(2, -1, width)
    else:
        send = []
        for chunk in range(chunks):
            part_send, *rest = prepare(queries, keys, values, ctx, chunk, chunks, ())
            send.append(part_send)
        rim, picked = rest
        received = [
            lax.all_to_all(part, "ctx", split_axis=0, concat_axis=0, tiled=True) for part in send
        ]
    summary, order = gather_ctx(picked)
    before = lax.ppermute(rim, "ctx", [(i, i + 1) for i in range(ctx - 1)])

    def home(chunk, waits):
        return home_sections(
            place_word, queries, keys, values, before, summary, order, chunk, chunks, waits
        )

    seat = lax.axis_index("head").astype(jnp.int32)

    def exchange(slabs, axis):
        count = len(slabs)
        moved = [slabs[0]]
        for slot in range(1, count):
            pairs = [(i, partner(i, slot, count)) for i in range(count)]
            moved.append(lax.ppermute(slabs[slot], axis, pairs))
        return moved

    held, other = [], []

    def swap(chunk, others):
        held.append(after(mine[chunk], others))
        other.append(lax.ppermute(held[-1], "ctx", sibling))

    moved, waits, arrived = [], (), ()
    if ctx > STRIDE:
        for chunk in range(chunks):
            lanes = slice(chunk * part, (chunk + 1) * part)
            homes, mark = home(chunk, waits)
            attended = (homes + stride_out[:, lanes].astype(F32)).astype(BF16)
            attended = attended.reshape(groups, tokens_dev // groups, part)
            owners = [partner(seat, slot, groups) for slot in range(groups)]
            moved.append(exchange([attended[owner] for owner in owners], "head"))
            waits = (mark,)
            if chunk < chunks - 1:
                swap(chunk, waits)
    else:
        seats = jnp.stack([seat, place.astype(jnp.int32)])
        homes, backs = [], []
        for chunk in range(chunks):
            *slabs, mark = stride_attend(place_word, received[chunk], waits)
            backs.append(exchange(slabs, "ctx"))
            waits = (mark,)
            for ready in range(chunk, chunks if chunk == chunks - 2 else chunk + 1):
                if ready >= len(homes):
                    sections, mark = home(ready, waits)
                    homes.append(sections)
                    waits = (mark,)
        for chunk in range(chunks):
            *slabs, mark = combine(seats, homes[chunk], backs[chunk], groups, (*waits, *arrived))
            moved.append(exchange(slabs, "head"))
            waits = (mark,)
            if chunk < chunks - 1:
                swap(chunk, waits)
                arrived = (*moved[-1][1:], other[-1])
    swap(chunks - 1, moved[-1][1:])
    sides = jnp.stack([side.astype(jnp.int32), seat])
    result = project(sides, moved, held, None)
    return project(sides, moved, other, result)


def solution(mesh):
    chunks = 2 if HEADS // mesh.shape["head"] > 1 else 1
    placed = (P("ctx", "head"), P("ctx", "head"), P("ctx", "head"), P("head", None))
    return jax.shard_map(
        functools.partial(body, chunks=chunks),
        mesh=mesh,
        in_specs=placed,
        out_specs=P(("ctx", "head"), None),
        check_vma=False,
    )
```

```python
import functools
import math

import jax
import jax.numpy as jnp
from jax import lax
from jax.experimental import pallas as pl
from jax.experimental.pallas import tpu as pltpu
from jax.sharding import PartitionSpec as P

HEADS = 16
HEAD_SIZE = 128
WINDOW = 512
STRIDE = 16
BLOCK = 128
SUMCOLS = 8

BIG_NEG = -1e30
TILE = 256
LOG_SCALE = HEAD_SIZE ** (-0.5) * math.log2(math.e)
F32 = jnp.float32
BF16 = jnp.bfloat16


def params(mib):
    return pltpu.CompilerParams(vmem_limit_bytes=mib * 1024 * 1024)


MARK = jax.ShapeDtypeStruct((8, 128), F32)


def mark_spec():
    return pl.BlockSpec(MARK.shape, lambda *place: (0, 0))


def moments(arrays):
    return [pl.BlockSpec(memory_space=pl.ANY)] * len(arrays)


def after(array, others):
    anywhere = pl.BlockSpec(memory_space=pl.ANY)
    return pl.pallas_call(
        lambda *refs: None,
        in_specs=[anywhere] * (1 + len(others)),
        out_specs=anywhere,
        out_shape=jax.ShapeDtypeStruct(array.shape, array.dtype),
        input_output_aliases={0: 0},
        compiler_params=params(60),
        cost_estimate=cost(0, 0),
        name="after",
    )(array, *others)


def cost(flops, bytes_accessed, exps=0):
    return pl.CostEstimate(
        flops=int(flops), bytes_accessed=int(bytes_accessed), transcendentals=int(exps)
    )


def partner(place, slot, count):
    assert count & (count - 1) == 0
    return place ^ slot


def iota2(shape, dim):
    return lax.broadcasted_iota(jnp.int32, shape, dim)


def scores(query, key_rows):
    return lax.dot_general(query, key_rows, (((1,), (1,)), ((), ())), preferred_element_type=F32)


def dot(left, right):
    return jnp.dot(left, right, preferred_element_type=F32)


def regroup_matrix():
    rows = iota2((TILE, TILE), 0)
    cols = iota2((TILE, TILE), 1)
    return (cols == (rows & 15) * 16 + (rows >> 4)).astype(BF16)


def with_ones(value_rows):
    return jnp.concatenate([value_rows, jnp.ones_like(value_rows)], axis=1)


def weighted(score_blocks, value_blocks, extra=None):
    top = functools.reduce(jnp.maximum, score_blocks)
    top = jnp.max(top, axis=-1, keepdims=True)
    if extra is not None:
        top = jnp.maximum(top, extra[0])
    total = None
    for block, value_block in zip(score_blocks, value_blocks):
        weights = jnp.exp2((block - top) * LOG_SCALE).astype(BF16)
        part = dot(weights, value_block)
        total = part if total is None else total + part
    if extra is not None:
        own = jnp.exp2((extra[0] - top) * LOG_SCALE).astype(BF16).astype(F32)
        total = total + own * extra[1].astype(F32)
    return total[:, :HEAD_SIZE] / total[:, HEAD_SIZE:]


def edge_kernel(k_ref, v_ref, rim_ref, sum_ref, *, rim_start):
    picks = TILE // BLOCK * SUMCOLS
    row = iota2((picks, TILE), 0)
    col = iota2((picks, TILE), 1)
    pick = (col == (row // SUMCOLS) * BLOCK + BLOCK - SUMCOLS + row % SUMCOLS).astype(BF16)
    sum_ref[0] = dot(pick, k_ref[...]).astype(BF16)
    sum_ref[1] = dot(pick, v_ref[...]).astype(BF16)

    @pl.when(pl.program_id(0) >= rim_start)
    def _():
        rim_ref[0] = k_ref[...]
        rim_ref[1] = v_ref[...]


def edges(keys, values):
    tokens_dev, width = keys.shape
    tiles = tokens_dev // TILE
    rim_start = tiles - WINDOW // TILE
    picks = TILE // BLOCK * SUMCOLS
    source = pl.BlockSpec((TILE, width), lambda b: (b, 0))
    return pl.pallas_call(
        functools.partial(edge_kernel, rim_start=rim_start),
        grid=(tiles,),
        in_specs=[source] * 2,
        out_specs=[
            pl.BlockSpec((2, TILE, width), lambda b: (0, jnp.maximum(b - rim_start, 0), 0)),
            pl.BlockSpec((2, picks, width), lambda b: (0, b, 0)),
        ],
        out_shape=[
            jax.ShapeDtypeStruct((2, WINDOW, width), BF16),
            jax.ShapeDtypeStruct((2, tiles * picks, width), BF16),
        ],
        compiler_params=params(60),
        cost_estimate=cost(4 * tokens_dev * picks * width, 7 * tokens_dev * width),
        name="edges",
    )(keys, values)


def prep_kernel(q_ref, k_ref, v_ref, *refs):
    send_ref = refs[-1]
    matrix = regroup_matrix()
    ctx, _, per, rows, width = send_ref.shape
    for number, ref in enumerate((q_ref, k_ref, v_ref)):
        grouped = dot(matrix, ref[...]).astype(BF16)
        send_ref[:, number] = grouped.reshape(ctx, per, rows, width)


def prepare(queries, keys, values, ctx, chunk, chunks, waits):
    tokens_dev, width = queries.shape
    per = STRIDE // ctx
    part = width // chunks
    return pl.pallas_call(
        prep_kernel,
        grid=(tokens_dev // TILE,),
        in_specs=[pl.BlockSpec((TILE, part), lambda b: (b, chunk))] * 3 + moments(waits),
        out_specs=pl.BlockSpec((ctx, 3, per, TILE // STRIDE, part), lambda b: (0, 0, 0, b, 0)),
        out_shape=jax.ShapeDtypeStruct((ctx, 3, per, tokens_dev // STRIDE, part), BF16),
        compiler_params=params(60),
        cost_estimate=cost(6 * tokens_dev * TILE * part, 12 * tokens_dev * part),
        name="prepare",
    )(queries, keys, values, *waits)


def home_kernel(place_ref, q_ref, k_ref, v_ref, rim_ref, *refs, order):
    sum_refs, (o_ref, mark_ref) = refs[: len(order)], refs[-2:]
    mark_ref[...] = jnp.zeros_like(mark_ref)
    place = place_ref[0]
    tokens_dev = q_ref.shape[0]
    back = WINDOW // TILE
    key_blocks = [rim_ref[0, e * TILE : (e + 1) * TILE] for e in range(back)]
    value_blocks = [with_ones(rim_ref[1, e * TILE : (e + 1) * TILE]) for e in range(back)]
    for e in range(tokens_dev // TILE):
        key_blocks.append(k_ref[e * TILE : (e + 1) * TILE])
        value_blocks.append(with_ones(v_ref[e * TILE : (e + 1) * TILE]))
    picks = sum_refs[0].shape[1]
    sum_keys = jnp.concatenate([ref[0] for ref in sum_refs])
    sum_values = with_ones(jnp.concatenate([ref[1] for ref in sum_refs]))
    sum_col = jnp.concatenate(
        [iota2((TILE, picks), 1) + (place ^ i) * picks for i in order], axis=1
    )
    row = iota2((TILE, TILE), 0)
    col = iota2((TILE, TILE), 1)
    for b in range(tokens_dev // TILE):
        query = q_ref[b * TILE : (b + 1) * TILE]
        blocks = []
        for e in range(back + 1):
            block = scores(query, key_blocks[b + e])
            allowed = None
            if e == 0:
                allowed = col > row
            if e == back:
                allowed = col <= row
            if b + e < back:
                held = place > 0
                allowed = held if allowed is None else allowed & held
            if allowed is not None:
                block = jnp.where(allowed, block, BIG_NEG)
            blocks.append(block)
        local = weighted(blocks, value_blocks[b : b + back + 1])
        pos = place * tokens_dev + b * TILE + iota2((TILE, 1), 0)
        within = pos % BLOCK
        held = pos // BLOCK * SUMCOLS + jnp.maximum(within - (BLOCK - SUMCOLS - 1), 0)
        block = jnp.where(sum_col < held, scores(query, sum_keys), BIG_NEG)
        own_key = key_blocks[b + back].astype(F32)
        own = jnp.sum(query.astype(F32) * own_key, axis=-1, keepdims=True)
        own = jnp.where(within < BLOCK - SUMCOLS, own, BIG_NEG)
        summary = weighted([block], [sum_values], (own, value_blocks[b + back]))
        o_ref[b * TILE : (b + 1) * TILE] = local + summary


def home_sections(place, queries, keys, values, rim, summary, order, chunk, chunks, waits):
    tokens_dev, width = queries.shape
    heads = width // chunks // HEAD_SIZE
    first = chunk * heads
    picks = summary[0].shape[1]
    total = len(summary) * picks
    own = pl.BlockSpec((tokens_dev, HEAD_SIZE), lambda h: (0, first + h))
    pairs = tokens_dev * (WINDOW + TILE + total) * heads
    return pl.pallas_call(
        functools.partial(home_kernel, order=order),
        grid=(heads,),
        in_specs=[
            pl.BlockSpec(memory_space=pltpu.SMEM),
            own,
            own,
            own,
            pl.BlockSpec((2, WINDOW, HEAD_SIZE), lambda h: (0, 0, first + h)),
        ]
        + [pl.BlockSpec((2, picks, HEAD_SIZE), lambda h: (0, 0, first + h))] * len(summary)
        + moments(waits),
        out_specs=[pl.BlockSpec((tokens_dev, HEAD_SIZE), lambda h: (0, h)), mark_spec()],
        out_shape=[jax.ShapeDtypeStruct((tokens_dev, heads * HEAD_SIZE), F32), MARK],
        compiler_params=params(24),
        cost_estimate=cost(8 * pairs * HEAD_SIZE, 14 * tokens_dev * width, pairs),
        name="home",
    )(place, queries, keys, values, rim, *summary, *waits)


def stride_kernel(place_ref, x_ref, *refs):
    ctx, _, _, rows, width = x_ref.shape
    o_refs, mark_ref, held_ref = refs[-ctx - 2 : -2], refs[-2], refs[-1]
    mark_ref[...] = jnp.zeros_like(mark_ref)
    count = ctx * rows
    row = iota2((TILE, TILE), 0)
    col = iota2((TILE, TILE), 1)
    sources = TILE // rows
    units = []
    for head in range(width // HEAD_SIZE):
        lanes = slice(head * HEAD_SIZE, (head + 1) * HEAD_SIZE)
        query = x_ref[:, 0, 0, :, lanes].reshape(count, HEAD_SIZE)
        key_rows = x_ref[:, 1, 0, :, lanes].reshape(count, HEAD_SIZE)
        value_rows = with_ones(x_ref[:, 2, 0, :, lanes].reshape(count, HEAD_SIZE))
        for b in range(count // TILE):
            part = query[b * TILE : (b + 1) * TILE]
            blocks = [scores(part, key_rows[e * TILE : (e + 1) * TILE]) for e in range(b + 1)]
            blocks[b] = jnp.where(col <= row, blocks[b], BIG_NEG)
            units.append((lanes, b, blocks, value_rows))
    for lanes, b, blocks, value_rows in units:
        result = weighted(
            blocks, [value_rows[e * TILE : (e + 1) * TILE] for e in range(b + 1)]
        ).astype(BF16)
        held_ref[b * sources : (b + 1) * sources, :, lanes] = result.reshape(
            sources, rows, HEAD_SIZE
        )
    for slot in range(ctx):
        o_refs[slot][0] = held_ref[partner(place_ref[0], slot, ctx)]


def stride_attend(place, moved, waits):
    ctx, _, per, rows, width = moved.shape
    count = ctx * rows
    pairs = per * (width // HEAD_SIZE) * count * (count + TILE) // 2
    return pl.pallas_call(
        stride_kernel,
        grid=(per,),
        in_specs=[
            pl.BlockSpec(memory_space=pltpu.SMEM),
            pl.BlockSpec((ctx, 3, 1, rows, width), lambda r: (0, 0, r, 0, 0)),
        ]
        + moments(waits),
        out_specs=[pl.BlockSpec((1, rows, width), lambda r: (r, 0, 0))] * ctx + [mark_spec()],
        out_shape=[jax.ShapeDtypeStruct((per, rows, width), BF16)] * ctx + [MARK],
        scratch_shapes=[pltpu.VMEM((ctx, rows, width), BF16)],
        compiler_params=params(24),
        cost_estimate=cost(8 * pairs * HEAD_SIZE, 8 * per * count * width, pairs),
        name="stride",
    )(place, moved, *waits)


def combine_kernel(seat_ref, home_ref, *refs, slots, ctx):
    back_refs, o_refs, mark_ref = refs[:ctx], refs[-slots - 1 : -1], refs[-1]
    mark_ref[...] = jnp.zeros_like(mark_ref)
    tokens_dev, width = home_ref.shape
    size = tokens_dev // slots
    per = STRIDE // ctx
    token = iota2((TILE, TILE), 0)
    col = iota2((TILE, TILE), 1)
    group = col >> 4
    residue = partner(seat_ref[1], group // per, ctx) * per + group % per
    matrix = (token == (col & 15) * 16 + residue).astype(BF16)
    for slot in range(slots):
        owner = partner(seat_ref[0], slot, slots)
        for b in range(size // TILE):
            first = owner * (size // TILE) + b
            here = pl.ds(pl.multiple_of(first * STRIDE, STRIDE), STRIDE)
            rows = [ref[r, here] for ref in back_refs for r in range(per)]
            back = dot(matrix, jnp.concatenate(rows))
            home = home_ref[pl.ds(pl.multiple_of(first * TILE, TILE), TILE)]
            o_refs[slot][b * TILE : (b + 1) * TILE] = (home + back).astype(BF16)


def combine(seat, home, backs, slots, waits):
    tokens_dev, width = home.shape
    size = tokens_dev // slots
    return pl.pallas_call(
        functools.partial(combine_kernel, slots=slots, ctx=len(backs)),
        in_specs=[pl.BlockSpec(memory_space=pltpu.SMEM)]
        + [pl.BlockSpec(memory_space=pltpu.VMEM)] * (1 + len(backs))
        + moments(waits),
        out_specs=[pl.BlockSpec(memory_space=pltpu.VMEM)] * (slots + 1),
        out_shape=[jax.ShapeDtypeStruct((size, width), BF16)] * slots + [MARK],
        compiler_params=params(24),
        cost_estimate=cost(2 * tokens_dev * TILE * width, 8 * tokens_dev * width),
        name="combine",
    )(seat, home, *backs, *waits)


def project_kernel(side_ref, *refs, slots, chunks):
    moved_refs, (mine_ref, other_ref, o_ref) = refs[: slots * chunks], refs[slots * chunks :]
    width = moved_refs[0].shape[1]

    def add_up(weight_ref):
        total = None
        for slot in range(slots):
            group = partner(side_ref[1], slot, slots)
            for chunk in range(chunks):
                rows = weight_ref[group, chunk * width : (chunk + 1) * width]
                part = dot(moved_refs[chunk * slots + slot][...], rows)
                total = part if total is None else total + part
        o_ref[...] = total.astype(BF16)

    @pl.when(pl.program_id(0) == 0)
    def _():
        add_up(mine_ref)

    @pl.when(pl.program_id(0) == 1)
    def _():
        add_up(other_ref)


def project(side, moved, mine, other):
    chunks, slots = len(moved), len(moved[0])
    tokens, part = moved[0][0].shape
    width, half = mine.shape[1:]
    tile = min(half, 256)
    tiles = half // tile
    block = (slots, width, tile)
    return pl.pallas_call(
        functools.partial(project_kernel, slots=slots, chunks=chunks),
        grid_spec=pltpu.PrefetchScalarGridSpec(
            num_scalar_prefetch=1,
            grid=(2, tiles),
            in_specs=[pl.BlockSpec((tokens, part), lambda s, j, side: (0, 0))] * (slots * chunks)
            + [
                pl.BlockSpec(block, lambda s, j, side: (0, 0, jnp.where(s == 0, j, tiles - 1))),
                pl.BlockSpec(block, lambda s, j, side: (0, 0, jnp.where(s == 0, 0, j))),
            ],
            out_specs=pl.BlockSpec(
                (tokens, tile), lambda s, j, side: (0, (s ^ side[0]) * tiles + j)
            ),
        ),
        out_shape=jax.ShapeDtypeStruct((tokens, 2 * half), BF16),
        compiler_params=params(24),
        cost_estimate=cost(
            4 * slots * tokens * width * half, 2 * slots * width * (2 * half + tokens)
        ),
        name="project",
    )(side, *[slab for slabs in moved for slab in slabs], mine, other)


def gather_ctx(rows):
    count = lax.axis_size("ctx")

    def swapped(piece, distance):
        return lax.ppermute(piece, "ctx", [(i, i ^ distance) for i in range(count)])

    order = list(range(0, count, 2))
    pieces = [rows] + [swapped(rows, distance) for distance in order[1:]]
    within = [swapped(piece, 1) for piece in pieces]
    return pieces, within, order + [i ^ 1 for i in order]


def stride_general(queries, keys, values):
    tokens_dev, width = queries.shape
    heads = width // HEAD_SIZE
    ctx = lax.axis_size("ctx")
    copies = max(ctx // STRIDE, 1)
    rows = tokens_dev // STRIDE
    held_rows = ctx * rows // copies
    own_copy = lax.axis_index("ctx") // STRIDE
    query_pos = (jnp.arange(held_rows) // (rows // copies)) * rows
    query_pos = query_pos + (jnp.arange(held_rows) % (rows // copies)) * copies + own_copy
    shaped = queries.reshape(1, rows // copies, ctx, width)
    query = lax.all_to_all(shaped, "ctx", split_axis=2, concat_axis=1, tiled=True)
    query = query.reshape(held_rows, heads, HEAD_SIZE)
    both = jnp.stack([keys, values]).reshape(2, rows, 1, STRIDE, width)
    both = jnp.broadcast_to(both, (2, rows, copies, STRIDE, width)).reshape(2, rows, ctx, width)
    both = lax.all_to_all(both, "ctx", split_axis=2, concat_axis=1, tiled=True)
    both = both.reshape(2, ctx * rows, heads, HEAD_SIZE)
    allowed = jnp.arange(ctx * rows)[None, :] <= query_pos[:, None]

    def one_head(operands):
        head_query, head_keys, head_values = operands
        masked = jnp.where(allowed, scores(head_query, head_keys), BIG_NEG)
        return weighted([masked], [with_ones(head_values)])

    result = lax.map(
        one_head,
        (query.transpose(1, 0, 2), both[0].transpose(1, 0, 2), both[1].transpose(1, 0, 2)),
    )
    result = result.transpose(1, 0, 2).reshape(ctx, rows // copies, 1, width).astype(BF16)
    back = lax.all_to_all(result, "ctx", split_axis=0, concat_axis=2, tiled=True)
    return back.reshape(tokens_dev, width)


def body(queries, keys, values, out_weight, chunks):
    tokens_dev, width = queries.shape
    ctx = lax.axis_size("ctx")
    groups = lax.axis_size("head")
    place = lax.axis_index("ctx")
    place_word = place.astype(jnp.int32).reshape(1)
    side = place % 2
    sibling = [(i, i ^ 1) for i in range(ctx)]

    half = out_weight.shape[1] // 2
    part = width // chunks
    weight_half = lax.dynamic_slice_in_dim(out_weight, side * half, half, axis=1)
    mine = lax.all_gather(weight_half, "head", axis=0)

    rim, picked = edges(keys, values)
    between, within, order = gather_ctx(picked)
    summary = between + within
    before = lax.ppermute(rim, "ctx", [(i, i + 1) for i in range(ctx - 1)])
    if ctx > STRIDE:
        stride_out = stride_general(queries, keys, values)
    else:
        received = []
        for chunk in range(chunks):
            send = prepare(queries, keys, values, ctx, chunk, chunks, (picked,))
            if chunk > 0:
                send = after(send, between[1:])
            received.append(
                lax.all_to_all(send, "ctx", split_axis=0, concat_axis=0, tiled=True)
            )

    def home(chunk, waits):
        return home_sections(
            place_word, queries, keys, values, before, summary, order, chunk, chunks, waits
        )

    seat = lax.axis_index("head").astype(jnp.int32)

    def exchange(slabs, axis):
        count = len(slabs)
        moved = [slabs[0]]
        for slot in range(1, count):
            pairs = [(i, partner(i, slot, count)) for i in range(count)]
            moved.append(lax.ppermute(slabs[slot], axis, pairs))
        return moved

    moved, waits = [], ()
    if ctx > STRIDE:
        for chunk in range(chunks):
            lanes = slice(chunk * part, (chunk + 1) * part)
            homes, mark = home(chunk, waits)
            attended = (homes + stride_out[:, lanes].astype(F32)).astype(BF16)
            attended = attended.reshape(groups, tokens_dev // groups, part)
            owners = [partner(seat, slot, groups) for slot in range(groups)]
            moved.append(exchange([attended[owner] for owner in owners], "head"))
            waits = (mark,)
    else:
        seats = jnp.stack([seat, place.astype(jnp.int32)])
        homes, backs = [], []
        for chunk in range(chunks):
            *slabs, mark = stride_attend(place_word, received[chunk], waits)
            backs.append(exchange(slabs, "ctx"))
            waits = (mark,)
            for ready in range(chunks) if chunk == 0 else ():
                sections, mark = home(ready, waits)
                homes.append(sections)
                waits = (mark,)
        for chunk in range(chunks):
            *slabs, mark = combine(seats, homes[chunk], backs[chunk], groups, waits)
            moved.append(exchange(slabs, "head"))
            waits = (mark, *moved[-1][1:])
    held = after(mine, moved[-1][2:])
    other = lax.ppermute(held, "ctx", sibling)
    sides = jnp.stack([side.astype(jnp.int32), seat])
    return project(sides, moved, held, other)


def solution(mesh):
    chunks = 2 if HEADS // mesh.shape["head"] > 1 else 1
    placed = (P("ctx", "head"), P("ctx", "head"), P("ctx", "head"), P("head", None))
    return jax.shard_map(
        functools.partial(body, chunks=chunks),
        mesh=mesh,
        in_specs=placed,
        out_specs=P(("ctx", "head"), None),
        check_vma=False,
    )
```

```python
import functools
import math

import jax
import jax.numpy as jnp
from jax import lax
from jax.experimental import pallas as pl
from jax.experimental.pallas import tpu as pltpu
from jax.sharding import PartitionSpec as P

HEADS = 16
HEAD_SIZE = 128
WINDOW = 512
STRIDE = 16
BLOCK = 128
SUMCOLS = 8

BIG_NEG = -1e30
TILE = 256
LOG_SCALE = HEAD_SIZE ** (-0.5) * math.log2(math.e)
F32 = jnp.float32
BF16 = jnp.bfloat16


def params(mib):
    return pltpu.CompilerParams(vmem_limit_bytes=mib * 1024 * 1024)


MARK = jax.ShapeDtypeStruct((8, 128), F32)


def mark_spec():
    return pl.BlockSpec(MARK.shape, lambda *place: (0, 0))


def moments(arrays):
    return [pl.BlockSpec(memory_space=pl.ANY)] * len(arrays)


def after(array, others):
    anywhere = pl.BlockSpec(memory_space=pl.ANY)
    return pl.pallas_call(
        lambda *refs: None,
        in_specs=[anywhere] * (1 + len(others)),
        out_specs=anywhere,
        out_shape=jax.ShapeDtypeStruct(array.shape, array.dtype),
        input_output_aliases={0: 0},
        compiler_params=params(60),
        cost_estimate=cost(0, 0),
        name="after",
    )(array, *others)


def cost(flops, bytes_accessed, exps=0):
    return pl.CostEstimate(
        flops=int(flops), bytes_accessed=int(bytes_accessed), transcendentals=int(exps)
    )


def partner(place, slot, count):
    assert count & (count - 1) == 0
    return place ^ slot


def iota2(shape, dim):
    return lax.broadcasted_iota(jnp.int32, shape, dim)


def scores(query, key_rows):
    return lax.dot_general(query, key_rows, (((1,), (1,)), ((), ())), preferred_element_type=F32)


def dot(left, right):
    return jnp.dot(left, right, preferred_element_type=F32)


def regroup_matrix():
    rows = iota2((TILE, TILE), 0)
    cols = iota2((TILE, TILE), 1)
    return (cols == (rows & 15) * 16 + (rows >> 4)).astype(BF16)


def with_ones(value_rows):
    return jnp.concatenate([value_rows, jnp.ones_like(value_rows)], axis=1)


def weighted(score_blocks, value_blocks, extra=None):
    top = functools.reduce(jnp.maximum, score_blocks)
    top = jnp.max(top, axis=-1, keepdims=True)
    if extra is not None:
        top = jnp.maximum(top, extra[0])
    total = None
    for block, value_block in zip(score_blocks, value_blocks):
        weights = jnp.exp2((block - top) * LOG_SCALE).astype(BF16)
        part = dot(weights, value_block)
        total = part if total is None else total + part
    if extra is not None:
        own = jnp.exp2((extra[0] - top) * LOG_SCALE).astype(BF16).astype(F32)
        total = total + own * extra[1].astype(F32)
    return total[:, :HEAD_SIZE] / total[:, HEAD_SIZE:]


def edge_kernel(k_ref, v_ref, k_ends_ref, v_ends_ref, rim_ref, sum_ref):
    rim_ref[0] = k_ref[...]
    rim_ref[1] = v_ref[...]

    @pl.when(pl.program_id(0) == 0)
    def _():
        for number, ref in enumerate((k_ends_ref, v_ends_ref)):
            rows = ref[...].astype(F32)[:, 16 - SUMCOLS :]
            sum_ref[number] = rows.reshape(sum_ref.shape[1:]).astype(BF16)


def edges(keys, values):
    tokens_dev, width = keys.shape
    blocks = tokens_dev // BLOCK
    first = (tokens_dev - WINDOW) // TILE
    source = pl.BlockSpec((TILE, width), lambda i: (first + i, 0))
    ends = pl.BlockSpec((blocks, 16, width), lambda i: (0, BLOCK // 16 - 1, 0))
    shape = (2, blocks * SUMCOLS, width)
    return pl.pallas_call(
        edge_kernel,
        grid=(WINDOW // TILE,),
        in_specs=[source] * 2 + [ends] * 2,
        out_specs=[
            pl.BlockSpec((2, TILE, width), lambda i: (0, i, 0)),
            pl.BlockSpec(shape, lambda i: (0, 0, 0)),
        ],
        out_shape=[
            jax.ShapeDtypeStruct((2, WINDOW, width), BF16),
            jax.ShapeDtypeStruct(shape, BF16),
        ],
        compiler_params=params(60),
        cost_estimate=cost(0, 8 * WINDOW * width),
        name="edges",
    )(
        keys,
        values,
        keys.reshape(blocks, BLOCK, width),
        values.reshape(blocks, BLOCK, width),
    )


def prep_kernel(q_ref, k_ref, v_ref, *refs):
    send_ref = refs[-1]
    matrix = regroup_matrix()
    ctx, _, per, rows, width = send_ref.shape
    for number, ref in enumerate((q_ref, k_ref, v_ref)):
        grouped = dot(matrix, ref[...]).astype(BF16)
        send_ref[:, number] = grouped.reshape(ctx, per, rows, width)


def prepare(queries, keys, values, ctx, chunk, chunks, waits):
    tokens_dev, width = queries.shape
    per = STRIDE // ctx
    part = width // chunks
    return pl.pallas_call(
        prep_kernel,
        grid=(tokens_dev // TILE,),
        in_specs=[pl.BlockSpec((TILE, part), lambda b: (b, chunk))] * 3 + moments(waits),
        out_specs=pl.BlockSpec((ctx, 3, per, TILE // STRIDE, part), lambda b: (0, 0, 0, b, 0)),
        out_shape=jax.ShapeDtypeStruct((ctx, 3, per, tokens_dev // STRIDE, part), BF16),
        compiler_params=params(60),
        cost_estimate=cost(6 * tokens_dev * TILE * part, 12 * tokens_dev * part),
        name="prepare",
    )(queries, keys, values, *waits)


def home_kernel(place_ref, q_ref, k_ref, v_ref, rim_ref, *refs, order):
    sum_refs, (o_ref, mark_ref) = refs[: len(order)], refs[-2:]
    mark_ref[...] = jnp.zeros_like(mark_ref)
    place = place_ref[0]
    tokens_dev = q_ref.shape[0]
    back = WINDOW // TILE
    key_blocks = [rim_ref[0, e * TILE : (e + 1) * TILE] for e in range(back)]
    value_blocks = [with_ones(rim_ref[1, e * TILE : (e + 1) * TILE]) for e in range(back)]
    for e in range(tokens_dev // TILE):
        key_blocks.append(k_ref[e * TILE : (e + 1) * TILE])
        value_blocks.append(with_ones(v_ref[e * TILE : (e + 1) * TILE]))
    picks = sum_refs[0].shape[1]
    sum_keys = jnp.concatenate([ref[0] for ref in sum_refs])
    sum_values = with_ones(jnp.concatenate([ref[1] for ref in sum_refs]))
    sum_col = jnp.concatenate(
        [iota2((TILE, picks), 1) + (place ^ i) * picks for i in order], axis=1
    )
    row = iota2((TILE, TILE), 0)
    col = iota2((TILE, TILE), 1)
    for b in range(tokens_dev // TILE):
        query = q_ref[b * TILE : (b + 1) * TILE]
        blocks = []
        for e in range(back + 1):
            block = scores(query, key_blocks[b + e])
            allowed = None
            if e == 0:
                allowed = col > row
            if e == back:
                allowed = col <= row
            if b + e < back:
                held = place > 0
                allowed = held if allowed is None else allowed & held
            if allowed is not None:
                block = jnp.where(allowed, block, BIG_NEG)
            blocks.append(block)
        local = weighted(blocks, value_blocks[b : b + back + 1])
        pos = place * tokens_dev + b * TILE + iota2((TILE, 1), 0)
        within = pos % BLOCK
        held = pos // BLOCK * SUMCOLS + jnp.maximum(within - (BLOCK - SUMCOLS - 1), 0)
        block = jnp.where(sum_col < held, scores(query, sum_keys), BIG_NEG)
        own_key = key_blocks[b + back].astype(F32)
        own = jnp.sum(query.astype(F32) * own_key, axis=-1, keepdims=True)
        own = jnp.where(within < BLOCK - SUMCOLS, own, BIG_NEG)
        summary = weighted([block], [sum_values], (own, value_blocks[b + back]))
        o_ref[b * TILE : (b + 1) * TILE] = local + summary


def home_sections(place, queries, keys, values, rim, summary, order, chunk, chunks, waits):
    tokens_dev, width = queries.shape
    heads = width // chunks // HEAD_SIZE
    first = chunk * heads
    picks = summary[0].shape[1]
    total = len(summary) * picks
    own = pl.BlockSpec((tokens_dev, HEAD_SIZE), lambda h: (0, first + h))
    pairs = tokens_dev * (WINDOW + TILE + total) * heads
    return pl.pallas_call(
        functools.partial(home_kernel, order=order),
        grid=(heads,),
        in_specs=[
            pl.BlockSpec(memory_space=pltpu.SMEM),
            own,
            own,
            own,
            pl.BlockSpec((2, WINDOW, HEAD_SIZE), lambda h: (0, 0, first + h)),
        ]
        + [pl.BlockSpec((2, picks, HEAD_SIZE), lambda h: (0, 0, first + h))] * len(summary)
        + moments(waits),
        out_specs=[pl.BlockSpec((tokens_dev, HEAD_SIZE), lambda h: (0, h)), mark_spec()],
        out_shape=[jax.ShapeDtypeStruct((tokens_dev, heads * HEAD_SIZE), F32), MARK],
        compiler_params=params(60),
        cost_estimate=cost(8 * pairs * HEAD_SIZE, 14 * tokens_dev * width, pairs),
        name="home",
    )(place, queries, keys, values, rim, *summary, *waits)


def stride_kernel(place_ref, x_ref, *refs):
    ctx, _, _, rows, width = x_ref.shape
    o_refs, mark_ref, held_ref = refs[-ctx - 2 : -2], refs[-2], refs[-1]
    mark_ref[...] = jnp.zeros_like(mark_ref)
    count = ctx * rows
    row = iota2((TILE, TILE), 0)
    col = iota2((TILE, TILE), 1)
    sources = TILE // rows
    units = []
    for head in range(width // HEAD_SIZE):
        lanes = slice(head * HEAD_SIZE, (head + 1) * HEAD_SIZE)
        query = x_ref[:, 0, 0, :, lanes].reshape(count, HEAD_SIZE)
        key_rows = x_ref[:, 1, 0, :, lanes].reshape(count, HEAD_SIZE)
        value_rows = with_ones(x_ref[:, 2, 0, :, lanes].reshape(count, HEAD_SIZE))
        for b in range(count // TILE):
            part = query[b * TILE : (b + 1) * TILE]
            blocks = [scores(part, key_rows[e * TILE : (e + 1) * TILE]) for e in range(b + 1)]
            blocks[b] = jnp.where(col <= row, blocks[b], BIG_NEG)
            units.append((lanes, b, blocks, value_rows))
    for lanes, b, blocks, value_rows in units:
        result = weighted(
            blocks, [value_rows[e * TILE : (e + 1) * TILE] for e in range(b + 1)]
        ).astype(BF16)
        held_ref[b * sources : (b + 1) * sources, :, lanes] = result.reshape(
            sources, rows, HEAD_SIZE
        )
    for slot in range(ctx):
        o_refs[slot][0] = held_ref[partner(place_ref[0], slot, ctx)]


def stride_attend(place, moved, waits):
    ctx, _, per, rows, width = moved.shape
    count = ctx * rows
    pairs = per * (width // HEAD_SIZE) * count * (count + TILE) // 2
    return pl.pallas_call(
        stride_kernel,
        grid=(per,),
        in_specs=[
            pl.BlockSpec(memory_space=pltpu.SMEM),
            pl.BlockSpec((ctx, 3, 1, rows, width), lambda r: (0, 0, r, 0, 0)),
        ]
        + moments(waits),
        out_specs=[pl.BlockSpec((1, rows, width), lambda r: (r, 0, 0))] * ctx + [mark_spec()],
        out_shape=[jax.ShapeDtypeStruct((per, rows, width), BF16)] * ctx + [MARK],
        scratch_shapes=[pltpu.VMEM((ctx, rows, width), BF16)],
        compiler_params=params(24),
        cost_estimate=cost(8 * pairs * HEAD_SIZE, 8 * per * count * width, pairs),
        name="stride",
    )(place, moved, *waits)


def combine_kernel(seat_ref, home_ref, *refs, slots, ctx):
    back_refs, o_refs, mark_ref = refs[:ctx], refs[-slots - 1 : -1], refs[-1]
    mark_ref[...] = jnp.zeros_like(mark_ref)
    tokens_dev, width = home_ref.shape
    size = tokens_dev // slots
    per = STRIDE // ctx
    token = iota2((TILE, TILE), 0)
    col = iota2((TILE, TILE), 1)
    group = col >> 4
    residue = partner(seat_ref[1], group // per, ctx) * per + group % per
    matrix = (token == (col & 15) * 16 + residue).astype(BF16)
    for slot in range(slots):
        owner = partner(seat_ref[0], slot, slots)
        for b in range(size // TILE):
            first = owner * (size // TILE) + b
            here = pl.ds(pl.multiple_of(first * STRIDE, STRIDE), STRIDE)
            rows = [ref[r, here] for ref in back_refs for r in range(per)]
            back = dot(matrix, jnp.concatenate(rows))
            home = home_ref[pl.ds(pl.multiple_of(first * TILE, TILE), TILE)]
            o_refs[slot][b * TILE : (b + 1) * TILE] = (home + back).astype(BF16)


def combine(seat, home, backs, slots, waits):
    tokens_dev, width = home.shape
    size = tokens_dev // slots
    return pl.pallas_call(
        functools.partial(combine_kernel, slots=slots, ctx=len(backs)),
        in_specs=[pl.BlockSpec(memory_space=pltpu.SMEM)]
        + [pl.BlockSpec(memory_space=pltpu.VMEM)] * (1 + len(backs))
        + moments(waits),
        out_specs=[pl.BlockSpec(memory_space=pltpu.VMEM)] * (slots + 1),
        out_shape=[jax.ShapeDtypeStruct((size, width), BF16)] * slots + [MARK],
        compiler_params=params(24),
        cost_estimate=cost(2 * tokens_dev * TILE * width, 8 * tokens_dev * width),
        name="combine",
    )(seat, home, *backs, *waits)


def project_kernel(side_ref, *refs, slots, chunks):
    moved_refs, (mine_ref, other_ref, o_ref) = refs[: slots * chunks], refs[slots * chunks :]
    width = moved_refs[0].shape[1]

    def add_up(weight_ref):
        total = None
        for slot in range(slots):
            group = partner(side_ref[1], slot, slots)
            for chunk in range(chunks):
                rows = weight_ref[group, chunk * width : (chunk + 1) * width]
                part = dot(moved_refs[chunk * slots + slot][...], rows)
                total = part if total is None else total + part
        o_ref[...] = total.astype(BF16)

    @pl.when(pl.program_id(0) == 0)
    def _():
        add_up(mine_ref)

    @pl.when(pl.program_id(0) == 1)
    def _():
        add_up(other_ref)


def project(side, moved, mine, other):
    chunks, slots = len(moved), len(moved[0])
    tokens, part = moved[0][0].shape
    width, half = mine.shape[1:]
    tile = min(half, 256)
    tiles = half // tile
    block = (slots, width, tile)
    return pl.pallas_call(
        functools.partial(project_kernel, slots=slots, chunks=chunks),
        grid_spec=pltpu.PrefetchScalarGridSpec(
            num_scalar_prefetch=1,
            grid=(2, tiles),
            in_specs=[pl.BlockSpec((tokens, part), lambda s, j, side: (0, 0))] * (slots * chunks)
            + [
                pl.BlockSpec(block, lambda s, j, side: (0, 0, jnp.where(s == 0, j, tiles - 1))),
                pl.BlockSpec(block, lambda s, j, side: (0, 0, jnp.where(s == 0, 0, j))),
            ],
            out_specs=pl.BlockSpec(
                (tokens, tile), lambda s, j, side: (0, (s ^ side[0]) * tiles + j)
            ),
        ),
        out_shape=jax.ShapeDtypeStruct((tokens, 2 * half), BF16),
        compiler_params=params(24),
        cost_estimate=cost(
            4 * slots * tokens * width * half, 2 * slots * width * (2 * half + tokens)
        ),
        name="project",
    )(side, *[slab for slabs in moved for slab in slabs], mine, other)


def gather_ctx(rows):
    count = lax.axis_size("ctx")

    def swapped(piece, distance):
        return lax.ppermute(piece, "ctx", [(i, i ^ distance) for i in range(count)])

    order = list(range(0, count, 2))
    pieces = [rows] + [swapped(rows, distance) for distance in order[1:]]
    within = [swapped(piece, 1) for piece in pieces]
    return pieces, within, order + [i ^ 1 for i in order]


def stride_general(queries, keys, values):
    tokens_dev, width = queries.shape
    heads = width // HEAD_SIZE
    ctx = lax.axis_size("ctx")
    copies = max(ctx // STRIDE, 1)
    rows = tokens_dev // STRIDE
    held_rows = ctx * rows // copies
    own_copy = lax.axis_index("ctx") // STRIDE
    query_pos = (jnp.arange(held_rows) // (rows // copies)) * rows
    query_pos = query_pos + (jnp.arange(held_rows) % (rows // copies)) * copies + own_copy
    shaped = queries.reshape(1, rows // copies, ctx, width)
    query = lax.all_to_all(shaped, "ctx", split_axis=2, concat_axis=1, tiled=True)
    query = query.reshape(held_rows, heads, HEAD_SIZE)
    both = jnp.stack([keys, values]).reshape(2, rows, 1, STRIDE, width)
    both = jnp.broadcast_to(both, (2, rows, copies, STRIDE, width)).reshape(2, rows, ctx, width)
    both = lax.all_to_all(both, "ctx", split_axis=2, concat_axis=1, tiled=True)
    both = both.reshape(2, ctx * rows, heads, HEAD_SIZE)
    allowed = jnp.arange(ctx * rows)[None, :] <= query_pos[:, None]

    def one_head(operands):
        head_query, head_keys, head_values = operands
        masked = jnp.where(allowed, scores(head_query, head_keys), BIG_NEG)
        return weighted([masked], [with_ones(head_values)])

    result = lax.map(
        one_head,
        (query.transpose(1, 0, 2), both[0].transpose(1, 0, 2), both[1].transpose(1, 0, 2)),
    )
    result = result.transpose(1, 0, 2).reshape(ctx, rows // copies, 1, width).astype(BF16)
    back = lax.all_to_all(result, "ctx", split_axis=0, concat_axis=2, tiled=True)
    return back.reshape(tokens_dev, width)


def body(queries, keys, values, out_weight, chunks):
    tokens_dev, width = queries.shape
    ctx = lax.axis_size("ctx")
    groups = lax.axis_size("head")
    place = lax.axis_index("ctx")
    place_word = place.astype(jnp.int32).reshape(1)
    side = place % 2
    sibling = [(i, i ^ 1) for i in range(ctx)]

    half = out_weight.shape[1] // 2
    part = width // chunks
    weight_half = lax.dynamic_slice_in_dim(out_weight, side * half, half, axis=1)
    mine = lax.all_gather(weight_half, "head", axis=0)

    rim, picked = edges(keys, values)
    between, within, order = gather_ctx(picked)
    summary = between + within
    before = lax.ppermute(rim, "ctx", [(i, i + 1) for i in range(ctx - 1)])
    if ctx > STRIDE:
        stride_out = stride_general(queries, keys, values)
    else:
        sends = [
            prepare(queries, keys, values, ctx, chunk, chunks, within[-1:] if chunk else (picked,))
            for chunk in range(chunks)
        ]
        sends[0] = after(sends[0], (between[-1], before))

    def home(chunk, waits):
        return home_sections(
            place_word, queries, keys, values, before, summary, order, chunk, chunks, waits
        )

    seat = lax.axis_index("head").astype(jnp.int32)

    def exchange(slabs, axis):
        count = len(slabs)
        moved = [slabs[0]]
        for slot in range(1, count):
            pairs = [(i, partner(i, slot, count)) for i in range(count)]
            moved.append(lax.ppermute(slabs[slot], axis, pairs))
        return moved

    moved, waits = [], ()
    if ctx > STRIDE:
        for chunk in range(chunks):
            lanes = slice(chunk * part, (chunk + 1) * part)
            homes, mark = home(chunk, waits)
            attended = (homes + stride_out[:, lanes].astype(F32)).astype(BF16)
            attended = attended.reshape(groups, tokens_dev // groups, part)
            owners = [partner(seat, slot, groups) for slot in range(groups)]
            moved.append(exchange([attended[owner] for owner in owners], "head"))
            waits = (mark,)
    else:
        seats = jnp.stack([seat, place.astype(jnp.int32)])
        homes, backs = [], []
        for chunk in range(chunks):
            sections, mark = home(chunk, waits)
            homes.append(sections)
            waits = (mark,)
        if chunks > 1:
            sends[1] = after(sends[1], waits)
        for chunk in range(chunks):
            received = lax.all_to_all(sends[chunk], "ctx", split_axis=0, concat_axis=0, tiled=True)
            *slabs, mark = stride_attend(place_word, received, waits)
            backs.append(exchange(slabs, "ctx"))
            waits = (mark,)
        for chunk in range(chunks):
            *slabs, mark = combine(seats, homes[chunk], backs[chunk], groups, waits)
            moved.append(exchange(slabs, "head"))
            waits = (mark, *moved[-1][1:])
    held = after(mine, (mark,))
    other = lax.ppermute(held, "ctx", sibling)
    sides = jnp.stack([side.astype(jnp.int32), seat])
    return project(sides, moved, held, other)


def solution(mesh):
    chunks = 2 if HEADS // mesh.shape["head"] > 1 else 1
    placed = (P("ctx", "head"), P("ctx", "head"), P("ctx", "head"), P("head", None))
    return jax.shard_map(
        functools.partial(body, chunks=chunks),
        mesh=mesh,
        in_specs=placed,
        out_specs=P(("ctx", "head"), None),
        check_vma=False,
    )
```

```python
import functools
import math

import jax
import jax.numpy as jnp
from jax import lax
from jax.experimental import pallas as pl
from jax.experimental.pallas import tpu as pltpu
from jax.sharding import PartitionSpec as P

HEADS = 16
HEAD_SIZE = 128
WINDOW = 512
STRIDE = 16
BLOCK = 128
SUMCOLS = 8

BIG_NEG = -1e30
TILE = 256
LOG_SCALE = HEAD_SIZE ** (-0.5) * math.log2(math.e)
F32 = jnp.float32
BF16 = jnp.bfloat16


def params(mib):
    return pltpu.CompilerParams(vmem_limit_bytes=mib * 1024 * 1024)


MARK = jax.ShapeDtypeStruct((8, 128), F32)


def mark_spec():
    return pl.BlockSpec(MARK.shape, lambda *place: (0, 0))


def moments(arrays):
    return [pl.BlockSpec(memory_space=pl.ANY)] * len(arrays)


def after(array, others):
    anywhere = pl.BlockSpec(memory_space=pl.ANY)
    return pl.pallas_call(
        lambda *refs: None,
        in_specs=[anywhere] * (1 + len(others)),
        out_specs=anywhere,
        out_shape=jax.ShapeDtypeStruct(array.shape, array.dtype),
        input_output_aliases={0: 0},
        compiler_params=params(60),
        cost_estimate=cost(0, 0),
        name="after",
    )(array, *others)


def cost(flops, bytes_accessed, exps=0):
    return pl.CostEstimate(
        flops=int(flops), bytes_accessed=int(bytes_accessed), transcendentals=int(exps)
    )


def partner(place, slot, count):
    assert count & (count - 1) == 0
    return place ^ slot


def iota2(shape, dim):
    return lax.broadcasted_iota(jnp.int32, shape, dim)


def scores(query, key_rows):
    return lax.dot_general(query, key_rows, (((1,), (1,)), ((), ())), preferred_element_type=F32)


def dot(left, right):
    return jnp.dot(left, right, preferred_element_type=F32)


def regroup_matrix():
    rows = iota2((TILE, TILE), 0)
    cols = iota2((TILE, TILE), 1)
    return (cols == (rows & 15) * 16 + (rows >> 4)).astype(BF16)


def with_ones(value_rows):
    return jnp.concatenate([value_rows, jnp.ones_like(value_rows)], axis=1)


def weighted(score_blocks, value_blocks, extra=None):
    top = functools.reduce(jnp.maximum, score_blocks)
    top = jnp.max(top, axis=-1, keepdims=True)
    if extra is not None:
        top = jnp.maximum(top, extra[0])
    total = None
    for block, value_block in zip(score_blocks, value_blocks):
        weights = jnp.exp2((block - top) * LOG_SCALE).astype(BF16)
        part = dot(weights, value_block)
        total = part if total is None else total + part
    if extra is not None:
        own = jnp.exp2((extra[0] - top) * LOG_SCALE).astype(BF16).astype(F32)
        total = total + own * extra[1].astype(F32)
    return total[:, :HEAD_SIZE] / total[:, HEAD_SIZE:]


def edge_kernel(k_ref, v_ref, k_ends_ref, v_ends_ref, *refs):
    rim_ref, sum_ref = refs[-2:]
    rim_ref[0] = k_ref[...]
    rim_ref[1] = v_ref[...]

    @pl.when(pl.program_id(0) == 0)
    def _():
        for number, ref in enumerate((k_ends_ref, v_ends_ref)):
            rows = ref[...].astype(F32)[:, 16 - SUMCOLS :]
            sum_ref[number] = rows.reshape(sum_ref.shape[1:]).astype(BF16)


def edges(keys, values, waits):
    tokens_dev, width = keys.shape
    blocks = tokens_dev // BLOCK
    first = (tokens_dev - WINDOW) // TILE
    source = pl.BlockSpec((TILE, width), lambda i: (first + i, 0))
    ends = pl.BlockSpec((blocks, 16, width), lambda i: (0, BLOCK // 16 - 1, 0))
    shape = (2, blocks * SUMCOLS, width)
    return pl.pallas_call(
        edge_kernel,
        grid=(WINDOW // TILE,),
        in_specs=[source] * 2 + [ends] * 2 + moments(waits),
        out_specs=[
            pl.BlockSpec((2, TILE, width), lambda i: (0, i, 0)),
            pl.BlockSpec(shape, lambda i: (0, 0, 0)),
        ],
        out_shape=[
            jax.ShapeDtypeStruct((2, WINDOW, width), BF16),
            jax.ShapeDtypeStruct(shape, BF16),
        ],
        compiler_params=params(60),
        cost_estimate=cost(0, 8 * WINDOW * width),
        name="edges",
    )(
        keys,
        values,
        keys.reshape(blocks, BLOCK, width),
        values.reshape(blocks, BLOCK, width),
        *waits,
    )


def prep_kernel(q_ref, k_ref, v_ref, *refs):
    send_ref = refs[-1]
    matrix = regroup_matrix()
    ctx, _, per, rows, width = send_ref.shape
    for number, ref in enumerate((q_ref, k_ref, v_ref)):
        grouped = dot(matrix, ref[...]).astype(BF16)
        send_ref[:, number] = grouped.reshape(ctx, per, rows, width)


def prepare(queries, keys, values, ctx, chunk, chunks, waits):
    tokens_dev, width = queries.shape
    per = STRIDE // ctx
    part = width // chunks
    return pl.pallas_call(
        prep_kernel,
        grid=(tokens_dev // TILE,),
        in_specs=[pl.BlockSpec((TILE, part), lambda b: (b, chunk))] * 3 + moments(waits),
        out_specs=pl.BlockSpec((ctx, 3, per, TILE // STRIDE, part), lambda b: (0, 0, 0, b, 0)),
        out_shape=jax.ShapeDtypeStruct((ctx, 3, per, tokens_dev // STRIDE, part), BF16),
        compiler_params=params(60),
        cost_estimate=cost(6 * tokens_dev * TILE * part, 12 * tokens_dev * part),
        name="prepare",
    )(queries, keys, values, *waits)


def home_kernel(place_ref, q_ref, k_ref, v_ref, rim_ref, *refs, order):
    sum_refs, (o_ref, mark_ref) = refs[: len(order)], refs[-2:]
    mark_ref[...] = jnp.zeros_like(mark_ref)
    place = place_ref[0]
    tokens_dev = q_ref.shape[0]
    back = WINDOW // TILE
    key_blocks = [rim_ref[0, e * TILE : (e + 1) * TILE] for e in range(back)]
    value_blocks = [with_ones(rim_ref[1, e * TILE : (e + 1) * TILE]) for e in range(back)]
    for e in range(tokens_dev // TILE):
        key_blocks.append(k_ref[e * TILE : (e + 1) * TILE])
        value_blocks.append(with_ones(v_ref[e * TILE : (e + 1) * TILE]))
    picks = sum_refs[0].shape[1]
    sum_keys = jnp.concatenate([ref[0] for ref in sum_refs])
    sum_values = with_ones(jnp.concatenate([ref[1] for ref in sum_refs]))
    sum_col = jnp.concatenate(
        [iota2((TILE, picks), 1) + (place ^ i) * picks for i in order], axis=1
    )
    row = iota2((TILE, TILE), 0)
    col = iota2((TILE, TILE), 1)
    for b in range(tokens_dev // TILE):
        query = q_ref[b * TILE : (b + 1) * TILE]
        blocks = []
        for e in range(back + 1):
            block = scores(query, key_blocks[b + e])
            allowed = None
            if e == 0:
                allowed = col > row
            if e == back:
                allowed = col <= row
            if b + e < back:
                held = place > 0
                allowed = held if allowed is None else allowed & held
            if allowed is not None:
                block = jnp.where(allowed, block, BIG_NEG)
            blocks.append(block)
        local = weighted(blocks, value_blocks[b : b + back + 1])
        pos = place * tokens_dev + b * TILE + iota2((TILE, 1), 0)
        within = pos % BLOCK
        held = pos // BLOCK * SUMCOLS + jnp.maximum(within - (BLOCK - SUMCOLS - 1), 0)
        block = jnp.where(sum_col < held, scores(query, sum_keys), BIG_NEG)
        own_key = key_blocks[b + back].astype(F32)
        own = jnp.sum(query.astype(F32) * own_key, axis=-1, keepdims=True)
        own = jnp.where(within < BLOCK - SUMCOLS, own, BIG_NEG)
        summary = weighted([block], [sum_values], (own, value_blocks[b + back]))
        o_ref[b * TILE : (b + 1) * TILE] = local + summary


def home_sections(place, queries, keys, values, rim, summary, order, chunk, chunks, waits):
    tokens_dev, width = queries.shape
    heads = width // chunks // HEAD_SIZE
    first = chunk * heads
    picks = summary[0].shape[1]
    total = len(summary) * picks
    own = pl.BlockSpec((tokens_dev, HEAD_SIZE), lambda h: (0, first + h))
    pairs = tokens_dev * (WINDOW + TILE + total) * heads
    return pl.pallas_call(
        functools.partial(home_kernel, order=order),
        grid=(heads,),
        in_specs=[
            pl.BlockSpec(memory_space=pltpu.SMEM),
            own,
            own,
            own,
            pl.BlockSpec((2, WINDOW, HEAD_SIZE), lambda h: (0, 0, first + h)),
        ]
        + [pl.BlockSpec((2, picks, HEAD_SIZE), lambda h: (0, 0, first + h))] * len(summary)
        + moments(waits),
        out_specs=[pl.BlockSpec((tokens_dev, HEAD_SIZE), lambda h: (0, h)), mark_spec()],
        out_shape=[jax.ShapeDtypeStruct((tokens_dev, heads * HEAD_SIZE), F32), MARK],
        compiler_params=params(60),
        cost_estimate=cost(8 * pairs * HEAD_SIZE, 14 * tokens_dev * width, pairs),
        name="home",
    )(place, queries, keys, values, rim, *summary, *waits)


def stride_kernel(place_ref, x_ref, *refs):
    ctx, _, _, rows, width = x_ref.shape
    o_refs, mark_ref, held_ref = refs[-ctx - 2 : -2], refs[-2], refs[-1]
    mark_ref[...] = jnp.zeros_like(mark_ref)
    count = ctx * rows
    row = iota2((TILE, TILE), 0)
    col = iota2((TILE, TILE), 1)
    sources = TILE // rows
    units = []
    for head in range(width // HEAD_SIZE):
        lanes = slice(head * HEAD_SIZE, (head + 1) * HEAD_SIZE)
        query = x_ref[:, 0, 0, :, lanes].reshape(count, HEAD_SIZE)
        key_rows = x_ref[:, 1, 0, :, lanes].reshape(count, HEAD_SIZE)
        value_rows = with_ones(x_ref[:, 2, 0, :, lanes].reshape(count, HEAD_SIZE))
        for b in range(count // TILE):
            part = query[b * TILE : (b + 1) * TILE]
            blocks = [scores(part, key_rows[e * TILE : (e + 1) * TILE]) for e in range(b + 1)]
            blocks[b] = jnp.where(col <= row, blocks[b], BIG_NEG)
            units.append((lanes, b, blocks, value_rows))
    for lanes, b, blocks, value_rows in units:
        result = weighted(
            blocks, [value_rows[e * TILE : (e + 1) * TILE] for e in range(b + 1)]
        ).astype(BF16)
        held_ref[b * sources : (b + 1) * sources, :, lanes] = result.reshape(
            sources, rows, HEAD_SIZE
        )
    for slot in range(ctx):
        o_refs[slot][0] = held_ref[partner(place_ref[0], slot, ctx)]


def stride_attend(place, moved, waits):
    ctx, _, per, rows, width = moved.shape
    count = ctx * rows
    pairs = per * (width // HEAD_SIZE) * count * (count + TILE) // 2
    return pl.pallas_call(
        stride_kernel,
        grid=(per,),
        in_specs=[
            pl.BlockSpec(memory_space=pltpu.SMEM),
            pl.BlockSpec((ctx, 3, 1, rows, width), lambda r: (0, 0, r, 0, 0)),
        ]
        + moments(waits),
        out_specs=[pl.BlockSpec((1, rows, width), lambda r: (r, 0, 0))] * ctx + [mark_spec()],
        out_shape=[jax.ShapeDtypeStruct((per, rows, width), BF16)] * ctx + [MARK],
        scratch_shapes=[pltpu.VMEM((ctx, rows, width), BF16)],
        compiler_params=params(24),
        cost_estimate=cost(8 * pairs * HEAD_SIZE, 8 * per * count * width, pairs),
        name="stride",
    )(place, moved, *waits)


def combine_kernel(seat_ref, home_ref, *refs, slots, ctx):
    back_refs, o_refs, mark_ref = refs[:ctx], refs[-slots - 1 : -1], refs[-1]
    mark_ref[...] = jnp.zeros_like(mark_ref)
    tokens_dev, width = home_ref.shape
    size = tokens_dev // slots
    per = STRIDE // ctx
    token = iota2((TILE, TILE), 0)
    col = iota2((TILE, TILE), 1)
    group = col >> 4
    residue = partner(seat_ref[1], group // per, ctx) * per + group % per
    matrix = (token == (col & 15) * 16 + residue).astype(BF16)
    for slot in range(slots):
        owner = partner(seat_ref[0], slot, slots)
        for b in range(size // TILE):
            first = owner * (size // TILE) + b
            here = pl.ds(pl.multiple_of(first * STRIDE, STRIDE), STRIDE)
            rows = [ref[r, here] for ref in back_refs for r in range(per)]
            back = dot(matrix, jnp.concatenate(rows))
            home = home_ref[pl.ds(pl.multiple_of(first * TILE, TILE), TILE)]
            o_refs[slot][b * TILE : (b + 1) * TILE] = (home + back).astype(BF16)


def combine(seat, home, backs, slots, waits):
    tokens_dev, width = home.shape
    size = tokens_dev // slots
    return pl.pallas_call(
        functools.partial(combine_kernel, slots=slots, ctx=len(backs)),
        in_specs=[pl.BlockSpec(memory_space=pltpu.SMEM)]
        + [pl.BlockSpec(memory_space=pltpu.VMEM)] * (1 + len(backs))
        + moments(waits),
        out_specs=[pl.BlockSpec(memory_space=pltpu.VMEM)] * (slots + 1),
        out_shape=[jax.ShapeDtypeStruct((size, width), BF16)] * slots + [MARK],
        compiler_params=params(24),
        cost_estimate=cost(2 * tokens_dev * TILE * width, 8 * tokens_dev * width),
        name="combine",
    )(seat, home, *backs, *waits)


def project_kernel(side_ref, *refs, slots, chunks):
    moved_refs, (mine_ref, other_ref, o_ref) = refs[: slots * chunks], refs[slots * chunks :]
    width = moved_refs[0].shape[1]

    def add_up(weight_ref):
        total = None
        for slot in range(slots):
            group = partner(side_ref[1], slot, slots)
            for chunk in range(chunks):
                rows = weight_ref[group, chunk * width : (chunk + 1) * width]
                part = dot(moved_refs[chunk * slots + slot][...], rows)
                total = part if total is None else total + part
        o_ref[...] = total.astype(BF16)

    @pl.when(pl.program_id(0) == 0)
    def _():
        add_up(mine_ref)

    @pl.when(pl.program_id(0) == 1)
    def _():
        add_up(other_ref)


def project(side, moved, mine, other):
    chunks, slots = len(moved), len(moved[0])
    tokens, part = moved[0][0].shape
    width, half = mine.shape[1:]
    tile = min(half, 256)
    tiles = half // tile
    block = (slots, width, tile)
    return pl.pallas_call(
        functools.partial(project_kernel, slots=slots, chunks=chunks),
        grid_spec=pltpu.PrefetchScalarGridSpec(
            num_scalar_prefetch=1,
            grid=(2, tiles),
            in_specs=[pl.BlockSpec((tokens, part), lambda s, j, side: (0, 0))] * (slots * chunks)
            + [
                pl.BlockSpec(block, lambda s, j, side: (0, 0, jnp.where(s == 0, j, tiles - 1))),
                pl.BlockSpec(block, lambda s, j, side: (0, 0, jnp.where(s == 0, 0, j))),
            ],
            out_specs=pl.BlockSpec(
                (tokens, tile), lambda s, j, side: (0, (s ^ side[0]) * tiles + j)
            ),
        ),
        out_shape=jax.ShapeDtypeStruct((tokens, 2 * half), BF16),
        compiler_params=params(24),
        cost_estimate=cost(
            4 * slots * tokens * width * half, 2 * slots * width * (2 * half + tokens)
        ),
        name="project",
    )(side, *[slab for slabs in moved for slab in slabs], mine, other)


def gather_ctx(rows):
    count = lax.axis_size("ctx")

    def swapped(piece, distance):
        return lax.ppermute(piece, "ctx", [(i, i ^ distance) for i in range(count)])

    order = list(range(0, count, 2))
    pieces = [rows] + [swapped(rows, distance) for distance in order[1:]]
    within = [swapped(piece, 1) for piece in pieces]
    return pieces, within, order + [i ^ 1 for i in order]


def stride_general(queries, keys, values):
    tokens_dev, width = queries.shape
    heads = width // HEAD_SIZE
    ctx = lax.axis_size("ctx")
    copies = max(ctx // STRIDE, 1)
    rows = tokens_dev // STRIDE
    held_rows = ctx * rows // copies
    own_copy = lax.axis_index("ctx") // STRIDE
    query_pos = (jnp.arange(held_rows) // (rows // copies)) * rows
    query_pos = query_pos + (jnp.arange(held_rows) % (rows // copies)) * copies + own_copy
    shaped = queries.reshape(1, rows // copies, ctx, width)
    query = lax.all_to_all(shaped, "ctx", split_axis=2, concat_axis=1, tiled=True)
    query = query.reshape(held_rows, heads, HEAD_SIZE)
    both = jnp.stack([keys, values]).reshape(2, rows, 1, STRIDE, width)
    both = jnp.broadcast_to(both, (2, rows, copies, STRIDE, width)).reshape(2, rows, ctx, width)
    both = lax.all_to_all(both, "ctx", split_axis=2, concat_axis=1, tiled=True)
    both = both.reshape(2, ctx * rows, heads, HEAD_SIZE)
    allowed = jnp.arange(ctx * rows)[None, :] <= query_pos[:, None]

    def one_head(operands):
        head_query, head_keys, head_values = operands
        masked = jnp.where(allowed, scores(head_query, head_keys), BIG_NEG)
        return weighted([masked], [with_ones(head_values)])

    result = lax.map(
        one_head,
        (query.transpose(1, 0, 2), both[0].transpose(1, 0, 2), both[1].transpose(1, 0, 2)),
    )
    result = result.transpose(1, 0, 2).reshape(ctx, rows // copies, 1, width).astype(BF16)
    back = lax.all_to_all(result, "ctx", split_axis=0, concat_axis=2, tiled=True)
    return back.reshape(tokens_dev, width)


def body(queries, keys, values, out_weight, chunks):
    tokens_dev, width = queries.shape
    ctx = lax.axis_size("ctx")
    groups = lax.axis_size("head")
    place = lax.axis_index("ctx")
    place_word = place.astype(jnp.int32).reshape(1)
    side = place % 2
    sibling = [(i, i ^ 1) for i in range(ctx)]

    half = out_weight.shape[1] // 2
    part = width // chunks
    weight_half = lax.dynamic_slice_in_dim(out_weight, side * half, half, axis=1)
    mine = lax.all_gather(weight_half, "head", axis=0)

    sends = []
    if ctx <= STRIDE:
        sends.append(prepare(queries, keys, values, ctx, 0, chunks, ()))
    rim, picked = edges(keys, values, sends)
    between, within, order = gather_ctx(picked)
    summary = between + within
    if ctx > STRIDE:
        stride_out = stride_general(queries, keys, values)
    for chunk in range(len(sends), chunks * len(sends)):
        sends.append(prepare(queries, keys, values, ctx, chunk, chunks, (picked,)))
    rim = after(rim, (*between[1:], *sends[1:]))
    before = lax.ppermute(rim, "ctx", [(i, i + 1) for i in range(ctx - 1)])
    sends[1:] = [after(send, between[1:]) for send in sends[1:]]

    def home(chunk, waits):
        return home_sections(
            place_word, queries, keys, values, before, summary, order, chunk, chunks, waits
        )

    seat = lax.axis_index("head").astype(jnp.int32)

    def exchange(slabs, axis):
        count = len(slabs)
        moved = [slabs[0]]
        for slot in range(1, count):
            pairs = [(i, partner(i, slot, count)) for i in range(count)]
            moved.append(lax.ppermute(slabs[slot], axis, pairs))
        return moved

    moved, waits = [], ()
    if ctx > STRIDE:
        for chunk in range(chunks):
            lanes = slice(chunk * part, (chunk + 1) * part)
            homes, mark = home(chunk, waits)
            attended = (homes + stride_out[:, lanes].astype(F32)).astype(BF16)
            attended = attended.reshape(groups, tokens_dev // groups, part)
            owners = [partner(seat, slot, groups) for slot in range(groups)]
            moved.append(exchange([attended[owner] for owner in owners], "head"))
            waits = (mark,)
    else:
        seats = jnp.stack([seat, place.astype(jnp.int32)])
        homes, backs = [], []
        for chunk in range(chunks):
            received = lax.all_to_all(sends[chunk], "ctx", split_axis=0, concat_axis=0, tiled=True)
            *slabs, mark = stride_attend(place_word, received, waits)
            backs.append(exchange(slabs, "ctx"))
            waits = (mark,)
            for ready in range(chunks) if chunk == 0 else ():
                sections, mark = home(ready, waits)
                homes.append(sections)
                waits = (mark,)
        for chunk in range(chunks):
            *slabs, mark = combine(seats, homes[chunk], backs[chunk], groups, waits)
            moved.append(exchange(slabs, "head"))
            waits = (mark, *moved[-1][1:3])
    held = after(mine, (mark,))
    other = lax.ppermute(held, "ctx", sibling)
    sides = jnp.stack([side.astype(jnp.int32), seat])
    return project(sides, moved, held, other)


def solution(mesh):
    chunks = 2 if HEADS // mesh.shape["head"] > 1 else 1
    placed = (P("ctx", "head"), P("ctx", "head"), P("ctx", "head"), P("head", None))
    return jax.shard_map(
        functools.partial(body, chunks=chunks),
        mesh=mesh,
        in_specs=placed,
        out_specs=P(("ctx", "head"), None),
        check_vma=False,
    )
```

```python
import functools
import math

import jax
import jax.numpy as jnp
from jax import lax
from jax.experimental import pallas as pl
from jax.experimental.pallas import tpu as pltpu
from jax.sharding import PartitionSpec as P

HEADS = 16
HEAD_SIZE = 128
WINDOW = 512
STRIDE = 16
BLOCK = 128
SUMCOLS = 8

BIG_NEG = -1e30
TILE = 256
LOG_SCALE = HEAD_SIZE ** (-0.5) * math.log2(math.e)
F32 = jnp.float32
BF16 = jnp.bfloat16


def params(mib):
    return pltpu.CompilerParams(vmem_limit_bytes=mib * 1024 * 1024)


MARK = jax.ShapeDtypeStruct((8, 128), F32)


def mark_spec():
    return pl.BlockSpec(MARK.shape, lambda *place: (0, 0))


def moments(arrays):
    return [pl.BlockSpec(memory_space=pl.ANY)] * len(arrays)


def after(array, others):
    anywhere = pl.BlockSpec(memory_space=pl.ANY)
    return pl.pallas_call(
        lambda *refs: None,
        in_specs=[anywhere] * (1 + len(others)),
        out_specs=anywhere,
        out_shape=jax.ShapeDtypeStruct(array.shape, array.dtype),
        input_output_aliases={0: 0},
        compiler_params=params(60),
        cost_estimate=cost(0, 0),
        name="after",
    )(array, *others)


def cost(flops, bytes_accessed, exps=0):
    return pl.CostEstimate(
        flops=int(flops), bytes_accessed=int(bytes_accessed), transcendentals=int(exps)
    )


def partner(place, slot, count):
    assert count & (count - 1) == 0
    return place ^ slot


def iota2(shape, dim):
    return lax.broadcasted_iota(jnp.int32, shape, dim)


def scores(query, key_rows):
    return lax.dot_general(query, key_rows, (((1,), (1,)), ((), ())), preferred_element_type=F32)


def dot(left, right):
    return jnp.dot(left, right, preferred_element_type=F32)


def regroup_matrix():
    rows = iota2((TILE, TILE), 0)
    cols = iota2((TILE, TILE), 1)
    return (cols == (rows & 15) * 16 + (rows >> 4)).astype(BF16)


def with_ones(value_rows):
    return jnp.concatenate([value_rows, jnp.ones_like(value_rows)], axis=1)


def weighted(score_blocks, value_blocks, extra=None):
    top = functools.reduce(jnp.maximum, score_blocks)
    top = jnp.max(top, axis=-1, keepdims=True)
    if extra is not None:
        top = jnp.maximum(top, extra[0])
    total = None
    for block, value_block in zip(score_blocks, value_blocks):
        weights = jnp.exp2((block - top) * LOG_SCALE).astype(BF16)
        part = dot(weights, value_block)
        total = part if total is None else total + part
    if extra is not None:
        own = jnp.exp2((extra[0] - top) * LOG_SCALE).astype(BF16).astype(F32)
        total = total + own * extra[1].astype(F32)
    return total[:, :HEAD_SIZE] / total[:, HEAD_SIZE:]


def edge_kernel(k_ref, v_ref, k_ends_ref, v_ends_ref, *refs):
    rim_ref, sum_ref = refs[-2:]
    rim_ref[0] = k_ref[...]
    rim_ref[1] = v_ref[...]

    @pl.when(pl.program_id(0) == 0)
    def _():
        for number, ref in enumerate((k_ends_ref, v_ends_ref)):
            rows = ref[...].astype(F32)[:, 16 - SUMCOLS :]
            sum_ref[number] = rows.reshape(sum_ref.shape[1:]).astype(BF16)


def edges(keys, values, waits):
    tokens_dev, width = keys.shape
    blocks = tokens_dev // BLOCK
    first = (tokens_dev - WINDOW) // TILE
    source = pl.BlockSpec((TILE, width), lambda i: (first + i, 0))
    ends = pl.BlockSpec((blocks, 16, width), lambda i: (0, BLOCK // 16 - 1, 0))
    shape = (2, blocks * SUMCOLS, width)
    return pl.pallas_call(
        edge_kernel,
        grid=(WINDOW // TILE,),
        in_specs=[source] * 2 + [ends] * 2 + moments(waits),
        out_specs=[
            pl.BlockSpec((2, TILE, width), lambda i: (0, i, 0)),
            pl.BlockSpec(shape, lambda i: (0, 0, 0)),
        ],
        out_shape=[
            jax.ShapeDtypeStruct((2, WINDOW, width), BF16),
            jax.ShapeDtypeStruct(shape, BF16),
        ],
        compiler_params=params(60),
        cost_estimate=cost(0, 8 * WINDOW * width),
        name="edges",
    )(
        keys,
        values,
        keys.reshape(blocks, BLOCK, width),
        values.reshape(blocks, BLOCK, width),
        *waits,
    )


def half_kernel(side_ref, weight_ref, *refs):
    refs[-1][...] = weight_ref[...]


def half_of(side, weight, waits):
    rows, width = weight.shape
    return pl.pallas_call(
        half_kernel,
        grid_spec=pltpu.PrefetchScalarGridSpec(
            num_scalar_prefetch=1,
            grid=(2,),
            in_specs=[pl.BlockSpec((rows // 2, width // 2), lambda i, side: (i, side[0]))]
            + moments(waits),
            out_specs=pl.BlockSpec((rows // 2, width // 2), lambda i, side: (i, 0)),
        ),
        out_shape=jax.ShapeDtypeStruct((rows, width // 2), BF16),
        compiler_params=params(60),
        cost_estimate=cost(0, 2 * rows * width),
        name="half",
    )(side, weight, *waits)


def prep_kernel(q_ref, k_ref, v_ref, *refs):
    send_ref = refs[-1]
    matrix = regroup_matrix()
    ctx, _, per, rows, width = send_ref.shape
    for number, ref in enumerate((q_ref, k_ref, v_ref)):
        grouped = dot(matrix, ref[...]).astype(BF16)
        send_ref[:, number] = grouped.reshape(ctx, per, rows, width)


def prepare(queries, keys, values, ctx, chunk, chunks, waits):
    tokens_dev, width = queries.shape
    per = STRIDE // ctx
    part = width // chunks
    return pl.pallas_call(
        prep_kernel,
        grid=(tokens_dev // TILE,),
        in_specs=[pl.BlockSpec((TILE, part), lambda b: (b, chunk))] * 3 + moments(waits),
        out_specs=pl.BlockSpec((ctx, 3, per, TILE // STRIDE, part), lambda b: (0, 0, 0, b, 0)),
        out_shape=jax.ShapeDtypeStruct((ctx, 3, per, tokens_dev // STRIDE, part), BF16),
        compiler_params=params(60),
        cost_estimate=cost(6 * tokens_dev * TILE * part, 12 * tokens_dev * part),
        name="prepare",
    )(queries, keys, values, *waits)


def home_kernel(place_ref, q_ref, k_ref, v_ref, rim_ref, *refs, order):
    sum_refs, (o_ref, mark_ref) = refs[: len(order)], refs[-2:]
    mark_ref[...] = jnp.zeros_like(mark_ref)
    place = place_ref[0]
    tokens_dev = q_ref.shape[0]
    back = WINDOW // TILE
    key_blocks = [rim_ref[0, e * TILE : (e + 1) * TILE] for e in range(back)]
    value_blocks = [with_ones(rim_ref[1, e * TILE : (e + 1) * TILE]) for e in range(back)]
    for e in range(tokens_dev // TILE):
        key_blocks.append(k_ref[e * TILE : (e + 1) * TILE])
        value_blocks.append(with_ones(v_ref[e * TILE : (e + 1) * TILE]))
    picks = sum_refs[0].shape[1]
    sum_keys = jnp.concatenate([ref[0] for ref in sum_refs])
    sum_values = with_ones(jnp.concatenate([ref[1] for ref in sum_refs]))
    sum_col = jnp.concatenate(
        [iota2((TILE, picks), 1) + (place ^ i) * picks for i in order], axis=1
    )
    row = iota2((TILE, TILE), 0)
    col = iota2((TILE, TILE), 1)
    for b in range(tokens_dev // TILE):
        query = q_ref[b * TILE : (b + 1) * TILE]
        blocks = []
        for e in range(back + 1):
            block = scores(query, key_blocks[b + e])
            allowed = None
            if e == 0:
                allowed = col > row
            if e == back:
                allowed = col <= row
            if b + e < back:
                held = place > 0
                allowed = held if allowed is None else allowed & held
            if allowed is not None:
                block = jnp.where(allowed, block, BIG_NEG)
            blocks.append(block)
        local = weighted(blocks, value_blocks[b : b + back + 1])
        pos = place * tokens_dev + b * TILE + iota2((TILE, 1), 0)
        within = pos % BLOCK
        held = pos // BLOCK * SUMCOLS + jnp.maximum(within - (BLOCK - SUMCOLS - 1), 0)
        block = jnp.where(sum_col < held, scores(query, sum_keys), BIG_NEG)
        own_key = key_blocks[b + back].astype(F32)
        own = jnp.sum(query.astype(F32) * own_key, axis=-1, keepdims=True)
        own = jnp.where(within < BLOCK - SUMCOLS, own, BIG_NEG)
        summary = weighted([block], [sum_values], (own, value_blocks[b + back]))
        o_ref[b * TILE : (b + 1) * TILE] = local + summary


def home_sections(place, queries, keys, values, rim, summary, order, chunk, chunks, waits):
    tokens_dev, width = queries.shape
    heads = width // chunks // HEAD_SIZE
    first = chunk * heads
    picks = summary[0].shape[1]
    total = len(summary) * picks
    own = pl.BlockSpec((tokens_dev, HEAD_SIZE), lambda h: (0, first + h))
    pairs = tokens_dev * (WINDOW + TILE + total) * heads
    return pl.pallas_call(
        functools.partial(home_kernel, order=order),
        grid=(heads,),
        in_specs=[
            pl.BlockSpec(memory_space=pltpu.SMEM),
            own,
            own,
            own,
            pl.BlockSpec((2, WINDOW, HEAD_SIZE), lambda h: (0, 0, first + h)),
        ]
        + [pl.BlockSpec((2, picks, HEAD_SIZE), lambda h: (0, 0, first + h))] * len(summary)
        + moments(waits),
        out_specs=[pl.BlockSpec((tokens_dev, HEAD_SIZE), lambda h: (0, h)), mark_spec()],
        out_shape=[jax.ShapeDtypeStruct((tokens_dev, heads * HEAD_SIZE), F32), MARK],
        compiler_params=params(60),
        cost_estimate=cost(64 * pairs * HEAD_SIZE, 14 * tokens_dev * width, 8 * pairs),
        name="home",
    )(place, queries, keys, values, rim, *summary, *waits)


def stride_kernel(place_ref, x_ref, *refs):
    ctx, _, _, rows, width = x_ref.shape
    o_refs, mark_ref, held_ref = refs[-ctx - 2 : -2], refs[-2], refs[-1]
    mark_ref[...] = jnp.zeros_like(mark_ref)
    count = ctx * rows
    row = iota2((TILE, TILE), 0)
    col = iota2((TILE, TILE), 1)
    sources = TILE // rows
    units = []
    for head in range(width // HEAD_SIZE):
        lanes = slice(head * HEAD_SIZE, (head + 1) * HEAD_SIZE)
        query = x_ref[:, 0, 0, :, lanes].reshape(count, HEAD_SIZE)
        key_rows = x_ref[:, 1, 0, :, lanes].reshape(count, HEAD_SIZE)
        value_rows = with_ones(x_ref[:, 2, 0, :, lanes].reshape(count, HEAD_SIZE))
        for b in range(count // TILE):
            part = query[b * TILE : (b + 1) * TILE]
            blocks = [scores(part, key_rows[e * TILE : (e + 1) * TILE]) for e in range(b + 1)]
            blocks[b] = jnp.where(col <= row, blocks[b], BIG_NEG)
            units.append((lanes, b, blocks, value_rows))
    for lanes, b, blocks, value_rows in units:
        result = weighted(
            blocks, [value_rows[e * TILE : (e + 1) * TILE] for e in range(b + 1)]
        ).astype(BF16)
        held_ref[b * sources : (b + 1) * sources, :, lanes] = result.reshape(
            sources, rows, HEAD_SIZE
        )
    for slot in range(ctx):
        o_refs[slot][0] = held_ref[partner(place_ref[0], slot, ctx)]


def stride_attend(place, moved, waits):
    ctx, _, per, rows, width = moved.shape
    count = ctx * rows
    pairs = per * (width // HEAD_SIZE) * count * (count + TILE) // 2
    return pl.pallas_call(
        stride_kernel,
        grid=(per,),
        in_specs=[
            pl.BlockSpec(memory_space=pltpu.SMEM),
            pl.BlockSpec((ctx, 3, 1, rows, width), lambda r: (0, 0, r, 0, 0)),
        ]
        + moments(waits),
        out_specs=[pl.BlockSpec((1, rows, width), lambda r: (r, 0, 0))] * ctx + [mark_spec()],
        out_shape=[jax.ShapeDtypeStruct((per, rows, width), BF16)] * ctx + [MARK],
        scratch_shapes=[pltpu.VMEM((ctx, rows, width), BF16)],
        compiler_params=params(24),
        cost_estimate=cost(8 * pairs * HEAD_SIZE, 8 * per * count * width, pairs),
        name="stride",
    )(place, moved, *waits)


def combine_kernel(seat_ref, home_ref, *refs, slots, ctx):
    back_refs, o_refs, mark_ref = refs[:ctx], refs[-slots - 1 : -1], refs[-1]
    mark_ref[...] = jnp.zeros_like(mark_ref)
    tokens_dev, width = home_ref.shape
    size = tokens_dev // slots
    per = STRIDE // ctx
    token = iota2((TILE, TILE), 0)
    col = iota2((TILE, TILE), 1)
    group = col >> 4
    residue = partner(seat_ref[1], group // per, ctx) * per + group % per
    matrix = (token == (col & 15) * 16 + residue).astype(BF16)
    for slot in range(slots):
        owner = partner(seat_ref[0], slot, slots)
        for b in range(size // TILE):
            first = owner * (size // TILE) + b
            here = pl.ds(pl.multiple_of(first * STRIDE, STRIDE), STRIDE)
            rows = [ref[r, here] for ref in back_refs for r in range(per)]
            back = dot(matrix, jnp.concatenate(rows))
            home = home_ref[pl.ds(pl.multiple_of(first * TILE, TILE), TILE)]
            o_refs[slot][b * TILE : (b + 1) * TILE] = (home + back).astype(BF16)


def combine(seat, home, backs, slots, waits):
    tokens_dev, width = home.shape
    size = tokens_dev // slots
    return pl.pallas_call(
        functools.partial(combine_kernel, slots=slots, ctx=len(backs)),
        in_specs=[pl.BlockSpec(memory_space=pltpu.SMEM)]
        + [pl.BlockSpec(memory_space=pltpu.VMEM)] * (1 + len(backs))
        + moments(waits),
        out_specs=[pl.BlockSpec(memory_space=pltpu.VMEM)] * (slots + 1),
        out_shape=[jax.ShapeDtypeStruct((size, width), BF16)] * slots + [MARK],
        compiler_params=params(24),
        cost_estimate=cost(2 * tokens_dev * TILE * width, 8 * tokens_dev * width),
        name="combine",
    )(seat, home, *backs, *waits)


def project_kernel(side_ref, *refs, slots, chunks):
    moved_refs, (mine_ref, other_ref, o_ref) = refs[: slots * chunks], refs[slots * chunks :]
    width = moved_refs[0].shape[1]

    def add_up(weight_ref):
        total = None
        for slot in range(slots):
            group = partner(side_ref[1], slot, slots)
            for chunk in range(chunks):
                rows = weight_ref[group, chunk * width : (chunk + 1) * width]
                part = dot(moved_refs[chunk * slots + slot][...], rows)
                total = part if total is None else total + part
        o_ref[...] = total.astype(BF16)

    @pl.when(pl.program_id(0) == 0)
    def _():
        add_up(mine_ref)

    @pl.when(pl.program_id(0) == 1)
    def _():
        add_up(other_ref)


def project(side, moved, mine, other):
    chunks, slots = len(moved), len(moved[0])
    tokens, part = moved[0][0].shape
    width, half = mine.shape[1:]
    tile = min(half, 256)
    tiles = half // tile
    block = (slots, width, tile)
    return pl.pallas_call(
        functools.partial(project_kernel, slots=slots, chunks=chunks),
        grid_spec=pltpu.PrefetchScalarGridSpec(
            num_scalar_prefetch=1,
            grid=(2, tiles),
            in_specs=[pl.BlockSpec((tokens, part), lambda s, j, side: (0, 0))] * (slots * chunks)
            + [
                pl.BlockSpec(block, lambda s, j, side: (0, 0, jnp.where(s == 0, j, tiles - 1))),
                pl.BlockSpec(block, lambda s, j, side: (0, 0, jnp.where(s == 0, 0, j))),
            ],
            out_specs=pl.BlockSpec(
                (tokens, tile), lambda s, j, side: (0, (s ^ side[0]) * tiles + j)
            ),
        ),
        out_shape=jax.ShapeDtypeStruct((tokens, 2 * half), BF16),
        compiler_params=params(60),
        cost_estimate=cost(
            4 * slots * tokens * width * half, 2 * slots * width * (2 * half + tokens)
        ),
        name="project",
    )(side, *[slab for slabs in moved for slab in slabs], mine, other)


def gather_ctx(rows):
    count = lax.axis_size("ctx")

    def swapped(piece, distance):
        return lax.ppermute(piece, "ctx", [(i, i ^ distance) for i in range(count)])

    order = list(range(0, count, 2))
    pieces = [rows] + [swapped(rows, distance) for distance in order[1:]]
    within = [swapped(piece, 1) for piece in pieces]
    return pieces, within, order + [i ^ 1 for i in order]


def stride_general(queries, keys, values):
    tokens_dev, width = queries.shape
    heads = width // HEAD_SIZE
    ctx = lax.axis_size("ctx")
    copies = max(ctx // STRIDE, 1)
    rows = tokens_dev // STRIDE
    held_rows = ctx * rows // copies
    own_copy = lax.axis_index("ctx") // STRIDE
    query_pos = (jnp.arange(held_rows) // (rows // copies)) * rows
    query_pos = query_pos + (jnp.arange(held_rows) % (rows // copies)) * copies + own_copy
    shaped = queries.reshape(1, rows // copies, ctx, width)
    query = lax.all_to_all(shaped, "ctx", split_axis=2, concat_axis=1, tiled=True)
    query = query.reshape(held_rows, heads, HEAD_SIZE)
    both = jnp.stack([keys, values]).reshape(2, rows, 1, STRIDE, width)
    both = jnp.broadcast_to(both, (2, rows, copies, STRIDE, width)).reshape(2, rows, ctx, width)
    both = lax.all_to_all(both, "ctx", split_axis=2, concat_axis=1, tiled=True)
    both = both.reshape(2, ctx * rows, heads, HEAD_SIZE)
    allowed = jnp.arange(ctx * rows)[None, :] <= query_pos[:, None]

    def one_head(operands):
        head_query, head_keys, head_values = operands
        masked = jnp.where(allowed, scores(head_query, head_keys), BIG_NEG)
        return weighted([masked], [with_ones(head_values)])

    result = lax.map(
        one_head,
        (query.transpose(1, 0, 2), both[0].transpose(1, 0, 2), both[1].transpose(1, 0, 2)),
    )
    result = result.transpose(1, 0, 2).reshape(ctx, rows // copies, 1, width).astype(BF16)
    back = lax.all_to_all(result, "ctx", split_axis=0, concat_axis=2, tiled=True)
    return back.reshape(tokens_dev, width)


def body(queries, keys, values, out_weight, chunks):
    tokens_dev, width = queries.shape
    ctx = lax.axis_size("ctx")
    groups = lax.axis_size("head")
    place = lax.axis_index("ctx")
    place_word = place.astype(jnp.int32).reshape(1)
    side = place % 2
    sibling = [(i, i ^ 1) for i in range(ctx)]

    part = width // chunks
    seat = lax.axis_index("head").astype(jnp.int32)
    sides = jnp.stack([side.astype(jnp.int32), seat])

    sends = []
    if ctx <= STRIDE:
        sends.append(prepare(queries, keys, values, ctx, 0, chunks, ()))
    mine = lax.all_gather(half_of(sides, out_weight, sends), "head", axis=0)
    rim, picked = edges(keys, values, sends)
    between, within, order = gather_ctx(picked)
    summary = between + within
    if ctx > STRIDE:
        stride_out = stride_general(queries, keys, values)
    for chunk in range(len(sends), chunks * len(sends)):
        sends.append(prepare(queries, keys, values, ctx, chunk, chunks, (picked,)))
    rim = after(rim, (*between[1:], *sends[1:]))
    before = lax.ppermute(rim, "ctx", [(i, i + 1) for i in range(ctx - 1)])
    sends[1:] = [after(send, (rim,)) for send in sends[1:]]

    def home(chunk, waits):
        return home_sections(
            place_word, queries, keys, values, before, summary, order, chunk, chunks, waits
        )

    def exchange(slabs, axis):
        count = len(slabs)
        moved = [slabs[0]]
        for slot in range(1, count):
            pairs = [(i, partner(i, slot, count)) for i in range(count)]
            moved.append(lax.ppermute(slabs[slot], axis, pairs))
        return moved

    moved, waits = [], ()
    if ctx > STRIDE:
        for chunk in range(chunks):
            lanes = slice(chunk * part, (chunk + 1) * part)
            homes, mark = home(chunk, waits)
            attended = (homes + stride_out[:, lanes].astype(F32)).astype(BF16)
            attended = attended.reshape(groups, tokens_dev // groups, part)
            owners = [partner(seat, slot, groups) for slot in range(groups)]
            moved.append(exchange([attended[owner] for owner in owners], "head"))
            waits = (mark,)
    else:
        seats = jnp.stack([seat, place.astype(jnp.int32)])
        arrived = ()
        for chunk in range(chunks + 1):
            if chunk < chunks:
                send = sends[chunk]
                received = lax.all_to_all(send, "ctx", split_axis=0, concat_axis=0, tiled=True)
                *slabs, mark = stride_attend(place_word, received, waits)
                backs = exchange(slabs, "ctx")
                waits = (mark,)
            if chunk > 0:
                seats = jnp.stack([seat, place.astype(jnp.int32)])
                *slabs, mark = combine(seats, sections, ready, groups, (*waits, *arrived))
                moved.append(exchange(slabs, "head"))
                waits = (mark,)
                arrived = moved[-1][1:]
            if chunk < chunks:
                sections, mark = home(chunk, waits)
                ready = backs
                waits = (mark,)
    held = after(mine, (mark,))
    other = lax.ppermute(held, "ctx", sibling)
    return project(sides, moved, held, other)


def solution(mesh):
    chunks = 2 if HEADS // mesh.shape["head"] > 1 else 1
    placed = (P("ctx", "head"), P("ctx", "head"), P("ctx", "head"), P("head", None))
    return jax.shard_map(
        functools.partial(body, chunks=chunks),
        mesh=mesh,
        in_specs=placed,
        out_specs=P(("ctx", "head"), None),
        check_vma=False,
    )
```

```python
import functools
import math

import jax
import jax.numpy as jnp
from jax import lax
from jax.experimental import pallas as pl
from jax.experimental.pallas import tpu as pltpu
from jax.sharding import PartitionSpec as P

HEADS = 16
HEAD_SIZE = 128
WINDOW = 512
STRIDE = 16
BLOCK = 128
SUMCOLS = 8

BIG_NEG = -1e30
TILE = 256
LOG_SCALE = HEAD_SIZE ** (-0.5) * math.log2(math.e)
F32 = jnp.float32
BF16 = jnp.bfloat16


def params(mib):
    return pltpu.CompilerParams(vmem_limit_bytes=mib * 1024 * 1024)


MARK = jax.ShapeDtypeStruct((8, 128), F32)


def mark_spec():
    return pl.BlockSpec(MARK.shape, lambda *place: (0, 0))


def moments(arrays):
    return [pl.BlockSpec(memory_space=pl.ANY)] * len(arrays)


def after(array, others):
    anywhere = pl.BlockSpec(memory_space=pl.ANY)
    return pl.pallas_call(
        lambda *refs: None,
        in_specs=[anywhere] * (1 + len(others)),
        out_specs=anywhere,
        out_shape=jax.ShapeDtypeStruct(array.shape, array.dtype),
        input_output_aliases={0: 0},
        compiler_params=params(60),
        cost_estimate=cost(0, 0),
        name="after",
    )(array, *others)


def cost(flops, bytes_accessed, exps=0):
    return pl.CostEstimate(
        flops=int(flops), bytes_accessed=int(bytes_accessed), transcendentals=int(exps)
    )


def partner(place, slot, count):
    assert count & (count - 1) == 0
    return place ^ slot


def iota2(shape, dim):
    return lax.broadcasted_iota(jnp.int32, shape, dim)


def scores(query, key_rows):
    return lax.dot_general(query, key_rows, (((1,), (1,)), ((), ())), preferred_element_type=F32)


def dot(left, right):
    return jnp.dot(left, right, preferred_element_type=F32)


def regroup_matrix():
    rows = iota2((TILE, TILE), 0)
    cols = iota2((TILE, TILE), 1)
    return (cols == (rows & 15) * 16 + (rows >> 4)).astype(BF16)


def with_ones(value_rows):
    return jnp.concatenate([value_rows, jnp.ones_like(value_rows)], axis=1)


def weighted(score_blocks, value_blocks, extra=None):
    top = functools.reduce(jnp.maximum, score_blocks)
    top = jnp.max(top, axis=-1, keepdims=True)
    if extra is not None:
        top = jnp.maximum(top, extra[0])
    total = None
    for block, value_block in zip(score_blocks, value_blocks):
        weights = jnp.exp2((block - top) * LOG_SCALE).astype(BF16)
        part = dot(weights, value_block)
        total = part if total is None else total + part
    if extra is not None:
        own = jnp.exp2((extra[0] - top) * LOG_SCALE).astype(BF16).astype(F32)
        total = total + own * extra[1].astype(F32)
    return total[:, :HEAD_SIZE] / total[:, HEAD_SIZE:]


def edge_kernel(k_ref, v_ref, k_ends_ref, v_ends_ref, *refs):
    rim_ref, sum_ref = refs[-2:]
    rim_ref[0] = k_ref[...]
    rim_ref[1] = v_ref[...]

    @pl.when(pl.program_id(0) == 0)
    def _():
        for number, ref in enumerate((k_ends_ref, v_ends_ref)):
            rows = ref[...].astype(F32)[:, 16 - SUMCOLS :]
            sum_ref[number] = rows.reshape(sum_ref.shape[1:]).astype(BF16)


def edges(keys, values, waits):
    tokens_dev, width = keys.shape
    blocks = tokens_dev // BLOCK
    first = (tokens_dev - WINDOW) // TILE
    source = pl.BlockSpec((TILE, width), lambda i: (first + i, 0))
    ends = pl.BlockSpec((blocks, 16, width), lambda i: (0, BLOCK // 16 - 1, 0))
    shape = (2, blocks * SUMCOLS, width)
    return pl.pallas_call(
        edge_kernel,
        grid=(WINDOW // TILE,),
        in_specs=[source] * 2 + [ends] * 2 + moments(waits),
        out_specs=[
            pl.BlockSpec((2, TILE, width), lambda i: (0, i, 0)),
            pl.BlockSpec(shape, lambda i: (0, 0, 0)),
        ],
        out_shape=[
            jax.ShapeDtypeStruct((2, WINDOW, width), BF16),
            jax.ShapeDtypeStruct(shape, BF16),
        ],
        compiler_params=params(60),
        cost_estimate=cost(0, 8 * WINDOW * width),
        name="edges",
    )(
        keys,
        values,
        keys.reshape(blocks, BLOCK, width),
        values.reshape(blocks, BLOCK, width),
        *waits,
    )


def half_kernel(side_ref, weight_ref, *refs):
    refs[-1][...] = weight_ref[...]


def half_of(side, weight, waits):
    rows, width = weight.shape
    return pl.pallas_call(
        half_kernel,
        grid_spec=pltpu.PrefetchScalarGridSpec(
            num_scalar_prefetch=1,
            grid=(2,),
            in_specs=[pl.BlockSpec((rows // 2, width // 2), lambda i, side: (i, side[0]))]
            + moments(waits),
            out_specs=pl.BlockSpec((rows // 2, width // 2), lambda i, side: (i, 0)),
        ),
        out_shape=jax.ShapeDtypeStruct((rows, width // 2), BF16),
        compiler_params=params(60),
        cost_estimate=cost(0, 2 * rows * width),
        name="half",
    )(side, weight, *waits)


def prep_kernel(q_ref, k_ref, v_ref, *refs):
    send_ref = refs[-1]
    matrix = regroup_matrix()
    ctx, _, per, rows, width = send_ref.shape
    for number, ref in enumerate((q_ref, k_ref, v_ref)):
        grouped = dot(matrix, ref[...]).astype(BF16)
        send_ref[:, number] = grouped.reshape(ctx, per, rows, width)


def prepare(queries, keys, values, ctx, chunk, chunks, waits):
    tokens_dev, width = queries.shape
    per = STRIDE // ctx
    part = width // chunks
    return pl.pallas_call(
        prep_kernel,
        grid=(tokens_dev // TILE,),
        in_specs=[pl.BlockSpec((TILE, part), lambda b: (b, chunk))] * 3 + moments(waits),
        out_specs=pl.BlockSpec((ctx, 3, per, TILE // STRIDE, part), lambda b: (0, 0, 0, b, 0)),
        out_shape=jax.ShapeDtypeStruct((ctx, 3, per, tokens_dev // STRIDE, part), BF16),
        compiler_params=params(60),
        cost_estimate=cost(6 * tokens_dev * TILE * part, 12 * tokens_dev * part),
        name="prepare",
    )(queries, keys, values, *waits)


def home_kernel(place_ref, q_ref, k_ref, v_ref, rim_ref, *refs, order):
    sum_refs, (o_ref, mark_ref) = refs[: len(order)], refs[-2:]
    mark_ref[...] = jnp.zeros_like(mark_ref)
    place = place_ref[0]
    tokens_dev = q_ref.shape[0]
    back = WINDOW // TILE
    key_blocks = [rim_ref[0, e * TILE : (e + 1) * TILE] for e in range(back)]
    value_blocks = [with_ones(rim_ref[1, e * TILE : (e + 1) * TILE]) for e in range(back)]
    for e in range(tokens_dev // TILE):
        key_blocks.append(k_ref[e * TILE : (e + 1) * TILE])
        value_blocks.append(with_ones(v_ref[e * TILE : (e + 1) * TILE]))
    picks = sum_refs[0].shape[1]
    sum_keys = jnp.concatenate([ref[0] for ref in sum_refs])
    sum_values = with_ones(jnp.concatenate([ref[1] for ref in sum_refs]))
    sum_col = jnp.concatenate(
        [iota2((TILE, picks), 1) + (place ^ i) * picks for i in order], axis=1
    )
    row = iota2((TILE, TILE), 0)
    col = iota2((TILE, TILE), 1)
    for b in range(tokens_dev // TILE):
        query = q_ref[b * TILE : (b + 1) * TILE]
        blocks = []
        for e in range(back + 1):
            block = scores(query, key_blocks[b + e])
            allowed = None
            if e == 0:
                allowed = col > row
            if e == back:
                allowed = col <= row
            if b + e < back:
                held = place > 0
                allowed = held if allowed is None else allowed & held
            if allowed is not None:
                block = jnp.where(allowed, block, BIG_NEG)
            blocks.append(block)
        local = weighted(blocks, value_blocks[b : b + back + 1])
        pos = place * tokens_dev + b * TILE + iota2((TILE, 1), 0)
        within = pos % BLOCK
        held = pos // BLOCK * SUMCOLS + jnp.maximum(within - (BLOCK - SUMCOLS - 1), 0)
        block = jnp.where(sum_col < held, scores(query, sum_keys), BIG_NEG)
        own_key = key_blocks[b + back].astype(F32)
        own = jnp.sum(query.astype(F32) * own_key, axis=-1, keepdims=True)
        own = jnp.where(within < BLOCK - SUMCOLS, own, BIG_NEG)
        summary = weighted([block], [sum_values], (own, value_blocks[b + back]))
        o_ref[b * TILE : (b + 1) * TILE] = local + summary


def home_sections(place, queries, keys, values, rim, summary, order, chunk, chunks, waits):
    tokens_dev, width = queries.shape
    heads = width // chunks // HEAD_SIZE
    first = chunk * heads
    picks = summary[0].shape[1]
    total = len(summary) * picks
    own = pl.BlockSpec((tokens_dev, HEAD_SIZE), lambda h: (0, first + h))
    pairs = tokens_dev * (WINDOW + TILE + total) * heads
    return pl.pallas_call(
        functools.partial(home_kernel, order=order),
        grid=(heads,),
        in_specs=[
            pl.BlockSpec(memory_space=pltpu.SMEM),
            own,
            own,
            own,
            pl.BlockSpec((2, WINDOW, HEAD_SIZE), lambda h: (0, 0, first + h)),
        ]
        + [pl.BlockSpec((2, picks, HEAD_SIZE), lambda h: (0, 0, first + h))] * len(summary)
        + moments(waits),
        out_specs=[pl.BlockSpec((tokens_dev, HEAD_SIZE), lambda h: (0, h)), mark_spec()],
        out_shape=[jax.ShapeDtypeStruct((tokens_dev, heads * HEAD_SIZE), F32), MARK],
        compiler_params=params(60),
        cost_estimate=cost(64 * pairs * HEAD_SIZE, 14 * tokens_dev * width, 8 * pairs),
        name="home",
    )(place, queries, keys, values, rim, *summary, *waits)


def stride_kernel(place_ref, x_ref, *refs):
    ctx, _, _, rows, width = x_ref.shape
    o_refs, mark_ref, held_ref = refs[-ctx - 2 : -2], refs[-2], refs[-1]
    mark_ref[...] = jnp.zeros_like(mark_ref)
    count = ctx * rows
    row = iota2((TILE, TILE), 0)
    col = iota2((TILE, TILE), 1)
    sources = TILE // rows
    units = []
    for head in range(width // HEAD_SIZE):
        lanes = slice(head * HEAD_SIZE, (head + 1) * HEAD_SIZE)
        query = x_ref[:, 0, 0, :, lanes].reshape(count, HEAD_SIZE)
        key_rows = x_ref[:, 1, 0, :, lanes].reshape(count, HEAD_SIZE)
        value_rows = with_ones(x_ref[:, 2, 0, :, lanes].reshape(count, HEAD_SIZE))
        for b in range(count // TILE):
            part = query[b * TILE : (b + 1) * TILE]
            blocks = [scores(part, key_rows[e * TILE : (e + 1) * TILE]) for e in range(b + 1)]
            blocks[b] = jnp.where(col <= row, blocks[b], BIG_NEG)
            units.append((lanes, b, blocks, value_rows))
    for lanes, b, blocks, value_rows in units:
        result = weighted(
            blocks, [value_rows[e * TILE : (e + 1) * TILE] for e in range(b + 1)]
        ).astype(BF16)
        held_ref[b * sources : (b + 1) * sources, :, lanes] = result.reshape(
            sources, rows, HEAD_SIZE
        )
    for slot in range(ctx):
        o_refs[slot][0] = held_ref[partner(place_ref[0], slot, ctx)]


def stride_attend(place, moved, waits):
    ctx, _, per, rows, width = moved.shape
    count = ctx * rows
    pairs = per * (width // HEAD_SIZE) * count * (count + TILE) // 2
    return pl.pallas_call(
        stride_kernel,
        grid=(per,),
        in_specs=[
            pl.BlockSpec(memory_space=pltpu.SMEM),
            pl.BlockSpec((ctx, 3, 1, rows, width), lambda r: (0, 0, r, 0, 0)),
        ]
        + moments(waits),
        out_specs=[pl.BlockSpec((1, rows, width), lambda r: (r, 0, 0))] * ctx + [mark_spec()],
        out_shape=[jax.ShapeDtypeStruct((per, rows, width), BF16)] * ctx + [MARK],
        scratch_shapes=[pltpu.VMEM((ctx, rows, width), BF16)],
        compiler_params=params(24),
        cost_estimate=cost(8 * pairs * HEAD_SIZE, 8 * per * count * width, pairs),
        name="stride",
    )(place, moved, *waits)


def combine_kernel(seat_ref, home_ref, *refs, slots, ctx):
    back_refs, o_refs, mark_ref = refs[:ctx], refs[-slots - 1 : -1], refs[-1]
    mark_ref[...] = jnp.zeros_like(mark_ref)
    tokens_dev, width = home_ref.shape
    size = tokens_dev // slots
    per = STRIDE // ctx
    token = iota2((TILE, TILE), 0)
    col = iota2((TILE, TILE), 1)
    group = col >> 4
    residue = partner(seat_ref[1], group // per, ctx) * per + group % per
    matrix = (token == (col & 15) * 16 + residue).astype(BF16)
    for slot in range(slots):
        owner = partner(seat_ref[0], slot, slots)
        for b in range(size // TILE):
            first = owner * (size // TILE) + b
            here = pl.ds(pl.multiple_of(first * STRIDE, STRIDE), STRIDE)
            rows = [ref[r, here] for ref in back_refs for r in range(per)]
            back = dot(matrix, jnp.concatenate(rows))
            home = home_ref[pl.ds(pl.multiple_of(first * TILE, TILE), TILE)]
            o_refs[slot][b * TILE : (b + 1) * TILE] = (home + back).astype(BF16)


def combine(seat, home, backs, slots, waits):
    tokens_dev, width = home.shape
    size = tokens_dev // slots
    return pl.pallas_call(
        functools.partial(combine_kernel, slots=slots, ctx=len(backs)),
        in_specs=[pl.BlockSpec(memory_space=pltpu.SMEM)]
        + [pl.BlockSpec(memory_space=pltpu.VMEM)] * (1 + len(backs))
        + moments(waits),
        out_specs=[pl.BlockSpec(memory_space=pltpu.VMEM)] * (slots + 1),
        out_shape=[jax.ShapeDtypeStruct((size, width), BF16)] * slots + [MARK],
        compiler_params=params(24),
        cost_estimate=cost(2 * tokens_dev * TILE * width, 8 * tokens_dev * width),
        name="combine",
    )(seat, home, *backs, *waits)


def project_kernel(side_ref, *refs, slots, chunks):
    moved_refs = refs[: slots * chunks]
    mine_ref, other_ref, o_ref, rows_ref = refs[slots * chunks :]
    part = moved_refs[0].shape[1]
    first = (pl.program_id(0) == 0) & (pl.program_id(1) == 0)

    @pl.when(first)
    def _():
        for slot in range(slots):
            group = partner(side_ref[1], slot, slots)
            for chunk in range(chunks):
                here = pl.ds(pl.multiple_of((group * chunks + chunk) * part, part), part)
                rows_ref[:, here] = moved_refs[chunk * slots + slot][...]

    def multiply(weight_ref):
        groups, width, tile = weight_ref.shape
        weight = weight_ref[...].reshape(groups * width, tile)
        o_ref[...] = dot(rows_ref[...], weight).astype(BF16)

    @pl.when(pl.program_id(0) == 0)
    def _():
        multiply(mine_ref)

    @pl.when(pl.program_id(0) == 1)
    def _():
        multiply(other_ref)


def project(side, moved, mine, other):
    chunks, slots = len(moved), len(moved[0])
    tokens, part = moved[0][0].shape
    width, half = mine.shape[1:]
    tile = min(half, 512)
    tiles = half // tile
    block = (slots, width, tile)
    return pl.pallas_call(
        functools.partial(project_kernel, slots=slots, chunks=chunks),
        grid_spec=pltpu.PrefetchScalarGridSpec(
            num_scalar_prefetch=1,
            grid=(2, tiles),
            in_specs=[pl.BlockSpec((tokens, part), lambda s, j, side: (0, 0))] * (slots * chunks)
            + [
                pl.BlockSpec(block, lambda s, j, side: (0, 0, jnp.where(s == 0, j, tiles - 1))),
                pl.BlockSpec(block, lambda s, j, side: (0, 0, jnp.where(s == 0, 0, j))),
            ],
            out_specs=pl.BlockSpec(
                (tokens, tile), lambda s, j, side: (0, (s ^ side[0]) * tiles + j)
            ),
            scratch_shapes=[pltpu.VMEM((tokens, slots * width), BF16)],
        ),
        out_shape=jax.ShapeDtypeStruct((tokens, 2 * half), BF16),
        compiler_params=params(24),
        cost_estimate=cost(
            4 * slots * tokens * width * half, 2 * slots * width * (2 * half + tokens)
        ),
        name="project",
    )(side, *[slab for slabs in moved for slab in slabs], mine, other)


def gather_ctx(rows):
    count = lax.axis_size("ctx")

    def swapped(piece, distance):
        return lax.ppermute(piece, "ctx", [(i, i ^ distance) for i in range(count)])

    order = list(range(0, count, 2))
    pieces = [rows] + [swapped(rows, distance) for distance in order[1:]]
    within = [swapped(piece, 1) for piece in pieces]
    return pieces, within, order + [i ^ 1 for i in order]


def stride_general(queries, keys, values):
    tokens_dev, width = queries.shape
    heads = width // HEAD_SIZE
    ctx = lax.axis_size("ctx")
    copies = max(ctx // STRIDE, 1)
    rows = tokens_dev // STRIDE
    held_rows = ctx * rows // copies
    own_copy = lax.axis_index("ctx") // STRIDE
    query_pos = (jnp.arange(held_rows) // (rows // copies)) * rows
    query_pos = query_pos + (jnp.arange(held_rows) % (rows // copies)) * copies + own_copy
    shaped = queries.reshape(1, rows // copies, ctx, width)
    query = lax.all_to_all(shaped, "ctx", split_axis=2, concat_axis=1, tiled=True)
    query = query.reshape(held_rows, heads, HEAD_SIZE)
    both = jnp.stack([keys, values]).reshape(2, rows, 1, STRIDE, width)
    both = jnp.broadcast_to(both, (2, rows, copies, STRIDE, width)).reshape(2, rows, ctx, width)
    both = lax.all_to_all(both, "ctx", split_axis=2, concat_axis=1, tiled=True)
    both = both.reshape(2, ctx * rows, heads, HEAD_SIZE)
    allowed = jnp.arange(ctx * rows)[None, :] <= query_pos[:, None]

    def one_head(operands):
        head_query, head_keys, head_values = operands
        masked = jnp.where(allowed, scores(head_query, head_keys), BIG_NEG)
        return weighted([masked], [with_ones(head_values)])

    result = lax.map(
        one_head,
        (query.transpose(1, 0, 2), both[0].transpose(1, 0, 2), both[1].transpose(1, 0, 2)),
    )
    result = result.transpose(1, 0, 2).reshape(ctx, rows // copies, 1, width).astype(BF16)
    back = lax.all_to_all(result, "ctx", split_axis=0, concat_axis=2, tiled=True)
    return back.reshape(tokens_dev, width)


def body(queries, keys, values, out_weight, chunks):
    tokens_dev, width = queries.shape
    ctx = lax.axis_size("ctx")
    groups = lax.axis_size("head")
    place = lax.axis_index("ctx")
    place_word = place.astype(jnp.int32).reshape(1)
    side = place % 2
    sibling = [(i, i ^ 1) for i in range(ctx)]

    part = width // chunks
    seat = lax.axis_index("head").astype(jnp.int32)
    sides = jnp.stack([side.astype(jnp.int32), seat])

    rim, picked = edges(keys, values, ())
    between, within, order = gather_ctx(picked)
    summary = between + within
    weight_half = half_of(sides, out_weight, (picked,))
    mine = lax.all_gather(weight_half, "head", axis=0)
    if ctx > STRIDE:
        stride_out = stride_general(queries, keys, values)
        sends = []
    else:
        sends = [prepare(queries, keys, values, ctx, 0, chunks, (weight_half,))]
    rim = after(rim, (*between[1:], *sends))
    sends = [after(send, (rim,)) for send in sends]
    before = lax.ppermute(rim, "ctx", [(i, i + 1) for i in range(ctx - 1)])
    for chunk in range(len(sends), chunks * len(sends)):
        sends.append(prepare(queries, keys, values, ctx, chunk, chunks, within[-1:]))

    def home(chunk, waits):
        return home_sections(
            place_word, queries, keys, values, before, summary, order, chunk, chunks, waits
        )

    def exchange(slabs, axis):
        count = len(slabs)
        moved = [slabs[0]]
        for slot in range(1, count):
            pairs = [(i, partner(i, slot, count)) for i in range(count)]
            moved.append(lax.ppermute(slabs[slot], axis, pairs))
        return moved

    moved, waits = [], ()
    if ctx > STRIDE:
        for chunk in range(chunks):
            lanes = slice(chunk * part, (chunk + 1) * part)
            homes, mark = home(chunk, waits)
            attended = (homes + stride_out[:, lanes].astype(F32)).astype(BF16)
            attended = attended.reshape(groups, tokens_dev // groups, part)
            owners = [partner(seat, slot, groups) for slot in range(groups)]
            moved.append(exchange([attended[owner] for owner in owners], "head"))
            waits = (mark,)
    else:
        seats = jnp.stack([seat, place.astype(jnp.int32)])
        seats = jnp.stack([seat, place.astype(jnp.int32)])
        sections, mark = home(0, ())
        homes, backs, waits = [sections], [], ()
        sends[1:] = [after(send, (mark,)) for send in sends[1:]]
        for chunk, send in enumerate(sends):
            received = lax.all_to_all(send, "ctx", split_axis=0, concat_axis=0, tiled=True)
            *slabs, mark = stride_attend(place_word, received, waits)
            backs.append(exchange(slabs, "ctx"))
            waits = (mark,)
            for later in range(1, chunks) if chunk == 0 else ():
                sections, mark = home(later, waits)
                homes.append(sections)
                waits = (mark,)
        for chunk in range(chunks):
            *slabs, mark = combine(seats, homes[chunk], backs[chunk], groups, waits)
            moved.append(exchange(slabs, "head"))
            waits = (mark, *moved[-1][1:])
    held = after(mine, (mark,))
    other = lax.ppermute(held, "ctx", sibling)
    return project(sides, moved, held, other)


def solution(mesh):
    chunks = 2 if HEADS // mesh.shape["head"] > 1 else 1
    placed = (P("ctx", "head"), P("ctx", "head"), P("ctx", "head"), P("head", None))
    return jax.shard_map(
        functools.partial(body, chunks=chunks),
        mesh=mesh,
        in_specs=placed,
        out_specs=P(("ctx", "head"), None),
        check_vma=False,
    )
```

```python
import functools
import math

import jax
import jax.numpy as jnp
from jax import lax
from jax.experimental import pallas as pl
from jax.experimental.pallas import tpu as pltpu
from jax.sharding import PartitionSpec as P

HEADS = 16
HEAD_SIZE = 128
WINDOW = 512
STRIDE = 16
BLOCK = 128
SUMCOLS = 8

BIG_NEG = -1e30
TILE = 256
LOG_SCALE = HEAD_SIZE ** (-0.5) * math.log2(math.e)
F32 = jnp.float32
BF16 = jnp.bfloat16


def params(mib):
    return pltpu.CompilerParams(vmem_limit_bytes=mib * 1024 * 1024)


MARK = jax.ShapeDtypeStruct((8, 128), F32)


def mark_spec():
    return pl.BlockSpec(MARK.shape, lambda *place: (0, 0))


def moments(arrays):
    return [pl.BlockSpec(memory_space=pl.ANY)] * len(arrays)


def after(arrays, others):
    anywhere = pl.BlockSpec(memory_space=pl.ANY)
    return pl.pallas_call(
        lambda *refs: None,
        in_specs=[anywhere] * (len(arrays) + len(others)),
        out_specs=[anywhere] * len(arrays),
        out_shape=[jax.ShapeDtypeStruct(array.shape, array.dtype) for array in arrays],
        input_output_aliases={i: i for i in range(len(arrays))},
        compiler_params=params(60),
        cost_estimate=cost(0, 0),
        name="after",
    )(*arrays, *others)


def cost(flops, bytes_accessed, exps=0):
    return pl.CostEstimate(
        flops=int(flops), bytes_accessed=int(bytes_accessed), transcendentals=int(exps)
    )


def partner(place, slot, count):
    assert count & (count - 1) == 0
    return place ^ slot


def iota2(shape, dim):
    return lax.broadcasted_iota(jnp.int32, shape, dim)


def scores(query, key_rows):
    return lax.dot_general(query, key_rows, (((1,), (1,)), ((), ())), preferred_element_type=F32)


def dot(left, right):
    return jnp.dot(left, right, preferred_element_type=F32)


def regroup_matrix():
    rows = iota2((TILE, TILE), 0)
    cols = iota2((TILE, TILE), 1)
    return (cols == (rows & 15) * 16 + (rows >> 4)).astype(BF16)


def with_ones(value_rows):
    return jnp.concatenate([value_rows, jnp.ones_like(value_rows)], axis=1)


def weighted(score_blocks, value_blocks, extra=None):
    top = functools.reduce(jnp.maximum, score_blocks)
    top = jnp.max(top, axis=-1, keepdims=True)
    if extra is not None:
        top = jnp.maximum(top, extra[0])
    total = None
    for block, value_block in zip(score_blocks, value_blocks):
        weights = jnp.exp2((block - top) * LOG_SCALE).astype(BF16)
        part = dot(weights, value_block)
        total = part if total is None else total + part
    if extra is not None:
        own = jnp.exp2((extra[0] - top) * LOG_SCALE).astype(BF16).astype(F32)
        total = total + own * extra[1].astype(F32)
    return total[:, :HEAD_SIZE] / total[:, HEAD_SIZE:]


def edge_kernel(k_ref, v_ref, k_ends_ref, v_ends_ref, *refs):
    rim_ref, sum_ref = refs[-2:]
    rim_ref[0] = k_ref[...]
    rim_ref[1] = v_ref[...]

    @pl.when(pl.program_id(0) == 0)
    def _():
        for number, ref in enumerate((k_ends_ref, v_ends_ref)):
            rows = ref[...].astype(F32)[:, 16 - SUMCOLS :]
            sum_ref[number] = rows.reshape(sum_ref.shape[1:]).astype(BF16)


def edges(keys, values, waits):
    tokens_dev, width = keys.shape
    blocks = tokens_dev // BLOCK
    first = (tokens_dev - WINDOW) // TILE
    source = pl.BlockSpec((TILE, width), lambda i: (first + i, 0))
    ends = pl.BlockSpec((blocks, 16, width), lambda i: (0, BLOCK // 16 - 1, 0))
    shape = (2, blocks * SUMCOLS, width)
    return pl.pallas_call(
        edge_kernel,
        grid=(WINDOW // TILE,),
        in_specs=[source] * 2 + [ends] * 2 + moments(waits),
        out_specs=[
            pl.BlockSpec((2, TILE, width), lambda i: (0, i, 0)),
            pl.BlockSpec(shape, lambda i: (0, 0, 0)),
        ],
        out_shape=[
            jax.ShapeDtypeStruct((2, WINDOW, width), BF16),
            jax.ShapeDtypeStruct(shape, BF16),
        ],
        compiler_params=params(60),
        cost_estimate=cost(0, 8 * WINDOW * width),
        name="edges",
    )(
        keys,
        values,
        keys.reshape(blocks, BLOCK, width),
        values.reshape(blocks, BLOCK, width),
        *waits,
    )


def half_kernel(side_ref, weight_ref, *refs):
    refs[-1][...] = weight_ref[...]


def half_of(side, weight, waits):
    rows, width = weight.shape
    return pl.pallas_call(
        half_kernel,
        grid_spec=pltpu.PrefetchScalarGridSpec(
            num_scalar_prefetch=1,
            grid=(1,),
            in_specs=[pl.BlockSpec((rows, width // 2), lambda i, side: (i, side[0]))]
            + moments(waits),
            out_specs=pl.BlockSpec((rows, width // 2), lambda i, side: (i, 0)),
        ),
        out_shape=jax.ShapeDtypeStruct((rows, width // 2), BF16),
        compiler_params=params(60),
        cost_estimate=cost(0, 2 * rows * width),
        name="half",
    )(side, weight, *waits)


def prep_kernel(q_ref, k_ref, v_ref, *refs):
    send_ref = refs[-1]
    matrix = regroup_matrix()
    ctx, _, per, rows, width = send_ref.shape
    for number, ref in enumerate((q_ref, k_ref, v_ref)):
        grouped = dot(matrix, ref[...]).astype(BF16)
        send_ref[:, number] = grouped.reshape(ctx, per, rows, width)


def prepare(queries, keys, values, ctx, waits):
    tokens_dev, width = queries.shape
    per = STRIDE // ctx
    return pl.pallas_call(
        prep_kernel,
        grid=(tokens_dev // TILE,),
        in_specs=[pl.BlockSpec((TILE, width), lambda b: (b, 0))] * 3 + moments(waits),
        out_specs=pl.BlockSpec((ctx, 3, per, TILE // STRIDE, width), lambda b: (0, 0, 0, b, 0)),
        out_shape=jax.ShapeDtypeStruct((ctx, 3, per, tokens_dev // STRIDE, width), BF16),
        compiler_params=params(60),
        cost_estimate=cost(6 * tokens_dev * TILE * width, 12 * tokens_dev * width),
        name="prepare",
    )(queries, keys, values, *waits)


def home_kernel(place_ref, q_ref, k_ref, v_ref, rim_ref, *refs, order):
    sum_refs, (o_ref, mark_ref) = refs[: len(order)], refs[-2:]
    mark_ref[...] = jnp.zeros_like(mark_ref)
    place = place_ref[0]
    tokens_dev = q_ref.shape[0]
    back = WINDOW // TILE
    key_blocks = [rim_ref[0, e * TILE : (e + 1) * TILE] for e in range(back)]
    value_blocks = [with_ones(rim_ref[1, e * TILE : (e + 1) * TILE]) for e in range(back)]
    for e in range(tokens_dev // TILE):
        key_blocks.append(k_ref[e * TILE : (e + 1) * TILE])
        value_blocks.append(with_ones(v_ref[e * TILE : (e + 1) * TILE]))
    picks = sum_refs[0].shape[1]
    sum_keys = jnp.concatenate([ref[0] for ref in sum_refs])
    sum_values = with_ones(jnp.concatenate([ref[1] for ref in sum_refs]))
    sum_col = jnp.concatenate(
        [iota2((TILE, picks), 1) + (place ^ i) * picks for i in order], axis=1
    )
    row = iota2((TILE, TILE), 0)
    col = iota2((TILE, TILE), 1)
    for b in range(tokens_dev // TILE):
        query = q_ref[b * TILE : (b + 1) * TILE]
        blocks = []
        for e in range(back + 1):
            block = scores(query, key_blocks[b + e])
            allowed = None
            if e == 0:
                allowed = col > row
            if e == back:
                allowed = col <= row
            if b + e < back:
                held = place > 0
                allowed = held if allowed is None else allowed & held
            if allowed is not None:
                block = jnp.where(allowed, block, BIG_NEG)
            blocks.append(block)
        local = weighted(blocks, value_blocks[b : b + back + 1])
        pos = place * tokens_dev + b * TILE + iota2((TILE, 1), 0)
        within = pos % BLOCK
        held = pos // BLOCK * SUMCOLS + jnp.maximum(within - (BLOCK - SUMCOLS - 1), 0)
        block = jnp.where(sum_col < held, scores(query, sum_keys), BIG_NEG)
        own_key = key_blocks[b + back].astype(F32)
        own = jnp.sum(query.astype(F32) * own_key, axis=-1, keepdims=True)
        own = jnp.where(within < BLOCK - SUMCOLS, own, BIG_NEG)
        summary = weighted([block], [sum_values], (own, value_blocks[b + back]))
        o_ref[b * TILE : (b + 1) * TILE] = local + summary


def home_sections(place, queries, keys, values, rim, summary, order, chunk, chunks, waits):
    tokens_dev, width = queries.shape
    heads = width // chunks // HEAD_SIZE
    first = chunk * heads
    picks = summary[0].shape[1]
    total = len(summary) * picks
    own = pl.BlockSpec((tokens_dev, HEAD_SIZE), lambda h: (0, first + h))
    pairs = tokens_dev * (WINDOW + TILE + total) * heads
    return pl.pallas_call(
        functools.partial(home_kernel, order=order),
        grid=(heads,),
        in_specs=[
            pl.BlockSpec(memory_space=pltpu.SMEM),
            own,
            own,
            own,
            pl.BlockSpec((2, WINDOW, HEAD_SIZE), lambda h: (0, 0, first + h)),
        ]
        + [pl.BlockSpec((2, picks, HEAD_SIZE), lambda h: (0, 0, first + h))] * len(summary)
        + moments(waits),
        out_specs=[pl.BlockSpec((tokens_dev, HEAD_SIZE), lambda h: (0, h)), mark_spec()],
        out_shape=[jax.ShapeDtypeStruct((tokens_dev, heads * HEAD_SIZE), F32), MARK],
        compiler_params=params(60),
        cost_estimate=cost(64 * pairs * HEAD_SIZE, 14 * tokens_dev * width, 8 * pairs),
        name="home",
    )(place, queries, keys, values, rim, *summary, *waits)


def stride_kernel(x_ref, *refs):
    ctx, _, _, rows, width = x_ref.shape
    o_ref, mark_ref = refs[-2:]
    mark_ref[...] = jnp.zeros_like(mark_ref)
    count = ctx * rows
    row = iota2((TILE, TILE), 0)
    col = iota2((TILE, TILE), 1)
    sources = TILE // rows
    units = []
    for head in range(width // HEAD_SIZE):
        lanes = slice(head * HEAD_SIZE, (head + 1) * HEAD_SIZE)
        query = x_ref[:, 0, 0, :, lanes].reshape(count, HEAD_SIZE)
        key_rows = x_ref[:, 1, 0, :, lanes].reshape(count, HEAD_SIZE)
        value_rows = with_ones(x_ref[:, 2, 0, :, lanes].reshape(count, HEAD_SIZE))
        for b in range(count // TILE):
            part = query[b * TILE : (b + 1) * TILE]
            blocks = [scores(part, key_rows[e * TILE : (e + 1) * TILE]) for e in range(b + 1)]
            blocks[b] = jnp.where(col <= row, blocks[b], BIG_NEG)
            units.append((lanes, b, blocks, value_rows))
    for lanes, b, blocks, value_rows in units:
        result = weighted(
            blocks, [value_rows[e * TILE : (e + 1) * TILE] for e in range(b + 1)]
        ).astype(BF16)
        o_ref[b * sources : (b + 1) * sources, 0, :, lanes] = result.reshape(
            sources, rows, HEAD_SIZE
        )


def stride_attend(moved, chunk, chunks, waits):
    ctx, _, per, rows, width = moved.shape
    part = width // chunks
    count = ctx * rows
    pairs = per * (part // HEAD_SIZE) * count * (count + TILE) // 2
    return pl.pallas_call(
        stride_kernel,
        grid=(per,),
        in_specs=[pl.BlockSpec((ctx, 3, 1, rows, part), lambda r: (0, 0, r, 0, chunk))]
        + moments(waits),
        out_specs=[pl.BlockSpec((ctx, 1, rows, part), lambda r: (0, r, 0, 0)), mark_spec()],
        out_shape=[jax.ShapeDtypeStruct((ctx, per, rows, part), BF16), MARK],
        compiler_params=params(24),
        cost_estimate=cost(8 * pairs * HEAD_SIZE, 8 * per * count * part, pairs),
        name="stride",
    )(moved, *waits)


def combine_kernel(seat_ref, home_ref, back_ref, *refs, slots):
    o_refs, mark_ref = refs[-slots - 1 : -1], refs[-1]
    mark_ref[...] = jnp.zeros_like(mark_ref)
    tokens_dev, width = home_ref.shape
    size = tokens_dev // slots
    matrix = regroup_matrix()
    for slot in range(slots):
        owner = partner(seat_ref[1], slot, slots)
        for b in range(size // TILE):
            first = owner * (size // TILE) + b
            here = pl.ds(pl.multiple_of(first * STRIDE, STRIDE), STRIDE)
            back = dot(matrix, back_ref[:, :, here].reshape(TILE, width))
            home = home_ref[pl.ds(pl.multiple_of(first * TILE, TILE), TILE)]
            o_refs[slot][b * TILE : (b + 1) * TILE] = (home + back).astype(BF16)


def combine(seat, home, back, slots, waits):
    tokens_dev, width = home.shape
    size = tokens_dev // slots
    return pl.pallas_call(
        functools.partial(combine_kernel, slots=slots),
        in_specs=[pl.BlockSpec(memory_space=pltpu.SMEM)]
        + [pl.BlockSpec(memory_space=pltpu.VMEM)] * 2
        + moments(waits),
        out_specs=[pl.BlockSpec(memory_space=pltpu.VMEM)] * (slots + 1),
        out_shape=[jax.ShapeDtypeStruct((size, width), BF16)] * slots + [MARK],
        compiler_params=params(24),
        cost_estimate=cost(2 * tokens_dev * TILE * width, 8 * tokens_dev * width),
        name="combine",
    )(seat, home, back, *waits)


def project_kernel(side_ref, *refs, slots, chunks):
    moved_refs = refs[: slots * chunks]
    mine_ref, other_ref, o_ref, total_ref = refs[slots * chunks :]
    part = moved_refs[0].shape[1]
    half = mine_ref.shape[2]
    phase, slot = pl.program_id(0), pl.program_id(1)

    def add_up(weight_ref):
        for one in range(slots):

            @pl.when(slot == one)
            def _():
                total = None if one == 0 else total_ref[...]
                for chunk in range(chunks):
                    rows = weight_ref[0, chunk * part : (chunk + 1) * part]
                    product = dot(moved_refs[chunk * slots + one][...], rows)
                    total = product if total is None else total + product
                if one < slots - 1:
                    total_ref[...] = total
                else:
                    first = pl.multiple_of((side_ref[0] ^ phase) * half, half)
                    o_ref[:, pl.ds(first, half)] = total.astype(BF16)

    @pl.when(phase == 0)
    def _():
        add_up(mine_ref)

    @pl.when(phase == 1)
    def _():
        add_up(other_ref)


def project(side, moved, mine, other):
    chunks, slots = len(moved), len(moved[0])
    tokens, part = moved[0][0].shape
    width, half = mine.shape[1:]

    def mine_group(p, s, side):
        return (side[1] ^ jnp.where(p == 0, s, slots - 1), 0, 0)

    def other_group(p, s, side):
        return (side[1] ^ jnp.where(p == 0, 0, s), 0, 0)

    return pl.pallas_call(
        functools.partial(project_kernel, slots=slots, chunks=chunks),
        grid_spec=pltpu.PrefetchScalarGridSpec(
            num_scalar_prefetch=1,
            grid=(2, slots),
            in_specs=[pl.BlockSpec((tokens, part), lambda p, s, side: (0, 0))] * (slots * chunks)
            + [pl.BlockSpec((1, width, half), mine_group)]
            + [pl.BlockSpec((1, width, half), other_group)],
            out_specs=pl.BlockSpec((tokens, 2 * half), lambda p, s, side: (0, 0)),
            scratch_shapes=[pltpu.VMEM((tokens, half), F32)],
        ),
        out_shape=jax.ShapeDtypeStruct((tokens, 2 * half), BF16),
        compiler_params=params(24),
        cost_estimate=cost(
            4 * slots * tokens * width * half, 2 * slots * width * (2 * half + tokens)
        ),
        name="project",
    )(side, *[slab for slabs in moved for slab in slabs], mine, other)


def gather_ctx(rows):
    count = lax.axis_size("ctx")

    def swapped(piece, distance):
        return lax.ppermute(piece, "ctx", [(i, i ^ distance) for i in range(count)])

    order = list(range(0, count, 2))
    pieces = [rows] + [swapped(rows, distance) for distance in order[1:]]
    within = [swapped(piece, 1) for piece in pieces]
    return pieces, within, order + [i ^ 1 for i in order]


def stride_general(queries, keys, values):
    tokens_dev, width = queries.shape
    heads = width // HEAD_SIZE
    ctx = lax.axis_size("ctx")
    copies = max(ctx // STRIDE, 1)
    rows = tokens_dev // STRIDE
    held_rows = ctx * rows // copies
    own_copy = lax.axis_index("ctx") // STRIDE
    query_pos = (jnp.arange(held_rows) // (rows // copies)) * rows
    query_pos = query_pos + (jnp.arange(held_rows) % (rows // copies)) * copies + own_copy
    shaped = queries.reshape(1, rows // copies, ctx, width)
    query = lax.all_to_all(shaped, "ctx", split_axis=2, concat_axis=1, tiled=True)
    query = query.reshape(held_rows, heads, HEAD_SIZE)
    both = jnp.stack([keys, values]).reshape(2, rows, 1, STRIDE, width)
    both = jnp.broadcast_to(both, (2, rows, copies, STRIDE, width)).reshape(2, rows, ctx, width)
    both = lax.all_to_all(both, "ctx", split_axis=2, concat_axis=1, tiled=True)
    both = both.reshape(2, ctx * rows, heads, HEAD_SIZE)
    allowed = jnp.arange(ctx * rows)[None, :] <= query_pos[:, None]

    def one_head(operands):
        head_query, head_keys, head_values = operands
        masked = jnp.where(allowed, scores(head_query, head_keys), BIG_NEG)
        return weighted([masked], [with_ones(head_values)])

    result = lax.map(
        one_head,
        (query.transpose(1, 0, 2), both[0].transpose(1, 0, 2), both[1].transpose(1, 0, 2)),
    )
    result = result.transpose(1, 0, 2).reshape(ctx, rows // copies, 1, width).astype(BF16)
    back = lax.all_to_all(result, "ctx", split_axis=0, concat_axis=2, tiled=True)
    return back.reshape(tokens_dev, width)


def body(queries, keys, values, out_weight, chunks):
    tokens_dev, width = queries.shape
    ctx = lax.axis_size("ctx")
    groups = lax.axis_size("head")
    place = lax.axis_index("ctx").astype(jnp.int32)
    place_word = place.reshape(1)
    seat = lax.axis_index("head").astype(jnp.int32)
    side = place % 2
    sibling = [(i, i ^ 1) for i in range(ctx)]
    part = width // chunks
    sides = jnp.stack([side, seat])

    def exchange(slabs, axis):
        count = len(slabs)
        moved = [slabs[0]]
        for slot in range(1, count):
            pairs = [(i, partner(i, slot, count)) for i in range(count)]
            moved.append(lax.ppermute(slabs[slot], axis, pairs))
        return moved

    rim, picked = edges(keys, values, ())
    between, within, order = gather_ctx(picked)
    summary = list(between) + within
    weight_half = half_of(sides, out_weight, (picked,))
    mine = lax.all_gather(weight_half, "head", axis=0)
    send = () if ctx > STRIDE else (prepare(queries, keys, values, ctx, (weight_half,)),)
    (rim,) = after([rim], (*between[1:], *send))
    before = lax.ppermute(rim, "ctx", [(i, i + 1) for i in range(ctx - 1)])

    def home(chunk, waits):
        return home_sections(
            place_word, queries, keys, values, before, summary, order, chunk, chunks, waits
        )

    moved, waits = [], ()
    if ctx > STRIDE:
        stride_out = stride_general(queries, keys, values)
        for chunk in range(chunks):
            lanes = slice(chunk * part, (chunk + 1) * part)
            homes, mark = home(chunk, waits)
            attended = (homes + stride_out[:, lanes].astype(F32)).astype(BF16)
            attended = attended.reshape(groups, tokens_dev // groups, part)
            owners = [partner(seat, slot, groups) for slot in range(groups)]
            moved.append(exchange([attended[owner] for owner in owners], "head"))
            waits = (mark,)
    else:
        (send,) = after(send, (rim,))
        received = lax.all_to_all(send, "ctx", split_axis=0, concat_axis=0, tiled=True)
        homes, backs = [], []
        for chunk in range(chunks):
            sections, mark = home(chunk, waits)
            homes.append(sections)
            waits = (mark,)
        for chunk in range(chunks):
            result, mark = stride_attend(received, chunk, chunks, waits)
            backs.append(lax.all_to_all(result, "ctx", split_axis=0, concat_axis=0, tiled=True))
            waits = (mark,)
        for chunk in range(chunks):
            *slabs, mark = combine(sides, homes[chunk], backs[chunk], groups, waits)
            moved.append(exchange(slabs, "head"))
            waits = (mark, *moved[-1][1:])
    (held,) = after([mine], (mark,))
    other = lax.ppermute(held, "ctx", sibling)
    return project(sides, moved, held, other)


def solution(mesh):
    chunks = 2 if HEADS // mesh.shape["head"] > 1 else 1
    placed = (P("ctx", "head"), P("ctx", "head"), P("ctx", "head"), P("head", None))
    return jax.shard_map(
        functools.partial(body, chunks=chunks),
        mesh=mesh,
        in_specs=placed,
        out_specs=P(("ctx", "head"), None),
        check_vma=False,
    )
```

```python
import functools
import math

import jax
import jax.numpy as jnp
from jax import lax
from jax.experimental import pallas as pl
from jax.experimental.pallas import tpu as pltpu
from jax.sharding import PartitionSpec as P

HEADS = 16
HEAD_SIZE = 128
WINDOW = 512
STRIDE = 16
BLOCK = 128
SUMCOLS = 8

BIG_NEG = -1e30
TILE = 256
LOG_SCALE = HEAD_SIZE ** (-0.5) * math.log2(math.e)
F32 = jnp.float32
BF16 = jnp.bfloat16


def params(mib):
    return pltpu.CompilerParams(vmem_limit_bytes=mib * 1024 * 1024)


MARK = jax.ShapeDtypeStruct((8, 128), F32)


def mark_spec():
    return pl.BlockSpec(MARK.shape, lambda *place: (0, 0))


def moments(arrays):
    return [pl.BlockSpec(memory_space=pl.ANY)] * len(arrays)


def after(arrays, others):
    anywhere = pl.BlockSpec(memory_space=pl.ANY)
    return pl.pallas_call(
        lambda *refs: None,
        in_specs=[anywhere] * (len(arrays) + len(others)),
        out_specs=[anywhere] * len(arrays),
        out_shape=[jax.ShapeDtypeStruct(array.shape, array.dtype) for array in arrays],
        input_output_aliases={i: i for i in range(len(arrays))},
        compiler_params=params(60),
        cost_estimate=cost(0, 0),
        name="after",
    )(*arrays, *others)


def cost(flops, bytes_accessed, exps=0):
    return pl.CostEstimate(
        flops=int(flops), bytes_accessed=int(bytes_accessed), transcendentals=int(exps)
    )


def partner(place, slot, count):
    assert count & (count - 1) == 0
    return place ^ slot


def iota2(shape, dim):
    return lax.broadcasted_iota(jnp.int32, shape, dim)


def scores(query, key_rows):
    return lax.dot_general(query, key_rows, (((1,), (1,)), ((), ())), preferred_element_type=F32)


def dot(left, right):
    return jnp.dot(left, right, preferred_element_type=F32)


def regroup_matrix():
    rows = iota2((TILE, TILE), 0)
    cols = iota2((TILE, TILE), 1)
    return (cols == (rows & 15) * 16 + (rows >> 4)).astype(BF16)


def with_ones(value_rows):
    return jnp.concatenate([value_rows, jnp.ones_like(value_rows)], axis=1)


def weighted(score_blocks, value_blocks, extra=None):
    top = functools.reduce(jnp.maximum, score_blocks)
    top = jnp.max(top, axis=-1, keepdims=True)
    if extra is not None:
        top = jnp.maximum(top, extra[0])
    total = None
    for block, value_block in zip(score_blocks, value_blocks):
        weights = jnp.exp2((block - top) * LOG_SCALE).astype(BF16)
        part = dot(weights, value_block)
        total = part if total is None else total + part
    if extra is not None:
        own = jnp.exp2((extra[0] - top) * LOG_SCALE).astype(BF16).astype(F32)
        total = total + own * extra[1].astype(F32)
    return total[:, :HEAD_SIZE] / total[:, HEAD_SIZE:]


def edge_kernel(k_ref, v_ref, k_ends_ref, v_ends_ref, *refs):
    rim_ref, sum_ref = refs[-2:]
    rim_ref[0] = k_ref[...]
    rim_ref[1] = v_ref[...]

    @pl.when(pl.program_id(0) == 0)
    def _():
        for number, ref in enumerate((k_ends_ref, v_ends_ref)):
            rows = ref[...].astype(F32)[:, 16 - SUMCOLS :]
            sum_ref[number] = rows.reshape(sum_ref.shape[1:]).astype(BF16)


def edges(keys, values, waits):
    tokens_dev, width = keys.shape
    blocks = tokens_dev // BLOCK
    first = (tokens_dev - WINDOW) // TILE
    source = pl.BlockSpec((TILE, width), lambda i: (first + i, 0))
    ends = pl.BlockSpec((blocks, 16, width), lambda i: (0, BLOCK // 16 - 1, 0))
    shape = (2, blocks * SUMCOLS, width)
    return pl.pallas_call(
        edge_kernel,
        grid=(WINDOW // TILE,),
        in_specs=[source] * 2 + [ends] * 2 + moments(waits),
        out_specs=[
            pl.BlockSpec((2, TILE, width), lambda i: (0, i, 0)),
            pl.BlockSpec(shape, lambda i: (0, 0, 0)),
        ],
        out_shape=[
            jax.ShapeDtypeStruct((2, WINDOW, width), BF16),
            jax.ShapeDtypeStruct(shape, BF16),
        ],
        compiler_params=params(60),
        cost_estimate=cost(0, 8 * WINDOW * width),
        name="edges",
    )(
        keys,
        values,
        keys.reshape(blocks, BLOCK, width),
        values.reshape(blocks, BLOCK, width),
        *waits,
    )


def cut_kernel(side_ref, weight_ref, *refs):
    refs[-1][...] = weight_ref[...]


def cut(side, weight, size, first, waits):
    rows = weight.shape[0]
    return pl.pallas_call(
        cut_kernel,
        grid_spec=pltpu.PrefetchScalarGridSpec(
            num_scalar_prefetch=1,
            grid=(1,),
            in_specs=[pl.BlockSpec((rows, size), lambda i, side: (0, first + side[0]))]
            + moments(waits),
            out_specs=pl.BlockSpec((rows, size), lambda i, side: (0, 0)),
        ),
        out_shape=jax.ShapeDtypeStruct((rows, size), BF16),
        compiler_params=params(60),
        cost_estimate=cost(0, 4 * rows * size),
        name="cut",
    )(side, weight, *waits)


def prep_kernel(q_ref, k_ref, v_ref, *refs):
    send_ref = refs[-1]
    matrix = regroup_matrix()
    ctx, _, per, rows, width = send_ref.shape
    for number, ref in enumerate((q_ref, k_ref, v_ref)):
        grouped = dot(matrix, ref[...]).astype(BF16)
        send_ref[:, number] = grouped.reshape(ctx, per, rows, width)


def prepare(queries, keys, values, ctx, chunk, chunks, waits):
    tokens_dev, width = queries.shape
    per = STRIDE // ctx
    part = width // chunks
    return pl.pallas_call(
        prep_kernel,
        grid=(tokens_dev // TILE,),
        in_specs=[pl.BlockSpec((TILE, part), lambda b: (b, chunk))] * 3 + moments(waits),
        out_specs=pl.BlockSpec((ctx, 3, per, TILE // STRIDE, part), lambda b: (0, 0, 0, b, 0)),
        out_shape=jax.ShapeDtypeStruct((ctx, 3, per, tokens_dev // STRIDE, part), BF16),
        compiler_params=params(60),
        cost_estimate=cost(6 * tokens_dev * TILE * part, 12 * tokens_dev * part),
        name="prepare",
    )(queries, keys, values, *waits)


def home_kernel(place_ref, q_ref, k_ref, v_ref, rim_ref, *refs, order):
    sum_refs, (o_ref, mark_ref) = refs[: len(order)], refs[-2:]
    mark_ref[...] = jnp.zeros_like(mark_ref)
    place = place_ref[0]
    tokens_dev = q_ref.shape[0]
    back = WINDOW // TILE
    key_blocks = [rim_ref[0, e * TILE : (e + 1) * TILE] for e in range(back)]
    value_blocks = [with_ones(rim_ref[1, e * TILE : (e + 1) * TILE]) for e in range(back)]
    for e in range(tokens_dev // TILE):
        key_blocks.append(k_ref[e * TILE : (e + 1) * TILE])
        value_blocks.append(with_ones(v_ref[e * TILE : (e + 1) * TILE]))
    picks = sum_refs[0].shape[1]
    sum_keys = jnp.concatenate([ref[0] for ref in sum_refs])
    sum_values = with_ones(jnp.concatenate([ref[1] for ref in sum_refs]))
    sum_col = jnp.concatenate(
        [iota2((TILE, picks), 1) + (place ^ i) * picks for i in order], axis=1
    )
    row = iota2((TILE, TILE), 0)
    col = iota2((TILE, TILE), 1)
    for b in range(tokens_dev // TILE):
        query = q_ref[b * TILE : (b + 1) * TILE]
        blocks = []
        for e in range(back + 1):
            block = scores(query, key_blocks[b + e])
            allowed = None
            if e == 0:
                allowed = col > row
            if e == back:
                allowed = col <= row
            if b + e < back:
                held = place > 0
                allowed = held if allowed is None else allowed & held
            if allowed is not None:
                block = jnp.where(allowed, block, BIG_NEG)
            blocks.append(block)
        local = weighted(blocks, value_blocks[b : b + back + 1])
        pos = place * tokens_dev + b * TILE + iota2((TILE, 1), 0)
        within = pos % BLOCK
        held = pos // BLOCK * SUMCOLS + jnp.maximum(within - (BLOCK - SUMCOLS - 1), 0)
        block = jnp.where(sum_col < held, scores(query, sum_keys), BIG_NEG)
        own_key = key_blocks[b + back].astype(F32)
        own = jnp.sum(query.astype(F32) * own_key, axis=-1, keepdims=True)
        own = jnp.where(within < BLOCK - SUMCOLS, own, BIG_NEG)
        summary = weighted([block], [sum_values], (own, value_blocks[b + back]))
        o_ref[b * TILE : (b + 1) * TILE] = local + summary


def home_sections(place, queries, keys, values, rim, summary, order, chunk, chunks, waits):
    tokens_dev, width = queries.shape
    heads = width // chunks // HEAD_SIZE
    first = chunk * heads
    picks = summary[0].shape[1]
    total = len(summary) * picks
    own = pl.BlockSpec((tokens_dev, HEAD_SIZE), lambda h: (0, first + h))
    pairs = tokens_dev * (WINDOW + TILE + total) * heads
    weight = 8 if chunk == 0 else 64
    return pl.pallas_call(
        functools.partial(home_kernel, order=order),
        grid=(heads,),
        in_specs=[
            pl.BlockSpec(memory_space=pltpu.SMEM),
            own,
            own,
            own,
            pl.BlockSpec((2, WINDOW, HEAD_SIZE), lambda h: (0, 0, first + h)),
        ]
        + [pl.BlockSpec((2, picks, HEAD_SIZE), lambda h: (0, 0, first + h))] * len(summary)
        + moments(waits),
        out_specs=[pl.BlockSpec((tokens_dev, HEAD_SIZE), lambda h: (0, h)), mark_spec()],
        out_shape=[jax.ShapeDtypeStruct((tokens_dev, heads * HEAD_SIZE), F32), MARK],
        compiler_params=params(60),
        cost_estimate=cost(weight * pairs * HEAD_SIZE, 14 * tokens_dev * width, weight * pairs // 8),
        name="home",
    )(place, queries, keys, values, rim, *summary, *waits)


def stride_kernel(place_ref, x_ref, *refs, slabs):
    ctx, _, _, rows, width = x_ref.shape
    o_refs, mark_ref, held_ref = refs[-2 - (ctx if slabs else 1) : -2], refs[-2], refs[-1]
    mark_ref[...] = jnp.zeros_like(mark_ref)
    count = ctx * rows
    row = iota2((TILE, TILE), 0)
    col = iota2((TILE, TILE), 1)
    sources = TILE // rows
    units = []
    for head in range(width // HEAD_SIZE):
        lanes = slice(head * HEAD_SIZE, (head + 1) * HEAD_SIZE)
        query = x_ref[:, 0, 0, :, lanes].reshape(count, HEAD_SIZE)
        key_rows = x_ref[:, 1, 0, :, lanes].reshape(count, HEAD_SIZE)
        value_rows = with_ones(x_ref[:, 2, 0, :, lanes].reshape(count, HEAD_SIZE))
        for b in range(count // TILE):
            part = query[b * TILE : (b + 1) * TILE]
            blocks = [scores(part, key_rows[e * TILE : (e + 1) * TILE]) for e in range(b + 1)]
            blocks[b] = jnp.where(col <= row, blocks[b], BIG_NEG)
            units.append((lanes, b, blocks, value_rows))
    for lanes, b, blocks, value_rows in units:
        result = weighted(
            blocks, [value_rows[e * TILE : (e + 1) * TILE] for e in range(b + 1)]
        ).astype(BF16)
        held_ref[b * sources : (b + 1) * sources, :, lanes] = result.reshape(
            sources, rows, HEAD_SIZE
        )
    if not slabs:
        o_refs[0][:, 0] = held_ref[...]
        return
    for slot in range(ctx):
        o_refs[slot][0] = held_ref[partner(place_ref[0], slot, ctx)]


def stride_attend(place, moved, slabs, waits):
    ctx, _, per, rows, width = moved.shape
    count = ctx * rows
    pairs = per * (width // HEAD_SIZE) * count * (count + TILE) // 2
    if slabs:
        out_specs = [pl.BlockSpec((1, rows, width), lambda r: (r, 0, 0))] * ctx
        out_shape = [jax.ShapeDtypeStruct((per, rows, width), BF16)] * ctx
    else:
        out_specs = [pl.BlockSpec((ctx, 1, rows, width), lambda r: (0, r, 0, 0))]
        out_shape = [jax.ShapeDtypeStruct((ctx, per, rows, width), BF16)]
    return pl.pallas_call(
        functools.partial(stride_kernel, slabs=slabs),
        grid=(per,),
        in_specs=[
            pl.BlockSpec(memory_space=pltpu.SMEM),
            pl.BlockSpec((ctx, 3, 1, rows, width), lambda r: (0, 0, r, 0, 0)),
        ]
        + moments(waits),
        out_specs=out_specs + [mark_spec()],
        out_shape=out_shape + [MARK],
        scratch_shapes=[pltpu.VMEM((ctx, rows, width), BF16)],
        compiler_params=params(24),
        cost_estimate=cost(8 * pairs * HEAD_SIZE, 8 * per * count * width, pairs),
        name="stride",
    )(place, moved, *waits)


def combine_kernel(seat_ref, home_ref, *refs, slots, arrays, ctx):
    back_refs, o_refs, mark_ref = refs[:arrays], refs[-slots - 1 : -1], refs[-1]
    mark_ref[...] = jnp.zeros_like(mark_ref)
    tokens_dev, width = home_ref.shape
    size = tokens_dev // slots
    per = STRIDE // ctx
    token = iota2((TILE, TILE), 0)
    col = iota2((TILE, TILE), 1)
    group = col >> 4
    owner = group // per if arrays == 1 else partner(seat_ref[1], group // per, ctx)
    matrix = (token == (col & 15) * 16 + owner * per + group % per).astype(BF16)
    for slot in range(slots):
        owner = partner(seat_ref[0], slot, slots)
        for b in range(size // TILE):
            first = owner * (size // TILE) + b
            here = pl.ds(pl.multiple_of(first * STRIDE, STRIDE), STRIDE)
            if arrays == 1:
                rows = back_refs[0][:, :, here].reshape(TILE, width)
            else:
                rows = jnp.concatenate([ref[r, here] for ref in back_refs for r in range(per)])
            back = dot(matrix, rows)
            home = home_ref[pl.ds(pl.multiple_of(first * TILE, TILE), TILE)]
            o_refs[slot][b * TILE : (b + 1) * TILE] = (home + back).astype(BF16)


def combine(seat, home, backs, slots, ctx, waits):
    tokens_dev, width = home.shape
    size = tokens_dev // slots
    return pl.pallas_call(
        functools.partial(combine_kernel, slots=slots, arrays=len(backs), ctx=ctx),
        in_specs=[pl.BlockSpec(memory_space=pltpu.SMEM)]
        + [pl.BlockSpec(memory_space=pltpu.VMEM)] * (1 + len(backs))
        + moments(waits),
        out_specs=[pl.BlockSpec(memory_space=pltpu.VMEM)] * (slots + 1),
        out_shape=[jax.ShapeDtypeStruct((size, width), BF16)] * slots + [MARK],
        compiler_params=params(24),
        cost_estimate=cost(2 * tokens_dev * TILE * width, 8 * tokens_dev * width),
        name="combine",
    )(seat, home, *backs, *waits)


def project_kernel(side_ref, *refs, slots, chunks):
    moved_refs = refs[: slots * chunks]
    mine_ref, other_ref, mine_last_ref, other_last_ref, o_ref, total_ref = refs[slots * chunks :]
    part = moved_refs[0].shape[1]
    half, last = mine_ref.shape[2], mine_last_ref.shape[2]
    phase, slot = pl.program_id(0), pl.program_id(1)

    def add_up(weight_ref, begin, first):
        size = weight_ref.shape[2]
        here = slice(begin, begin + size)
        for one in range(slots):

            @pl.when(slot == one)
            def _():
                total = None if one == 0 else total_ref[:, here]
                for chunk in range(chunks):
                    rows = weight_ref[0, chunk * part : (chunk + 1) * part]
                    product = dot(moved_refs[chunk * slots + one][...], rows)
                    total = product if total is None else total + product
                if one < slots - 1:
                    total_ref[:, here] = total
                else:
                    o_ref[:, pl.ds(pl.multiple_of(first, size), size)] = total.astype(BF16)

    @pl.when(phase == 0)
    def _():
        add_up(mine_ref, 0, side_ref[0] * half)

    @pl.when(phase == 1)
    def _():
        add_up(other_ref, 0, (1 - side_ref[0]) * half)

    @pl.when(phase == 2)
    def _():
        add_up(mine_last_ref, 0, 2 * half + side_ref[0] * last)
        add_up(other_last_ref, last, 2 * half + (1 - side_ref[0]) * last)


def project(side, moved, mine, other, mine_last, other_last):
    chunks, slots = len(moved), len(moved[0])
    tokens, part = moved[0][0].shape
    width, half = mine.shape[1:]
    last = mine_last.shape[2]

    def mine_group(p, s, side):
        return (side[1] ^ jnp.where(p == 0, s, slots - 1), 0, 0)

    def other_group(p, s, side):
        return (side[1] ^ jnp.where(p == 0, 0, jnp.where(p == 1, s, slots - 1)), 0, 0)

    def last_slot(p, s, side):
        return (jnp.where(p == 2, s, 0), 0, 0)

    total = 2 * (half + last)
    return pl.pallas_call(
        functools.partial(project_kernel, slots=slots, chunks=chunks),
        grid_spec=pltpu.PrefetchScalarGridSpec(
            num_scalar_prefetch=1,
            grid=(3, slots),
            in_specs=[pl.BlockSpec((tokens, part), lambda p, s, side: (0, 0))] * (slots * chunks)
            + [pl.BlockSpec((1, width, half), mine_group)]
            + [pl.BlockSpec((1, width, half), other_group)]
            + [pl.BlockSpec((1, width, last), last_slot)] * 2,
            out_specs=pl.BlockSpec((tokens, total), lambda p, s, side: (0, 0)),
            scratch_shapes=[pltpu.VMEM((tokens, max(half, 2 * last)), F32)],
        ),
        out_shape=jax.ShapeDtypeStruct((tokens, total), BF16),
        compiler_params=params(24),
        cost_estimate=cost(
            2 * slots * tokens * width * total, 2 * slots * width * (total + tokens)
        ),
        name="project",
    )(side, *[slab for slabs in moved for slab in slabs], mine, other, mine_last, other_last)


def gather_ctx(rows):
    count = lax.axis_size("ctx")

    def swapped(piece, distance):
        return lax.ppermute(piece, "ctx", [(i, i ^ distance) for i in range(count)])

    order = list(range(0, count, 2))
    pieces = [rows] + [swapped(rows, distance) for distance in order[1:]]
    within = [swapped(piece, 1) for piece in pieces]
    return pieces, within, order + [i ^ 1 for i in order]


def stride_general(queries, keys, values):
    tokens_dev, width = queries.shape
    heads = width // HEAD_SIZE
    ctx = lax.axis_size("ctx")
    copies = max(ctx // STRIDE, 1)
    rows = tokens_dev // STRIDE
    held_rows = ctx * rows // copies
    own_copy = lax.axis_index("ctx") // STRIDE
    query_pos = (jnp.arange(held_rows) // (rows // copies)) * rows
    query_pos = query_pos + (jnp.arange(held_rows) % (rows // copies)) * copies + own_copy
    shaped = queries.reshape(1, rows // copies, ctx, width)
    query = lax.all_to_all(shaped, "ctx", split_axis=2, concat_axis=1, tiled=True)
    query = query.reshape(held_rows, heads, HEAD_SIZE)
    both = jnp.stack([keys, values]).reshape(2, rows, 1, STRIDE, width)
    both = jnp.broadcast_to(both, (2, rows, copies, STRIDE, width)).reshape(2, rows, ctx, width)
    both = lax.all_to_all(both, "ctx", split_axis=2, concat_axis=1, tiled=True)
    both = both.reshape(2, ctx * rows, heads, HEAD_SIZE)
    allowed = jnp.arange(ctx * rows)[None, :] <= query_pos[:, None]

    def one_head(operands):
        head_query, head_keys, head_values = operands
        masked = jnp.where(allowed, scores(head_query, head_keys), BIG_NEG)
        return weighted([masked], [with_ones(head_values)])

    result = lax.map(
        one_head,
        (query.transpose(1, 0, 2), both[0].transpose(1, 0, 2), both[1].transpose(1, 0, 2)),
    )
    result = result.transpose(1, 0, 2).reshape(ctx, rows // copies, 1, width).astype(BF16)
    back = lax.all_to_all(result, "ctx", split_axis=0, concat_axis=2, tiled=True)
    return back.reshape(tokens_dev, width)


def body(queries, keys, values, out_weight, chunks):
    tokens_dev, width = queries.shape
    ctx = lax.axis_size("ctx")
    groups = lax.axis_size("head")
    place = lax.axis_index("ctx")
    place_word = place.astype(jnp.int32).reshape(1)
    side = place % 2
    sibling = [(i, i ^ 1) for i in range(ctx)]

    part = width // chunks
    seat = lax.axis_index("head").astype(jnp.int32)
    sides = jnp.stack([side.astype(jnp.int32), seat])

    def exchange(slabs, axis):
        count = len(slabs)
        moved = [slabs[0]]
        for slot in range(1, count):
            pairs = [(i, partner(i, slot, count)) for i in range(count)]
            moved.append(lax.ppermute(slabs[slot], axis, pairs))
        return moved

    rim, picked = edges(keys, values, ())
    between, within, order = gather_ctx(picked)
    summary = between + within
    eighth = out_weight.shape[1] // 8
    weight_half = cut(sides, out_weight, 3 * eighth, 0, (picked,))
    mine = lax.all_gather(weight_half, "head", axis=0)
    if ctx > STRIDE:
        stride_out = stride_general(queries, keys, values)
        sends = []
    else:
        sends = [prepare(queries, keys, values, ctx, 0, chunks, (weight_half,))]
    weight_last = cut(sides, out_weight, eighth, 6, sends)
    mine_last = jnp.stack(exchange([weight_last] * groups, "head"))
    (rim,) = after([rim], (*between[1:], *sends))
    if sends:
        sends = list(after(sends, (rim,)))
    before = lax.ppermute(rim, "ctx", [(i, i + 1) for i in range(ctx - 1)])
    for chunk in range(len(sends), chunks * len(sends)):
        sends.append(prepare(queries, keys, values, ctx, chunk, chunks, within[-1:]))

    def home(chunk, waits):
        return home_sections(
            place_word, queries, keys, values, before, summary, order, chunk, chunks, waits
        )


    moved, waits = [], ()
    if ctx > STRIDE:
        for chunk in range(chunks):
            lanes = slice(chunk * part, (chunk + 1) * part)
            homes, mark = home(chunk, waits)
            attended = (homes + stride_out[:, lanes].astype(F32)).astype(BF16)
            attended = attended.reshape(groups, tokens_dev // groups, part)
            owners = [partner(seat, slot, groups) for slot in range(groups)]
            moved.append(exchange([attended[owner] for owner in owners], "head"))
            waits = (mark,)
    else:
        seats = jnp.stack([seat, place.astype(jnp.int32)])
        seats = jnp.stack([seat, place.astype(jnp.int32)])
        sections, mark = home(0, (mine_last,))
        homes, backs, waits = [sections], [], ()
        if chunks > 1:
            sends[1:] = list(after(sends[1:], (mark,)))
        for chunk, send in enumerate(sends):
            received = lax.all_to_all(send, "ctx", split_axis=0, concat_axis=0, tiled=True)
            beside = chunk < chunks - 1
            *slabs, mark = stride_attend(place_word, received, beside, waits)
            if beside:
                backs.append(exchange(slabs, "ctx"))
            else:
                back = lax.all_to_all(slabs[0], "ctx", split_axis=0, concat_axis=0, tiled=True)
                backs.append([back])
            waits = (mark,)
            for later in range(1, chunks) if chunk == 0 else ():
                sections, mark = home(later, waits)
                homes.append(sections)
                waits = (mark, *backs[0][1:-1])
        for chunk in range(chunks):
            *slabs, mark = combine(seats, homes[chunk], backs[chunk], groups, ctx, waits)
            moved.append(exchange(slabs, "head"))
            waits = (mark, *moved[-1][1:])
    held, held_last = after([mine, mine_last], (mark,))
    other = lax.ppermute(held, "ctx", sibling)
    other_last = lax.ppermute(held_last, "ctx", sibling)
    return project(sides, moved, held, other, held_last, other_last)


def solution(mesh):
    chunks = 2 if HEADS // mesh.shape["head"] > 1 else 1
    placed = (P("ctx", "head"), P("ctx", "head"), P("ctx", "head"), P("head", None))
    return jax.shard_map(
        functools.partial(body, chunks=chunks),
        mesh=mesh,
        in_specs=placed,
        out_specs=P(("ctx", "head"), None),
        check_vma=False,
    )
```

```python
import functools
import math

import jax
import jax.numpy as jnp
from jax import lax
from jax.experimental import pallas as pl
from jax.experimental.pallas import tpu as pltpu
from jax.sharding import PartitionSpec as P

HEADS = 16
HEAD_SIZE = 128
WINDOW = 512
STRIDE = 16
BLOCK = 128
SUMCOLS = 8

BIG_NEG = -1e30
TILE = 256
LOG_SCALE = HEAD_SIZE ** (-0.5) * math.log2(math.e)
F32 = jnp.float32
BF16 = jnp.bfloat16


def params(mib):
    return pltpu.CompilerParams(vmem_limit_bytes=mib * 1024 * 1024)


MARK = jax.ShapeDtypeStruct((8, 128), F32)


def mark_spec():
    return pl.BlockSpec(MARK.shape, lambda *place: (0, 0))


def moments(arrays):
    return [pl.BlockSpec(memory_space=pl.ANY)] * len(arrays)


def after(arrays, others):
    anywhere = pl.BlockSpec(memory_space=pl.ANY)
    return pl.pallas_call(
        lambda *refs: None,
        in_specs=[anywhere] * (len(arrays) + len(others)),
        out_specs=[anywhere] * len(arrays),
        out_shape=[jax.ShapeDtypeStruct(array.shape, array.dtype) for array in arrays],
        input_output_aliases={i: i for i in range(len(arrays))},
        compiler_params=params(60),
        cost_estimate=cost(0, 0),
        name="after",
    )(*arrays, *others)


def cost(flops, bytes_accessed, exps=0):
    return pl.CostEstimate(
        flops=int(flops), bytes_accessed=int(bytes_accessed), transcendentals=int(exps)
    )


def partner(place, slot, count):
    assert count & (count - 1) == 0
    return place ^ slot


def iota2(shape, dim):
    return lax.broadcasted_iota(jnp.int32, shape, dim)


def scores(query, key_rows):
    return lax.dot_general(query, key_rows, (((1,), (1,)), ((), ())), preferred_element_type=F32)


def dot(left, right):
    return jnp.dot(left, right, preferred_element_type=F32)


def regroup_matrix():
    rows = iota2((TILE, TILE), 0)
    cols = iota2((TILE, TILE), 1)
    return (cols == (rows & 15) * 16 + (rows >> 4)).astype(BF16)


def with_ones(value_rows):
    return jnp.concatenate([value_rows, jnp.ones_like(value_rows)], axis=1)


def weighted(score_blocks, value_blocks, extra=None):
    top = functools.reduce(jnp.maximum, score_blocks)
    top = jnp.max(top, axis=-1, keepdims=True)
    if extra is not None:
        top = jnp.maximum(top, extra[0])
    total = None
    for block, value_block in zip(score_blocks, value_blocks):
        weights = jnp.exp2((block - top) * LOG_SCALE).astype(BF16)
        part = dot(weights, value_block)
        total = part if total is None else total + part
    if extra is not None:
        own = jnp.exp2((extra[0] - top) * LOG_SCALE).astype(BF16).astype(F32)
        total = total + own * extra[1].astype(F32)
    return total[:, :HEAD_SIZE] / total[:, HEAD_SIZE:]


def edge_kernel(k_ref, v_ref, k_ends_ref, v_ends_ref, *refs):
    rim_ref, sum_ref = refs[-2:]
    rim_ref[0] = k_ref[...]
    rim_ref[1] = v_ref[...]

    @pl.when(pl.program_id(0) == 0)
    def _():
        for number, ref in enumerate((k_ends_ref, v_ends_ref)):
            rows = ref[...].astype(F32)[:, 16 - SUMCOLS :]
            sum_ref[number] = rows.reshape(sum_ref.shape[1:]).astype(BF16)


def edges(keys, values, waits):
    tokens_dev, width = keys.shape
    blocks = tokens_dev // BLOCK
    first = (tokens_dev - WINDOW) // TILE
    source = pl.BlockSpec((TILE, width), lambda i: (first + i, 0))
    ends = pl.BlockSpec((blocks, 16, width), lambda i: (0, BLOCK // 16 - 1, 0))
    shape = (2, blocks * SUMCOLS, width)
    return pl.pallas_call(
        edge_kernel,
        grid=(WINDOW // TILE,),
        in_specs=[source] * 2 + [ends] * 2 + moments(waits),
        out_specs=[
            pl.BlockSpec((2, TILE, width), lambda i: (0, i, 0)),
            pl.BlockSpec(shape, lambda i: (0, 0, 0)),
        ],
        out_shape=[
            jax.ShapeDtypeStruct((2, WINDOW, width), BF16),
            jax.ShapeDtypeStruct(shape, BF16),
        ],
        compiler_params=params(60),
        cost_estimate=cost(0, 8 * WINDOW * width),
        name="edges",
    )(
        keys,
        values,
        keys.reshape(blocks, BLOCK, width),
        values.reshape(blocks, BLOCK, width),
        *waits,
    )


def cut_kernel(side_ref, weight_ref, *refs):
    refs[-1][...] = weight_ref[...]


def cut(side, weight, size, first, waits):
    rows = weight.shape[0]
    return pl.pallas_call(
        cut_kernel,
        grid_spec=pltpu.PrefetchScalarGridSpec(
            num_scalar_prefetch=1,
            grid=(1,),
            in_specs=[pl.BlockSpec((rows, size), lambda i, side: (0, first + side[0]))]
            + moments(waits),
            out_specs=pl.BlockSpec((rows, size), lambda i, side: (0, 0)),
        ),
        out_shape=jax.ShapeDtypeStruct((rows, size), BF16),
        compiler_params=params(60),
        cost_estimate=cost(0, 4 * rows * size),
        name="cut",
    )(side, weight, *waits)


def prep_kernel(q_ref, k_ref, v_ref, *refs):
    send_ref = refs[-1]
    matrix = regroup_matrix()
    ctx, _, per, rows, width = send_ref.shape
    for number, ref in enumerate((q_ref, k_ref, v_ref)):
        grouped = dot(matrix, ref[...]).astype(BF16)
        send_ref[:, number] = grouped.reshape(ctx, per, rows, width)


def prepare(queries, keys, values, ctx, chunk, chunks, waits):
    tokens_dev, width = queries.shape
    per = STRIDE // ctx
    part = width // chunks
    return pl.pallas_call(
        prep_kernel,
        grid=(tokens_dev // TILE,),
        in_specs=[pl.BlockSpec((TILE, part), lambda b: (b, chunk))] * 3 + moments(waits),
        out_specs=pl.BlockSpec((ctx, 3, per, TILE // STRIDE, part), lambda b: (0, 0, 0, b, 0)),
        out_shape=jax.ShapeDtypeStruct((ctx, 3, per, tokens_dev // STRIDE, part), BF16),
        compiler_params=params(60),
        cost_estimate=cost(6 * tokens_dev * TILE * part, 12 * tokens_dev * part),
        name="prepare",
    )(queries, keys, values, *waits)


def home_kernel(place_ref, q_ref, k_ref, v_ref, rim_ref, *refs, order):
    sum_refs, (o_ref, mark_ref) = refs[: len(order)], refs[-2:]
    mark_ref[...] = jnp.zeros_like(mark_ref)
    place = place_ref[0]
    tokens_dev = q_ref.shape[0]
    back = WINDOW // TILE
    key_blocks = [rim_ref[0, e * TILE : (e + 1) * TILE] for e in range(back)]
    value_blocks = [with_ones(rim_ref[1, e * TILE : (e + 1) * TILE]) for e in range(back)]
    for e in range(tokens_dev // TILE):
        key_blocks.append(k_ref[e * TILE : (e + 1) * TILE])
        value_blocks.append(with_ones(v_ref[e * TILE : (e + 1) * TILE]))
    picks = sum_refs[0].shape[1]
    sum_keys = jnp.concatenate([ref[0] for ref in sum_refs])
    sum_values = with_ones(jnp.concatenate([ref[1] for ref in sum_refs]))
    sum_col = jnp.concatenate(
        [iota2((TILE, picks), 1) + (place ^ i) * picks for i in order], axis=1
    )
    row = iota2((TILE, TILE), 0)
    col = iota2((TILE, TILE), 1)
    for b in range(tokens_dev // TILE):
        query = q_ref[b * TILE : (b + 1) * TILE]
        blocks = []
        for e in range(back + 1):
            block = scores(query, key_blocks[b + e])
            allowed = None
            if e == 0:
                allowed = col > row
            if e == back:
                allowed = col <= row
            if b + e < back:
                held = place > 0
                allowed = held if allowed is None else allowed & held
            if allowed is not None:
                block = jnp.where(allowed, block, BIG_NEG)
            blocks.append(block)
        local = weighted(blocks, value_blocks[b : b + back + 1])
        pos = place * tokens_dev + b * TILE + iota2((TILE, 1), 0)
        within = pos % BLOCK
        held = pos // BLOCK * SUMCOLS + jnp.maximum(within - (BLOCK - SUMCOLS - 1), 0)
        block = jnp.where(sum_col < held, scores(query, sum_keys), BIG_NEG)
        own_key = key_blocks[b + back].astype(F32)
        own = jnp.sum(query.astype(F32) * own_key, axis=-1, keepdims=True)
        own = jnp.where(within < BLOCK - SUMCOLS, own, BIG_NEG)
        summary = weighted([block], [sum_values], (own, value_blocks[b + back]))
        o_ref[b * TILE : (b + 1) * TILE] = local + summary


def home_sections(place, queries, keys, values, rim, summary, order, chunk, chunks, waits):
    tokens_dev, width = queries.shape
    heads = width // chunks // HEAD_SIZE
    first = chunk * heads
    picks = summary[0].shape[1]
    total = len(summary) * picks
    own = pl.BlockSpec((tokens_dev, HEAD_SIZE), lambda h: (0, first + h))
    pairs = tokens_dev * (WINDOW + TILE + total) * heads
    return pl.pallas_call(
        functools.partial(home_kernel, order=order),
        grid=(heads,),
        in_specs=[
            pl.BlockSpec(memory_space=pltpu.SMEM),
            own,
            own,
            own,
            pl.BlockSpec((2, WINDOW, HEAD_SIZE), lambda h: (0, 0, first + h)),
        ]
        + [pl.BlockSpec((2, picks, HEAD_SIZE), lambda h: (0, 0, first + h))] * len(summary)
        + moments(waits),
        out_specs=[pl.BlockSpec((tokens_dev, HEAD_SIZE), lambda h: (0, h)), mark_spec()],
        out_shape=[jax.ShapeDtypeStruct((tokens_dev, heads * HEAD_SIZE), F32), MARK],
        compiler_params=params(60),
        cost_estimate=cost(64 * pairs * HEAD_SIZE, 14 * tokens_dev * width, 8 * pairs),
        name="home",
    )(place, queries, keys, values, rim, *summary, *waits)


def stride_kernel(place_ref, x_ref, *refs, slabs):
    ctx, _, _, rows, width = x_ref.shape
    o_refs, mark_ref, held_ref = refs[-2 - (ctx if slabs else 1) : -2], refs[-2], refs[-1]
    mark_ref[...] = jnp.zeros_like(mark_ref)
    count = ctx * rows
    row = iota2((TILE, TILE), 0)
    col = iota2((TILE, TILE), 1)
    sources = TILE // rows
    units = []
    for head in range(width // HEAD_SIZE):
        lanes = slice(head * HEAD_SIZE, (head + 1) * HEAD_SIZE)
        query = x_ref[:, 0, 0, :, lanes].reshape(count, HEAD_SIZE)
        key_rows = x_ref[:, 1, 0, :, lanes].reshape(count, HEAD_SIZE)
        value_rows = with_ones(x_ref[:, 2, 0, :, lanes].reshape(count, HEAD_SIZE))
        for b in range(count // TILE):
            part = query[b * TILE : (b + 1) * TILE]
            blocks = [scores(part, key_rows[e * TILE : (e + 1) * TILE]) for e in range(b + 1)]
            blocks[b] = jnp.where(col <= row, blocks[b], BIG_NEG)
            units.append((lanes, b, blocks, value_rows))
    for lanes, b, blocks, value_rows in units:
        result = weighted(
            blocks, [value_rows[e * TILE : (e + 1) * TILE] for e in range(b + 1)]
        ).astype(BF16)
        held_ref[b * sources : (b + 1) * sources, :, lanes] = result.reshape(
            sources, rows, HEAD_SIZE
        )
    if not slabs:
        o_refs[0][:, 0] = held_ref[...]
        return
    for slot in range(ctx):
        o_refs[slot][0] = held_ref[partner(place_ref[0], slot, ctx)]


def stride_attend(place, moved, slabs, waits):
    ctx, _, per, rows, width = moved.shape
    count = ctx * rows
    pairs = per * (width // HEAD_SIZE) * count * (count + TILE) // 2
    if slabs:
        out_specs = [pl.BlockSpec((1, rows, width), lambda r: (r, 0, 0))] * ctx
        out_shape = [jax.ShapeDtypeStruct((per, rows, width), BF16)] * ctx
    else:
        out_specs = [pl.BlockSpec((ctx, 1, rows, width), lambda r: (0, r, 0, 0))]
        out_shape = [jax.ShapeDtypeStruct((ctx, per, rows, width), BF16)]
    return pl.pallas_call(
        functools.partial(stride_kernel, slabs=slabs),
        grid=(per,),
        in_specs=[
            pl.BlockSpec(memory_space=pltpu.SMEM),
            pl.BlockSpec((ctx, 3, 1, rows, width), lambda r: (0, 0, r, 0, 0)),
        ]
        + moments(waits),
        out_specs=out_specs + [mark_spec()],
        out_shape=out_shape + [MARK],
        scratch_shapes=[pltpu.VMEM((ctx, rows, width), BF16)],
        compiler_params=params(24),
        cost_estimate=cost(8 * pairs * HEAD_SIZE, 8 * per * count * width, pairs),
        name="stride",
    )(place, moved, *waits)


def combine_kernel(seat_ref, home_ref, *refs, slots, arrays, ctx):
    back_refs, o_refs, mark_ref = refs[:arrays], refs[-slots - 1 : -1], refs[-1]
    mark_ref[...] = jnp.zeros_like(mark_ref)
    tokens_dev, width = home_ref.shape
    size = tokens_dev // slots
    per = STRIDE // ctx
    token = iota2((TILE, TILE), 0)
    col = iota2((TILE, TILE), 1)
    group = col >> 4
    owner = group // per if arrays == 1 else partner(seat_ref[1], group // per, ctx)
    matrix = (token == (col & 15) * 16 + owner * per + group % per).astype(BF16)
    for slot in range(slots):
        owner = partner(seat_ref[0], slot, slots)
        for b in range(size // TILE):
            first = owner * (size // TILE) + b
            here = pl.ds(pl.multiple_of(first * STRIDE, STRIDE), STRIDE)
            if arrays == 1:
                rows = back_refs[0][:, :, here].reshape(TILE, width)
            else:
                rows = jnp.concatenate([ref[r, here] for ref in back_refs for r in range(per)])
            back = dot(matrix, rows)
            home = home_ref[pl.ds(pl.multiple_of(first * TILE, TILE), TILE)]
            o_refs[slot][b * TILE : (b + 1) * TILE] = (home + back).astype(BF16)


def combine(seat, home, backs, slots, ctx, waits):
    tokens_dev, width = home.shape
    size = tokens_dev // slots
    return pl.pallas_call(
        functools.partial(combine_kernel, slots=slots, arrays=len(backs), ctx=ctx),
        in_specs=[pl.BlockSpec(memory_space=pltpu.SMEM)]
        + [pl.BlockSpec(memory_space=pltpu.VMEM)] * (1 + len(backs))
        + moments(waits),
        out_specs=[pl.BlockSpec(memory_space=pltpu.VMEM)] * (slots + 1),
        out_shape=[jax.ShapeDtypeStruct((size, width), BF16)] * slots + [MARK],
        compiler_params=params(24),
        cost_estimate=cost(56 * tokens_dev * TILE * width, 8 * tokens_dev * width),
        name="combine",
    )(seat, home, *backs, *waits)


def project_kernel(side_ref, *refs, slots, adds):
    moved_refs, (mine_ref, other_ref), refs = refs[:slots], refs[slots : slots + 2], refs[slots + 2 :]
    o_ref, mark_ref, total_ref = refs[-3:]
    mark_ref[...] = jnp.zeros_like(mark_ref)
    half = mine_ref.shape[2]
    phase, slot = pl.program_id(0), pl.program_id(1)
    here = pl.ds(pl.multiple_of((side_ref[0] ^ phase) * half, half), half)

    def add_up(weight_ref):
        for one in range(slots):

            @pl.when(slot == one)
            def _():
                total = dot(moved_refs[one][...], weight_ref[0])
                if one > 0:
                    total = total + total_ref[...]
                elif adds:
                    total = total + refs[0][:, here]
                if one < slots - 1:
                    total_ref[...] = total
                else:
                    o_ref[:, here] = total.astype(o_ref.dtype)

    @pl.when(phase == 0)
    def _():
        add_up(mine_ref)

    @pl.when(phase == 1)
    def _():
        add_up(other_ref)


def project(side, moved, mine, other, chunk, before, dtype):
    slots = len(moved)
    tokens, part = moved[0].shape
    half = mine.shape[2]

    def mine_group(p, s, side):
        return (side[1] ^ jnp.where(p == 0, s, slots - 1), chunk, 0)

    def other_group(p, s, side):
        return (side[1] ^ jnp.where(p == 0, 0, s), chunk, 0)

    whole = pl.BlockSpec((tokens, 2 * half), lambda p, s, side: (0, 0))
    return pl.pallas_call(
        functools.partial(project_kernel, slots=slots, adds=len(before) > 0),
        grid_spec=pltpu.PrefetchScalarGridSpec(
            num_scalar_prefetch=1,
            grid=(2, slots),
            in_specs=[pl.BlockSpec((tokens, part), lambda p, s, side: (0, 0))] * slots
            + [pl.BlockSpec((1, part, half), mine_group)]
            + [pl.BlockSpec((1, part, half), other_group)]
            + [whole] * len(before),
            out_specs=[whole, mark_spec()],
            scratch_shapes=[pltpu.VMEM((tokens, half), F32)],
        ),
        out_shape=[jax.ShapeDtypeStruct((tokens, 2 * half), dtype), MARK],
        compiler_params=params(24),
        cost_estimate=cost(
            4 * slots * tokens * part * half, 2 * slots * part * (2 * half + tokens)
        ),
        name="project",
    )(side, *moved, mine, other, *before)


def gather_ctx(rows):
    count = lax.axis_size("ctx")

    def swapped(piece, distance):
        return lax.ppermute(piece, "ctx", [(i, i ^ distance) for i in range(count)])

    order = list(range(0, count, 2))
    pieces = [rows] + [swapped(rows, distance) for distance in order[1:]]
    within = [swapped(piece, 1) for piece in pieces]
    return pieces, within, order + [i ^ 1 for i in order]


def stride_general(queries, keys, values):
    tokens_dev, width = queries.shape
    heads = width // HEAD_SIZE
    ctx = lax.axis_size("ctx")
    copies = max(ctx // STRIDE, 1)
    rows = tokens_dev // STRIDE
    held_rows = ctx * rows // copies
    own_copy = lax.axis_index("ctx") // STRIDE
    query_pos = (jnp.arange(held_rows) // (rows // copies)) * rows
    query_pos = query_pos + (jnp.arange(held_rows) % (rows // copies)) * copies + own_copy
    shaped = queries.reshape(1, rows // copies, ctx, width)
    query = lax.all_to_all(shaped, "ctx", split_axis=2, concat_axis=1, tiled=True)
    query = query.reshape(held_rows, heads, HEAD_SIZE)
    both = jnp.stack([keys, values]).reshape(2, rows, 1, STRIDE, width)
    both = jnp.broadcast_to(both, (2, rows, copies, STRIDE, width)).reshape(2, rows, ctx, width)
    both = lax.all_to_all(both, "ctx", split_axis=2, concat_axis=1, tiled=True)
    both = both.reshape(2, ctx * rows, heads, HEAD_SIZE)
    allowed = jnp.arange(ctx * rows)[None, :] <= query_pos[:, None]

    def one_head(operands):
        head_query, head_keys, head_values = operands
        masked = jnp.where(allowed, scores(head_query, head_keys), BIG_NEG)
        return weighted([masked], [with_ones(head_values)])

    result = lax.map(
        one_head,
        (query.transpose(1, 0, 2), both[0].transpose(1, 0, 2), both[1].transpose(1, 0, 2)),
    )
    result = result.transpose(1, 0, 2).reshape(ctx, rows // copies, 1, width).astype(BF16)
    back = lax.all_to_all(result, "ctx", split_axis=0, concat_axis=2, tiled=True)
    return back.reshape(tokens_dev, width)


def body(queries, keys, values, out_weight, chunks):
    tokens_dev, width = queries.shape
    ctx = lax.axis_size("ctx")
    groups = lax.axis_size("head")
    place = lax.axis_index("ctx")
    place_word = place.astype(jnp.int32).reshape(1)
    side = place % 2
    sibling = [(i, i ^ 1) for i in range(ctx)]

    part = width // chunks
    seat = lax.axis_index("head").astype(jnp.int32)
    sides = jnp.stack([side.astype(jnp.int32), seat])

    def exchange(slabs, axis):
        count = len(slabs)
        moved = [slabs[0]]
        for slot in range(1, count):
            pairs = [(i, partner(i, slot, count)) for i in range(count)]
            moved.append(lax.ppermute(slabs[slot], axis, pairs))
        return moved

    weight_half = cut(sides, out_weight, out_weight.shape[1] // 2, 0, ())
    mine = lax.all_gather(weight_half, "head", axis=0)
    rim, picked = edges(keys, values, (weight_half,))
    between, within, order = gather_ctx(picked)
    summary = between + within
    if ctx > STRIDE:
        stride_out = stride_general(queries, keys, values)
        sends = []
    else:
        sends = [prepare(queries, keys, values, ctx, 0, chunks, (weight_half,))]
    (rim,) = after([rim], (*between[1:], *sends))
    if sends:
        sends = list(after(sends, (rim,)))
    before = lax.ppermute(rim, "ctx", [(i, i + 1) for i in range(ctx - 1)])
    for chunk in range(len(sends), chunks * len(sends)):
        sends.append(prepare(queries, keys, values, ctx, chunk, chunks, within[-1:]))

    def home(chunk, waits):
        return home_sections(
            place_word, queries, keys, values, before, summary, order, chunk, chunks, waits
        )


    moved, waits = [], ()
    if ctx > STRIDE:
        for chunk in range(chunks):
            lanes = slice(chunk * part, (chunk + 1) * part)
            homes, mark = home(chunk, waits)
            attended = (homes + stride_out[:, lanes].astype(F32)).astype(BF16)
            attended = attended.reshape(groups, tokens_dev // groups, part)
            owners = [partner(seat, slot, groups) for slot in range(groups)]
            moved.append(exchange([attended[owner] for owner in owners], "head"))
            waits = (mark,)
    else:
        seats = jnp.stack([seat, place.astype(jnp.int32)])
        seats = jnp.stack([seat, place.astype(jnp.int32)])
        sections, mark = home(0, ())
        homes, backs, waits = [sections], [], ()
        if chunks > 1:
            sends[1:] = list(after(sends[1:], (mark,)))
        for chunk, send in enumerate(sends):
            received = lax.all_to_all(send, "ctx", split_axis=0, concat_axis=0, tiled=True)
            beside = chunk < chunks - 1
            *slabs, mark = stride_attend(place_word, received, beside, waits)
            if beside:
                backs.append(exchange(slabs, "ctx"))
            else:
                back = lax.all_to_all(slabs[0], "ctx", split_axis=0, concat_axis=0, tiled=True)
                backs.append([back])
            waits = (mark,)
            for later in range(1, chunks) if chunk == 0 else ():
                sections, mark = home(later, waits)
                homes.append(sections)
                waits = (mark,)
        for chunk in range(chunks):
            *slabs, mark = combine(seats, homes[chunk], backs[chunk], groups, ctx, waits)
            moved.append(exchange(slabs, "head"))
            waits = (mark, *moved[-1][1:3])
    (held,) = after([mine], (mark,))
    other = lax.ppermute(held, "ctx", sibling)
    total = ()
    for chunk in range(chunks):
        dtype = BF16 if chunk == chunks - 1 else F32
        *total, _ = project(sides, moved[chunk], held, other, chunk, total, dtype)
    return total[0]


def solution(mesh):
    chunks = 2 if HEADS // mesh.shape["head"] > 1 else 1
    placed = (P("ctx", "head"), P("ctx", "head"), P("ctx", "head"), P("head", None))
    return jax.shard_map(
        functools.partial(body, chunks=chunks),
        mesh=mesh,
        in_specs=placed,
        out_specs=P(("ctx", "head"), None),
        check_vma=False,
    )
```

```python
import functools
import math

import jax
import jax.numpy as jnp
from jax import lax
from jax.experimental import pallas as pl
from jax.experimental.pallas import tpu as pltpu
from jax.sharding import PartitionSpec as P

HEADS = 16
HEAD_SIZE = 128
WINDOW = 512
STRIDE = 16
BLOCK = 128
SUMCOLS = 8

BIG_NEG = -1e30
TILE = 256
LOG_SCALE = HEAD_SIZE ** (-0.5) * math.log2(math.e)
F32 = jnp.float32
BF16 = jnp.bfloat16


def params(mib):
    return pltpu.CompilerParams(vmem_limit_bytes=mib * 1024 * 1024)


MARK = jax.ShapeDtypeStruct((8, 128), F32)


def mark_spec():
    return pl.BlockSpec(MARK.shape, lambda *place: (0, 0))


def moments(arrays):
    return [pl.BlockSpec(memory_space=pl.ANY)] * len(arrays)


def after(arrays, others):
    anywhere = pl.BlockSpec(memory_space=pl.ANY)
    return pl.pallas_call(
        lambda *refs: None,
        in_specs=[anywhere] * (len(arrays) + len(others)),
        out_specs=[anywhere] * len(arrays),
        out_shape=[jax.ShapeDtypeStruct(array.shape, array.dtype) for array in arrays],
        input_output_aliases={i: i for i in range(len(arrays))},
        compiler_params=params(60),
        cost_estimate=cost(0, 0),
        name="after",
    )(*arrays, *others)


def cost(flops, bytes_accessed, exps=0):
    return pl.CostEstimate(
        flops=int(flops), bytes_accessed=int(bytes_accessed), transcendentals=int(exps)
    )


def partner(place, slot, count):
    assert count & (count - 1) == 0
    return place ^ slot


def iota2(shape, dim):
    return lax.broadcasted_iota(jnp.int32, shape, dim)


def scores(query, key_rows):
    return lax.dot_general(query, key_rows, (((1,), (1,)), ((), ())), preferred_element_type=F32)


def dot(left, right):
    return jnp.dot(left, right, preferred_element_type=F32)


def regroup_matrix():
    rows = iota2((TILE, TILE), 0)
    cols = iota2((TILE, TILE), 1)
    return (cols == (rows & 15) * 16 + (rows >> 4)).astype(BF16)


def with_ones(value_rows):
    return jnp.concatenate([value_rows, jnp.ones_like(value_rows)], axis=1)


def weighted(score_blocks, value_blocks, extra=None):
    top = functools.reduce(jnp.maximum, score_blocks)
    top = jnp.max(top, axis=-1, keepdims=True)
    if extra is not None:
        top = jnp.maximum(top, extra[0])
    total = None
    for block, value_block in zip(score_blocks, value_blocks):
        weights = jnp.exp2((block - top) * LOG_SCALE).astype(BF16)
        part = dot(weights, value_block)
        total = part if total is None else total + part
    if extra is not None:
        own = jnp.exp2((extra[0] - top) * LOG_SCALE).astype(BF16).astype(F32)
        total = total + own * extra[1].astype(F32)
    return total[:, :HEAD_SIZE] / total[:, HEAD_SIZE:]


def edge_kernel(k_ref, v_ref, k_ends_ref, v_ends_ref, *refs):
    rim_ref, sum_ref = refs[-2:]
    rim_ref[0] = k_ref[...]
    rim_ref[1] = v_ref[...]

    @pl.when(pl.program_id(0) == 0)
    def _():
        for number, ref in enumerate((k_ends_ref, v_ends_ref)):
            rows = ref[...].astype(F32)[:, 16 - SUMCOLS :]
            sum_ref[number] = rows.reshape(sum_ref.shape[1:]).astype(BF16)


def edges(keys, values, waits):
    tokens_dev, width = keys.shape
    blocks = tokens_dev // BLOCK
    first = (tokens_dev - WINDOW) // TILE
    source = pl.BlockSpec((TILE, width), lambda i: (first + i, 0))
    ends = pl.BlockSpec((blocks, 16, width), lambda i: (0, BLOCK // 16 - 1, 0))
    shape = (2, blocks * SUMCOLS, width)
    return pl.pallas_call(
        edge_kernel,
        grid=(WINDOW // TILE,),
        in_specs=[source] * 2 + [ends] * 2 + moments(waits),
        out_specs=[
            pl.BlockSpec((2, TILE, width), lambda i: (0, i, 0)),
            pl.BlockSpec(shape, lambda i: (0, 0, 0)),
        ],
        out_shape=[
            jax.ShapeDtypeStruct((2, WINDOW, width), BF16),
            jax.ShapeDtypeStruct(shape, BF16),
        ],
        compiler_params=params(60),
        cost_estimate=cost(0, 8 * WINDOW * width),
        name="edges",
    )(
        keys,
        values,
        keys.reshape(blocks, BLOCK, width),
        values.reshape(blocks, BLOCK, width),
        *waits,
    )


def cut_kernel(side_ref, weight_ref, *refs):
    refs[-1][...] = weight_ref[...]


def cut(side, weight, size, first, waits):
    rows = weight.shape[0]
    return pl.pallas_call(
        cut_kernel,
        grid_spec=pltpu.PrefetchScalarGridSpec(
            num_scalar_prefetch=1,
            grid=(4,),
            in_specs=[pl.BlockSpec((rows // 4, size), lambda i, side: (i, first + side[0]))]
            + moments(waits),
            out_specs=pl.BlockSpec((rows // 4, size), lambda i, side: (i, 0)),
        ),
        out_shape=jax.ShapeDtypeStruct((rows, size), BF16),
        compiler_params=params(60),
        cost_estimate=cost(0, 4 * rows * size),
        name="cut",
    )(side, weight, *waits)


def prep_kernel(q_ref, k_ref, v_ref, *refs):
    send_ref = refs[-1]
    matrix = regroup_matrix()
    ctx, _, per, rows, width = send_ref.shape
    for number, ref in enumerate((q_ref, k_ref, v_ref)):
        grouped = dot(matrix, ref[...]).astype(BF16)
        send_ref[:, number] = grouped.reshape(ctx, per, rows, width)


def prepare(queries, keys, values, ctx, chunk, chunks, waits):
    tokens_dev, width = queries.shape
    per = STRIDE // ctx
    part = width // chunks
    return pl.pallas_call(
        prep_kernel,
        grid=(tokens_dev // TILE,),
        in_specs=[pl.BlockSpec((TILE, part), lambda b: (b, chunk))] * 3 + moments(waits),
        out_specs=pl.BlockSpec((ctx, 3, per, TILE // STRIDE, part), lambda b: (0, 0, 0, b, 0)),
        out_shape=jax.ShapeDtypeStruct((ctx, 3, per, tokens_dev // STRIDE, part), BF16),
        compiler_params=params(60),
        cost_estimate=cost(6 * tokens_dev * TILE * part, 12 * tokens_dev * part),
        name="prepare",
    )(queries, keys, values, *waits)


def home_kernel(place_ref, q_ref, k_ref, v_ref, rim_ref, *refs, order):
    sum_refs, (o_ref, mark_ref) = refs[: len(order)], refs[-2:]
    mark_ref[...] = jnp.zeros_like(mark_ref)
    place = place_ref[0]
    tokens_dev = q_ref.shape[0]
    back = WINDOW // TILE
    key_blocks = [rim_ref[0, e * TILE : (e + 1) * TILE] for e in range(back)]
    value_blocks = [with_ones(rim_ref[1, e * TILE : (e + 1) * TILE]) for e in range(back)]
    for e in range(tokens_dev // TILE):
        key_blocks.append(k_ref[e * TILE : (e + 1) * TILE])
        value_blocks.append(with_ones(v_ref[e * TILE : (e + 1) * TILE]))
    picks = sum_refs[0].shape[1]
    sum_keys = jnp.concatenate([ref[0] for ref in sum_refs])
    sum_values = with_ones(jnp.concatenate([ref[1] for ref in sum_refs]))
    sum_col = jnp.concatenate(
        [iota2((TILE, picks), 1) + (place ^ i) * picks for i in order], axis=1
    )
    row = iota2((TILE, TILE), 0)
    col = iota2((TILE, TILE), 1)
    for b in range(tokens_dev // TILE):
        query = q_ref[b * TILE : (b + 1) * TILE]
        blocks = []
        for e in range(back + 1):
            block = scores(query, key_blocks[b + e])
            allowed = None
            if e == 0:
                allowed = col > row
            if e == back:
                allowed = col <= row
            if b + e < back:
                held = place > 0
                allowed = held if allowed is None else allowed & held
            if allowed is not None:
                block = jnp.where(allowed, block, BIG_NEG)
            blocks.append(block)
        local = weighted(blocks, value_blocks[b : b + back + 1])
        pos = place * tokens_dev + b * TILE + iota2((TILE, 1), 0)
        within = pos % BLOCK
        held = pos // BLOCK * SUMCOLS + jnp.maximum(within - (BLOCK - SUMCOLS - 1), 0)
        block = jnp.where(sum_col < held, scores(query, sum_keys), BIG_NEG)
        own_key = key_blocks[b + back].astype(F32)
        own = jnp.sum(query.astype(F32) * own_key, axis=-1, keepdims=True)
        own = jnp.where(within < BLOCK - SUMCOLS, own, BIG_NEG)
        summary = weighted([block], [sum_values], (own, value_blocks[b + back]))
        o_ref[b * TILE : (b + 1) * TILE] = local + summary


def home_sections(place, queries, keys, values, rim, summary, order, chunk, chunks, waits):
    tokens_dev, width = queries.shape
    heads = width // chunks // HEAD_SIZE
    first = chunk * heads
    picks = summary[0].shape[1]
    total = len(summary) * picks
    own = pl.BlockSpec((tokens_dev, HEAD_SIZE), lambda h: (0, first + h))
    pairs = tokens_dev * (WINDOW + TILE + total) * heads
    return pl.pallas_call(
        functools.partial(home_kernel, order=order),
        grid=(heads,),
        in_specs=[
            pl.BlockSpec(memory_space=pltpu.SMEM),
            own,
            own,
            own,
            pl.BlockSpec((2, WINDOW, HEAD_SIZE), lambda h: (0, 0, first + h)),
        ]
        + [pl.BlockSpec((2, picks, HEAD_SIZE), lambda h: (0, 0, first + h))] * len(summary)
        + moments(waits),
        out_specs=[pl.BlockSpec((tokens_dev, HEAD_SIZE), lambda h: (0, h)), mark_spec()],
        out_shape=[jax.ShapeDtypeStruct((tokens_dev, heads * HEAD_SIZE), F32), MARK],
        compiler_params=params(60),
        cost_estimate=cost(64 * pairs * HEAD_SIZE, 14 * tokens_dev * width, 8 * pairs),
        name="home",
    )(place, queries, keys, values, rim, *summary, *waits)


def stride_kernel(place_ref, x_ref, *refs, slabs):
    ctx, _, _, rows, width = x_ref.shape
    o_refs, mark_ref, held_ref = refs[-2 - (ctx if slabs else 1) : -2], refs[-2], refs[-1]
    mark_ref[...] = jnp.zeros_like(mark_ref)
    count = ctx * rows
    row = iota2((TILE, TILE), 0)
    col = iota2((TILE, TILE), 1)
    sources = TILE // rows
    units = []
    for head in range(width // HEAD_SIZE):
        lanes = slice(head * HEAD_SIZE, (head + 1) * HEAD_SIZE)
        query = x_ref[:, 0, 0, :, lanes].reshape(count, HEAD_SIZE)
        key_rows = x_ref[:, 1, 0, :, lanes].reshape(count, HEAD_SIZE)
        value_rows = with_ones(x_ref[:, 2, 0, :, lanes].reshape(count, HEAD_SIZE))
        for b in range(count // TILE):
            part = query[b * TILE : (b + 1) * TILE]
            blocks = [scores(part, key_rows[e * TILE : (e + 1) * TILE]) for e in range(b + 1)]
            blocks[b] = jnp.where(col <= row, blocks[b], BIG_NEG)
            units.append((lanes, b, blocks, value_rows))
    for lanes, b, blocks, value_rows in units:
        result = weighted(
            blocks, [value_rows[e * TILE : (e + 1) * TILE] for e in range(b + 1)]
        ).astype(BF16)
        held_ref[b * sources : (b + 1) * sources, :, lanes] = result.reshape(
            sources, rows, HEAD_SIZE
        )
    if not slabs:
        o_refs[0][:, 0] = held_ref[...]
        return
    for slot in range(ctx):
        o_refs[slot][0] = held_ref[partner(place_ref[0], slot, ctx)]


def stride_attend(place, moved, slabs, waits):
    ctx, _, per, rows, width = moved.shape
    count = ctx * rows
    pairs = per * (width // HEAD_SIZE) * count * (count + TILE) // 2
    if slabs:
        out_specs = [pl.BlockSpec((1, rows, width), lambda r: (r, 0, 0))] * ctx
        out_shape = [jax.ShapeDtypeStruct((per, rows, width), BF16)] * ctx
    else:
        out_specs = [pl.BlockSpec((ctx, 1, rows, width), lambda r: (0, r, 0, 0))]
        out_shape = [jax.ShapeDtypeStruct((ctx, per, rows, width), BF16)]
    return pl.pallas_call(
        functools.partial(stride_kernel, slabs=slabs),
        grid=(per,),
        in_specs=[
            pl.BlockSpec(memory_space=pltpu.SMEM),
            pl.BlockSpec((ctx, 3, 1, rows, width), lambda r: (0, 0, r, 0, 0)),
        ]
        + moments(waits),
        out_specs=out_specs + [mark_spec()],
        out_shape=out_shape + [MARK],
        scratch_shapes=[pltpu.VMEM((ctx, rows, width), BF16)],
        compiler_params=params(24),
        cost_estimate=cost(8 * pairs * HEAD_SIZE, 8 * per * count * width, pairs),
        name="stride",
    )(place, moved, *waits)


def combine_kernel(seat_ref, home_ref, *refs, slots, arrays, ctx):
    back_refs, o_refs, mark_ref = refs[:arrays], refs[-slots - 1 : -1], refs[-1]
    mark_ref[...] = jnp.zeros_like(mark_ref)
    tokens_dev, width = home_ref.shape
    size = tokens_dev // slots
    per = STRIDE // ctx
    token = iota2((TILE, TILE), 0)
    col = iota2((TILE, TILE), 1)
    group = col >> 4
    owner = group // per if arrays == 1 else partner(seat_ref[1], group // per, ctx)
    matrix = (token == (col & 15) * 16 + owner * per + group % per).astype(BF16)
    for slot in range(slots):
        owner = partner(seat_ref[0], slot, slots)
        for b in range(size // TILE):
            first = owner * (size // TILE) + b
            here = pl.ds(pl.multiple_of(first * STRIDE, STRIDE), STRIDE)
            if arrays == 1:
                rows = back_refs[0][:, :, here].reshape(TILE, width)
            else:
                rows = jnp.concatenate([ref[r, here] for ref in back_refs for r in range(per)])
            back = dot(matrix, rows)
            home = home_ref[pl.ds(pl.multiple_of(first * TILE, TILE), TILE)]
            o_refs[slot][b * TILE : (b + 1) * TILE] = (home + back).astype(BF16)


def combine(seat, home, backs, slots, ctx, waits):
    tokens_dev, width = home.shape
    size = tokens_dev // slots
    return pl.pallas_call(
        functools.partial(combine_kernel, slots=slots, arrays=len(backs), ctx=ctx),
        in_specs=[pl.BlockSpec(memory_space=pltpu.SMEM)]
        + [pl.BlockSpec(memory_space=pltpu.VMEM)] * (1 + len(backs))
        + moments(waits),
        out_specs=[pl.BlockSpec(memory_space=pltpu.VMEM)] * (slots + 1),
        out_shape=[jax.ShapeDtypeStruct((size, width), BF16)] * slots + [MARK],
        compiler_params=params(24),
        cost_estimate=cost(56 * tokens_dev * TILE * width, 8 * tokens_dev * width),
        name="combine",
    )(seat, home, *backs, *waits)


def project_kernel(side_ref, *refs, slots, chunk, adds):
    moved_refs, weight_refs, refs = refs[:slots], refs[slots : slots + 2], refs[slots + 2 :]
    o_ref = refs[-1]
    part = moved_refs[0].shape[1]
    half = weight_refs[0].shape[2]
    tile = min(half, 512)
    for phase, weight_ref in enumerate(weight_refs):
        for j in range(half // tile):
            first = pl.multiple_of((side_ref[0] ^ phase) * half + j * tile, tile)
            here = pl.ds(first, tile)
            total = refs[0][:, here] if adds else None
            for slot in range(slots):
                rows = weight_ref[
                    partner(side_ref[1], slot, slots),
                    chunk * part : (chunk + 1) * part,
                    j * tile : (j + 1) * tile,
                ]
                product = dot(moved_refs[slot][...], rows)
                total = product if total is None else total + product
            o_ref[:, here] = total.astype(o_ref.dtype)


def project(side, moved, mine, other, chunk, before, dtype):
    slots = len(moved)
    tokens, part = moved[0].shape
    half = mine.shape[2]
    whole = pl.BlockSpec(memory_space=pltpu.VMEM)
    return pl.pallas_call(
        functools.partial(project_kernel, slots=slots, chunk=chunk, adds=len(before) > 0),
        in_specs=[pl.BlockSpec(memory_space=pltpu.SMEM)] + [whole] * (slots + 2 + len(before)),
        out_specs=whole,
        out_shape=jax.ShapeDtypeStruct((tokens, 2 * half), dtype),
        compiler_params=params(24),
        cost_estimate=cost(
            4 * slots * tokens * part * half, 2 * slots * part * (2 * half + tokens)
        ),
        name="project",
    )(side, *moved, mine, other, *before)


def gather_ctx(rows):
    count = lax.axis_size("ctx")

    def swapped(piece, distance):
        return lax.ppermute(piece, "ctx", [(i, i ^ distance) for i in range(count)])

    order = list(range(0, count, 2))
    pieces = [rows] + [swapped(rows, distance) for distance in order[1:]]
    within = [swapped(piece, 1) for piece in pieces]
    return pieces, within, order + [i ^ 1 for i in order]


def stride_general(queries, keys, values):
    tokens_dev, width = queries.shape
    heads = width // HEAD_SIZE
    ctx = lax.axis_size("ctx")
    copies = max(ctx // STRIDE, 1)
    rows = tokens_dev // STRIDE
    held_rows = ctx * rows // copies
    own_copy = lax.axis_index("ctx") // STRIDE
    query_pos = (jnp.arange(held_rows) // (rows // copies)) * rows
    query_pos = query_pos + (jnp.arange(held_rows) % (rows // copies)) * copies + own_copy
    shaped = queries.reshape(1, rows // copies, ctx, width)
    query = lax.all_to_all(shaped, "ctx", split_axis=2, concat_axis=1, tiled=True)
    query = query.reshape(held_rows, heads, HEAD_SIZE)
    both = jnp.stack([keys, values]).reshape(2, rows, 1, STRIDE, width)
    both = jnp.broadcast_to(both, (2, rows, copies, STRIDE, width)).reshape(2, rows, ctx, width)
    both = lax.all_to_all(both, "ctx", split_axis=2, concat_axis=1, tiled=True)
    both = both.reshape(2, ctx * rows, heads, HEAD_SIZE)
    allowed = jnp.arange(ctx * rows)[None, :] <= query_pos[:, None]

    def one_head(operands):
        head_query, head_keys, head_values = operands
        masked = jnp.where(allowed, scores(head_query, head_keys), BIG_NEG)
        return weighted([masked], [with_ones(head_values)])

    result = lax.map(
        one_head,
        (query.transpose(1, 0, 2), both[0].transpose(1, 0, 2), both[1].transpose(1, 0, 2)),
    )
    result = result.transpose(1, 0, 2).reshape(ctx, rows // copies, 1, width).astype(BF16)
    back = lax.all_to_all(result, "ctx", split_axis=0, concat_axis=2, tiled=True)
    return back.reshape(tokens_dev, width)


def body(queries, keys, values, out_weight, chunks):
    tokens_dev, width = queries.shape
    ctx = lax.axis_size("ctx")
    groups = lax.axis_size("head")
    place = lax.axis_index("ctx")
    place_word = place.astype(jnp.int32).reshape(1)
    side = place % 2
    sibling = [(i, i ^ 1) for i in range(ctx)]

    part = width // chunks
    seat = lax.axis_index("head").astype(jnp.int32)
    sides = jnp.stack([side.astype(jnp.int32), seat])

    def exchange(slabs, axis):
        count = len(slabs)
        moved = [slabs[0]]
        for slot in range(1, count):
            pairs = [(i, partner(i, slot, count)) for i in range(count)]
            moved.append(lax.ppermute(slabs[slot], axis, pairs))
        return moved

    weight_half = cut(sides, out_weight, out_weight.shape[1] // 2, 0, ())
    mine = lax.all_gather(weight_half, "head", axis=0)
    rim, picked = edges(keys, values, (weight_half,))
    between, within, order = gather_ctx(picked)
    summary = between + within
    if ctx > STRIDE:
        stride_out = stride_general(queries, keys, values)
        sends = []
    else:
        sends = [prepare(queries, keys, values, ctx, 0, chunks, (weight_half,))]
    (rim,) = after([rim], (*between[1:], *sends))
    if sends:
        sends = list(after(sends, (rim,)))
    before = lax.ppermute(rim, "ctx", [(i, i + 1) for i in range(ctx - 1)])
    for chunk in range(len(sends), chunks * len(sends)):
        sends.append(prepare(queries, keys, values, ctx, chunk, chunks, within[-1:]))

    def home(chunk, waits):
        return home_sections(
            place_word, queries, keys, values, before, summary, order, chunk, chunks, waits
        )


    moved, waits = [], ()
    if ctx > STRIDE:
        for chunk in range(chunks):
            lanes = slice(chunk * part, (chunk + 1) * part)
            homes, mark = home(chunk, waits)
            attended = (homes + stride_out[:, lanes].astype(F32)).astype(BF16)
            attended = attended.reshape(groups, tokens_dev // groups, part)
            owners = [partner(seat, slot, groups) for slot in range(groups)]
            moved.append(exchange([attended[owner] for owner in owners], "head"))
            waits = (mark,)
    else:
        seats = jnp.stack([seat, place.astype(jnp.int32)])
        seats = jnp.stack([seat, place.astype(jnp.int32)])
        sections, mark = home(0, ())
        homes, backs, waits = [sections], [], ()
        if chunks > 1:
            sends[1:] = list(after(sends[1:], (mark,)))
        for chunk, send in enumerate(sends):
            received = lax.all_to_all(send, "ctx", split_axis=0, concat_axis=0, tiled=True)
            beside = chunk < chunks - 1
            *slabs, mark = stride_attend(place_word, received, beside, waits)
            if beside:
                backs.append(exchange(slabs, "ctx"))
            else:
                back = lax.all_to_all(slabs[0], "ctx", split_axis=0, concat_axis=0, tiled=True)
                backs.append([back])
            waits = (mark,)
            for later in range(1, chunks) if chunk == 0 else ():
                sections, mark = home(later, waits)
                homes.append(sections)
                waits = (mark,)
        for chunk in range(chunks):
            *slabs, mark = combine(seats, homes[chunk], backs[chunk], groups, ctx, waits)
            moved.append(exchange(slabs, "head"))
            waits = (mark, *moved[-1][1:3])
    (held,) = after([mine], (mark,))
    other = lax.ppermute(held, "ctx", sibling)
    total = ()
    for chunk in range(chunks):
        dtype = BF16 if chunk == chunks - 1 else F32
        total = (project(sides, moved[chunk], held, other, chunk, total, dtype),)
    return total[0]


def solution(mesh):
    chunks = 2 if HEADS // mesh.shape["head"] > 1 else 1
    placed = (P("ctx", "head"), P("ctx", "head"), P("ctx", "head"), P("head", None))
    return jax.shard_map(
        functools.partial(body, chunks=chunks),
        mesh=mesh,
        in_specs=placed,
        out_specs=P(("ctx", "head"), None),
        check_vma=False,
    )
```

```python
import functools
import math

import jax
import jax.numpy as jnp
from jax import lax
from jax.experimental import pallas as pl
from jax.experimental.pallas import tpu as pltpu
from jax.sharding import PartitionSpec as P

HEADS = 16
HEAD_SIZE = 128
WINDOW = 512
STRIDE = 16
BLOCK = 128
SUMCOLS = 8

BIG_NEG = -1e30
TILE = 256
LOG_SCALE = HEAD_SIZE ** (-0.5) * math.log2(math.e)
F32 = jnp.float32
BF16 = jnp.bfloat16


def params(mib):
    return pltpu.CompilerParams(vmem_limit_bytes=mib * 1024 * 1024)


MARK = jax.ShapeDtypeStruct((8, 128), F32)


def mark_spec():
    return pl.BlockSpec(MARK.shape, lambda *place: (0, 0))


def moments(arrays):
    return [pl.BlockSpec(memory_space=pl.ANY)] * len(arrays)


def after(arrays, others):
    anywhere = pl.BlockSpec(memory_space=pl.ANY)
    return pl.pallas_call(
        lambda *refs: None,
        in_specs=[anywhere] * (len(arrays) + len(others)),
        out_specs=[anywhere] * len(arrays),
        out_shape=[jax.ShapeDtypeStruct(array.shape, array.dtype) for array in arrays],
        input_output_aliases={i: i for i in range(len(arrays))},
        compiler_params=params(60),
        cost_estimate=cost(0, 0),
        name="after",
    )(*arrays, *others)


def cost(flops, bytes_accessed, exps=0):
    return pl.CostEstimate(
        flops=int(flops), bytes_accessed=int(bytes_accessed), transcendentals=int(exps)
    )


def partner(place, slot, count):
    assert count & (count - 1) == 0
    return place ^ slot


def iota2(shape, dim):
    return lax.broadcasted_iota(jnp.int32, shape, dim)


def scores(query, key_rows):
    return lax.dot_general(query, key_rows, (((1,), (1,)), ((), ())), preferred_element_type=F32)


def dot(left, right):
    return jnp.dot(left, right, preferred_element_type=F32)


def regroup_matrix():
    rows = iota2((TILE, TILE), 0)
    cols = iota2((TILE, TILE), 1)
    return (cols == (rows & 15) * 16 + (rows >> 4)).astype(BF16)


def with_ones(value_rows):
    return jnp.concatenate([value_rows, jnp.ones_like(value_rows)], axis=1)


def weighted(score_blocks, value_blocks, extra=None):
    top = functools.reduce(jnp.maximum, score_blocks)
    top = jnp.max(top, axis=-1, keepdims=True)
    if extra is not None:
        top = jnp.maximum(top, extra[0])
    total = None
    for block, value_block in zip(score_blocks, value_blocks):
        weights = jnp.exp2((block - top) * LOG_SCALE).astype(BF16)
        part = dot(weights, value_block)
        total = part if total is None else total + part
    if extra is not None:
        own = jnp.exp2((extra[0] - top) * LOG_SCALE).astype(BF16).astype(F32)
        total = total + own * extra[1].astype(F32)
    return total[:, :HEAD_SIZE] / total[:, HEAD_SIZE:]


def start_copies(source, target, sems, first, rows):
    count = sems.shape[0]
    each = rows // count
    copies = []
    for i in range(count):
        copies.append(
            pltpu.make_async_copy(
                source(pl.ds(first + i * each, each)), target(pl.ds(i * each, each)), sems.at[i]
            )
        )
        copies[-1].start()
    return copies


def edge_kernel(k_ref, v_ref, k_ends_ref, v_ends_ref, *refs):
    rim_ref, sum_ref, k_sems, v_sems = refs[-4:]
    first = k_ref.shape[0] - WINDOW
    copies = start_copies(
        lambda rows: k_ref.at[rows], lambda rows: rim_ref.at[0, rows], k_sems, first, WINDOW
    )
    copies += start_copies(
        lambda rows: v_ref.at[rows], lambda rows: rim_ref.at[1, rows], v_sems, first, WINDOW
    )
    for number, ref in enumerate((k_ends_ref, v_ends_ref)):
        rows = ref[...].astype(F32)[:, 16 - SUMCOLS :]
        sum_ref[number] = rows.reshape(sum_ref.shape[1:]).astype(BF16)
    for copy in copies:
        copy.wait()


def edges(keys, values, waits):
    tokens_dev, width = keys.shape
    blocks = tokens_dev // BLOCK
    anywhere = pl.BlockSpec(memory_space=pl.ANY)
    ends = pl.BlockSpec((blocks, 16, width), lambda i: (0, BLOCK // 16 - 1, 0))
    shape = (2, blocks * SUMCOLS, width)
    return pl.pallas_call(
        edge_kernel,
        grid=(1,),
        in_specs=[anywhere] * 2 + [ends] * 2 + moments(waits),
        out_specs=[anywhere, pl.BlockSpec(shape, lambda i: (0, 0, 0))],
        out_shape=[
            jax.ShapeDtypeStruct((2, WINDOW, width), BF16),
            jax.ShapeDtypeStruct(shape, BF16),
        ],
        scratch_shapes=[pltpu.SemaphoreType.DMA((2,))] * 2,
        compiler_params=params(60),
        cost_estimate=cost(0, 8 * WINDOW * width),
        name="edges",
    )(
        keys,
        values,
        keys.reshape(blocks, BLOCK, width),
        values.reshape(blocks, BLOCK, width),
        *waits,
    )


def cut_kernel(side_ref, weight_ref, o_ref, sems):
    rows, half = o_ref.shape
    columns = pl.ds(pl.multiple_of(side_ref[0] * half, half), half)
    copies = start_copies(
        lambda rows: weight_ref.at[rows, columns], lambda rows: o_ref.at[rows], sems, 0, rows
    )
    for copy in copies:
        copy.wait()


def cut(side, weight):
    rows, width = weight.shape
    anywhere = pl.BlockSpec(memory_space=pl.ANY)
    return pl.pallas_call(
        cut_kernel,
        in_specs=[pl.BlockSpec(memory_space=pltpu.SMEM), anywhere],
        out_specs=anywhere,
        out_shape=jax.ShapeDtypeStruct((rows, width // 2), BF16),
        scratch_shapes=[pltpu.SemaphoreType.DMA((4,))],
        compiler_params=params(60),
        cost_estimate=cost(0, 2 * rows * width),
        name="cut",
    )(side, weight)


def prep_kernel(q_ref, k_ref, v_ref, *refs):
    send_ref = refs[-1]
    matrix = regroup_matrix()
    ctx, _, per, _, width = send_ref.shape
    rows = TILE // STRIDE
    for number, ref in enumerate((q_ref, k_ref, v_ref)):
        for t in range(ref.shape[0] // TILE):
            grouped = dot(matrix, ref[t * TILE : (t + 1) * TILE]).astype(BF16)
            send_ref[:, number, :, t * rows : (t + 1) * rows] = grouped.reshape(
                ctx, per, rows, width
            )


def prepare(queries, keys, values, ctx, chunk, chunks, waits):
    tokens_dev, width = queries.shape
    per = STRIDE // ctx
    part = width // chunks
    size = tokens_dev // 2 if tokens_dev % (2 * TILE) == 0 else TILE
    return pl.pallas_call(
        prep_kernel,
        grid=(tokens_dev // size,),
        in_specs=[pl.BlockSpec((size, part), lambda b: (b, chunk))] * 3 + moments(waits),
        out_specs=pl.BlockSpec((ctx, 3, per, size // STRIDE, part), lambda b: (0, 0, 0, b, 0)),
        out_shape=jax.ShapeDtypeStruct((ctx, 3, per, tokens_dev // STRIDE, part), BF16),
        compiler_params=params(60),
        cost_estimate=cost(6 * tokens_dev * TILE * part, 12 * tokens_dev * part),
        name="prepare",
    )(queries, keys, values, *waits)


def home_kernel(place_ref, q_ref, k_ref, v_ref, rim_ref, *refs, order):
    sum_refs, (o_ref, mark_ref) = refs[: len(order)], refs[-2:]
    mark_ref[...] = jnp.zeros_like(mark_ref)
    place = place_ref[0]
    tokens_dev = q_ref.shape[0]
    back = WINDOW // TILE
    key_blocks = [rim_ref[0, e * TILE : (e + 1) * TILE] for e in range(back)]
    value_blocks = [with_ones(rim_ref[1, e * TILE : (e + 1) * TILE]) for e in range(back)]
    for e in range(tokens_dev // TILE):
        key_blocks.append(k_ref[e * TILE : (e + 1) * TILE])
        value_blocks.append(with_ones(v_ref[e * TILE : (e + 1) * TILE]))
    picks = sum_refs[0].shape[1]
    sum_keys = jnp.concatenate([ref[0] for ref in sum_refs])
    sum_values = with_ones(jnp.concatenate([ref[1] for ref in sum_refs]))
    sum_col = jnp.concatenate(
        [iota2((TILE, picks), 1) + (place ^ i) * picks for i in order], axis=1
    )
    row = iota2((TILE, TILE), 0)
    col = iota2((TILE, TILE), 1)
    for b in range(tokens_dev // TILE):
        query = q_ref[b * TILE : (b + 1) * TILE]
        blocks = []
        for e in range(back + 1):
            block = scores(query, key_blocks[b + e])
            allowed = None
            if e == 0:
                allowed = col > row
            if e == back:
                allowed = col <= row
            if b + e < back:
                held = place > 0
                allowed = held if allowed is None else allowed & held
            if allowed is not None:
                block = jnp.where(allowed, block, BIG_NEG)
            blocks.append(block)
        local = weighted(blocks, value_blocks[b : b + back + 1])
        pos = place * tokens_dev + b * TILE + iota2((TILE, 1), 0)
        within = pos % BLOCK
        held = pos // BLOCK * SUMCOLS + jnp.maximum(within - (BLOCK - SUMCOLS - 1), 0)
        block = jnp.where(sum_col < held, scores(query, sum_keys), BIG_NEG)
        own_key = key_blocks[b + back].astype(F32)
        own = jnp.sum(query.astype(F32) * own_key, axis=-1, keepdims=True)
        own = jnp.where(within < BLOCK - SUMCOLS, own, BIG_NEG)
        summary = weighted([block], [sum_values], (own, value_blocks[b + back]))
        o_ref[b * TILE : (b + 1) * TILE] = local + summary


def home_sections(place, queries, keys, values, rim, summary, order, chunk, chunks, waits):
    tokens_dev, width = queries.shape
    heads = width // chunks // HEAD_SIZE
    first = chunk * heads
    picks = summary[0].shape[1]
    total = len(summary) * picks
    own = pl.BlockSpec((tokens_dev, HEAD_SIZE), lambda h: (0, first + h))
    pairs = tokens_dev * (WINDOW + TILE + total) * heads
    return pl.pallas_call(
        functools.partial(home_kernel, order=order),
        grid=(heads,),
        in_specs=[
            pl.BlockSpec(memory_space=pltpu.SMEM),
            own,
            own,
            own,
            pl.BlockSpec((2, WINDOW, HEAD_SIZE), lambda h: (0, 0, first + h)),
        ]
        + [pl.BlockSpec((2, picks, HEAD_SIZE), lambda h: (0, 0, first + h))] * len(summary)
        + moments(waits),
        out_specs=[pl.BlockSpec((tokens_dev, HEAD_SIZE), lambda h: (0, h)), mark_spec()],
        out_shape=[jax.ShapeDtypeStruct((tokens_dev, heads * HEAD_SIZE), F32), MARK],
        compiler_params=params(60),
        cost_estimate=cost(64 * pairs * HEAD_SIZE, 14 * tokens_dev * width, 8 * pairs),
        name="home",
    )(place, queries, keys, values, rim, *summary, *waits)


def stride_kernel(place_ref, x_ref, *refs, slabs):
    ctx, _, _, rows, width = x_ref.shape
    o_refs, mark_ref, held_ref = refs[-2 - (ctx if slabs else 1) : -2], refs[-2], refs[-1]
    mark_ref[...] = jnp.zeros_like(mark_ref)
    count = ctx * rows
    row = iota2((TILE, TILE), 0)
    col = iota2((TILE, TILE), 1)
    sources = TILE // rows
    units = []
    for head in range(width // HEAD_SIZE):
        lanes = slice(head * HEAD_SIZE, (head + 1) * HEAD_SIZE)
        query = x_ref[:, 0, 0, :, lanes].reshape(count, HEAD_SIZE)
        key_rows = x_ref[:, 1, 0, :, lanes].reshape(count, HEAD_SIZE)
        value_rows = with_ones(x_ref[:, 2, 0, :, lanes].reshape(count, HEAD_SIZE))
        for b in range(count // TILE):
            part = query[b * TILE : (b + 1) * TILE]
            blocks = [scores(part, key_rows[e * TILE : (e + 1) * TILE]) for e in range(b + 1)]
            blocks[b] = jnp.where(col <= row, blocks[b], BIG_NEG)
            units.append((lanes, b, blocks, value_rows))
    for lanes, b, blocks, value_rows in units:
        result = weighted(
            blocks, [value_rows[e * TILE : (e + 1) * TILE] for e in range(b + 1)]
        ).astype(BF16)
        held_ref[b * sources : (b + 1) * sources, :, lanes] = result.reshape(
            sources, rows, HEAD_SIZE
        )
    if not slabs:
        o_refs[0][:, 0] = held_ref[...]
        return
    for slot in range(ctx):
        o_refs[slot][0] = held_ref[partner(place_ref[0], slot, ctx)]


def stride_attend(place, moved, slabs, waits):
    ctx, _, per, rows, width = moved.shape
    count = ctx * rows
    pairs = per * (width // HEAD_SIZE) * count * (count + TILE) // 2
    if slabs:
        out_specs = [pl.BlockSpec((1, rows, width), lambda r: (r, 0, 0))] * ctx
        out_shape = [jax.ShapeDtypeStruct((per, rows, width), BF16)] * ctx
    else:
        out_specs = [pl.BlockSpec((ctx, 1, rows, width), lambda r: (0, r, 0, 0))]
        out_shape = [jax.ShapeDtypeStruct((ctx, per, rows, width), BF16)]
    return pl.pallas_call(
        functools.partial(stride_kernel, slabs=slabs),
        grid=(per,),
        in_specs=[
            pl.BlockSpec(memory_space=pltpu.SMEM),
            pl.BlockSpec((ctx, 3, 1, rows, width), lambda r: (0, 0, r, 0, 0)),
        ]
        + moments(waits),
        out_specs=out_specs + [mark_spec()],
        out_shape=out_shape + [MARK],
        scratch_shapes=[pltpu.VMEM((ctx, rows, width), BF16)],
        compiler_params=params(24),
        cost_estimate=cost(8 * pairs * HEAD_SIZE, 8 * per * count * width, pairs),
        name="stride",
    )(place, moved, *waits)


def combine_kernel(seat_ref, home_ref, *refs, slots, arrays, ctx):
    back_refs, o_refs, mark_ref = refs[:arrays], refs[-slots - 1 : -1], refs[-1]
    mark_ref[...] = jnp.zeros_like(mark_ref)
    tokens_dev, width = home_ref.shape
    size = tokens_dev // slots
    per = STRIDE // ctx
    token = iota2((TILE, TILE), 0)
    col = iota2((TILE, TILE), 1)
    group = col >> 4
    owner = group // per if arrays == 1 else partner(seat_ref[1], group // per, ctx)
    matrix = (token == (col & 15) * 16 + owner * per + group % per).astype(BF16)
    for slot in range(slots):
        owner = partner(seat_ref[0], slot, slots)
        for b in range(size // TILE):
            first = owner * (size // TILE) + b
            here = pl.ds(pl.multiple_of(first * STRIDE, STRIDE), STRIDE)
            if arrays == 1:
                rows = back_refs[0][:, :, here].reshape(TILE, width)
            else:
                rows = jnp.concatenate([ref[r, here] for ref in back_refs for r in range(per)])
            back = dot(matrix, rows)
            home = home_ref[pl.ds(pl.multiple_of(first * TILE, TILE), TILE)]
            o_refs[slot][b * TILE : (b + 1) * TILE] = (home + back).astype(BF16)


def combine(seat, home, backs, slots, ctx, waits):
    tokens_dev, width = home.shape
    size = tokens_dev // slots
    return pl.pallas_call(
        functools.partial(combine_kernel, slots=slots, arrays=len(backs), ctx=ctx),
        in_specs=[pl.BlockSpec(memory_space=pltpu.SMEM)]
        + [pl.BlockSpec(memory_space=pltpu.VMEM)] * (1 + len(backs))
        + moments(waits),
        out_specs=[pl.BlockSpec(memory_space=pltpu.VMEM)] * (slots + 1),
        out_shape=[jax.ShapeDtypeStruct((size, width), BF16)] * slots + [MARK],
        compiler_params=params(24),
        cost_estimate=cost(56 * tokens_dev * TILE * width, 8 * tokens_dev * width),
        name="combine",
    )(seat, home, *backs, *waits)


def project_kernel(side_ref, *refs, slots, chunk, adds):
    moved_refs, weight_refs, refs = refs[:slots], refs[slots : slots + 2], refs[slots + 2 :]
    o_ref = refs[-1]
    part = moved_refs[0].shape[1]
    half = weight_refs[0].shape[2]
    tile = min(half, 512)
    for phase, weight_ref in enumerate(weight_refs):
        for j in range(half // tile):
            first = pl.multiple_of((side_ref[0] ^ phase) * half + j * tile, tile)
            here = pl.ds(first, tile)
            total = refs[0][:, here] if adds else None
            for slot in range(slots):
                rows = weight_ref[
                    partner(side_ref[1], slot, slots),
                    chunk * part : (chunk + 1) * part,
                    j * tile : (j + 1) * tile,
                ]
                product = dot(moved_refs[slot][...], rows)
                total = product if total is None else total + product
            o_ref[:, here] = total.astype(o_ref.dtype)


def project(side, moved, mine, other, chunk, before, dtype):
    slots = len(moved)
    tokens, part = moved[0].shape
    half = mine.shape[2]
    whole = pl.BlockSpec(memory_space=pltpu.VMEM)
    return pl.pallas_call(
        functools.partial(project_kernel, slots=slots, chunk=chunk, adds=len(before) > 0),
        in_specs=[pl.BlockSpec(memory_space=pltpu.SMEM)] + [whole] * (slots + 2 + len(before)),
        out_specs=whole,
        out_shape=jax.ShapeDtypeStruct((tokens, 2 * half), dtype),
        compiler_params=params(24),
        cost_estimate=cost(
            4 * slots * tokens * part * half, 2 * slots * part * (2 * half + tokens)
        ),
        name="project",
    )(side, *moved, mine, other, *before)


def gather_ctx(rows):
    count = lax.axis_size("ctx")

    def swapped(piece, distance):
        return lax.ppermute(piece, "ctx", [(i, i ^ distance) for i in range(count)])

    order = list(range(0, count, 2))
    pieces = [rows] + [swapped(rows, distance) for distance in order[1:]]
    within = [swapped(piece, 1) for piece in pieces]
    return pieces, within, order + [i ^ 1 for i in order]


def stride_general(queries, keys, values):
    tokens_dev, width = queries.shape
    heads = width // HEAD_SIZE
    ctx = lax.axis_size("ctx")
    copies = max(ctx // STRIDE, 1)
    rows = tokens_dev // STRIDE
    held_rows = ctx * rows // copies
    own_copy = lax.axis_index("ctx") // STRIDE
    query_pos = (jnp.arange(held_rows) // (rows // copies)) * rows
    query_pos = query_pos + (jnp.arange(held_rows) % (rows // copies)) * copies + own_copy
    shaped = queries.reshape(1, rows // copies, ctx, width)
    query = lax.all_to_all(shaped, "ctx", split_axis=2, concat_axis=1, tiled=True)
    query = query.reshape(held_rows, heads, HEAD_SIZE)
    both = jnp.stack([keys, values]).reshape(2, rows, 1, STRIDE, width)
    both = jnp.broadcast_to(both, (2, rows, copies, STRIDE, width)).reshape(2, rows, ctx, width)
    both = lax.all_to_all(both, "ctx", split_axis=2, concat_axis=1, tiled=True)
    both = both.reshape(2, ctx * rows, heads, HEAD_SIZE)
    allowed = jnp.arange(ctx * rows)[None, :] <= query_pos[:, None]

    def one_head(operands):
        head_query, head_keys, head_values = operands
        masked = jnp.where(allowed, scores(head_query, head_keys), BIG_NEG)
        return weighted([masked], [with_ones(head_values)])

    result = lax.map(
        one_head,
        (query.transpose(1, 0, 2), both[0].transpose(1, 0, 2), both[1].transpose(1, 0, 2)),
    )
    result = result.transpose(1, 0, 2).reshape(ctx, rows // copies, 1, width).astype(BF16)
    back = lax.all_to_all(result, "ctx", split_axis=0, concat_axis=2, tiled=True)
    return back.reshape(tokens_dev, width)


def body(queries, keys, values, out_weight, chunks):
    tokens_dev, width = queries.shape
    ctx = lax.axis_size("ctx")
    groups = lax.axis_size("head")
    place = lax.axis_index("ctx")
    place_word = place.astype(jnp.int32).reshape(1)
    side = place % 2
    sibling = [(i, i ^ 1) for i in range(ctx)]

    part = width // chunks
    seat = lax.axis_index("head").astype(jnp.int32)
    sides = jnp.stack([side.astype(jnp.int32), seat])

    def exchange(slabs, axis):
        count = len(slabs)
        moved = [slabs[0]]
        for slot in range(1, count):
            pairs = [(i, partner(i, slot, count)) for i in range(count)]
            moved.append(lax.ppermute(slabs[slot], axis, pairs))
        return moved

    weight_half = cut(sides, out_weight)
    mine = lax.all_gather(weight_half, "head", axis=0)
    rim, picked = edges(keys, values, (weight_half,))
    between, within, order = gather_ctx(picked)
    summary = between + within
    if ctx > STRIDE:
        stride_out = stride_general(queries, keys, values)
        sends = []
    else:
        sends = [prepare(queries, keys, values, ctx, 0, chunks, (weight_half,))]
    (rim,) = after([rim], (*between[1:], *sends))
    if sends:
        sends = list(after(sends, (rim,)))
    before = lax.ppermute(rim, "ctx", [(i, i + 1) for i in range(ctx - 1)])
    for chunk in range(len(sends), chunks * len(sends)):
        sends.append(prepare(queries, keys, values, ctx, chunk, chunks, within[-1:]))

    def home(chunk, waits):
        return home_sections(
            place_word, queries, keys, values, before, summary, order, chunk, chunks, waits
        )


    moved, waits = [], ()
    if ctx > STRIDE:
        for chunk in range(chunks):
            lanes = slice(chunk * part, (chunk + 1) * part)
            homes, mark = home(chunk, waits)
            attended = (homes + stride_out[:, lanes].astype(F32)).astype(BF16)
            attended = attended.reshape(groups, tokens_dev // groups, part)
            owners = [partner(seat, slot, groups) for slot in range(groups)]
            moved.append(exchange([attended[owner] for owner in owners], "head"))
            waits = (mark,)
    else:
        seats = jnp.stack([seat, place.astype(jnp.int32)])
        seats = jnp.stack([seat, place.astype(jnp.int32)])
        sections, mark = home(0, ())
        homes, backs, waits = [sections], [], ()
        if chunks > 1:
            sends[1:] = list(after(sends[1:], (mark,)))
        for chunk, send in enumerate(sends):
            received = lax.all_to_all(send, "ctx", split_axis=0, concat_axis=0, tiled=True)
            beside = chunk < chunks - 1
            *slabs, mark = stride_attend(place_word, received, beside, waits)
            if beside:
                backs.append(exchange(slabs, "ctx"))
            else:
                back = lax.all_to_all(slabs[0], "ctx", split_axis=0, concat_axis=0, tiled=True)
                backs.append([back])
            waits = (mark,)
            for later in range(1, chunks) if chunk == 0 else ():
                sections, mark = home(later, waits)
                homes.append(sections)
                waits = (mark,)
        for chunk in range(chunks):
            *slabs, mark = combine(seats, homes[chunk], backs[chunk], groups, ctx, waits)
            moved.append(exchange(slabs, "head"))
            waits = (mark, *moved[-1][1:3])
    (held,) = after([mine], (mark,))
    other = lax.ppermute(held, "ctx", sibling)
    total = ()
    for chunk in range(chunks):
        dtype = BF16 if chunk == chunks - 1 else F32
        total = (project(sides, moved[chunk], held, other, chunk, total, dtype),)
    return total[0]


def solution(mesh):
    chunks = 2 if HEADS // mesh.shape["head"] > 1 else 1
    placed = (P("ctx", "head"), P("ctx", "head"), P("ctx", "head"), P("head", None))
    return jax.shard_map(
        functools.partial(body, chunks=chunks),
        mesh=mesh,
        in_specs=placed,
        out_specs=P(("ctx", "head"), None),
        check_vma=False,
    )
```

```python
import functools
import math

import jax
import jax.numpy as jnp
from jax import lax
from jax.experimental import pallas as pl
from jax.experimental.pallas import tpu as pltpu
from jax.sharding import PartitionSpec as P

HEADS = 16
HEAD_SIZE = 128
WINDOW = 512
STRIDE = 16
BLOCK = 128
SUMCOLS = 8

BIG_NEG = -1e30
TILE = 256
LOG_SCALE = HEAD_SIZE ** (-0.5) * math.log2(math.e)
F32 = jnp.float32
BF16 = jnp.bfloat16


def params(mib):
    return pltpu.CompilerParams(vmem_limit_bytes=mib * 1024 * 1024)


MARK = jax.ShapeDtypeStruct((8, 128), F32)


def mark_spec():
    return pl.BlockSpec(MARK.shape, lambda *place: (0, 0))


def moments(arrays):
    return [pl.BlockSpec(memory_space=pl.ANY)] * len(arrays)


def after(arrays, others):
    anywhere = pl.BlockSpec(memory_space=pl.ANY)
    return pl.pallas_call(
        lambda *refs: None,
        in_specs=[anywhere] * (len(arrays) + len(others)),
        out_specs=[anywhere] * len(arrays),
        out_shape=[jax.ShapeDtypeStruct(array.shape, array.dtype) for array in arrays],
        input_output_aliases={i: i for i in range(len(arrays))},
        compiler_params=params(60),
        cost_estimate=cost(0, 0),
        name="after",
    )(*arrays, *others)


def cost(flops, bytes_accessed, exps=0):
    return pl.CostEstimate(
        flops=int(flops), bytes_accessed=int(bytes_accessed), transcendentals=int(exps)
    )


def partner(place, slot, count):
    assert count & (count - 1) == 0
    return place ^ slot


def iota2(shape, dim):
    return lax.broadcasted_iota(jnp.int32, shape, dim)


def scores(query, key_rows):
    return lax.dot_general(query, key_rows, (((1,), (1,)), ((), ())), preferred_element_type=F32)


def dot(left, right):
    return jnp.dot(left, right, preferred_element_type=F32)


def regroup_matrix():
    rows = iota2((TILE, TILE), 0)
    cols = iota2((TILE, TILE), 1)
    return (cols == (rows & 15) * 16 + (rows >> 4)).astype(BF16)


def with_ones(value_rows):
    return jnp.concatenate([value_rows, jnp.ones_like(value_rows)], axis=1)


def weighted(score_blocks, value_blocks, extra=None):
    top = functools.reduce(jnp.maximum, score_blocks)
    top = jnp.max(top, axis=-1, keepdims=True)
    if extra is not None:
        top = jnp.maximum(top, extra[0])
    total = None
    for block, value_block in zip(score_blocks, value_blocks):
        weights = jnp.exp2((block - top) * LOG_SCALE).astype(BF16)
        part = dot(weights, value_block)
        total = part if total is None else total + part
    if extra is not None:
        own = jnp.exp2((extra[0] - top) * LOG_SCALE).astype(BF16).astype(F32)
        total = total + own * extra[1].astype(F32)
    return total[:, :HEAD_SIZE] / total[:, HEAD_SIZE:]


def start_copies(sources, held, sems):
    copies = [
        pltpu.make_async_copy(source, held.at[i], sems.at[0, i])
        for i, source in enumerate(sources)
    ]
    for copy in copies:
        copy.start()
    return copies


def finish_copies(copies, held, targets, sems):
    leaving = []
    for i, (copy, target) in enumerate(zip(copies, targets)):
        copy.wait()
        leaving.append(pltpu.make_async_copy(held.at[i], target, sems.at[1, i]))
        leaving[-1].start()
    for copy in leaving:
        copy.wait()


def edge_kernel(k_ref, v_ref, k_ends_ref, v_ends_ref, *refs):
    rim_ref, sum_ref, held, sems = refs[-4:]
    first = k_ref.shape[0] - WINDOW
    size = held.shape[1]
    pieces = range(WINDOW // size)
    sources = [ref.at[pl.ds(first + i * size, size)] for ref in (k_ref, v_ref) for i in pieces]
    targets = [rim_ref.at[n, pl.ds(i * size, size)] for n in range(2) for i in pieces]
    copies = start_copies(sources, held, sems)
    for number, ref in enumerate((k_ends_ref, v_ends_ref)):
        rows = ref[...].astype(F32)[:, 16 - SUMCOLS :]
        sum_ref[number] = rows.reshape(sum_ref.shape[1:]).astype(BF16)
    finish_copies(copies, held, targets, sems)


def edges(keys, values, waits):
    tokens_dev, width = keys.shape
    blocks = tokens_dev // BLOCK
    anywhere = pl.BlockSpec(memory_space=pl.ANY)
    ends = pl.BlockSpec((blocks, 16, width), lambda i: (0, BLOCK // 16 - 1, 0))
    shape = (2, blocks * SUMCOLS, width)
    return pl.pallas_call(
        edge_kernel,
        grid=(1,),
        in_specs=[anywhere] * 2 + [ends] * 2 + moments(waits),
        out_specs=[anywhere, pl.BlockSpec(shape, lambda i: (0, 0, 0))],
        out_shape=[
            jax.ShapeDtypeStruct((2, WINDOW, width), BF16),
            jax.ShapeDtypeStruct(shape, BF16),
        ],
        scratch_shapes=[
            pltpu.VMEM((4, WINDOW // 2, width), BF16),
            pltpu.SemaphoreType.DMA((2, 4)),
        ],
        compiler_params=params(60),
        cost_estimate=cost(0, 8 * WINDOW * width),
        name="edges",
    )(
        keys,
        values,
        keys.reshape(blocks, BLOCK, width),
        values.reshape(blocks, BLOCK, width),
        *waits,
    )


def cut_kernel(weight_ref, o_ref, held, sems):
    half = o_ref.shape[1]
    size = held.shape[1]
    side = lax.axis_index("ctx") % 2
    columns = pl.ds(pl.multiple_of(side * half, half), half)
    pieces = range(held.shape[0])
    copies = start_copies(
        [weight_ref.at[pl.ds(i * size, size), columns] for i in pieces], held, sems
    )
    finish_copies(copies, held, [o_ref.at[pl.ds(i * size, size)] for i in pieces], sems)


def cut(weight):
    rows, width = weight.shape
    pieces = 4
    anywhere = pl.BlockSpec(memory_space=pl.ANY)
    return pl.pallas_call(
        cut_kernel,
        in_specs=[anywhere],
        out_specs=anywhere,
        out_shape=jax.ShapeDtypeStruct((rows, width // 2), BF16),
        scratch_shapes=[
            pltpu.VMEM((pieces, rows // pieces, width // 2), BF16),
            pltpu.SemaphoreType.DMA((2, pieces)),
        ],
        compiler_params=params(60),
        cost_estimate=cost(0, 2 * rows * width),
        name="cut",
    )(weight)


def prep_kernel(q_ref, k_ref, v_ref, *refs):
    send_ref = refs[-1]
    matrix = regroup_matrix()
    ctx, _, per, _, width = send_ref.shape
    rows = TILE // STRIDE
    for number, ref in enumerate((q_ref, k_ref, v_ref)):
        for t in range(ref.shape[0] // TILE):
            grouped = dot(matrix, ref[t * TILE : (t + 1) * TILE]).astype(BF16)
            send_ref[:, number, :, t * rows : (t + 1) * rows] = grouped.reshape(
                ctx, per, rows, width
            )


def prepare(queries, keys, values, ctx, chunk, chunks, waits):
    tokens_dev, width = queries.shape
    per = STRIDE // ctx
    part = width // chunks
    size = tokens_dev // 2 if tokens_dev % (2 * TILE) == 0 else TILE
    return pl.pallas_call(
        prep_kernel,
        grid=(tokens_dev // size,),
        in_specs=[pl.BlockSpec((size, part), lambda b: (b, chunk))] * 3 + moments(waits),
        out_specs=pl.BlockSpec((ctx, 3, per, size // STRIDE, part), lambda b: (0, 0, 0, b, 0)),
        out_shape=jax.ShapeDtypeStruct((ctx, 3, per, tokens_dev // STRIDE, part), BF16),
        compiler_params=params(60),
        cost_estimate=cost(6 * tokens_dev * TILE * part, 12 * tokens_dev * part),
        name="prepare",
    )(queries, keys, values, *waits)


def home_kernel(place_ref, q_ref, k_ref, v_ref, rim_ref, *refs, order):
    sum_refs, (o_ref, mark_ref) = refs[: len(order)], refs[-2:]
    mark_ref[...] = jnp.zeros_like(mark_ref)
    place = place_ref[0]
    tokens_dev = q_ref.shape[0]
    back = WINDOW // TILE
    key_blocks = [rim_ref[0, e * TILE : (e + 1) * TILE] for e in range(back)]
    value_blocks = [with_ones(rim_ref[1, e * TILE : (e + 1) * TILE]) for e in range(back)]
    for e in range(tokens_dev // TILE):
        key_blocks.append(k_ref[e * TILE : (e + 1) * TILE])
        value_blocks.append(with_ones(v_ref[e * TILE : (e + 1) * TILE]))
    picks = sum_refs[0].shape[1]
    sum_keys = jnp.concatenate([ref[0] for ref in sum_refs])
    sum_values = with_ones(jnp.concatenate([ref[1] for ref in sum_refs]))
    sum_col = jnp.concatenate(
        [iota2((TILE, picks), 1) + (place ^ i) * picks for i in order], axis=1
    )
    row = iota2((TILE, TILE), 0)
    col = iota2((TILE, TILE), 1)
    for b in range(tokens_dev // TILE):
        query = q_ref[b * TILE : (b + 1) * TILE]
        blocks = []
        for e in range(back + 1):
            block = scores(query, key_blocks[b + e])
            allowed = None
            if e == 0:
                allowed = col > row
            if e == back:
                allowed = col <= row
            if b + e < back:
                held = place > 0
                allowed = held if allowed is None else allowed & held
            if allowed is not None:
                block = jnp.where(allowed, block, BIG_NEG)
            blocks.append(block)
        local = weighted(blocks, value_blocks[b : b + back + 1])
        pos = place * tokens_dev + b * TILE + iota2((TILE, 1), 0)
        within = pos % BLOCK
        held = pos // BLOCK * SUMCOLS + jnp.maximum(within - (BLOCK - SUMCOLS - 1), 0)
        block = jnp.where(sum_col < held, scores(query, sum_keys), BIG_NEG)
        own_key = key_blocks[b + back].astype(F32)
        own = jnp.sum(query.astype(F32) * own_key, axis=-1, keepdims=True)
        own = jnp.where(within < BLOCK - SUMCOLS, own, BIG_NEG)
        summary = weighted([block], [sum_values], (own, value_blocks[b + back]))
        o_ref[b * TILE : (b + 1) * TILE] = local + summary


def home_sections(place, queries, keys, values, rim, summary, order, chunk, chunks, waits):
    tokens_dev, width = queries.shape
    heads = width // chunks // HEAD_SIZE
    first = chunk * heads
    picks = summary[0].shape[1]
    total = len(summary) * picks
    own = pl.BlockSpec((tokens_dev, HEAD_SIZE), lambda h: (0, first + h))
    pairs = tokens_dev * (WINDOW + TILE + total) * heads
    return pl.pallas_call(
        functools.partial(home_kernel, order=order),
        grid=(heads,),
        in_specs=[
            pl.BlockSpec(memory_space=pltpu.SMEM),
            own,
            own,
            own,
            pl.BlockSpec((2, WINDOW, HEAD_SIZE), lambda h: (0, 0, first + h)),
        ]
        + [pl.BlockSpec((2, picks, HEAD_SIZE), lambda h: (0, 0, first + h))] * len(summary)
        + moments(waits),
        out_specs=[pl.BlockSpec((tokens_dev, HEAD_SIZE), lambda h: (0, h)), mark_spec()],
        out_shape=[jax.ShapeDtypeStruct((tokens_dev, heads * HEAD_SIZE), F32), MARK],
        compiler_params=params(60),
        cost_estimate=cost(64 * pairs * HEAD_SIZE, 14 * tokens_dev * width, 8 * pairs),
        name="home",
    )(place, queries, keys, values, rim, *summary, *waits)


def stride_kernel(place_ref, x_ref, *refs, slabs):
    ctx, _, _, rows, width = x_ref.shape
    o_refs, mark_ref, held_ref = refs[-2 - (ctx if slabs else 1) : -2], refs[-2], refs[-1]
    mark_ref[...] = jnp.zeros_like(mark_ref)
    count = ctx * rows
    row = iota2((TILE, TILE), 0)
    col = iota2((TILE, TILE), 1)
    sources = TILE // rows
    units = []
    for head in range(width // HEAD_SIZE):
        lanes = slice(head * HEAD_SIZE, (head + 1) * HEAD_SIZE)
        query = x_ref[:, 0, 0, :, lanes].reshape(count, HEAD_SIZE)
        key_rows = x_ref[:, 1, 0, :, lanes].reshape(count, HEAD_SIZE)
        value_rows = with_ones(x_ref[:, 2, 0, :, lanes].reshape(count, HEAD_SIZE))
        for b in range(count // TILE):
            part = query[b * TILE : (b + 1) * TILE]
            blocks = [scores(part, key_rows[e * TILE : (e + 1) * TILE]) for e in range(b + 1)]
            blocks[b] = jnp.where(col <= row, blocks[b], BIG_NEG)
            units.append((lanes, b, blocks, value_rows))
    for lanes, b, blocks, value_rows in units:
        result = weighted(
            blocks, [value_rows[e * TILE : (e + 1) * TILE] for e in range(b + 1)]
        ).astype(BF16)
        held_ref[b * sources : (b + 1) * sources, :, lanes] = result.reshape(
            sources, rows, HEAD_SIZE
        )
    if not slabs:
        o_refs[0][:, 0] = held_ref[...]
        return
    for slot in range(ctx):
        o_refs[slot][0] = held_ref[partner(place_ref[0], slot, ctx)]


def stride_attend(place, moved, slabs, waits):
    ctx, _, per, rows, width = moved.shape
    count = ctx * rows
    pairs = per * (width // HEAD_SIZE) * count * (count + TILE) // 2
    if slabs:
        out_specs = [pl.BlockSpec((1, rows, width), lambda r: (r, 0, 0))] * ctx
        out_shape = [jax.ShapeDtypeStruct((per, rows, width), BF16)] * ctx
    else:
        out_specs = [pl.BlockSpec((ctx, 1, rows, width), lambda r: (0, r, 0, 0))]
        out_shape = [jax.ShapeDtypeStruct((ctx, per, rows, width), BF16)]
    return pl.pallas_call(
        functools.partial(stride_kernel, slabs=slabs),
        grid=(per,),
        in_specs=[
            pl.BlockSpec(memory_space=pltpu.SMEM),
            pl.BlockSpec((ctx, 3, 1, rows, width), lambda r: (0, 0, r, 0, 0)),
        ]
        + moments(waits),
        out_specs=out_specs + [mark_spec()],
        out_shape=out_shape + [MARK],
        scratch_shapes=[pltpu.VMEM((ctx, rows, width), BF16)],
        compiler_params=params(24),
        cost_estimate=cost(8 * pairs * HEAD_SIZE, 8 * per * count * width, pairs),
        name="stride",
    )(place, moved, *waits)


def combine_kernel(seat_ref, home_ref, *refs, slots, arrays, ctx):
    back_refs, o_refs, mark_ref = refs[:arrays], refs[-slots - 1 : -1], refs[-1]
    mark_ref[...] = jnp.zeros_like(mark_ref)
    tokens_dev, width = home_ref.shape
    size = tokens_dev // slots
    per = STRIDE // ctx
    token = iota2((TILE, TILE), 0)
    col = iota2((TILE, TILE), 1)
    group = col >> 4
    owner = group // per if arrays == 1 else partner(seat_ref[1], group // per, ctx)
    matrix = (token == (col & 15) * 16 + owner * per + group % per).astype(BF16)
    for slot in range(slots):
        owner = partner(seat_ref[0], slot, slots)
        for b in range(size // TILE):
            first = owner * (size // TILE) + b
            here = pl.ds(pl.multiple_of(first * STRIDE, STRIDE), STRIDE)
            if arrays == 1:
                rows = back_refs[0][:, :, here].reshape(TILE, width)
            else:
                rows = jnp.concatenate([ref[r, here] for ref in back_refs for r in range(per)])
            back = dot(matrix, rows)
            home = home_ref[pl.ds(pl.multiple_of(first * TILE, TILE), TILE)]
            o_refs[slot][b * TILE : (b + 1) * TILE] = (home + back).astype(BF16)


def combine(seat, home, backs, slots, ctx, waits):
    tokens_dev, width = home.shape
    size = tokens_dev // slots
    return pl.pallas_call(
        functools.partial(combine_kernel, slots=slots, arrays=len(backs), ctx=ctx),
        in_specs=[pl.BlockSpec(memory_space=pltpu.SMEM)]
        + [pl.BlockSpec(memory_space=pltpu.VMEM)] * (1 + len(backs))
        + moments(waits),
        out_specs=[pl.BlockSpec(memory_space=pltpu.VMEM)] * (slots + 1),
        out_shape=[jax.ShapeDtypeStruct((size, width), BF16)] * slots + [MARK],
        compiler_params=params(24),
        cost_estimate=cost(56 * tokens_dev * TILE * width, 8 * tokens_dev * width),
        name="combine",
    )(seat, home, *backs, *waits)


def project_kernel(side_ref, *refs, slots, chunk, adds):
    moved_refs, weight_refs, refs = refs[:slots], refs[slots : slots + 2], refs[slots + 2 :]
    o_ref = refs[-1]
    part = moved_refs[0].shape[1]
    half = weight_refs[0].shape[2]
    tile = min(half, 512)
    for phase, weight_ref in enumerate(weight_refs):
        for j in range(half // tile):
            first = pl.multiple_of((side_ref[0] ^ phase) * half + j * tile, tile)
            here = pl.ds(first, tile)
            total = refs[0][:, here] if adds else None
            for slot in range(slots):
                rows = weight_ref[
                    partner(side_ref[1], slot, slots),
                    chunk * part : (chunk + 1) * part,
                    j * tile : (j + 1) * tile,
                ]
                product = dot(moved_refs[slot][...], rows)
                total = product if total is None else total + product
            o_ref[:, here] = total.astype(o_ref.dtype)


def project(side, moved, mine, other, chunk, before, dtype):
    slots = len(moved)
    tokens, part = moved[0].shape
    half = mine.shape[2]
    whole = pl.BlockSpec(memory_space=pltpu.VMEM)
    return pl.pallas_call(
        functools.partial(project_kernel, slots=slots, chunk=chunk, adds=len(before) > 0),
        in_specs=[pl.BlockSpec(memory_space=pltpu.SMEM)] + [whole] * (slots + 2 + len(before)),
        out_specs=whole,
        out_shape=jax.ShapeDtypeStruct((tokens, 2 * half), dtype),
        compiler_params=params(24),
        cost_estimate=cost(
            4 * slots * tokens * part * half, 2 * slots * part * (2 * half + tokens)
        ),
        name="project",
    )(side, *moved, mine, other, *before)


def gather_ctx(rows):
    count = lax.axis_size("ctx")

    def swapped(piece, distance):
        return lax.ppermute(piece, "ctx", [(i, i ^ distance) for i in range(count)])

    order = list(range(0, count, 2))
    pieces = [rows] + [swapped(rows, distance) for distance in order[1:]]
    within = [swapped(piece, 1) for piece in pieces]
    return pieces, within, order + [i ^ 1 for i in order]


def stride_general(queries, keys, values):
    tokens_dev, width = queries.shape
    heads = width // HEAD_SIZE
    ctx = lax.axis_size("ctx")
    copies = max(ctx // STRIDE, 1)
    rows = tokens_dev // STRIDE
    held_rows = ctx * rows // copies
    own_copy = lax.axis_index("ctx") // STRIDE
    query_pos = (jnp.arange(held_rows) // (rows // copies)) * rows
    query_pos = query_pos + (jnp.arange(held_rows) % (rows // copies)) * copies + own_copy
    shaped = queries.reshape(1, rows // copies, ctx, width)
    query = lax.all_to_all(shaped, "ctx", split_axis=2, concat_axis=1, tiled=True)
    query = query.reshape(held_rows, heads, HEAD_SIZE)
    both = jnp.stack([keys, values]).reshape(2, rows, 1, STRIDE, width)
    both = jnp.broadcast_to(both, (2, rows, copies, STRIDE, width)).reshape(2, rows, ctx, width)
    both = lax.all_to_all(both, "ctx", split_axis=2, concat_axis=1, tiled=True)
    both = both.reshape(2, ctx * rows, heads, HEAD_SIZE)
    allowed = jnp.arange(ctx * rows)[None, :] <= query_pos[:, None]

    def one_head(operands):
        head_query, head_keys, head_values = operands
        masked = jnp.where(allowed, scores(head_query, head_keys), BIG_NEG)
        return weighted([masked], [with_ones(head_values)])

    result = lax.map(
        one_head,
        (query.transpose(1, 0, 2), both[0].transpose(1, 0, 2), both[1].transpose(1, 0, 2)),
    )
    result = result.transpose(1, 0, 2).reshape(ctx, rows // copies, 1, width).astype(BF16)
    back = lax.all_to_all(result, "ctx", split_axis=0, concat_axis=2, tiled=True)
    return back.reshape(tokens_dev, width)


def body(queries, keys, values, out_weight, chunks):
    tokens_dev, width = queries.shape
    ctx = lax.axis_size("ctx")
    groups = lax.axis_size("head")
    place = lax.axis_index("ctx")
    place_word = place.astype(jnp.int32).reshape(1)
    side = place % 2
    sibling = [(i, i ^ 1) for i in range(ctx)]

    part = width // chunks
    seat = lax.axis_index("head").astype(jnp.int32)
    sides = jnp.stack([side.astype(jnp.int32), seat])

    def exchange(slabs, axis):
        count = len(slabs)
        moved = [slabs[0]]
        for slot in range(1, count):
            pairs = [(i, partner(i, slot, count)) for i in range(count)]
            moved.append(lax.ppermute(slabs[slot], axis, pairs))
        return moved

    weight_half = cut(out_weight)
    mine = lax.all_gather(weight_half, "head", axis=0)
    rim, picked = edges(keys, values, (weight_half,))
    between, within, order = gather_ctx(picked)
    summary = between + within
    if ctx > STRIDE:
        stride_out = stride_general(queries, keys, values)
        sends = []
    else:
        sends = [prepare(queries, keys, values, ctx, 0, chunks, (weight_half,))]
    (rim,) = after([rim], (*between[1:], *sends))
    if sends:
        sends = list(after(sends, (rim,)))
    before = lax.ppermute(rim, "ctx", [(i, i + 1) for i in range(ctx - 1)])
    for chunk in range(len(sends), chunks * len(sends)):
        sends.append(prepare(queries, keys, values, ctx, chunk, chunks, within[-1:]))

    def home(chunk, waits):
        return home_sections(
            place_word, queries, keys, values, before, summary, order, chunk, chunks, waits
        )


    moved, waits = [], ()
    if ctx > STRIDE:
        for chunk in range(chunks):
            lanes = slice(chunk * part, (chunk + 1) * part)
            homes, mark = home(chunk, waits)
            attended = (homes + stride_out[:, lanes].astype(F32)).astype(BF16)
            attended = attended.reshape(groups, tokens_dev // groups, part)
            owners = [partner(seat, slot, groups) for slot in range(groups)]
            moved.append(exchange([attended[owner] for owner in owners], "head"))
            waits = (mark,)
    else:
        seats = jnp.stack([seat, place.astype(jnp.int32)])
        seats = jnp.stack([seat, place.astype(jnp.int32)])
        sections, mark = home(0, ())
        homes, backs, waits = [sections], [], ()
        if chunks > 1:
            sends[1:] = list(after(sends[1:], (mark,)))
        for chunk, send in enumerate(sends):
            received = lax.all_to_all(send, "ctx", split_axis=0, concat_axis=0, tiled=True)
            beside = chunk < chunks - 1
            *slabs, mark = stride_attend(place_word, received, beside, waits)
            if beside:
                backs.append(exchange(slabs, "ctx"))
            else:
                back = lax.all_to_all(slabs[0], "ctx", split_axis=0, concat_axis=0, tiled=True)
                backs.append([back])
            waits = (mark,)
            for later in range(1, chunks) if chunk == 0 else ():
                sections, mark = home(later, waits)
                homes.append(sections)
                waits = (mark,)
        for chunk in range(chunks):
            *slabs, mark = combine(seats, homes[chunk], backs[chunk], groups, ctx, waits)
            moved.append(exchange(slabs, "head"))
            waits = (mark, *moved[-1][1:3])
    (held,) = after([mine], (mark,))
    other = lax.ppermute(held, "ctx", sibling)
    total = ()
    for chunk in range(chunks):
        dtype = BF16 if chunk == chunks - 1 else F32
        total = (project(sides, moved[chunk], held, other, chunk, total, dtype),)
    return total[0]


def solution(mesh):
    chunks = 2 if HEADS // mesh.shape["head"] > 1 else 1
    placed = (P("ctx", "head"), P("ctx", "head"), P("ctx", "head"), P("head", None))
    return jax.shard_map(
        functools.partial(body, chunks=chunks),
        mesh=mesh,
        in_specs=placed,
        out_specs=P(("ctx", "head"), None),
        check_vma=False,
    )
```

```python
import functools
import math

import jax
import jax.numpy as jnp
from jax import lax
from jax.experimental import pallas as pl
from jax.experimental.pallas import tpu as pltpu
from jax.sharding import PartitionSpec as P

HEADS = 16
HEAD_SIZE = 128
WINDOW = 512
STRIDE = 16
BLOCK = 128
SUMCOLS = 8

BIG_NEG = -1e30
TILE = 256
LOG_SCALE = HEAD_SIZE ** (-0.5) * math.log2(math.e)
F32 = jnp.float32
BF16 = jnp.bfloat16


def params(mib):
    return pltpu.CompilerParams(vmem_limit_bytes=mib * 1024 * 1024)


MARK = jax.ShapeDtypeStruct((8, 128), F32)


def mark_spec():
    return pl.BlockSpec(MARK.shape, lambda *place: (0, 0))


def moments(arrays):
    return [pl.BlockSpec(memory_space=pl.ANY)] * len(arrays)


def after(arrays, others):
    anywhere = pl.BlockSpec(memory_space=pl.ANY)
    return pl.pallas_call(
        lambda *refs: None,
        in_specs=[anywhere] * (len(arrays) + len(others)),
        out_specs=[anywhere] * len(arrays),
        out_shape=[jax.ShapeDtypeStruct(array.shape, array.dtype) for array in arrays],
        input_output_aliases={i: i for i in range(len(arrays))},
        compiler_params=params(60),
        cost_estimate=cost(0, 0),
        name="after",
    )(*arrays, *others)


def cost(flops, bytes_accessed, exps=0):
    return pl.CostEstimate(
        flops=int(flops), bytes_accessed=int(bytes_accessed), transcendentals=int(exps)
    )


def partner(place, slot, count):
    assert count & (count - 1) == 0
    return place ^ slot


def iota2(shape, dim):
    return lax.broadcasted_iota(jnp.int32, shape, dim)


def scores(query, key_rows):
    return lax.dot_general(query, key_rows, (((1,), (1,)), ((), ())), preferred_element_type=F32)


def dot(left, right):
    return jnp.dot(left, right, preferred_element_type=F32)


def regroup_matrix():
    rows = iota2((TILE, TILE), 0)
    cols = iota2((TILE, TILE), 1)
    return (cols == (rows & 15) * 16 + (rows >> 4)).astype(BF16)


def with_ones(value_rows):
    return jnp.concatenate([value_rows, jnp.ones_like(value_rows)], axis=1)


def weighted(score_blocks, value_blocks, extra=None):
    top = functools.reduce(jnp.maximum, score_blocks)
    top = jnp.max(top, axis=-1, keepdims=True)
    if extra is not None:
        top = jnp.maximum(top, extra[0])
    total = None
    for block, value_block in zip(score_blocks, value_blocks):
        weights = jnp.exp2((block - top) * LOG_SCALE).astype(BF16)
        part = dot(weights, value_block)
        total = part if total is None else total + part
    if extra is not None:
        own = jnp.exp2((extra[0] - top) * LOG_SCALE).astype(BF16).astype(F32)
        total = total + own * extra[1].astype(F32)
    return total[:, :HEAD_SIZE] / total[:, HEAD_SIZE:]


def start_copies(sources, held, sems):
    copies = [
        pltpu.make_async_copy(source, held.at[i], sems.at[0, i])
        for i, source in enumerate(sources)
    ]
    for copy in copies:
        copy.start()
    return copies


def finish_copies(copies, held, targets, sems):
    leaving = []
    for i, (copy, target) in enumerate(zip(copies, targets)):
        copy.wait()
        leaving.append(pltpu.make_async_copy(held.at[i], target, sems.at[1, i]))
        leaving[-1].start()
    for copy in leaving:
        copy.wait()


def edge_kernel(k_ref, v_ref, k_ends_ref, v_ends_ref, *refs):
    rim_ref, sum_ref = refs[-2:]
    rim_ref[0] = k_ref[...]
    rim_ref[1] = v_ref[...]

    @pl.when(pl.program_id(0) == 0)
    def _():
        for number, ref in enumerate((k_ends_ref, v_ends_ref)):
            rows = ref[...].astype(F32)[:, 16 - SUMCOLS :]
            sum_ref[number] = rows.reshape(sum_ref.shape[1:]).astype(BF16)


def edges(keys, values, waits):
    tokens_dev, width = keys.shape
    blocks = tokens_dev // BLOCK
    first = (tokens_dev - WINDOW) // TILE
    source = pl.BlockSpec((TILE, width), lambda i: (first + i, 0))
    ends = pl.BlockSpec((blocks, 16, width), lambda i: (0, BLOCK // 16 - 1, 0))
    shape = (2, blocks * SUMCOLS, width)
    return pl.pallas_call(
        edge_kernel,
        grid=(WINDOW // TILE,),
        in_specs=[source] * 2 + [ends] * 2 + moments(waits),
        out_specs=[
            pl.BlockSpec((2, TILE, width), lambda i: (0, i, 0)),
            pl.BlockSpec(shape, lambda i: (0, 0, 0)),
        ],
        out_shape=[
            jax.ShapeDtypeStruct((2, WINDOW, width), BF16),
            jax.ShapeDtypeStruct(shape, BF16),
        ],
        compiler_params=params(60),
        cost_estimate=cost(0, 8 * WINDOW * width),
        name="edges",
    )(
        keys,
        values,
        keys.reshape(blocks, BLOCK, width),
        values.reshape(blocks, BLOCK, width),
        *waits,
    )


def cut_kernel(weight_ref, o_ref, held, sems):
    half = o_ref.shape[1]
    size = held.shape[1]
    side = lax.axis_index("ctx") % 2
    columns = pl.ds(pl.multiple_of(side * half, half), half)
    pieces = range(held.shape[0])
    copies = start_copies(
        [weight_ref.at[pl.ds(i * size, size), columns] for i in pieces], held, sems
    )
    finish_copies(copies, held, [o_ref.at[pl.ds(i * size, size)] for i in pieces], sems)


def cut(weight):
    rows, width = weight.shape
    pieces = 4
    anywhere = pl.BlockSpec(memory_space=pl.ANY)
    return pl.pallas_call(
        cut_kernel,
        in_specs=[anywhere],
        out_specs=anywhere,
        out_shape=jax.ShapeDtypeStruct((rows, width // 2), BF16),
        scratch_shapes=[
            pltpu.VMEM((pieces, rows // pieces, width // 2), BF16),
            pltpu.SemaphoreType.DMA((2, pieces)),
        ],
        compiler_params=params(60),
        cost_estimate=cost(0, 2 * rows * width),
        name="cut",
    )(weight)


def prep_kernel(q_ref, k_ref, v_ref, *refs):
    send_ref = refs[-1]
    matrix = regroup_matrix()
    ctx, _, per, _, width = send_ref.shape
    rows = TILE // STRIDE
    for number, ref in enumerate((q_ref, k_ref, v_ref)):
        for t in range(ref.shape[0] // TILE):
            grouped = dot(matrix, ref[t * TILE : (t + 1) * TILE]).astype(BF16)
            send_ref[:, number, :, t * rows : (t + 1) * rows] = grouped.reshape(
                ctx, per, rows, width
            )


def prepare(queries, keys, values, ctx, chunk, chunks, waits):
    tokens_dev, width = queries.shape
    per = STRIDE // ctx
    part = width // chunks
    size = tokens_dev // 2 if tokens_dev % (2 * TILE) == 0 else TILE
    return pl.pallas_call(
        prep_kernel,
        grid=(tokens_dev // size,),
        in_specs=[pl.BlockSpec((size, part), lambda b: (b, chunk))] * 3 + moments(waits),
        out_specs=pl.BlockSpec((ctx, 3, per, size // STRIDE, part), lambda b: (0, 0, 0, b, 0)),
        out_shape=jax.ShapeDtypeStruct((ctx, 3, per, tokens_dev // STRIDE, part), BF16),
        compiler_params=params(60),
        cost_estimate=cost(6 * tokens_dev * TILE * part, 12 * tokens_dev * part),
        name="prepare",
    )(queries, keys, values, *waits)


def home_kernel(place_ref, q_ref, k_ref, v_ref, rim_ref, *refs, order):
    sum_refs, (o_ref, mark_ref) = refs[: len(order)], refs[-2:]
    mark_ref[...] = jnp.zeros_like(mark_ref)
    place = place_ref[0]
    tokens_dev = q_ref.shape[0]
    back = WINDOW // TILE
    key_blocks = [rim_ref[0, e * TILE : (e + 1) * TILE] for e in range(back)]
    value_blocks = [with_ones(rim_ref[1, e * TILE : (e + 1) * TILE]) for e in range(back)]
    for e in range(tokens_dev // TILE):
        key_blocks.append(k_ref[e * TILE : (e + 1) * TILE])
        value_blocks.append(with_ones(v_ref[e * TILE : (e + 1) * TILE]))
    picks = sum_refs[0].shape[1]
    sum_keys = jnp.concatenate([ref[0] for ref in sum_refs])
    sum_values = with_ones(jnp.concatenate([ref[1] for ref in sum_refs]))
    sum_col = jnp.concatenate(
        [iota2((TILE, picks), 1) + (place ^ i) * picks for i in order], axis=1
    )
    row = iota2((TILE, TILE), 0)
    col = iota2((TILE, TILE), 1)
    for b in range(tokens_dev // TILE):
        query = q_ref[b * TILE : (b + 1) * TILE]
        blocks = []
        for e in range(back + 1):
            block = scores(query, key_blocks[b + e])
            allowed = None
            if e == 0:
                allowed = col > row
            if e == back:
                allowed = col <= row
            if b + e < back:
                held = place > 0
                allowed = held if allowed is None else allowed & held
            if allowed is not None:
                block = jnp.where(allowed, block, BIG_NEG)
            blocks.append(block)
        local = weighted(blocks, value_blocks[b : b + back + 1])
        pos = place * tokens_dev + b * TILE + iota2((TILE, 1), 0)
        within = pos % BLOCK
        held = pos // BLOCK * SUMCOLS + jnp.maximum(within - (BLOCK - SUMCOLS - 1), 0)
        block = jnp.where(sum_col < held, scores(query, sum_keys), BIG_NEG)
        own_key = key_blocks[b + back].astype(F32)
        own = jnp.sum(query.astype(F32) * own_key, axis=-1, keepdims=True)
        own = jnp.where(within < BLOCK - SUMCOLS, own, BIG_NEG)
        summary = weighted([block], [sum_values], (own, value_blocks[b + back]))
        o_ref[b * TILE : (b + 1) * TILE] = local + summary


def home_sections(place, queries, keys, values, rim, summary, order, chunk, chunks, waits):
    tokens_dev, width = queries.shape
    heads = width // chunks // HEAD_SIZE
    first = chunk * heads
    picks = summary[0].shape[1]
    total = len(summary) * picks
    own = pl.BlockSpec((tokens_dev, HEAD_SIZE), lambda h: (0, first + h))
    pairs = tokens_dev * (WINDOW + TILE + total) * heads
    return pl.pallas_call(
        functools.partial(home_kernel, order=order),
        grid=(heads,),
        in_specs=[
            pl.BlockSpec(memory_space=pltpu.SMEM),
            own,
            own,
            own,
            pl.BlockSpec((2, WINDOW, HEAD_SIZE), lambda h: (0, 0, first + h)),
        ]
        + [pl.BlockSpec((2, picks, HEAD_SIZE), lambda h: (0, 0, first + h))] * len(summary)
        + moments(waits),
        out_specs=[pl.BlockSpec((tokens_dev, HEAD_SIZE), lambda h: (0, h)), mark_spec()],
        out_shape=[jax.ShapeDtypeStruct((tokens_dev, heads * HEAD_SIZE), F32), MARK],
        compiler_params=params(60),
        cost_estimate=cost(64 * pairs * HEAD_SIZE, 14 * tokens_dev * width, 8 * pairs),
        name="home",
    )(place, queries, keys, values, rim, *summary, *waits)


def stride_kernel(place_ref, x_ref, *refs, slabs):
    ctx, _, _, rows, width = x_ref.shape
    o_refs, mark_ref, held_ref = refs[-2 - (ctx if slabs else 1) : -2], refs[-2], refs[-1]
    mark_ref[...] = jnp.zeros_like(mark_ref)
    count = ctx * rows
    row = iota2((TILE, TILE), 0)
    col = iota2((TILE, TILE), 1)
    sources = TILE // rows
    units = []
    for head in range(width // HEAD_SIZE):
        lanes = slice(head * HEAD_SIZE, (head + 1) * HEAD_SIZE)
        query = x_ref[:, 0, 0, :, lanes].reshape(count, HEAD_SIZE)
        key_rows = x_ref[:, 1, 0, :, lanes].reshape(count, HEAD_SIZE)
        value_rows = with_ones(x_ref[:, 2, 0, :, lanes].reshape(count, HEAD_SIZE))
        for b in range(count // TILE):
            part = query[b * TILE : (b + 1) * TILE]
            blocks = [scores(part, key_rows[e * TILE : (e + 1) * TILE]) for e in range(b + 1)]
            blocks[b] = jnp.where(col <= row, blocks[b], BIG_NEG)
            units.append((lanes, b, blocks, value_rows))
    for lanes, b, blocks, value_rows in units:
        result = weighted(
            blocks, [value_rows[e * TILE : (e + 1) * TILE] for e in range(b + 1)]
        ).astype(BF16)
        held_ref[b * sources : (b + 1) * sources, :, lanes] = result.reshape(
            sources, rows, HEAD_SIZE
        )
    if not slabs:
        o_refs[0][:, 0] = held_ref[...]
        return
    for slot in range(ctx):
        o_refs[slot][0] = held_ref[partner(place_ref[0], slot, ctx)]


def stride_attend(place, moved, slabs, waits):
    ctx, _, per, rows, width = moved.shape
    count = ctx * rows
    pairs = per * (width // HEAD_SIZE) * count * (count + TILE) // 2
    if slabs:
        out_specs = [pl.BlockSpec((1, rows, width), lambda r: (r, 0, 0))] * ctx
        out_shape = [jax.ShapeDtypeStruct((per, rows, width), BF16)] * ctx
    else:
        out_specs = [pl.BlockSpec((ctx, 1, rows, width), lambda r: (0, r, 0, 0))]
        out_shape = [jax.ShapeDtypeStruct((ctx, per, rows, width), BF16)]
    return pl.pallas_call(
        functools.partial(stride_kernel, slabs=slabs),
        grid=(per,),
        in_specs=[
            pl.BlockSpec(memory_space=pltpu.SMEM),
            pl.BlockSpec((ctx, 3, 1, rows, width), lambda r: (0, 0, r, 0, 0)),
        ]
        + moments(waits),
        out_specs=out_specs + [mark_spec()],
        out_shape=out_shape + [MARK],
        scratch_shapes=[pltpu.VMEM((ctx, rows, width), BF16)],
        compiler_params=params(24),
        cost_estimate=cost(8 * pairs * HEAD_SIZE, 8 * per * count * width, pairs),
        name="stride",
    )(place, moved, *waits)


def combine_kernel(home_ref, *refs, slots, arrays, ctx):
    seat, place = lax.axis_index("head"), lax.axis_index("ctx")
    back_refs, o_refs, mark_ref = refs[:arrays], refs[-slots - 1 : -1], refs[-1]
    mark_ref[...] = jnp.zeros_like(mark_ref)
    tokens_dev, width = home_ref.shape
    size = tokens_dev // slots
    per = STRIDE // ctx
    token = iota2((TILE, TILE), 0)
    col = iota2((TILE, TILE), 1)
    group = col >> 4
    owner = group // per if arrays == 1 else partner(place, group // per, ctx)
    matrix = (token == (col & 15) * 16 + owner * per + group % per).astype(BF16)
    for slot in range(slots):
        owner = partner(seat, slot, slots)
        for b in range(size // TILE):
            first = owner * (size // TILE) + b
            here = pl.ds(pl.multiple_of(first * STRIDE, STRIDE), STRIDE)
            if arrays == 1:
                rows = back_refs[0][:, :, here].reshape(TILE, width)
            else:
                rows = jnp.concatenate([ref[r, here] for ref in back_refs for r in range(per)])
            back = dot(matrix, rows)
            home = home_ref[pl.ds(pl.multiple_of(first * TILE, TILE), TILE)]
            o_refs[slot][b * TILE : (b + 1) * TILE] = (home + back).astype(BF16)


def combine(home, backs, slots, ctx, waits):
    tokens_dev, width = home.shape
    size = tokens_dev // slots
    return pl.pallas_call(
        functools.partial(combine_kernel, slots=slots, arrays=len(backs), ctx=ctx),
        in_specs=[pl.BlockSpec(memory_space=pltpu.VMEM)] * (1 + len(backs))
        + moments(waits),
        out_specs=[pl.BlockSpec(memory_space=pltpu.VMEM)] * (slots + 1),
        out_shape=[jax.ShapeDtypeStruct((size, width), BF16)] * slots + [MARK],
        compiler_params=params(24),
        cost_estimate=cost(56 * tokens_dev * TILE * width, 8 * tokens_dev * width),
        name="combine",
    )(home, *backs, *waits)


def project_kernel(*refs, slots, chunk, adds):
    side, seat = lax.axis_index("ctx") % 2, lax.axis_index("head")
    moved_refs, weight_refs, refs = refs[:slots], refs[slots : slots + 2], refs[slots + 2 :]
    o_ref = refs[-1]
    part = moved_refs[0].shape[1]
    half = weight_refs[0].shape[2]
    tile = min(half, 512)
    for phase, weight_ref in enumerate(weight_refs):
        for j in range(half // tile):
            first = pl.multiple_of((side ^ phase) * half + j * tile, tile)
            here = pl.ds(first, tile)
            total = refs[0][:, here] if adds else None
            for slot in range(slots):
                rows = weight_ref[
                    partner(seat, slot, slots),
                    chunk * part : (chunk + 1) * part,
                    j * tile : (j + 1) * tile,
                ]
                product = dot(moved_refs[slot][...], rows)
                total = product if total is None else total + product
            o_ref[:, here] = total.astype(o_ref.dtype)


def project(moved, mine, other, chunk, before, dtype):
    slots = len(moved)
    tokens, part = moved[0].shape
    half = mine.shape[2]
    whole = pl.BlockSpec(memory_space=pltpu.VMEM)
    return pl.pallas_call(
        functools.partial(project_kernel, slots=slots, chunk=chunk, adds=len(before) > 0),
        in_specs=[whole] * (slots + 2 + len(before)),
        out_specs=whole,
        out_shape=jax.ShapeDtypeStruct((tokens, 2 * half), dtype),
        compiler_params=params(24),
        cost_estimate=cost(
            4 * slots * tokens * part * half, 2 * slots * part * (2 * half + tokens)
        ),
        name="project",
    )(*moved, mine, other, *before)


def gather_ctx(rows):
    count = lax.axis_size("ctx")

    def swapped(piece, distance):
        return lax.ppermute(piece, "ctx", [(i, i ^ distance) for i in range(count)])

    order = list(range(0, count, 2))
    pieces = [rows] + [swapped(rows, distance) for distance in order[1:]]
    within = [swapped(piece, 1) for piece in pieces]
    return pieces, within, order + [i ^ 1 for i in order]


def stride_general(queries, keys, values):
    tokens_dev, width = queries.shape
    heads = width // HEAD_SIZE
    ctx = lax.axis_size("ctx")
    copies = max(ctx // STRIDE, 1)
    rows = tokens_dev // STRIDE
    held_rows = ctx * rows // copies
    own_copy = lax.axis_index("ctx") // STRIDE
    query_pos = (jnp.arange(held_rows) // (rows // copies)) * rows
    query_pos = query_pos + (jnp.arange(held_rows) % (rows // copies)) * copies + own_copy
    shaped = queries.reshape(1, rows // copies, ctx, width)
    query = lax.all_to_all(shaped, "ctx", split_axis=2, concat_axis=1, tiled=True)
    query = query.reshape(held_rows, heads, HEAD_SIZE)
    both = jnp.stack([keys, values]).reshape(2, rows, 1, STRIDE, width)
    both = jnp.broadcast_to(both, (2, rows, copies, STRIDE, width)).reshape(2, rows, ctx, width)
    both = lax.all_to_all(both, "ctx", split_axis=2, concat_axis=1, tiled=True)
    both = both.reshape(2, ctx * rows, heads, HEAD_SIZE)
    allowed = jnp.arange(ctx * rows)[None, :] <= query_pos[:, None]

    def one_head(operands):
        head_query, head_keys, head_values = operands
        masked = jnp.where(allowed, scores(head_query, head_keys), BIG_NEG)
        return weighted([masked], [with_ones(head_values)])

    result = lax.map(
        one_head,
        (query.transpose(1, 0, 2), both[0].transpose(1, 0, 2), both[1].transpose(1, 0, 2)),
    )
    result = result.transpose(1, 0, 2).reshape(ctx, rows // copies, 1, width).astype(BF16)
    back = lax.all_to_all(result, "ctx", split_axis=0, concat_axis=2, tiled=True)
    return back.reshape(tokens_dev, width)


def body(queries, keys, values, out_weight, chunks):
    tokens_dev, width = queries.shape
    ctx = lax.axis_size("ctx")
    groups = lax.axis_size("head")
    place = lax.axis_index("ctx")
    place_word = place.astype(jnp.int32).reshape(1)
    sibling = [(i, i ^ 1) for i in range(ctx)]

    part = width // chunks
    seat = lax.axis_index("head").astype(jnp.int32)

    def exchange(slabs, axis):
        count = len(slabs)
        moved = [slabs[0]]
        for slot in range(1, count):
            pairs = [(i, partner(i, slot, count)) for i in range(count)]
            moved.append(lax.ppermute(slabs[slot], axis, pairs))
        return moved

    weight_half = cut(out_weight)
    mine = lax.all_gather(weight_half, "head", axis=0)
    rim, picked = edges(keys, values, (weight_half,))
    between, within, order = gather_ctx(picked)
    summary = between + within
    if ctx > STRIDE:
        stride_out = stride_general(queries, keys, values)
        sends = []
    else:
        sends = [prepare(queries, keys, values, ctx, 0, chunks, (weight_half,))]
    (rim,) = after([rim], (*between[1:], *sends))
    if sends:
        sends = list(after(sends, (rim,)))
    before = lax.ppermute(rim, "ctx", [(i, i + 1) for i in range(ctx - 1)])
    for chunk in range(len(sends), chunks * len(sends)):
        sends.append(prepare(queries, keys, values, ctx, chunk, chunks, within[-1:]))

    def home(chunk, waits):
        return home_sections(
            place_word, queries, keys, values, before, summary, order, chunk, chunks, waits
        )


    moved, waits = [], ()
    if ctx > STRIDE:
        for chunk in range(chunks):
            lanes = slice(chunk * part, (chunk + 1) * part)
            homes, mark = home(chunk, waits)
            attended = (homes + stride_out[:, lanes].astype(F32)).astype(BF16)
            attended = attended.reshape(groups, tokens_dev // groups, part)
            owners = [partner(seat, slot, groups) for slot in range(groups)]
            moved.append(exchange([attended[owner] for owner in owners], "head"))
            waits = (mark,)
    else:
        sections, mark = home(0, ())
        homes, backs, waits = [sections], [], ()
        if chunks > 1:
            sends[1:] = list(after(sends[1:], (mark,)))
        for chunk, send in enumerate(sends):
            received = lax.all_to_all(send, "ctx", split_axis=0, concat_axis=0, tiled=True)
            beside = chunk < chunks - 1
            *slabs, mark = stride_attend(place_word, received, beside, waits)
            if beside:
                backs.append(exchange(slabs, "ctx"))
            else:
                back = lax.all_to_all(slabs[0], "ctx", split_axis=0, concat_axis=0, tiled=True)
                backs.append([back])
            waits = (mark,)
            for later in range(1, chunks) if chunk == 0 else ():
                sections, mark = home(later, waits)
                homes.append(sections)
                waits = (mark,)
        for chunk in range(chunks):
            *slabs, mark = combine(homes[chunk], backs[chunk], groups, ctx, waits)
            moved.append(exchange(slabs, "head"))
            waits = (mark, *moved[-1][1:3])
    (held,) = after([mine], (mark,))
    other = lax.ppermute(held, "ctx", sibling)
    total = ()
    for chunk in range(chunks):
        dtype = BF16 if chunk == chunks - 1 else F32
        total = (project(moved[chunk], held, other, chunk, total, dtype),)
    return total[0]


def solution(mesh):
    chunks = 2 if HEADS // mesh.shape["head"] > 1 else 1
    placed = (P("ctx", "head"), P("ctx", "head"), P("ctx", "head"), P("head", None))
    return jax.shard_map(
        functools.partial(body, chunks=chunks),
        mesh=mesh,
        in_specs=placed,
        out_specs=P(("ctx", "head"), None),
        check_vma=False,
    )
```

```python
import functools
import math

import jax
import jax.numpy as jnp
from jax import lax
from jax.experimental import pallas as pl
from jax.experimental.pallas import tpu as pltpu
from jax.sharding import PartitionSpec as P

HEADS = 16
HEAD_SIZE = 128
WINDOW = 512
STRIDE = 16
BLOCK = 128
SUMCOLS = 8

BIG_NEG = -1e30
TILE = 256
LOG_SCALE = HEAD_SIZE ** (-0.5) * math.log2(math.e)
F32 = jnp.float32
BF16 = jnp.bfloat16


def params(mib):
    return pltpu.CompilerParams(vmem_limit_bytes=mib * 1024 * 1024)


MARK = jax.ShapeDtypeStruct((8, 128), F32)


def mark_spec():
    return pl.BlockSpec(memory_space=pltpu.HBM)


def moments(arrays):
    return [pl.BlockSpec(memory_space=pl.ANY)] * len(arrays)


def gate(arrays):
    return pl.pallas_call(
        lambda *refs: None,
        in_specs=moments(arrays),
        out_specs=mark_spec(),
        out_shape=MARK,
        compiler_params=params(24),
        cost_estimate=cost(0, 0),
        name="gate",
    )(*arrays)


def after(arrays, others):
    anywhere = pl.BlockSpec(memory_space=pl.ANY)
    return pl.pallas_call(
        lambda *refs: None,
        in_specs=[anywhere] * (len(arrays) + len(others)),
        out_specs=[anywhere] * len(arrays),
        out_shape=[jax.ShapeDtypeStruct(array.shape, array.dtype) for array in arrays],
        input_output_aliases={i: i for i in range(len(arrays))},
        compiler_params=params(52),
        cost_estimate=cost(0, 0),
        name="after",
    )(*arrays, *others)


def cost(flops, bytes_accessed, exps=0):
    return pl.CostEstimate(
        flops=int(flops), bytes_accessed=int(bytes_accessed), transcendentals=int(exps)
    )


def partner(place, slot, count):
    assert count & (count - 1) == 0
    return place ^ slot


def iota2(shape, dim):
    return lax.broadcasted_iota(jnp.int32, shape, dim)


def scores(query, key_rows):
    return lax.dot_general(query, key_rows, (((1,), (1,)), ((), ())), preferred_element_type=F32)


def dot(left, right):
    return jnp.dot(left, right, preferred_element_type=F32)


def regroup_matrix():
    rows = iota2((TILE, TILE), 0)
    cols = iota2((TILE, TILE), 1)
    return (cols == (rows & 15) * 16 + (rows >> 4)).astype(BF16)


def with_ones(value_rows):
    return jnp.concatenate([value_rows, jnp.ones_like(value_rows)], axis=1)


def weighted(score_blocks, value_blocks, extra=None):
    top = functools.reduce(jnp.maximum, score_blocks)
    top = jnp.max(top, axis=-1, keepdims=True)
    if extra is not None:
        top = jnp.maximum(top, extra[0])
    total = None
    for block, value_block in zip(score_blocks, value_blocks):
        weights = jnp.exp2((block - top) * LOG_SCALE).astype(BF16)
        part = dot(weights, value_block)
        total = part if total is None else total + part
    if extra is not None:
        own = jnp.exp2((extra[0] - top) * LOG_SCALE).astype(BF16).astype(F32)
        total = total + own * extra[1].astype(F32)
    return total[:, :HEAD_SIZE] / total[:, HEAD_SIZE:]


def start_copies(sources, held, sems):
    copies = [
        pltpu.make_async_copy(source, held.at[i], sems.at[0, i])
        for i, source in enumerate(sources)
    ]
    for copy in copies:
        copy.start()
    return copies


def finish_copies(copies, held, targets, sems):
    leaving = []
    for i, (copy, target) in enumerate(zip(copies, targets)):
        copy.wait()
        leaving.append(pltpu.make_async_copy(held.at[i], target, sems.at[1, i]))
        leaving[-1].start()
    for copy in leaving:
        copy.wait()


def edge_kernel(k_ref, v_ref, k_ends_ref, v_ends_ref, *refs):
    rim_ref, sum_ref = refs[-2:]
    rim_ref[0] = k_ref[...]
    rim_ref[1] = v_ref[...]

    @pl.when(pl.program_id(0) == 0)
    def _():
        for number, ref in enumerate((k_ends_ref, v_ends_ref)):
            rows = ref[...].astype(F32)[:, 16 - SUMCOLS :]
            sum_ref[number] = rows.reshape(sum_ref.shape[1:]).astype(BF16)


def edges(keys, values, waits):
    tokens_dev, width = keys.shape
    blocks = tokens_dev // BLOCK
    first = (tokens_dev - WINDOW) // TILE
    source = pl.BlockSpec((TILE, width), lambda i: (first + i, 0))
    ends = pl.BlockSpec((blocks, 16, width), lambda i: (0, BLOCK // 16 - 1, 0))
    shape = (2, blocks * SUMCOLS, width)
    return pl.pallas_call(
        edge_kernel,
        grid=(WINDOW // TILE,),
        in_specs=[source] * 2 + [ends] * 2 + moments(waits),
        out_specs=[
            pl.BlockSpec((2, TILE, width), lambda i: (0, i, 0)),
            pl.BlockSpec(shape, lambda i: (0, 0, 0)),
        ],
        out_shape=[
            jax.ShapeDtypeStruct((2, WINDOW, width), BF16),
            jax.ShapeDtypeStruct(shape, BF16),
        ],
        compiler_params=params(60),
        cost_estimate=cost(0, 8 * WINDOW * width),
        name="edges",
    )(
        keys,
        values,
        keys.reshape(blocks, BLOCK, width),
        values.reshape(blocks, BLOCK, width),
        *waits,
    )


def cut_kernel(weight_ref, o_ref, held, sems):
    half = o_ref.shape[1]
    size = held.shape[1]
    side = lax.axis_index("ctx") % 2
    columns = pl.ds(pl.multiple_of(side * half, half), half)
    pieces = range(held.shape[0])
    copies = start_copies(
        [weight_ref.at[pl.ds(i * size, size), columns] for i in pieces], held, sems
    )
    finish_copies(copies, held, [o_ref.at[pl.ds(i * size, size)] for i in pieces], sems)


def cut(weight):
    rows, width = weight.shape
    pieces = 4
    anywhere = pl.BlockSpec(memory_space=pl.ANY)
    return pl.pallas_call(
        cut_kernel,
        in_specs=[anywhere],
        out_specs=anywhere,
        out_shape=jax.ShapeDtypeStruct((rows, width // 2), BF16),
        scratch_shapes=[
            pltpu.VMEM((pieces, rows // pieces, width // 2), BF16),
            pltpu.SemaphoreType.DMA((2, pieces)),
        ],
        compiler_params=params(60),
        cost_estimate=cost(0, 2 * rows * width),
        name="cut",
    )(weight)


def prep_kernel(q_ref, k_ref, v_ref, *refs):
    send_ref = refs[-1]
    matrix = regroup_matrix()
    ctx, _, per, _, width = send_ref.shape
    rows = TILE // STRIDE
    for number, ref in enumerate((q_ref, k_ref, v_ref)):
        for t in range(ref.shape[0] // TILE):
            grouped = dot(matrix, ref[t * TILE : (t + 1) * TILE]).astype(BF16)
            send_ref[:, number, :, t * rows : (t + 1) * rows] = grouped.reshape(
                ctx, per, rows, width
            )


def prepare(queries, keys, values, ctx, chunk, chunks, waits):
    tokens_dev, width = queries.shape
    per = STRIDE // ctx
    part = width // chunks
    size = tokens_dev // 2 if tokens_dev % (2 * TILE) == 0 else TILE
    return pl.pallas_call(
        prep_kernel,
        grid=(tokens_dev // size,),
        in_specs=[pl.BlockSpec((size, part), lambda b: (b, chunk))] * 3 + moments(waits),
        out_specs=pl.BlockSpec((ctx, 3, per, size // STRIDE, part), lambda b: (0, 0, 0, b, 0)),
        out_shape=jax.ShapeDtypeStruct((ctx, 3, per, tokens_dev // STRIDE, part), BF16),
        compiler_params=params(60),
        cost_estimate=cost(6 * tokens_dev * TILE * part, 12 * tokens_dev * part),
        name="prepare",
    )(queries, keys, values, *waits)


def home_kernel(place_ref, q_ref, k_ref, v_ref, rim_ref, *refs, order):
    sum_refs, (o_ref, mark_ref) = refs[: len(order)], refs[-2:]
    place = place_ref[0]
    tokens_dev = q_ref.shape[0]
    back = WINDOW // TILE
    key_blocks = [rim_ref[0, e * TILE : (e + 1) * TILE] for e in range(back)]
    value_blocks = [with_ones(rim_ref[1, e * TILE : (e + 1) * TILE]) for e in range(back)]
    for e in range(tokens_dev // TILE):
        key_blocks.append(k_ref[e * TILE : (e + 1) * TILE])
        value_blocks.append(with_ones(v_ref[e * TILE : (e + 1) * TILE]))
    picks = sum_refs[0].shape[1]
    sum_keys = jnp.concatenate([ref[0] for ref in sum_refs])
    sum_values = with_ones(jnp.concatenate([ref[1] for ref in sum_refs]))
    sum_col = jnp.concatenate(
        [iota2((TILE, picks), 1) + (place ^ i) * picks for i in order], axis=1
    )
    row = iota2((TILE, TILE), 0)
    col = iota2((TILE, TILE), 1)
    for b in range(tokens_dev // TILE):
        query = q_ref[b * TILE : (b + 1) * TILE]
        blocks = []
        for e in range(back + 1):
            block = scores(query, key_blocks[b + e])
            allowed = None
            if e == 0:
                allowed = col > row
            if e == back:
                allowed = col <= row
            if b + e < back:
                held = place > 0
                allowed = held if allowed is None else allowed & held
            if allowed is not None:
                block = jnp.where(allowed, block, BIG_NEG)
            blocks.append(block)
        local = weighted(blocks, value_blocks[b : b + back + 1])
        pos = place * tokens_dev + b * TILE + iota2((TILE, 1), 0)
        within = pos % BLOCK
        held = pos // BLOCK * SUMCOLS + jnp.maximum(within - (BLOCK - SUMCOLS - 1), 0)
        block = jnp.where(sum_col < held, scores(query, sum_keys), BIG_NEG)
        own_key = key_blocks[b + back].astype(F32)
        own = jnp.sum(query.astype(F32) * own_key, axis=-1, keepdims=True)
        own = jnp.where(within < BLOCK - SUMCOLS, own, BIG_NEG)
        summary = weighted([block], [sum_values], (own, value_blocks[b + back]))
        o_ref[b * TILE : (b + 1) * TILE] = local + summary


def home_sections(place, queries, keys, values, rim, summary, order, chunk, chunks, waits):
    tokens_dev, width = queries.shape
    heads = width // chunks // HEAD_SIZE
    first = chunk * heads
    picks = summary[0].shape[1]
    total = len(summary) * picks
    own = pl.BlockSpec((tokens_dev, HEAD_SIZE), lambda h: (0, first + h))
    pairs = tokens_dev * (WINDOW + TILE + total) * heads
    return pl.pallas_call(
        functools.partial(home_kernel, order=order),
        grid=(heads,),
        in_specs=[
            pl.BlockSpec(memory_space=pltpu.SMEM),
            own,
            own,
            own,
            pl.BlockSpec((2, WINDOW, HEAD_SIZE), lambda h: (0, 0, first + h)),
        ]
        + [pl.BlockSpec((2, picks, HEAD_SIZE), lambda h: (0, 0, first + h))] * len(summary)
        + moments(waits),
        out_specs=[pl.BlockSpec((tokens_dev, HEAD_SIZE), lambda h: (0, h)), mark_spec()],
        out_shape=[jax.ShapeDtypeStruct((tokens_dev, heads * HEAD_SIZE), F32), MARK],
        compiler_params=params(60),
        cost_estimate=cost(64 * pairs * HEAD_SIZE, 14 * tokens_dev * width, 8 * pairs),
        name="home",
    )(place, queries, keys, values, rim, *summary, *waits)


def stride_kernel(place_ref, x_ref, *refs, slabs):
    ctx, _, _, rows, width = x_ref.shape
    o_refs, mark_ref, held_ref = refs[-2 - (ctx if slabs else 1) : -2], refs[-2], refs[-1]
    count = ctx * rows
    row = iota2((TILE, TILE), 0)
    col = iota2((TILE, TILE), 1)
    sources = TILE // rows
    units = []
    for head in range(width // HEAD_SIZE):
        lanes = slice(head * HEAD_SIZE, (head + 1) * HEAD_SIZE)
        query = x_ref[:, 0, 0, :, lanes].reshape(count, HEAD_SIZE)
        key_rows = x_ref[:, 1, 0, :, lanes].reshape(count, HEAD_SIZE)
        value_rows = with_ones(x_ref[:, 2, 0, :, lanes].reshape(count, HEAD_SIZE))
        for b in range(count // TILE):
            part = query[b * TILE : (b + 1) * TILE]
            blocks = [scores(part, key_rows[e * TILE : (e + 1) * TILE]) for e in range(b + 1)]
            blocks[b] = jnp.where(col <= row, blocks[b], BIG_NEG)
            units.append((lanes, b, blocks, value_rows))
    for lanes, b, blocks, value_rows in units:
        result = weighted(
            blocks, [value_rows[e * TILE : (e + 1) * TILE] for e in range(b + 1)]
        ).astype(BF16)
        held_ref[b * sources : (b + 1) * sources, :, lanes] = result.reshape(
            sources, rows, HEAD_SIZE
        )
    if not slabs:
        o_refs[0][:, 0] = held_ref[...]
        return
    for slot in range(ctx):
        o_refs[slot][0] = held_ref[partner(place_ref[0], slot, ctx)]


def stride_attend(place, moved, slabs, waits):
    ctx, _, per, rows, width = moved.shape
    count = ctx * rows
    pairs = per * (width // HEAD_SIZE) * count * (count + TILE) // 2
    if slabs:
        out_specs = [pl.BlockSpec((1, rows, width), lambda r: (r, 0, 0))] * ctx
        out_shape = [jax.ShapeDtypeStruct((per, rows, width), BF16)] * ctx
    else:
        out_specs = [pl.BlockSpec((ctx, 1, rows, width), lambda r: (0, r, 0, 0))]
        out_shape = [jax.ShapeDtypeStruct((ctx, per, rows, width), BF16)]
    return pl.pallas_call(
        functools.partial(stride_kernel, slabs=slabs),
        grid=(per,),
        in_specs=[
            pl.BlockSpec(memory_space=pltpu.SMEM),
            pl.BlockSpec((ctx, 3, 1, rows, width), lambda r: (0, 0, r, 0, 0)),
        ]
        + moments(waits),
        out_specs=out_specs + [mark_spec()],
        out_shape=out_shape + [MARK],
        scratch_shapes=[pltpu.VMEM((ctx, rows, width), BF16)],
        compiler_params=params(24),
        cost_estimate=cost(8 * pairs * HEAD_SIZE, 8 * per * count * width, pairs),
        name="stride",
    )(place, moved, *waits)


def combine_kernel(home_ref, *refs, slots, arrays, ctx):
    seat, place = lax.axis_index("head"), lax.axis_index("ctx")
    back_refs, o_refs, mark_ref = refs[:arrays], refs[-slots - 1 : -1], refs[-1]
    tokens_dev, width = home_ref.shape
    size = tokens_dev // slots
    per = STRIDE // ctx
    token = iota2((TILE, TILE), 0)
    col = iota2((TILE, TILE), 1)
    group = col >> 4
    owner = group // per if arrays == 1 else partner(place, group // per, ctx)
    matrix = (token == (col & 15) * 16 + owner * per + group % per).astype(BF16)
    for slot in range(slots):
        owner = partner(seat, slot, slots)
        for b in range(size // TILE):
            first = owner * (size // TILE) + b
            here = pl.ds(pl.multiple_of(first * STRIDE, STRIDE), STRIDE)
            if arrays == 1:
                rows = back_refs[0][:, :, here].reshape(TILE, width)
            else:
                rows = jnp.concatenate([ref[r, here] for ref in back_refs for r in range(per)])
            back = dot(matrix, rows)
            home = home_ref[pl.ds(pl.multiple_of(first * TILE, TILE), TILE)]
            o_refs[slot][b * TILE : (b + 1) * TILE] = (home + back).astype(BF16)


def combine(home, backs, slots, ctx, waits):
    tokens_dev, width = home.shape
    size = tokens_dev // slots
    return pl.pallas_call(
        functools.partial(combine_kernel, slots=slots, arrays=len(backs), ctx=ctx),
        in_specs=[pl.BlockSpec(memory_space=pltpu.VMEM)] * (1 + len(backs))
        + moments(waits),
        out_specs=[pl.BlockSpec(memory_space=pltpu.VMEM)] * slots + [mark_spec()],
        out_shape=[jax.ShapeDtypeStruct((size, width), BF16)] * slots + [MARK],
        compiler_params=params(24),
        cost_estimate=cost(56 * tokens_dev * TILE * width, 8 * tokens_dev * width),
        name="combine",
    )(home, *backs, *waits)


def project_kernel(*refs, slots, chunk, adds):
    side, seat = lax.axis_index("ctx") % 2, lax.axis_index("head")
    moved_refs, weight_refs, refs = refs[:slots], refs[slots : slots + 2], refs[slots + 2 :]
    o_ref = refs[-1]
    part = moved_refs[0].shape[1]
    half = weight_refs[0].shape[2]
    tile = min(half, 512)
    for phase, weight_ref in enumerate(weight_refs):
        for j in range(half // tile):
            first = pl.multiple_of((side ^ phase) * half + j * tile, tile)
            here = pl.ds(first, tile)
            total = refs[0][:, here] if adds else None
            for slot in range(slots):
                rows = weight_ref[
                    partner(seat, slot, slots),
                    chunk * part : (chunk + 1) * part,
                    j * tile : (j + 1) * tile,
                ]
                product = dot(moved_refs[slot][...], rows)
                total = product if total is None else total + product
            o_ref[:, here] = total.astype(o_ref.dtype)


def project(moved, mine, other, chunk, before, dtype):
    slots = len(moved)
    tokens, part = moved[0].shape
    half = mine.shape[2]
    whole = pl.BlockSpec(memory_space=pltpu.VMEM)
    return pl.pallas_call(
        functools.partial(project_kernel, slots=slots, chunk=chunk, adds=len(before) > 0),
        in_specs=[whole] * (slots + 2 + len(before)),
        out_specs=whole,
        out_shape=jax.ShapeDtypeStruct((tokens, 2 * half), dtype),
        compiler_params=params(24),
        cost_estimate=cost(
            4 * slots * tokens * part * half, 2 * slots * part * (2 * half + tokens)
        ),
        name="project",
    )(*moved, mine, other, *before)


def gather_ctx(rows):
    count = lax.axis_size("ctx")

    def swapped(piece, distance):
        return lax.ppermute(piece, "ctx", [(i, i ^ distance) for i in range(count)])

    order = list(range(0, count, 2))
    pieces = [rows] + [swapped(rows, distance) for distance in order[1:]]
    within = [swapped(piece, 1) for piece in pieces]
    return pieces, within, order + [i ^ 1 for i in order]


def stride_general(queries, keys, values):
    tokens_dev, width = queries.shape
    heads = width // HEAD_SIZE
    ctx = lax.axis_size("ctx")
    copies = max(ctx // STRIDE, 1)
    rows = tokens_dev // STRIDE
    held_rows = ctx * rows // copies
    own_copy = lax.axis_index("ctx") // STRIDE
    query_pos = (jnp.arange(held_rows) // (rows // copies)) * rows
    query_pos = query_pos + (jnp.arange(held_rows) % (rows // copies)) * copies + own_copy
    shaped = queries.reshape(1, rows // copies, ctx, width)
    query = lax.all_to_all(shaped, "ctx", split_axis=2, concat_axis=1, tiled=True)
    query = query.reshape(held_rows, heads, HEAD_SIZE)
    both = jnp.stack([keys, values]).reshape(2, rows, 1, STRIDE, width)
    both = jnp.broadcast_to(both, (2, rows, copies, STRIDE, width)).reshape(2, rows, ctx, width)
    both = lax.all_to_all(both, "ctx", split_axis=2, concat_axis=1, tiled=True)
    both = both.reshape(2, ctx * rows, heads, HEAD_SIZE)
    allowed = jnp.arange(ctx * rows)[None, :] <= query_pos[:, None]

    def one_head(operands):
        head_query, head_keys, head_values = operands
        masked = jnp.where(allowed, scores(head_query, head_keys), BIG_NEG)
        return weighted([masked], [with_ones(head_values)])

    result = lax.map(
        one_head,
        (query.transpose(1, 0, 2), both[0].transpose(1, 0, 2), both[1].transpose(1, 0, 2)),
    )
    result = result.transpose(1, 0, 2).reshape(ctx, rows // copies, 1, width).astype(BF16)
    back = lax.all_to_all(result, "ctx", split_axis=0, concat_axis=2, tiled=True)
    return back.reshape(tokens_dev, width)


def body(queries, keys, values, out_weight, chunks):
    tokens_dev, width = queries.shape
    ctx = lax.axis_size("ctx")
    groups = lax.axis_size("head")
    place = lax.axis_index("ctx")
    place_word = place.astype(jnp.int32).reshape(1)
    sibling = [(i, i ^ 1) for i in range(ctx)]

    part = width // chunks
    seat = lax.axis_index("head").astype(jnp.int32)

    def exchange(slabs, axis):
        count = len(slabs)
        moved = [slabs[0]]
        for slot in range(1, count):
            pairs = [(i, partner(i, slot, count)) for i in range(count)]
            moved.append(lax.ppermute(slabs[slot], axis, pairs))
        return moved

    weight_half = cut(out_weight)
    mine = lax.all_gather(weight_half, "head", axis=0)
    rim, picked = edges(keys, values, (weight_half,))
    between, within, order = gather_ctx(picked)
    summary = between + within
    if ctx > STRIDE:
        stride_out = stride_general(queries, keys, values)
        sends = []
    else:
        sends = [prepare(queries, keys, values, ctx, 0, chunks, (weight_half,))]
    (rim,) = after([rim], (*between[1:], *sends))
    if sends:
        sends = list(after(sends, (rim,)))
    before = lax.ppermute(rim, "ctx", [(i, i + 1) for i in range(ctx - 1)])
    for chunk in range(len(sends), chunks * len(sends)):
        sends.append(prepare(queries, keys, values, ctx, chunk, chunks, within[-1:]))

    def home(chunk, waits):
        return home_sections(
            place_word, queries, keys, values, before, summary, order, chunk, chunks, waits
        )


    moved, waits = [], ()
    if ctx > STRIDE:
        for chunk in range(chunks):
            lanes = slice(chunk * part, (chunk + 1) * part)
            homes, mark = home(chunk, waits)
            attended = (homes + stride_out[:, lanes].astype(F32)).astype(BF16)
            attended = attended.reshape(groups, tokens_dev // groups, part)
            owners = [partner(seat, slot, groups) for slot in range(groups)]
            moved.append(exchange([attended[owner] for owner in owners], "head"))
            waits = (mark,)
    else:
        sections, mark = home(0, ())
        homes, backs, waits = [sections], [], ()
        if chunks > 1:
            sends[1:] = list(after(sends[1:], (mark,)))
        for chunk, send in enumerate(sends):
            received = lax.all_to_all(send, "ctx", split_axis=0, concat_axis=0, tiled=True)
            beside = chunk < chunks - 1
            *slabs, mark = stride_attend(place_word, received, beside, waits)
            if beside:
                backs.append(exchange(slabs, "ctx"))
            else:
                back = lax.all_to_all(slabs[0], "ctx", split_axis=0, concat_axis=0, tiled=True)
                backs.append([back])
            waits = (mark,)
            for later in range(1, chunks) if chunk == 0 else ():
                sections, mark = home(later, waits)
                homes.append(sections)
                waits = (mark,)
        for chunk in range(chunks):
            *slabs, mark = combine(homes[chunk], backs[chunk], groups, ctx, waits)
            moved.append(exchange(slabs, "head"))
            waits = (mark, *moved[-1][1:2])
    (held,) = after([mine], (gate((mark, *moved[0][2:])),))
    other = lax.ppermute(held, "ctx", sibling)
    total = ()
    for chunk in range(chunks):
        dtype = BF16 if chunk == chunks - 1 else F32
        total = (project(moved[chunk], held, other, chunk, total, dtype),)
    return total[0]


def solution(mesh):
    chunks = 2 if HEADS // mesh.shape["head"] > 1 else 1
    placed = (P("ctx", "head"), P("ctx", "head"), P("ctx", "head"), P("head", None))
    return jax.shard_map(
        functools.partial(body, chunks=chunks),
        mesh=mesh,
        in_specs=placed,
        out_specs=P(("ctx", "head"), None),
        check_vma=False,
    )
```

```python
import functools
import math

import jax
import jax.numpy as jnp
from jax import lax
from jax.experimental import pallas as pl
from jax.experimental.pallas import tpu as pltpu
from jax.sharding import PartitionSpec as P

HEADS = 16
HEAD_SIZE = 128
WINDOW = 512
STRIDE = 16
BLOCK = 128
SUMCOLS = 8

BIG_NEG = -1e30
TILE = 256
LOG_SCALE = HEAD_SIZE ** (-0.5) * math.log2(math.e)
F32 = jnp.float32
BF16 = jnp.bfloat16


def params(mib):
    return pltpu.CompilerParams(vmem_limit_bytes=mib * 1024 * 1024)


MARK = jax.ShapeDtypeStruct((8, 128), F32)


def mark_spec():
    return pl.BlockSpec(memory_space=pltpu.HBM)


def moments(arrays):
    return [pl.BlockSpec(memory_space=pl.ANY)] * len(arrays)


def after(arrays, others):
    anywhere = pl.BlockSpec(memory_space=pl.ANY)
    return pl.pallas_call(
        lambda *refs: None,
        in_specs=[anywhere] * len(arrays) + moments(others),
        out_specs=[anywhere] * len(arrays),
        out_shape=[jax.ShapeDtypeStruct(array.shape, array.dtype) for array in arrays],
        input_output_aliases={i: i for i in range(len(arrays))},
        compiler_params=params(52),
        cost_estimate=cost(0, 0),
        name="after",
    )(*arrays, *others)


def cost(flops, bytes_accessed, exps=0):
    return pl.CostEstimate(
        flops=int(flops), bytes_accessed=int(bytes_accessed), transcendentals=int(exps)
    )


def partner(place, slot, count):
    assert count & (count - 1) == 0
    return place ^ slot


def iota2(shape, dim):
    return lax.broadcasted_iota(jnp.int32, shape, dim)


def scores(query, key_rows):
    return lax.dot_general(query, key_rows, (((1,), (1,)), ((), ())), preferred_element_type=F32)


def dot(left, right):
    return jnp.dot(left, right, preferred_element_type=F32)


def regroup_matrix():
    rows = iota2((TILE, TILE), 0)
    cols = iota2((TILE, TILE), 1)
    return (cols == (rows & 15) * 16 + (rows >> 4)).astype(BF16)


def with_ones(value_rows):
    return jnp.concatenate([value_rows, jnp.ones_like(value_rows)], axis=1)


def weighted(score_blocks, value_blocks, extra=None):
    top = functools.reduce(jnp.maximum, score_blocks)
    top = jnp.max(top, axis=-1, keepdims=True)
    if extra is not None:
        top = jnp.maximum(top, extra[0])
    total = None
    for block, value_block in zip(score_blocks, value_blocks):
        weights = jnp.exp2((block - top) * LOG_SCALE).astype(BF16)
        part = dot(weights, value_block)
        total = part if total is None else total + part
    if extra is not None:
        own = jnp.exp2((extra[0] - top) * LOG_SCALE).astype(BF16).astype(F32)
        total = total + own * extra[1].astype(F32)
    return total[:, :HEAD_SIZE] / total[:, HEAD_SIZE:]


def start_copies(sources, held, sems):
    copies = [
        pltpu.make_async_copy(source, held.at[i], sems.at[0, i])
        for i, source in enumerate(sources)
    ]
    for copy in copies:
        copy.start()
    return copies


def finish_copies(copies, held, targets, sems):
    leaving = []
    for i, (copy, target) in enumerate(zip(copies, targets)):
        copy.wait()
        leaving.append(pltpu.make_async_copy(held.at[i], target, sems.at[1, i]))
        leaving[-1].start()
    for copy in leaving:
        copy.wait()


def edge_kernel(k_ref, v_ref, k_ends_ref, v_ends_ref, *refs):
    rim_ref, sum_ref = refs[-2:]
    rim_ref[0] = k_ref[...]
    rim_ref[1] = v_ref[...]

    @pl.when(pl.program_id(0) == 0)
    def _():
        for number, ref in enumerate((k_ends_ref, v_ends_ref)):
            rows = ref[...].astype(F32)[:, 16 - SUMCOLS :]
            sum_ref[number] = rows.reshape(sum_ref.shape[1:]).astype(BF16)


def edges(keys, values, waits):
    tokens_dev, width = keys.shape
    blocks = tokens_dev // BLOCK
    first = (tokens_dev - WINDOW) // TILE
    source = pl.BlockSpec((TILE, width), lambda i: (first + i, 0))
    ends = pl.BlockSpec((blocks, 16, width), lambda i: (0, BLOCK // 16 - 1, 0))
    shape = (2, blocks * SUMCOLS, width)
    return pl.pallas_call(
        edge_kernel,
        grid=(WINDOW // TILE,),
        in_specs=[source] * 2 + [ends] * 2 + moments(waits),
        out_specs=[
            pl.BlockSpec((2, TILE, width), lambda i: (0, i, 0)),
            pl.BlockSpec(shape, lambda i: (0, 0, 0)),
        ],
        out_shape=[
            jax.ShapeDtypeStruct((2, WINDOW, width), BF16),
            jax.ShapeDtypeStruct(shape, BF16),
        ],
        compiler_params=params(60),
        cost_estimate=cost(0, 8 * WINDOW * width),
        name="edges",
    )(
        keys,
        values,
        keys.reshape(blocks, BLOCK, width),
        values.reshape(blocks, BLOCK, width),
        *waits,
    )


def cut_kernel(weight_ref, o_ref, held, sems):
    half = o_ref.shape[1]
    size = held.shape[1]
    side = lax.axis_index("ctx") % 2
    columns = pl.ds(pl.multiple_of(side * half, half), half)
    pieces = range(held.shape[0])
    copies = start_copies(
        [weight_ref.at[pl.ds(i * size, size), columns] for i in pieces], held, sems
    )
    finish_copies(copies, held, [o_ref.at[pl.ds(i * size, size)] for i in pieces], sems)


def cut(weight):
    rows, width = weight.shape
    pieces = 4
    anywhere = pl.BlockSpec(memory_space=pl.ANY)
    return pl.pallas_call(
        cut_kernel,
        in_specs=[anywhere],
        out_specs=anywhere,
        out_shape=jax.ShapeDtypeStruct((rows, width // 2), BF16),
        scratch_shapes=[
            pltpu.VMEM((pieces, rows // pieces, width // 2), BF16),
            pltpu.SemaphoreType.DMA((2, pieces)),
        ],
        compiler_params=params(60),
        cost_estimate=cost(0, 2 * rows * width),
        name="cut",
    )(weight)


def prep_kernel(q_ref, k_ref, v_ref, *refs):
    send_ref = refs[-1]
    matrix = regroup_matrix()
    ctx, _, per, _, width = send_ref.shape
    rows = TILE // STRIDE
    for number, ref in enumerate((q_ref, k_ref, v_ref)):
        for t in range(ref.shape[0] // TILE):
            grouped = dot(matrix, ref[t * TILE : (t + 1) * TILE]).astype(BF16)
            send_ref[:, number, :, t * rows : (t + 1) * rows] = grouped.reshape(
                ctx, per, rows, width
            )


def prepare(queries, keys, values, ctx, chunk, chunks, waits):
    tokens_dev, width = queries.shape
    per = STRIDE // ctx
    part = width // chunks
    size = tokens_dev // 2 if tokens_dev % (2 * TILE) == 0 else TILE
    return pl.pallas_call(
        prep_kernel,
        grid=(tokens_dev // size,),
        in_specs=[pl.BlockSpec((size, part), lambda b: (b, chunk))] * 3 + moments(waits),
        out_specs=pl.BlockSpec((ctx, 3, per, size // STRIDE, part), lambda b: (0, 0, 0, b, 0)),
        out_shape=jax.ShapeDtypeStruct((ctx, 3, per, tokens_dev // STRIDE, part), BF16),
        compiler_params=params(60),
        cost_estimate=cost(6 * tokens_dev * TILE * part, 12 * tokens_dev * part),
        name="prepare",
    )(queries, keys, values, *waits)


def home_kernel(place_ref, q_ref, k_ref, v_ref, rim_ref, *refs, order):
    sum_refs, o_ref = refs[: len(order)], refs[-2]
    place = place_ref[0]
    tokens_dev = q_ref.shape[0]
    back = WINDOW // TILE
    key_blocks = [rim_ref[0, e * TILE : (e + 1) * TILE] for e in range(back)]
    value_blocks = [with_ones(rim_ref[1, e * TILE : (e + 1) * TILE]) for e in range(back)]
    for e in range(tokens_dev // TILE):
        key_blocks.append(k_ref[e * TILE : (e + 1) * TILE])
        value_blocks.append(with_ones(v_ref[e * TILE : (e + 1) * TILE]))
    picks = sum_refs[0].shape[1]
    sum_keys = jnp.concatenate([ref[0] for ref in sum_refs])
    sum_values = with_ones(jnp.concatenate([ref[1] for ref in sum_refs]))
    sum_col = jnp.concatenate(
        [iota2((TILE, picks), 1) + (place ^ i) * picks for i in order], axis=1
    )
    row = iota2((TILE, TILE), 0)
    col = iota2((TILE, TILE), 1)
    for b in range(tokens_dev // TILE):
        query = q_ref[b * TILE : (b + 1) * TILE]
        blocks = []
        for e in range(back + 1):
            block = scores(query, key_blocks[b + e])
            allowed = None
            if e == 0:
                allowed = col > row
            if e == back:
                allowed = col <= row
            if b + e < back:
                held = place > 0
                allowed = held if allowed is None else allowed & held
            if allowed is not None:
                block = jnp.where(allowed, block, BIG_NEG)
            blocks.append(block)
        local = weighted(blocks, value_blocks[b : b + back + 1])
        pos = place * tokens_dev + b * TILE + iota2((TILE, 1), 0)
        within = pos % BLOCK
        held = pos // BLOCK * SUMCOLS + jnp.maximum(within - (BLOCK - SUMCOLS - 1), 0)
        block = jnp.where(sum_col < held, scores(query, sum_keys), BIG_NEG)
        own_key = key_blocks[b + back].astype(F32)
        own = jnp.sum(query.astype(F32) * own_key, axis=-1, keepdims=True)
        own = jnp.where(within < BLOCK - SUMCOLS, own, BIG_NEG)
        summary = weighted([block], [sum_values], (own, value_blocks[b + back]))
        o_ref[b * TILE : (b + 1) * TILE] = local + summary


def home_sections(place, queries, keys, values, rim, summary, order, chunk, chunks, waits):
    tokens_dev, width = queries.shape
    heads = width // chunks // HEAD_SIZE
    first = chunk * heads
    picks = summary[0].shape[1]
    total = len(summary) * picks
    own = pl.BlockSpec((tokens_dev, HEAD_SIZE), lambda h: (0, first + h))
    pairs = tokens_dev * (WINDOW + TILE + total) * heads
    return pl.pallas_call(
        functools.partial(home_kernel, order=order),
        grid=(heads,),
        in_specs=[
            pl.BlockSpec(memory_space=pltpu.SMEM),
            own,
            own,
            own,
            pl.BlockSpec((2, WINDOW, HEAD_SIZE), lambda h: (0, 0, first + h)),
        ]
        + [pl.BlockSpec((2, picks, HEAD_SIZE), lambda h: (0, 0, first + h))] * len(summary)
        + moments(waits),
        out_specs=[pl.BlockSpec((tokens_dev, HEAD_SIZE), lambda h: (0, h)), mark_spec()],
        out_shape=[jax.ShapeDtypeStruct((tokens_dev, heads * HEAD_SIZE), F32), MARK],
        compiler_params=params(60),
        cost_estimate=cost(64 * pairs * HEAD_SIZE, 14 * tokens_dev * width, 8 * pairs),
        name="home",
    )(place, queries, keys, values, rim, *summary, *waits)


def stride_kernel(place_ref, x_ref, *refs, slabs):
    ctx, _, _, rows, width = x_ref.shape
    o_refs, held_ref = refs[-2 - (ctx if slabs else 1) : -2], refs[-1]
    count = ctx * rows
    row = iota2((TILE, TILE), 0)
    col = iota2((TILE, TILE), 1)
    sources = TILE // rows
    units = []
    for head in range(width // HEAD_SIZE):
        lanes = slice(head * HEAD_SIZE, (head + 1) * HEAD_SIZE)
        query = x_ref[:, 0, 0, :, lanes].reshape(count, HEAD_SIZE)
        key_rows = x_ref[:, 1, 0, :, lanes].reshape(count, HEAD_SIZE)
        value_rows = with_ones(x_ref[:, 2, 0, :, lanes].reshape(count, HEAD_SIZE))
        for b in range(count // TILE):
            part = query[b * TILE : (b + 1) * TILE]
            blocks = [scores(part, key_rows[e * TILE : (e + 1) * TILE]) for e in range(b + 1)]
            blocks[b] = jnp.where(col <= row, blocks[b], BIG_NEG)
            units.append((lanes, b, blocks, value_rows))
    for lanes, b, blocks, value_rows in units:
        result = weighted(
            blocks, [value_rows[e * TILE : (e + 1) * TILE] for e in range(b + 1)]
        ).astype(BF16)
        held_ref[b * sources : (b + 1) * sources, :, lanes] = result.reshape(
            sources, rows, HEAD_SIZE
        )
    if not slabs:
        o_refs[0][:, 0] = held_ref[...]
        return
    for slot in range(ctx):
        o_refs[slot][0] = held_ref[partner(place_ref[0], slot, ctx)]


def stride_attend(place, moved, slabs, waits):
    ctx, _, per, rows, width = moved.shape
    count = ctx * rows
    pairs = per * (width // HEAD_SIZE) * count * (count + TILE) // 2
    if slabs:
        out_specs = [pl.BlockSpec((1, rows, width), lambda r: (r, 0, 0))] * ctx
        out_shape = [jax.ShapeDtypeStruct((per, rows, width), BF16)] * ctx
    else:
        out_specs = [pl.BlockSpec((ctx, 1, rows, width), lambda r: (0, r, 0, 0))]
        out_shape = [jax.ShapeDtypeStruct((ctx, per, rows, width), BF16)]
    return pl.pallas_call(
        functools.partial(stride_kernel, slabs=slabs),
        grid=(per,),
        in_specs=[
            pl.BlockSpec(memory_space=pltpu.SMEM),
            pl.BlockSpec((ctx, 3, 1, rows, width), lambda r: (0, 0, r, 0, 0)),
        ]
        + moments(waits),
        out_specs=out_specs + [mark_spec()],
        out_shape=out_shape + [MARK],
        scratch_shapes=[pltpu.VMEM((ctx, rows, width), BF16)],
        compiler_params=params(24),
        cost_estimate=cost(8 * pairs * HEAD_SIZE, 8 * per * count * width, pairs),
        name="stride",
    )(place, moved, *waits)


def combine_kernel(home_ref, *refs, slots, arrays, ctx):
    seat, place = lax.axis_index("head"), lax.axis_index("ctx")
    back_refs, o_refs = refs[:arrays], refs[-slots - 1 : -1]
    tokens_dev, width = home_ref.shape
    size = tokens_dev // slots
    per = STRIDE // ctx
    token = iota2((TILE, TILE), 0)
    col = iota2((TILE, TILE), 1)
    group = col >> 4
    owner = group // per if arrays == 1 else partner(place, group // per, ctx)
    matrix = (token == (col & 15) * 16 + owner * per + group % per).astype(BF16)
    for slot in range(slots):
        owner = partner(seat, slot, slots)
        for b in range(size // TILE):
            first = owner * (size // TILE) + b
            here = pl.ds(pl.multiple_of(first * STRIDE, STRIDE), STRIDE)
            if arrays == 1:
                rows = back_refs[0][:, :, here].reshape(TILE, width)
            else:
                rows = jnp.concatenate([ref[r, here] for ref in back_refs for r in range(per)])
            back = dot(matrix, rows)
            home = home_ref[pl.ds(pl.multiple_of(first * TILE, TILE), TILE)]
            o_refs[slot][b * TILE : (b + 1) * TILE] = (home + back).astype(BF16)


def combine(home, backs, slots, ctx, waits):
    tokens_dev, width = home.shape
    size = tokens_dev // slots
    return pl.pallas_call(
        functools.partial(combine_kernel, slots=slots, arrays=len(backs), ctx=ctx),
        in_specs=[pl.BlockSpec(memory_space=pltpu.VMEM)] * (1 + len(backs))
        + moments(waits),
        out_specs=[pl.BlockSpec(memory_space=pltpu.VMEM)] * slots + [mark_spec()],
        out_shape=[jax.ShapeDtypeStruct((size, width), BF16)] * slots + [MARK],
        compiler_params=params(24),
        cost_estimate=cost(56 * tokens_dev * TILE * width, 8 * tokens_dev * width),
        name="combine",
    )(home, *backs, *waits)


def project_kernel(*refs, slots, chunk, adds):
    side, seat = lax.axis_index("ctx") % 2, lax.axis_index("head")
    moved_refs, weight_refs, refs = refs[:slots], refs[slots : slots + 2], refs[slots + 2 :]
    o_ref = refs[-1]
    part = moved_refs[0].shape[1]
    half = weight_refs[0].shape[2]
    tile = min(half, 512)
    for phase, weight_ref in enumerate(weight_refs):
        for j in range(half // tile):
            first = pl.multiple_of((side ^ phase) * half + j * tile, tile)
            here = pl.ds(first, tile)
            total = refs[0][:, here] if adds else None
            for slot in range(slots):
                rows = weight_ref[
                    partner(seat, slot, slots),
                    chunk * part : (chunk + 1) * part,
                    j * tile : (j + 1) * tile,
                ]
                product = dot(moved_refs[slot][...], rows)
                total = product if total is None else total + product
            o_ref[:, here] = total.astype(o_ref.dtype)


def project(moved, mine, other, chunk, before, dtype):
    slots = len(moved)
    tokens, part = moved[0].shape
    half = mine.shape[2]
    whole = pl.BlockSpec(memory_space=pltpu.VMEM)
    return pl.pallas_call(
        functools.partial(project_kernel, slots=slots, chunk=chunk, adds=len(before) > 0),
        in_specs=[whole] * (slots + 2 + len(before)),
        out_specs=whole,
        out_shape=jax.ShapeDtypeStruct((tokens, 2 * half), dtype),
        compiler_params=params(24),
        cost_estimate=cost(
            4 * slots * tokens * part * half, 2 * slots * part * (2 * half + tokens)
        ),
        name="project",
    )(*moved, mine, other, *before)


def gather_ctx(rows):
    count = lax.axis_size("ctx")

    def swapped(piece, distance):
        return lax.ppermute(piece, "ctx", [(i, i ^ distance) for i in range(count)])

    order = list(range(0, count, 2))
    pieces = [rows] + [swapped(rows, distance) for distance in order[1:]]
    within = [swapped(piece, 1) for piece in pieces]
    return pieces, within, order + [i ^ 1 for i in order]


def stride_general(queries, keys, values):
    tokens_dev, width = queries.shape
    heads = width // HEAD_SIZE
    ctx = lax.axis_size("ctx")
    copies = max(ctx // STRIDE, 1)
    rows = tokens_dev // STRIDE
    held_rows = ctx * rows // copies
    own_copy = lax.axis_index("ctx") // STRIDE
    query_pos = (jnp.arange(held_rows) // (rows // copies)) * rows
    query_pos = query_pos + (jnp.arange(held_rows) % (rows // copies)) * copies + own_copy
    shaped = queries.reshape(1, rows // copies, ctx, width)
    query = lax.all_to_all(shaped, "ctx", split_axis=2, concat_axis=1, tiled=True)
    query = query.reshape(held_rows, heads, HEAD_SIZE)
    both = jnp.stack([keys, values]).reshape(2, rows, 1, STRIDE, width)
    both = jnp.broadcast_to(both, (2, rows, copies, STRIDE, width)).reshape(2, rows, ctx, width)
    both = lax.all_to_all(both, "ctx", split_axis=2, concat_axis=1, tiled=True)
    both = both.reshape(2, ctx * rows, heads, HEAD_SIZE)
    allowed = jnp.arange(ctx * rows)[None, :] <= query_pos[:, None]

    def one_head(operands):
        head_query, head_keys, head_values = operands
        masked = jnp.where(allowed, scores(head_query, head_keys), BIG_NEG)
        return weighted([masked], [with_ones(head_values)])

    result = lax.map(
        one_head,
        (query.transpose(1, 0, 2), both[0].transpose(1, 0, 2), both[1].transpose(1, 0, 2)),
    )
    result = result.transpose(1, 0, 2).reshape(ctx, rows // copies, 1, width).astype(BF16)
    back = lax.all_to_all(result, "ctx", split_axis=0, concat_axis=2, tiled=True)
    return back.reshape(tokens_dev, width)


def body(queries, keys, values, out_weight, chunks):
    tokens_dev, width = queries.shape
    ctx = lax.axis_size("ctx")
    groups = lax.axis_size("head")
    place = lax.axis_index("ctx")
    place_word = place.astype(jnp.int32).reshape(1)
    sibling = [(i, i ^ 1) for i in range(ctx)]

    part = width // chunks
    seat = lax.axis_index("head").astype(jnp.int32)

    def exchange(slabs, axis):
        count = len(slabs)
        moved = [slabs[0]]
        for slot in range(1, count):
            pairs = [(i, partner(i, slot, count)) for i in range(count)]
            moved.append(lax.ppermute(slabs[slot], axis, pairs))
        return moved

    weight_half = cut(out_weight)
    mine = lax.all_gather(weight_half, "head", axis=0)
    rim, picked = edges(keys, values, (weight_half,))
    between, within, order = gather_ctx(picked)
    summary = between + within
    if ctx > STRIDE:
        stride_out = stride_general(queries, keys, values)
        sends = []
    else:
        sends = [prepare(queries, keys, values, ctx, 0, chunks, (weight_half,))]
    (rim,) = after([rim], (*between[1:], *sends))
    if sends:
        sends = list(after(sends, (rim,)))
    before = lax.ppermute(rim, "ctx", [(i, i + 1) for i in range(ctx - 1)])
    for chunk in range(len(sends), chunks * len(sends)):
        sends.append(prepare(queries, keys, values, ctx, chunk, chunks, within[-1:]))

    def home(chunk, waits):
        return home_sections(
            place_word, queries, keys, values, before, summary, order, chunk, chunks, waits
        )


    moved, waits = [], ()
    if ctx > STRIDE:
        for chunk in range(chunks):
            lanes = slice(chunk * part, (chunk + 1) * part)
            homes, mark = home(chunk, waits)
            attended = (homes + stride_out[:, lanes].astype(F32)).astype(BF16)
            attended = attended.reshape(groups, tokens_dev // groups, part)
            owners = [partner(seat, slot, groups) for slot in range(groups)]
            moved.append(exchange([attended[owner] for owner in owners], "head"))
            waits = (mark,)
    else:
        sections, mark = home(0, ())
        homes, backs, waits = [sections], [], ()
        if chunks > 1:
            sends[1:] = list(after(sends[1:], (mark,)))
        for chunk, send in enumerate(sends):
            received = lax.all_to_all(send, "ctx", split_axis=0, concat_axis=0, tiled=True)
            beside = chunk < chunks - 1
            *slabs, mark = stride_attend(place_word, received, beside, waits)
            if beside:
                backs.append(exchange(slabs, "ctx"))
            else:
                back = lax.all_to_all(slabs[0], "ctx", split_axis=0, concat_axis=0, tiled=True)
                backs.append([back])
            waits = (mark,)
            for later in range(1, chunks) if chunk == 0 else ():
                sections, mark = home(later, waits)
                homes.append(sections)
                waits = (mark,)
        for chunk in range(chunks):
            *slabs, mark = combine(homes[chunk], backs[chunk], groups, ctx, waits)
            moved.append(exchange(slabs, "head"))
            waits = (mark, *moved[-1][1:3])
    (held,) = after([mine], (mark,))
    other = lax.ppermute(held, "ctx", sibling)
    total = ()
    for chunk in range(chunks):
        dtype = BF16 if chunk == chunks - 1 else F32
        total = (project(moved[chunk], held, other, chunk, total, dtype),)
    return total[0]


def solution(mesh):
    chunks = 2 if HEADS // mesh.shape["head"] > 1 else 1
    placed = (P("ctx", "head"), P("ctx", "head"), P("ctx", "head"), P("head", None))
    return jax.shard_map(
        functools.partial(body, chunks=chunks),
        mesh=mesh,
        in_specs=placed,
        out_specs=P(("ctx", "head"), None),
        check_vma=False,
    )
```

```python
import functools
import math

import jax
import jax.numpy as jnp
from jax import lax
from jax.experimental import pallas as pl
from jax.experimental.pallas import tpu as pltpu
from jax.sharding import PartitionSpec as P

HEADS = 16
HEAD_SIZE = 128
WINDOW = 512
STRIDE = 16
BLOCK = 128
SUMCOLS = 8

BIG_NEG = -1e30
TILE = 256
LOG_SCALE = HEAD_SIZE ** (-0.5) * math.log2(math.e)
F32 = jnp.float32
BF16 = jnp.bfloat16


def params(mib):
    return pltpu.CompilerParams(vmem_limit_bytes=mib * 1024 * 1024)


MARK = jax.ShapeDtypeStruct((8, 128), F32)


def mark_spec():
    return pl.BlockSpec(memory_space=pltpu.HBM)


def moments(arrays):
    return [pl.BlockSpec(memory_space=pl.ANY)] * len(arrays)


def after(arrays, others):
    anywhere = pl.BlockSpec(memory_space=pl.ANY)
    return pl.pallas_call(
        lambda *refs: None,
        in_specs=[anywhere] * len(arrays) + moments(others),
        out_specs=[anywhere] * len(arrays),
        out_shape=[jax.ShapeDtypeStruct(array.shape, array.dtype) for array in arrays],
        input_output_aliases={i: i for i in range(len(arrays))},
        compiler_params=params(52),
        cost_estimate=cost(0, 0),
        name="after",
    )(*arrays, *others)


def cost(flops, bytes_accessed, exps=0):
    return pl.CostEstimate(
        flops=int(flops), bytes_accessed=int(bytes_accessed), transcendentals=int(exps)
    )


def partner(place, slot, count):
    assert count & (count - 1) == 0
    return place ^ slot


def iota2(shape, dim):
    return lax.broadcasted_iota(jnp.int32, shape, dim)


def scores(query, key_rows):
    return lax.dot_general(query, key_rows, (((1,), (1,)), ((), ())), preferred_element_type=F32)


def dot(left, right):
    return jnp.dot(left, right, preferred_element_type=F32)


def regroup_matrix():
    rows = iota2((TILE, TILE), 0)
    cols = iota2((TILE, TILE), 1)
    return (cols == (rows & 15) * 16 + (rows >> 4)).astype(BF16)


def with_ones(value_rows):
    return jnp.concatenate([value_rows, jnp.ones_like(value_rows)], axis=1)


def weighted(score_blocks, value_blocks, extra=None):
    top = functools.reduce(jnp.maximum, score_blocks)
    top = jnp.max(top, axis=-1, keepdims=True)
    if extra is not None:
        top = jnp.maximum(top, extra[0])
    total = None
    for block, value_block in zip(score_blocks, value_blocks):
        weights = jnp.exp2((block - top) * LOG_SCALE).astype(BF16)
        part = dot(weights, value_block)
        total = part if total is None else total + part
    if extra is not None:
        own = jnp.exp2((extra[0] - top) * LOG_SCALE).astype(BF16).astype(F32)
        total = total + own * extra[1].astype(F32)
    return total[:, :HEAD_SIZE] / total[:, HEAD_SIZE:]


def start_copies(sources, held, sems):
    copies = [
        pltpu.make_async_copy(source, held.at[i], sems.at[0, i])
        for i, source in enumerate(sources)
    ]
    for copy in copies:
        copy.start()
    return copies


def finish_copies(copies, held, targets, sems):
    leaving = []
    for i, (copy, target) in enumerate(zip(copies, targets)):
        copy.wait()
        leaving.append(pltpu.make_async_copy(held.at[i], target, sems.at[1, i]))
        leaving[-1].start()
    for copy in leaving:
        copy.wait()


def edge_kernel(k_ref, v_ref, k_ends_ref, v_ends_ref, *refs):
    rim_ref, sum_ref = refs[-2:]
    rim_ref[0] = k_ref[...]
    rim_ref[1] = v_ref[...]

    @pl.when(pl.program_id(0) == 0)
    def _():
        for number, ref in enumerate((k_ends_ref, v_ends_ref)):
            rows = ref[...].astype(F32)[:, 16 - SUMCOLS :]
            sum_ref[number] = rows.reshape(sum_ref.shape[1:]).astype(BF16)


def edges(keys, values, waits):
    tokens_dev, width = keys.shape
    blocks = tokens_dev // BLOCK
    first = (tokens_dev - WINDOW) // TILE
    source = pl.BlockSpec((TILE, width), lambda i: (first + i, 0))
    ends = pl.BlockSpec((blocks, 16, width), lambda i: (0, BLOCK // 16 - 1, 0))
    shape = (2, blocks * SUMCOLS, width)
    return pl.pallas_call(
        edge_kernel,
        grid=(WINDOW // TILE,),
        in_specs=[source] * 2 + [ends] * 2 + moments(waits),
        out_specs=[
            pl.BlockSpec((2, TILE, width), lambda i: (0, i, 0)),
            pl.BlockSpec(shape, lambda i: (0, 0, 0)),
        ],
        out_shape=[
            jax.ShapeDtypeStruct((2, WINDOW, width), BF16),
            jax.ShapeDtypeStruct(shape, BF16),
        ],
        compiler_params=params(60),
        cost_estimate=cost(0, 8 * WINDOW * width),
        name="edges",
    )(
        keys,
        values,
        keys.reshape(blocks, BLOCK, width),
        values.reshape(blocks, BLOCK, width),
        *waits,
    )


def cut_kernel(weight_ref, o_ref, held, sems):
    half = o_ref.shape[1]
    size = held.shape[1]
    side = lax.axis_index("ctx") % 2
    columns = pl.ds(pl.multiple_of(side * half, half), half)
    pieces = range(held.shape[0])
    copies = start_copies(
        [weight_ref.at[pl.ds(i * size, size), columns] for i in pieces], held, sems
    )
    finish_copies(copies, held, [o_ref.at[pl.ds(i * size, size)] for i in pieces], sems)


def cut(weight):
    rows, width = weight.shape
    pieces = 4
    anywhere = pl.BlockSpec(memory_space=pl.ANY)
    return pl.pallas_call(
        cut_kernel,
        in_specs=[anywhere],
        out_specs=anywhere,
        out_shape=jax.ShapeDtypeStruct((rows, width // 2), BF16),
        scratch_shapes=[
            pltpu.VMEM((pieces, rows // pieces, width // 2), BF16),
            pltpu.SemaphoreType.DMA((2, pieces)),
        ],
        compiler_params=params(60),
        cost_estimate=cost(0, 2 * rows * width),
        name="cut",
    )(weight)


def prep_kernel(q_ref, k_ref, v_ref, *refs):
    send_ref = refs[-1]
    matrix = regroup_matrix()
    ctx, _, per, _, width = send_ref.shape
    rows = TILE // STRIDE
    for number, ref in enumerate((q_ref, k_ref, v_ref)):
        for t in range(ref.shape[0] // TILE):
            grouped = dot(matrix, ref[t * TILE : (t + 1) * TILE]).astype(BF16)
            send_ref[:, number, :, t * rows : (t + 1) * rows] = grouped.reshape(
                ctx, per, rows, width
            )


def prepare(queries, keys, values, ctx, chunk, chunks, waits):
    tokens_dev, width = queries.shape
    per = STRIDE // ctx
    part = width // chunks
    size = tokens_dev // 2 if tokens_dev % (2 * TILE) == 0 else TILE
    return pl.pallas_call(
        prep_kernel,
        grid=(tokens_dev // size,),
        in_specs=[pl.BlockSpec((size, part), lambda b: (b, chunk))] * 3 + moments(waits),
        out_specs=pl.BlockSpec((ctx, 3, per, size // STRIDE, part), lambda b: (0, 0, 0, b, 0)),
        out_shape=jax.ShapeDtypeStruct((ctx, 3, per, tokens_dev // STRIDE, part), BF16),
        compiler_params=params(60),
        cost_estimate=cost(6 * tokens_dev * TILE * part, 12 * tokens_dev * part),
        name="prepare",
    )(queries, keys, values, *waits)


def home_kernel(place_ref, q_ref, k_ref, v_ref, rim_ref, *refs, order):
    sum_refs, o_ref = refs[: len(order)], refs[-2]
    place = place_ref[0]
    tokens_dev = q_ref.shape[0]
    back = WINDOW // TILE
    key_blocks = [rim_ref[0, e * TILE : (e + 1) * TILE] for e in range(back)]
    value_blocks = [with_ones(rim_ref[1, e * TILE : (e + 1) * TILE]) for e in range(back)]
    for e in range(tokens_dev // TILE):
        key_blocks.append(k_ref[e * TILE : (e + 1) * TILE])
        value_blocks.append(with_ones(v_ref[e * TILE : (e + 1) * TILE]))
    picks = sum_refs[0].shape[1]
    sum_keys = jnp.concatenate([ref[0] for ref in sum_refs])
    sum_values = with_ones(jnp.concatenate([ref[1] for ref in sum_refs]))
    sum_col = jnp.concatenate(
        [iota2((TILE, picks), 1) + (place ^ i) * picks for i in order], axis=1
    )
    row = iota2((TILE, TILE), 0)
    col = iota2((TILE, TILE), 1)
    for b in range(tokens_dev // TILE):
        query = q_ref[b * TILE : (b + 1) * TILE]
        blocks = []
        for e in range(back + 1):
            block = scores(query, key_blocks[b + e])
            allowed = None
            if e == 0:
                allowed = col > row
            if e == back:
                allowed = col <= row
            if b + e < back:
                held = place > 0
                allowed = held if allowed is None else allowed & held
            if allowed is not None:
                block = jnp.where(allowed, block, BIG_NEG)
            blocks.append(block)
        local = weighted(blocks, value_blocks[b : b + back + 1])
        pos = place * tokens_dev + b * TILE + iota2((TILE, 1), 0)
        within = pos % BLOCK
        held = pos // BLOCK * SUMCOLS + jnp.maximum(within - (BLOCK - SUMCOLS - 1), 0)
        block = jnp.where(sum_col < held, scores(query, sum_keys), BIG_NEG)
        own_key = key_blocks[b + back].astype(F32)
        own = jnp.sum(query.astype(F32) * own_key, axis=-1, keepdims=True)
        own = jnp.where(within < BLOCK - SUMCOLS, own, BIG_NEG)
        summary = weighted([block], [sum_values], (own, value_blocks[b + back]))
        o_ref[b * TILE : (b + 1) * TILE] = local + summary


def home_sections(place, queries, keys, values, rim, summary, order, chunk, chunks, waits):
    tokens_dev, width = queries.shape
    heads = width // chunks // HEAD_SIZE
    first = chunk * heads
    picks = summary[0].shape[1]
    total = len(summary) * picks
    own = pl.BlockSpec((tokens_dev, HEAD_SIZE), lambda h: (0, first + h))
    pairs = tokens_dev * (WINDOW + TILE + total) * heads
    return pl.pallas_call(
        functools.partial(home_kernel, order=order),
        grid=(heads,),
        in_specs=[
            pl.BlockSpec(memory_space=pltpu.SMEM),
            own,
            own,
            own,
            pl.BlockSpec((2, WINDOW, HEAD_SIZE), lambda h: (0, 0, first + h)),
        ]
        + [pl.BlockSpec((2, picks, HEAD_SIZE), lambda h: (0, 0, first + h))] * len(summary)
        + moments(waits),
        out_specs=[pl.BlockSpec((tokens_dev, HEAD_SIZE), lambda h: (0, h)), mark_spec()],
        out_shape=[jax.ShapeDtypeStruct((tokens_dev, heads * HEAD_SIZE), F32), MARK],
        compiler_params=params(60),
        cost_estimate=cost(64 * pairs * HEAD_SIZE, 14 * tokens_dev * width, 8 * pairs),
        name="home",
    )(place, queries, keys, values, rim, *summary, *waits)


def stride_kernel(place_ref, x_ref, *refs, slabs):
    ctx, _, _, rows, width = x_ref.shape
    o_refs, held_ref = refs[-2 - (ctx if slabs else 1) : -2], refs[-1]
    count = ctx * rows
    row = iota2((TILE, TILE), 0)
    col = iota2((TILE, TILE), 1)
    sources = TILE // rows
    units = []
    for head in range(width // HEAD_SIZE):
        lanes = slice(head * HEAD_SIZE, (head + 1) * HEAD_SIZE)
        query = x_ref[:, 0, 0, :, lanes].reshape(count, HEAD_SIZE)
        key_rows = x_ref[:, 1, 0, :, lanes].reshape(count, HEAD_SIZE)
        value_rows = with_ones(x_ref[:, 2, 0, :, lanes].reshape(count, HEAD_SIZE))
        for b in range(count // TILE):
            part = query[b * TILE : (b + 1) * TILE]
            blocks = [scores(part, key_rows[e * TILE : (e + 1) * TILE]) for e in range(b + 1)]
            blocks[b] = jnp.where(col <= row, blocks[b], BIG_NEG)
            units.append((lanes, b, blocks, value_rows))
    for lanes, b, blocks, value_rows in units:
        result = weighted(
            blocks, [value_rows[e * TILE : (e + 1) * TILE] for e in range(b + 1)]
        ).astype(BF16)
        held_ref[b * sources : (b + 1) * sources, :, lanes] = result.reshape(
            sources, rows, HEAD_SIZE
        )
    if not slabs:
        o_refs[0][:, 0] = held_ref[...]
        return
    for slot in range(ctx):
        o_refs[slot][0] = held_ref[partner(place_ref[0], slot, ctx)]


def stride_attend(place, moved, slabs, waits):
    ctx, _, per, rows, width = moved.shape
    count = ctx * rows
    pairs = per * (width // HEAD_SIZE) * count * (count + TILE) // 2
    if slabs:
        out_specs = [pl.BlockSpec((1, rows, width), lambda r: (r, 0, 0))] * ctx
        out_shape = [jax.ShapeDtypeStruct((per, rows, width), BF16)] * ctx
    else:
        out_specs = [pl.BlockSpec((ctx, 1, rows, width), lambda r: (0, r, 0, 0))]
        out_shape = [jax.ShapeDtypeStruct((ctx, per, rows, width), BF16)]
    return pl.pallas_call(
        functools.partial(stride_kernel, slabs=slabs),
        grid=(per,),
        in_specs=[
            pl.BlockSpec(memory_space=pltpu.SMEM),
            pl.BlockSpec((ctx, 3, 1, rows, width), lambda r: (0, 0, r, 0, 0)),
        ]
        + moments(waits),
        out_specs=out_specs + [mark_spec()],
        out_shape=out_shape + [MARK],
        scratch_shapes=[pltpu.VMEM((ctx, rows, width), BF16)],
        compiler_params=params(24),
        cost_estimate=cost(8 * pairs * HEAD_SIZE, 8 * per * count * width, pairs),
        name="stride",
    )(place, moved, *waits)


def combine_kernel(home_ref, *refs, slots, arrays, ctx, slabs):
    seat, place = lax.axis_index("head"), lax.axis_index("ctx")
    back_refs, o_refs = refs[:arrays], refs[-1 - (slots if slabs else 1) : -1]
    tokens_dev, width = home_ref.shape
    size = tokens_dev // slots
    per = STRIDE // ctx
    token = iota2((TILE, TILE), 0)
    col = iota2((TILE, TILE), 1)
    group = col >> 4
    owner = group // per if arrays == 1 else partner(place, group // per, ctx)
    matrix = (token == (col & 15) * 16 + owner * per + group % per).astype(BF16)
    for slot in range(slots):
        owner = partner(seat, slot, slots) if slabs else slot
        for b in range(size // TILE):
            first = owner * (size // TILE) + b
            here = pl.ds(pl.multiple_of(first * STRIDE, STRIDE), STRIDE)
            if arrays == 1:
                rows = back_refs[0][:, :, here].reshape(TILE, width)
            else:
                rows = jnp.concatenate([ref[r, here] for ref in back_refs for r in range(per)])
            back = dot(matrix, rows)
            home = home_ref[pl.ds(pl.multiple_of(first * TILE, TILE), TILE)]
            o_ref = o_refs[slot] if slabs else o_refs[0].at[slot]
            o_ref[b * TILE : (b + 1) * TILE] = (home + back).astype(BF16)


def combine(home, backs, slots, ctx, slabs, waits):
    tokens_dev, width = home.shape
    size = tokens_dev // slots
    if slabs:
        out_shape = [jax.ShapeDtypeStruct((size, width), BF16)] * slots
    else:
        out_shape = [jax.ShapeDtypeStruct((slots, size, width), BF16)]
    return pl.pallas_call(
        functools.partial(
            combine_kernel, slots=slots, arrays=len(backs), ctx=ctx, slabs=slabs
        ),
        in_specs=[pl.BlockSpec(memory_space=pltpu.VMEM)] * (1 + len(backs))
        + moments(waits),
        out_specs=[pl.BlockSpec(memory_space=pltpu.VMEM)] * len(out_shape) + [mark_spec()],
        out_shape=out_shape + [MARK],
        compiler_params=params(24),
        cost_estimate=cost(56 * tokens_dev * TILE * width, 8 * tokens_dev * width),
        name="combine",
    )(home, *backs, *waits)


def project_kernel(*refs, slots, arrays, chunk, adds):
    side, seat = lax.axis_index("ctx") % 2, lax.axis_index("head")
    moved_refs, weight_refs, refs = refs[:arrays], refs[arrays : arrays + 2], refs[arrays + 2 :]
    o_ref = refs[-1]
    part = moved_refs[0].shape[-1]
    half = weight_refs[0].shape[2]
    tile = min(half, 512)
    for phase, weight_ref in enumerate(weight_refs):
        for j in range(half // tile):
            first = pl.multiple_of((side ^ phase) * half + j * tile, tile)
            here = pl.ds(first, tile)
            total = refs[0][:, here] if adds else None
            for slot in range(slots):
                rows = weight_ref[
                    slot if arrays == 1 else partner(seat, slot, slots),
                    chunk * part : (chunk + 1) * part,
                    j * tile : (j + 1) * tile,
                ]
                moved = moved_refs[0][slot] if arrays == 1 else moved_refs[slot][...]
                product = dot(moved, rows)
                total = product if total is None else total + product
            o_ref[:, here] = total.astype(o_ref.dtype)


def project(moved, mine, other, chunk, before, dtype):
    slots, _, half = mine.shape
    tokens, part = moved[0].shape[-2:]
    whole = pl.BlockSpec(memory_space=pltpu.VMEM)
    return pl.pallas_call(
        functools.partial(
            project_kernel, slots=slots, arrays=len(moved), chunk=chunk, adds=len(before) > 0
        ),
        in_specs=[whole] * (len(moved) + 2 + len(before)),
        out_specs=whole,
        out_shape=jax.ShapeDtypeStruct((tokens, 2 * half), dtype),
        compiler_params=params(24),
        cost_estimate=cost(
            4 * slots * tokens * part * half, 2 * slots * part * (2 * half + tokens)
        ),
        name="project",
    )(*moved, mine, other, *before)


def gather_ctx(rows):
    count = lax.axis_size("ctx")

    def swapped(piece, distance):
        return lax.ppermute(piece, "ctx", [(i, i ^ distance) for i in range(count)])

    order = list(range(0, count, 2))
    pieces = [rows] + [swapped(rows, distance) for distance in order[1:]]
    within = [swapped(piece, 1) for piece in pieces]
    return pieces, within, order + [i ^ 1 for i in order]


def stride_general(queries, keys, values):
    tokens_dev, width = queries.shape
    heads = width // HEAD_SIZE
    ctx = lax.axis_size("ctx")
    copies = max(ctx // STRIDE, 1)
    rows = tokens_dev // STRIDE
    held_rows = ctx * rows // copies
    own_copy = lax.axis_index("ctx") // STRIDE
    query_pos = (jnp.arange(held_rows) // (rows // copies)) * rows
    query_pos = query_pos + (jnp.arange(held_rows) % (rows // copies)) * copies + own_copy
    shaped = queries.reshape(1, rows // copies, ctx, width)
    query = lax.all_to_all(shaped, "ctx", split_axis=2, concat_axis=1, tiled=True)
    query = query.reshape(held_rows, heads, HEAD_SIZE)
    both = jnp.stack([keys, values]).reshape(2, rows, 1, STRIDE, width)
    both = jnp.broadcast_to(both, (2, rows, copies, STRIDE, width)).reshape(2, rows, ctx, width)
    both = lax.all_to_all(both, "ctx", split_axis=2, concat_axis=1, tiled=True)
    both = both.reshape(2, ctx * rows, heads, HEAD_SIZE)
    allowed = jnp.arange(ctx * rows)[None, :] <= query_pos[:, None]

    def one_head(operands):
        head_query, head_keys, head_values = operands
        masked = jnp.where(allowed, scores(head_query, head_keys), BIG_NEG)
        return weighted([masked], [with_ones(head_values)])

    result = lax.map(
        one_head,
        (query.transpose(1, 0, 2), both[0].transpose(1, 0, 2), both[1].transpose(1, 0, 2)),
    )
    result = result.transpose(1, 0, 2).reshape(ctx, rows // copies, 1, width).astype(BF16)
    back = lax.all_to_all(result, "ctx", split_axis=0, concat_axis=2, tiled=True)
    return back.reshape(tokens_dev, width)


def body(queries, keys, values, out_weight, chunks):
    tokens_dev, width = queries.shape
    ctx = lax.axis_size("ctx")
    groups = lax.axis_size("head")
    place = lax.axis_index("ctx")
    place_word = place.astype(jnp.int32).reshape(1)
    sibling = [(i, i ^ 1) for i in range(ctx)]

    part = width // chunks
    seat = lax.axis_index("head").astype(jnp.int32)

    def exchange(slabs, axis):
        count = len(slabs)
        moved = [slabs[0]]
        for slot in range(1, count):
            pairs = [(i, partner(i, slot, count)) for i in range(count)]
            moved.append(lax.ppermute(slabs[slot], axis, pairs))
        return moved

    weight_half = cut(out_weight)
    mine = lax.all_gather(weight_half, "head", axis=0)
    rim, picked = edges(keys, values, (weight_half,))
    between, within, order = gather_ctx(picked)
    summary = between + within
    if ctx > STRIDE:
        stride_out = stride_general(queries, keys, values)
        sends = []
    else:
        sends = [prepare(queries, keys, values, ctx, 0, chunks, (weight_half,))]
    (rim,) = after([rim], (*between[1:], *sends))
    if sends:
        sends = list(after(sends, (rim,)))
    before = lax.ppermute(rim, "ctx", [(i, i + 1) for i in range(ctx - 1)])
    for chunk in range(len(sends), chunks * len(sends)):
        sends.append(prepare(queries, keys, values, ctx, chunk, chunks, within[-1:]))

    def home(chunk, waits):
        return home_sections(
            place_word, queries, keys, values, before, summary, order, chunk, chunks, waits
        )


    moved, waits = [], ()
    if ctx > STRIDE:
        for chunk in range(chunks):
            lanes = slice(chunk * part, (chunk + 1) * part)
            homes, mark = home(chunk, waits)
            attended = (homes + stride_out[:, lanes].astype(F32)).astype(BF16)
            attended = attended.reshape(groups, tokens_dev // groups, part)
            owners = [partner(seat, slot, groups) for slot in range(groups)]
            moved.append(exchange([attended[owner] for owner in owners], "head"))
            waits = (mark,)
    else:
        sections, mark = home(0, ())
        homes, backs, waits = [sections], [], ()
        if chunks > 1:
            sends[1:] = list(after(sends[1:], (mark,)))
        for chunk, send in enumerate(sends):
            received = lax.all_to_all(send, "ctx", split_axis=0, concat_axis=0, tiled=True)
            beside = chunk < chunks - 1
            *slabs, mark = stride_attend(place_word, received, beside, waits)
            if beside:
                backs.append(exchange(slabs, "ctx"))
            else:
                back = lax.all_to_all(slabs[0], "ctx", split_axis=0, concat_axis=0, tiled=True)
                backs.append([back])
            waits = (mark,)
            for later in range(1, chunks) if chunk == 0 else ():
                sections, mark = home(later, waits)
                homes.append(sections)
                waits = (mark,)
        for chunk in range(chunks):
            beside = chunk < chunks - 1
            *slabs, mark = combine(homes[chunk], backs[chunk], groups, ctx, beside, waits)
            if beside:
                moved.append(exchange(slabs, "head"))
            else:
                rows = lax.all_to_all(slabs[0], "head", split_axis=0, concat_axis=0, tiled=True)
                moved.append([rows])
            waits = (mark, *moved[-1][1:3])
    (held,) = after([mine], (mark,))
    other = lax.ppermute(held, "ctx", sibling)
    total = ()
    for chunk in range(chunks):
        dtype = BF16 if chunk == chunks - 1 else F32
        total = (project(moved[chunk], held, other, chunk, total, dtype),)
    return total[0]


def solution(mesh):
    chunks = 2 if HEADS // mesh.shape["head"] > 1 else 1
    placed = (P("ctx", "head"), P("ctx", "head"), P("ctx", "head"), P("head", None))
    return jax.shard_map(
        functools.partial(body, chunks=chunks),
        mesh=mesh,
        in_specs=placed,
        out_specs=P(("ctx", "head"), None),
        check_vma=False,
    )
```

```python
import functools
import math

import jax
import jax.numpy as jnp
from jax import lax
from jax.experimental import pallas as pl
from jax.experimental.pallas import tpu as pltpu
from jax.sharding import PartitionSpec as P

HEADS = 16
HEAD_SIZE = 128
WINDOW = 512
STRIDE = 16
BLOCK = 128
SUMCOLS = 8

BIG_NEG = -1e30
TILE = 256
LOG_SCALE = HEAD_SIZE ** (-0.5) * math.log2(math.e)
F32 = jnp.float32
BF16 = jnp.bfloat16


def params(mib):
    return pltpu.CompilerParams(vmem_limit_bytes=mib * 1024 * 1024)


MARK = jax.ShapeDtypeStruct((8, 128), F32)


def mark_spec():
    return pl.BlockSpec(memory_space=pltpu.HBM)


def moments(arrays):
    return [pl.BlockSpec(memory_space=pl.ANY)] * len(arrays)


def after(arrays, others):
    anywhere = pl.BlockSpec(memory_space=pl.ANY)
    return pl.pallas_call(
        lambda *refs: None,
        in_specs=[anywhere] * len(arrays) + moments(others),
        out_specs=[anywhere] * len(arrays),
        out_shape=[jax.ShapeDtypeStruct(array.shape, array.dtype) for array in arrays],
        input_output_aliases={i: i for i in range(len(arrays))},
        compiler_params=params(52),
        cost_estimate=cost(0, 0),
        name="after",
    )(*arrays, *others)


def cost(flops, bytes_accessed, exps=0):
    return pl.CostEstimate(
        flops=int(flops), bytes_accessed=int(bytes_accessed), transcendentals=int(exps)
    )


def partner(place, slot, count):
    assert count & (count - 1) == 0
    return place ^ slot


def iota2(shape, dim):
    return lax.broadcasted_iota(jnp.int32, shape, dim)


def scores(query, key_rows):
    return lax.dot_general(query, key_rows, (((1,), (1,)), ((), ())), preferred_element_type=F32)


def dot(left, right):
    return jnp.dot(left, right, preferred_element_type=F32)


def regroup_matrix():
    rows = iota2((TILE, TILE), 0)
    cols = iota2((TILE, TILE), 1)
    return (cols == (rows & 15) * 16 + (rows >> 4)).astype(BF16)


def with_ones(value_rows):
    return jnp.concatenate([value_rows, jnp.ones_like(value_rows)], axis=1)


def weighted(score_blocks, value_blocks, extra=None):
    top = functools.reduce(jnp.maximum, score_blocks)
    top = jnp.max(top, axis=-1, keepdims=True)
    if extra is not None:
        top = jnp.maximum(top, extra[0])
    total = None
    for block, value_block in zip(score_blocks, value_blocks):
        weights = jnp.exp2((block - top) * LOG_SCALE).astype(BF16)
        part = dot(weights, value_block)
        total = part if total is None else total + part
    if extra is not None:
        own = jnp.exp2((extra[0] - top) * LOG_SCALE).astype(BF16).astype(F32)
        total = total + own * extra[1].astype(F32)
    return total[:, :HEAD_SIZE] / total[:, HEAD_SIZE:]


def start_copies(sources, held, sems):
    copies = [
        pltpu.make_async_copy(source, held.at[i], sems.at[0, i])
        for i, source in enumerate(sources)
    ]
    for copy in copies:
        copy.start()
    return copies


def finish_copies(copies, held, targets, sems):
    leaving = []
    for i, (copy, target) in enumerate(zip(copies, targets)):
        copy.wait()
        leaving.append(pltpu.make_async_copy(held.at[i], target, sems.at[1, i]))
        leaving[-1].start()
    for copy in leaving:
        copy.wait()


def edge_kernel(k_ref, v_ref, k_ends_ref, v_ends_ref, *refs):
    rim_ref, sum_ref = refs[-2:]
    rim_ref[0] = k_ref[...]
    rim_ref[1] = v_ref[...]

    @pl.when(pl.program_id(0) == 0)
    def _():
        for number, ref in enumerate((k_ends_ref, v_ends_ref)):
            rows = ref[...].astype(F32)[:, 16 - SUMCOLS :]
            sum_ref[number] = rows.reshape(sum_ref.shape[1:]).astype(BF16)


def edges(keys, values, waits):
    tokens_dev, width = keys.shape
    blocks = tokens_dev // BLOCK
    first = tokens_dev // WINDOW - 1
    source = pl.BlockSpec((WINDOW, width), lambda i: (first, 0))
    ends = pl.BlockSpec((blocks, 16, width), lambda i: (0, BLOCK // 16 - 1, 0))
    shape = (2, blocks * SUMCOLS, width)
    return pl.pallas_call(
        edge_kernel,
        grid=(1,),
        in_specs=[source] * 2 + [ends] * 2 + moments(waits),
        out_specs=[
            pl.BlockSpec((2, WINDOW, width), lambda i: (0, 0, 0)),
            pl.BlockSpec(shape, lambda i: (0, 0, 0)),
        ],
        out_shape=[
            jax.ShapeDtypeStruct((2, WINDOW, width), BF16),
            jax.ShapeDtypeStruct(shape, BF16),
        ],
        compiler_params=params(60),
        cost_estimate=cost(0, 8 * WINDOW * width),
        name="edges",
    )(
        keys,
        values,
        keys.reshape(blocks, BLOCK, width),
        values.reshape(blocks, BLOCK, width),
        *waits,
    )


def cut_kernel(weight_ref, o_ref, held, sems):
    half = o_ref.shape[1]
    size = held.shape[1]
    side = lax.axis_index("ctx") % 2
    columns = pl.ds(pl.multiple_of(side * half, half), half)
    pieces = range(held.shape[0])
    copies = start_copies(
        [weight_ref.at[pl.ds(i * size, size), columns] for i in pieces], held, sems
    )
    finish_copies(copies, held, [o_ref.at[pl.ds(i * size, size)] for i in pieces], sems)


def cut(weight):
    rows, width = weight.shape
    pieces = 4
    anywhere = pl.BlockSpec(memory_space=pl.ANY)
    return pl.pallas_call(
        cut_kernel,
        in_specs=[anywhere],
        out_specs=anywhere,
        out_shape=jax.ShapeDtypeStruct((rows, width // 2), BF16),
        scratch_shapes=[
            pltpu.VMEM((pieces, rows // pieces, width // 2), BF16),
            pltpu.SemaphoreType.DMA((2, pieces)),
        ],
        compiler_params=params(60),
        cost_estimate=cost(0, 2 * rows * width),
        name="cut",
    )(weight)


def prep_kernel(q_ref, k_ref, v_ref, *refs):
    send_ref = refs[-1]
    matrix = regroup_matrix()
    ctx, _, per, _, width = send_ref.shape
    rows = TILE // STRIDE
    for number, ref in enumerate((q_ref, k_ref, v_ref)):
        for t in range(ref.shape[0] // TILE):
            grouped = dot(matrix, ref[t * TILE : (t + 1) * TILE]).astype(BF16)
            send_ref[:, number, :, t * rows : (t + 1) * rows] = grouped.reshape(
                ctx, per, rows, width
            )


def prepare(queries, keys, values, ctx, chunk, chunks, waits):
    tokens_dev, width = queries.shape
    per = STRIDE // ctx
    part = width // chunks
    size = tokens_dev // 2 if tokens_dev % (2 * TILE) == 0 else TILE
    return pl.pallas_call(
        prep_kernel,
        grid=(tokens_dev // size,),
        in_specs=[pl.BlockSpec((size, part), lambda b: (b, chunk))] * 3 + moments(waits),
        out_specs=pl.BlockSpec((ctx, 3, per, size // STRIDE, part), lambda b: (0, 0, 0, b, 0)),
        out_shape=jax.ShapeDtypeStruct((ctx, 3, per, tokens_dev // STRIDE, part), BF16),
        compiler_params=params(60),
        cost_estimate=cost(6 * tokens_dev * TILE * part, 12 * tokens_dev * part),
        name="prepare",
    )(queries, keys, values, *waits)


def home_kernel(place_ref, q_ref, k_ref, v_ref, rim_ref, *refs, order):
    sum_refs, o_ref = refs[: len(order)], refs[-2]
    place = place_ref[0]
    tokens_dev = q_ref.shape[0]
    back = WINDOW // TILE
    key_blocks = [rim_ref[0, e * TILE : (e + 1) * TILE] for e in range(back)]
    value_blocks = [with_ones(rim_ref[1, e * TILE : (e + 1) * TILE]) for e in range(back)]
    for e in range(tokens_dev // TILE):
        key_blocks.append(k_ref[e * TILE : (e + 1) * TILE])
        value_blocks.append(with_ones(v_ref[e * TILE : (e + 1) * TILE]))
    picks = sum_refs[0].shape[1]
    sum_keys = jnp.concatenate([ref[0] for ref in sum_refs])
    sum_values = with_ones(jnp.concatenate([ref[1] for ref in sum_refs]))
    sum_col = jnp.concatenate(
        [iota2((TILE, picks), 1) + (place ^ i) * picks for i in order], axis=1
    )
    row = iota2((TILE, TILE), 0)
    col = iota2((TILE, TILE), 1)
    for b in range(tokens_dev // TILE):
        query = q_ref[b * TILE : (b + 1) * TILE]
        blocks = []
        for e in range(back + 1):
            block = scores(query, key_blocks[b + e])
            allowed = None
            if e == 0:
                allowed = col > row
            if e == back:
                allowed = col <= row
            if b + e < back:
                held = place > 0
                allowed = held if allowed is None else allowed & held
            if allowed is not None:
                block = jnp.where(allowed, block, BIG_NEG)
            blocks.append(block)
        local = weighted(blocks, value_blocks[b : b + back + 1])
        pos = place * tokens_dev + b * TILE + iota2((TILE, 1), 0)
        within = pos % BLOCK
        held = pos // BLOCK * SUMCOLS + jnp.maximum(within - (BLOCK - SUMCOLS - 1), 0)
        block = jnp.where(sum_col < held, scores(query, sum_keys), BIG_NEG)
        own_key = key_blocks[b + back].astype(F32)
        own = jnp.sum(query.astype(F32) * own_key, axis=-1, keepdims=True)
        own = jnp.where(within < BLOCK - SUMCOLS, own, BIG_NEG)
        summary = weighted([block], [sum_values], (own, value_blocks[b + back]))
        o_ref[b * TILE : (b + 1) * TILE] = local + summary


def home_sections(place, queries, keys, values, rim, summary, order, chunk, chunks, waits):
    tokens_dev, width = queries.shape
    heads = width // chunks // HEAD_SIZE
    first = chunk * heads
    picks = summary[0].shape[1]
    total = len(summary) * picks
    own = pl.BlockSpec((tokens_dev, HEAD_SIZE), lambda h: (0, first + h))
    pairs = tokens_dev * (WINDOW + TILE + total) * heads
    return pl.pallas_call(
        functools.partial(home_kernel, order=order),
        grid=(heads,),
        in_specs=[
            pl.BlockSpec(memory_space=pltpu.SMEM),
            own,
            own,
            own,
            pl.BlockSpec((2, WINDOW, HEAD_SIZE), lambda h: (0, 0, first + h)),
        ]
        + [pl.BlockSpec((2, picks, HEAD_SIZE), lambda h: (0, 0, first + h))] * len(summary)
        + moments(waits),
        out_specs=[pl.BlockSpec((tokens_dev, HEAD_SIZE), lambda h: (0, h)), mark_spec()],
        out_shape=[jax.ShapeDtypeStruct((tokens_dev, heads * HEAD_SIZE), F32), MARK],
        compiler_params=params(60),
        cost_estimate=cost(64 * pairs * HEAD_SIZE, 14 * tokens_dev * width, 8 * pairs),
        name="home",
    )(place, queries, keys, values, rim, *summary, *waits)


def stride_kernel(place_ref, x_ref, *refs, slabs):
    ctx, _, _, rows, width = x_ref.shape
    o_refs, held_ref = refs[-2 - (ctx if slabs else 1) : -2], refs[-1]
    count = ctx * rows
    row = iota2((TILE, TILE), 0)
    col = iota2((TILE, TILE), 1)
    sources = TILE // rows
    units = []
    for head in range(width // HEAD_SIZE):
        lanes = slice(head * HEAD_SIZE, (head + 1) * HEAD_SIZE)
        query = x_ref[:, 0, 0, :, lanes].reshape(count, HEAD_SIZE)
        key_rows = x_ref[:, 1, 0, :, lanes].reshape(count, HEAD_SIZE)
        value_rows = with_ones(x_ref[:, 2, 0, :, lanes].reshape(count, HEAD_SIZE))
        for b in range(count // TILE):
            part = query[b * TILE : (b + 1) * TILE]
            blocks = [scores(part, key_rows[e * TILE : (e + 1) * TILE]) for e in range(b + 1)]
            blocks[b] = jnp.where(col <= row, blocks[b], BIG_NEG)
            units.append((lanes, b, blocks, value_rows))
    for lanes, b, blocks, value_rows in units:
        result = weighted(
            blocks, [value_rows[e * TILE : (e + 1) * TILE] for e in range(b + 1)]
        ).astype(BF16)
        held_ref[b * sources : (b + 1) * sources, :, lanes] = result.reshape(
            sources, rows, HEAD_SIZE
        )
    if not slabs:
        o_refs[0][:, 0] = held_ref[...]
        return
    for slot in range(ctx):
        o_refs[slot][0] = held_ref[partner(place_ref[0], slot, ctx)]


def stride_attend(place, moved, slabs, waits):
    ctx, _, per, rows, width = moved.shape
    count = ctx * rows
    pairs = per * (width // HEAD_SIZE) * count * (count + TILE) // 2
    if slabs:
        out_specs = [pl.BlockSpec((1, rows, width), lambda r: (r, 0, 0))] * ctx
        out_shape = [jax.ShapeDtypeStruct((per, rows, width), BF16)] * ctx
    else:
        out_specs = [pl.BlockSpec((ctx, 1, rows, width), lambda r: (0, r, 0, 0))]
        out_shape = [jax.ShapeDtypeStruct((ctx, per, rows, width), BF16)]
    return pl.pallas_call(
        functools.partial(stride_kernel, slabs=slabs),
        grid=(per,),
        in_specs=[
            pl.BlockSpec(memory_space=pltpu.SMEM),
            pl.BlockSpec((ctx, 3, 1, rows, width), lambda r: (0, 0, r, 0, 0)),
        ]
        + moments(waits),
        out_specs=out_specs + [mark_spec()],
        out_shape=out_shape + [MARK],
        scratch_shapes=[pltpu.VMEM((ctx, rows, width), BF16)],
        compiler_params=params(24),
        cost_estimate=cost(8 * pairs * HEAD_SIZE, 8 * per * count * width, pairs),
        name="stride",
    )(place, moved, *waits)


def combine_kernel(home_ref, *refs, slots, arrays, ctx):
    seat, place = lax.axis_index("head"), lax.axis_index("ctx")
    back_refs, o_refs = refs[:arrays], refs[-slots - 1 : -1]
    tokens_dev, width = home_ref.shape
    size = tokens_dev // slots
    per = STRIDE // ctx
    token = iota2((TILE, TILE), 0)
    col = iota2((TILE, TILE), 1)
    group = col >> 4
    owner = group // per if arrays == 1 else partner(place, group // per, ctx)
    matrix = (token == (col & 15) * 16 + owner * per + group % per).astype(BF16)
    for slot in range(slots):
        owner = partner(seat, slot, slots)
        for b in range(size // TILE):
            first = owner * (size // TILE) + b
            here = pl.ds(pl.multiple_of(first * STRIDE, STRIDE), STRIDE)
            if arrays == 1:
                rows = back_refs[0][:, :, here].reshape(TILE, width)
            else:
                rows = jnp.concatenate([ref[r, here] for ref in back_refs for r in range(per)])
            back = dot(matrix, rows)
            home = home_ref[pl.ds(pl.multiple_of(first * TILE, TILE), TILE)]
            o_refs[slot][b * TILE : (b + 1) * TILE] = (home + back).astype(BF16)


def combine(home, backs, slots, ctx, waits):
    tokens_dev, width = home.shape
    size = tokens_dev // slots
    return pl.pallas_call(
        functools.partial(combine_kernel, slots=slots, arrays=len(backs), ctx=ctx),
        in_specs=[pl.BlockSpec(memory_space=pltpu.VMEM)] * (1 + len(backs))
        + moments(waits),
        out_specs=[pl.BlockSpec(memory_space=pltpu.VMEM)] * slots + [mark_spec()],
        out_shape=[jax.ShapeDtypeStruct((size, width), BF16)] * slots + [MARK],
        compiler_params=params(24),
        cost_estimate=cost(56 * tokens_dev * TILE * width, 8 * tokens_dev * width),
        name="combine",
    )(home, *backs, *waits)


def project_kernel(*refs, slots, chunk, adds):
    side, seat = lax.axis_index("ctx") % 2, lax.axis_index("head")
    moved_refs, weight_refs, refs = refs[:slots], refs[slots : slots + 2], refs[slots + 2 :]
    o_ref = refs[-1]
    part = moved_refs[0].shape[1]
    half = weight_refs[0].shape[2]
    tile = min(half, 512)
    for phase, weight_ref in enumerate(weight_refs):
        for j in range(half // tile):
            first = pl.multiple_of((side ^ phase) * half + j * tile, tile)
            here = pl.ds(first, tile)
            total = refs[0][:, here] if adds else None
            for slot in range(slots):
                rows = weight_ref[
                    partner(seat, slot, slots),
                    chunk * part : (chunk + 1) * part,
                    j * tile : (j + 1) * tile,
                ]
                product = dot(moved_refs[slot][...], rows)
                total = product if total is None else total + product
            o_ref[:, here] = total.astype(o_ref.dtype)


def project(moved, mine, other, chunk, before, dtype):
    slots = len(moved)
    tokens, part = moved[0].shape
    half = mine.shape[2]
    whole = pl.BlockSpec(memory_space=pltpu.VMEM)
    return pl.pallas_call(
        functools.partial(project_kernel, slots=slots, chunk=chunk, adds=len(before) > 0),
        in_specs=[whole] * (slots + 2 + len(before)),
        out_specs=whole,
        out_shape=jax.ShapeDtypeStruct((tokens, 2 * half), dtype),
        compiler_params=params(24),
        cost_estimate=cost(
            4 * slots * tokens * part * half, 2 * slots * part * (2 * half + tokens)
        ),
        name="project",
    )(*moved, mine, other, *before)


def gather_ctx(rows):
    count = lax.axis_size("ctx")

    def swapped(piece, distance):
        return lax.ppermute(piece, "ctx", [(i, i ^ distance) for i in range(count)])

    order = list(range(0, count, 2))
    pieces = [rows] + [swapped(rows, distance) for distance in order[1:]]
    within = [swapped(piece, 1) for piece in pieces]
    return pieces, within, order + [i ^ 1 for i in order]


def stride_general(queries, keys, values):
    tokens_dev, width = queries.shape
    heads = width // HEAD_SIZE
    ctx = lax.axis_size("ctx")
    copies = max(ctx // STRIDE, 1)
    rows = tokens_dev // STRIDE
    held_rows = ctx * rows // copies
    own_copy = lax.axis_index("ctx") // STRIDE
    query_pos = (jnp.arange(held_rows) // (rows // copies)) * rows
    query_pos = query_pos + (jnp.arange(held_rows) % (rows // copies)) * copies + own_copy
    shaped = queries.reshape(1, rows // copies, ctx, width)
    query = lax.all_to_all(shaped, "ctx", split_axis=2, concat_axis=1, tiled=True)
    query = query.reshape(held_rows, heads, HEAD_SIZE)
    both = jnp.stack([keys, values]).reshape(2, rows, 1, STRIDE, width)
    both = jnp.broadcast_to(both, (2, rows, copies, STRIDE, width)).reshape(2, rows, ctx, width)
    both = lax.all_to_all(both, "ctx", split_axis=2, concat_axis=1, tiled=True)
    both = both.reshape(2, ctx * rows, heads, HEAD_SIZE)
    allowed = jnp.arange(ctx * rows)[None, :] <= query_pos[:, None]

    def one_head(operands):
        head_query, head_keys, head_values = operands
        masked = jnp.where(allowed, scores(head_query, head_keys), BIG_NEG)
        return weighted([masked], [with_ones(head_values)])

    result = lax.map(
        one_head,
        (query.transpose(1, 0, 2), both[0].transpose(1, 0, 2), both[1].transpose(1, 0, 2)),
    )
    result = result.transpose(1, 0, 2).reshape(ctx, rows // copies, 1, width).astype(BF16)
    back = lax.all_to_all(result, "ctx", split_axis=0, concat_axis=2, tiled=True)
    return back.reshape(tokens_dev, width)


def body(queries, keys, values, out_weight, chunks):
    tokens_dev, width = queries.shape
    ctx = lax.axis_size("ctx")
    groups = lax.axis_size("head")
    place = lax.axis_index("ctx")
    place_word = place.astype(jnp.int32).reshape(1)
    sibling = [(i, i ^ 1) for i in range(ctx)]

    part = width // chunks
    seat = lax.axis_index("head").astype(jnp.int32)

    def exchange(slabs, axis):
        count = len(slabs)
        moved = [slabs[0]]
        for slot in range(1, count):
            pairs = [(i, partner(i, slot, count)) for i in range(count)]
            moved.append(lax.ppermute(slabs[slot], axis, pairs))
        return moved

    weight_half = cut(out_weight)
    mine = lax.all_gather(weight_half, "head", axis=0)
    rim, picked = edges(keys, values, (weight_half,))
    between, within, order = gather_ctx(picked)
    summary = between + within
    if ctx > STRIDE:
        stride_out = stride_general(queries, keys, values)
        sends = []
    else:
        sends = [prepare(queries, keys, values, ctx, 0, chunks, (weight_half,))]
    (rim,) = after([rim], (*between[1:], *sends))
    if sends:
        sends = list(after(sends, (rim,)))
    before = lax.ppermute(rim, "ctx", [(i, i + 1) for i in range(ctx - 1)])
    for chunk in range(len(sends), chunks * len(sends)):
        sends.append(prepare(queries, keys, values, ctx, chunk, chunks, within[-1:]))

    def home(chunk, waits):
        return home_sections(
            place_word, queries, keys, values, before, summary, order, chunk, chunks, waits
        )


    moved, waits = [], ()
    if ctx > STRIDE:
        for chunk in range(chunks):
            lanes = slice(chunk * part, (chunk + 1) * part)
            homes, mark = home(chunk, waits)
            attended = (homes + stride_out[:, lanes].astype(F32)).astype(BF16)
            attended = attended.reshape(groups, tokens_dev // groups, part)
            owners = [partner(seat, slot, groups) for slot in range(groups)]
            moved.append(exchange([attended[owner] for owner in owners], "head"))
            waits = (mark,)
    else:
        sections, mark = home(0, ())
        homes, backs, waits = [sections], [], ()
        if chunks > 1:
            sends[1:] = list(after(sends[1:], (mark,)))
        for chunk, send in enumerate(sends):
            received = lax.all_to_all(send, "ctx", split_axis=0, concat_axis=0, tiled=True)
            beside = chunk < chunks - 1
            *slabs, mark = stride_attend(place_word, received, beside, waits)
            if beside:
                backs.append(exchange(slabs, "ctx"))
            else:
                back = lax.all_to_all(slabs[0], "ctx", split_axis=0, concat_axis=0, tiled=True)
                backs.append([back])
            waits = (mark,)
            for later in range(1, chunks) if chunk == 0 else ():
                sections, mark = home(later, waits)
                homes.append(sections)
                waits = (mark,)
        for chunk in range(chunks):
            *slabs, mark = combine(homes[chunk], backs[chunk], groups, ctx, waits)
            moved.append(exchange(slabs, "head"))
            waits = (mark, *moved[-1][1:3])
    (held,) = after([mine], (mark,))
    other = lax.ppermute(held, "ctx", sibling)
    total = ()
    for chunk in range(chunks):
        dtype = BF16 if chunk == chunks - 1 else F32
        total = (project(moved[chunk], held, other, chunk, total, dtype),)
    return total[0]


def solution(mesh):
    chunks = 2 if HEADS // mesh.shape["head"] > 1 else 1
    placed = (P("ctx", "head"), P("ctx", "head"), P("ctx", "head"), P("head", None))
    return jax.shard_map(
        functools.partial(body, chunks=chunks),
        mesh=mesh,
        in_specs=placed,
        out_specs=P(("ctx", "head"), None),
        check_vma=False,
    )
```
